128 devices in a mesh: img: 8 (over z, x_lo), txt: 16 (over x_hi, y, core).
Axes of the slice: x: 4 (x_hi: 2, x_lo: 2; x = x_hi * 2 + x_lo), y: 4, z: 4, core: 2. Of those that a mesh axis runs over, the one named last changes fastest.
Arguments:
- image_feat: bfloat16 [16384, 1152], P(('img', 'txt')), may hold values from -6 to 6
- text_feat: bfloat16 [16384, 1152], P(('img', 'txt')), may hold values from -6 to 6
- image_head: bfloat16 [1152, 1152], replicated, may hold values from -0.1875 to 0.1875
- text_head: bfloat16 [1152, 1152], replicated, may hold values from -0.1875 to 0.1875
- group_bias: float32 [32], replicated, may hold values from -6 to -4
- text_lang: int32 [16384], P(('img', 'txt')), may hold values from 0 to 31
- partner: int32 [16384], P(('img', 'txt')), may hold values from 0 to 16383, each once
Outputs:
- image_grad: float32 [16384, 1152], P(('img', 'txt'))
- text_grad: float32 [16384, 1152], P(('img', 'txt'))
- image_head_grad: float32 [1152, 1152], P(('img', 'txt'))
- text_head_grad: float32 [1152, 1152], P(('img', 'txt'))
The draws below stay inside these ranges and needn't reach their ends.
Inputs may be any that keep to these rules, and one draw needn't show every extreme that they name: partner names every image exactly once.
All inputs are finite; a program needn't handle non-finite values.
Results may differ from the reference program's by a relative error of at most 0.02.
Values may be sent and summed in bfloat16 or wider, within the bound.
No kernel may reach another device: no remote copies, remote signals or barrier semaphores. Data moves between devices by JAX's collectives and lax.ppermute only.
A program may use at most 128 MiB of HBM per device.

```python
import math
import jax
import jax.numpy as jnp
import numpy as np
from jax import lax

D = 1152
GROUPS = 32
BATCH = 16384


def set_ends(entries, key, least, high):
    longest = entries.shape.index(max(entries.shape))
    spots = []
    for shift in (0, 1):
        where = [jax.random.randint(jax.random.fold_in(key, axis), (), 0, length) for axis, length in enumerate(entries.shape)]
        where[longest] = (where[longest] + shift) % entries.shape[longest]
        spots.append(tuple(where))
    return entries.at[spots[0]].set(least).at[spots[1]].set(high)


def block_scale(own_key, dims, shards, low, largest):
    level = 1.0
    for axis_at, blocks in shards:
        heights = jax.random.uniform(jax.random.fold_in(jax.random.fold_in(own_key, 6), axis_at), (blocks,), jnp.float32, low / len(shards), largest / len(shards))
        level = level * jnp.repeat(jnp.exp(heights), dims[axis_at] // blocks).reshape((-1,) + (1,) * (len(dims) - 1 - axis_at))
    return level


def rank_bounds(amount, slope):
    portions = [(1 << 20) // math.isqrt(grade ** slope) + 1 for grade in range(1, amount + 1)]
    spread = 1 + sum(portions) // (1 << 30)
    return np.cumsum(np.array([max(1, weight // spread) for weight in portions]))


def skewed_ids(rng, extent, count, skew):
    table = rank_bounds(count, skew)
    ticket = jax.random.randint(jax.random.fold_in(rng, 1), extent, 0, int(table[count - 1]))
    grade = jnp.searchsorted(jnp.asarray(table, jnp.int32), ticket, side="right")
    return jax.random.permutation(jax.random.fold_in(rng, 2), count)[grade].astype(jnp.int32)


def scatter_about(stream_key, extent, spread, limit, cuts=(), kind=jnp.bfloat16):
    values = spread * jax.random.normal(stream_key, extent, jnp.float32)
    if cuts:
        values = values * block_scale(stream_key, extent, cuts, -0.22, 0.18)
    return jnp.clip(values, -limit, limit).astype(kind)


def setup_inputs(seed: int = 0) -> dict:
    arg_keys = jax.random.split(jax.random.key(seed), 8)
    return {
        "image_feat": scatter_about(arg_keys[0], (BATCH, D), 1.0, 6.0, ((0, 128),)),
        "text_feat": scatter_about(arg_keys[1], (BATCH, D), 1.0, 6.0, ((0, 128),)),
        "image_head": scatter_about(arg_keys[2], (D, D), D ** -0.5, 0.1875),
        "text_head": scatter_about(arg_keys[3], (D, D), D ** -0.5, 0.1875),
        "group_bias": jnp.clip(jax.random.uniform(arg_keys[4], (GROUPS,), jnp.float32, -6.0, -4.0), -6.0, -4.0),
        "text_lang": set_ends(skewed_ids(arg_keys[5], (BATCH,), GROUPS, 2), jax.random.fold_in(arg_keys[5], 3), 0, GROUPS - 1).astype(jnp.int32),
        "partner": jax.random.permutation(arg_keys[6], BATCH).astype(jnp.int32),
    }


logit_scale = 64.0
epsilon = 1e-06

def unit_rows(features, head):
    projected = jnp.dot(features, head, preferred_element_type=jnp.float32)
    row_norm = jnp.sqrt(lax.optimization_barrier(jnp.sum(projected * projected, axis=1, keepdims=True)) + epsilon)
    return (projected, row_norm, (projected / row_norm).astype(jnp.bfloat16))

def back_norm(projected, row_norm, upstream):
    inner = lax.optimization_barrier(jnp.sum(projected * upstream, axis=1, keepdims=True)) / (row_norm * row_norm)
    return ((upstream - projected * inner) / row_norm).astype(jnp.bfloat16)

def reference(image_feat, text_feat, image_head, text_head, group_bias, text_lang, partner):
    proj_img, norm_img, unit_img = unit_rows(image_feat, image_head)
    proj_txt, norm_txt, unit_txt = unit_rows(text_feat, text_head)
    groups = group_bias.shape[0]
    is_group = text_lang[:, None] == jnp.arange(groups).astype(jnp.int32)[None, :]
    text_bias = lax.optimization_barrier(jnp.sum(jnp.where(is_group, group_bias[None, :], 0.0), axis=1))
    total_rows = image_feat.shape[0]
    block_rows = math.gcd(total_rows, 1024)
    blocks = total_rows // block_rows
    image_blocks = unit_img.reshape(blocks, block_rows, -1)
    image_index = jnp.arange(total_rows).astype(jnp.int32).reshape(blocks, block_rows)

    def one_block(text_acc, inputs):
        block_units, block_index = inputs
        scores = logit_scale * jnp.dot(block_units, unit_txt.T, preferred_element_type=jnp.float32) + text_bias[None, :]
        positive = (partner[None, :] == block_index[:, None]).astype(jnp.float32)
        slopes = (jax.nn.sigmoid(scores) - positive).astype(jnp.bfloat16)
        image_part = logit_scale * jnp.dot(slopes, unit_txt, preferred_element_type=jnp.float32)
        text_acc = text_acc + logit_scale * jnp.dot(slopes.T, block_units, preferred_element_type=jnp.float32)
        return (text_acc, image_part)
    text_up, image_up = lax.scan(one_block, jnp.zeros(unit_txt.shape, jnp.float32), (image_blocks, image_index))
    image_up = image_up.reshape(total_rows, -1)
    grad_img = back_norm(proj_img, norm_img, image_up)
    grad_txt = back_norm(proj_txt, norm_txt, text_up)
    image_grad = jnp.dot(grad_img, image_head.T, preferred_element_type=jnp.float32)
    text_grad = jnp.dot(grad_txt, text_head.T, preferred_element_type=jnp.float32)
    image_head_grad = jnp.dot(image_feat.T, grad_img, preferred_element_type=jnp.float32)
    text_head_grad = jnp.dot(text_feat.T, grad_txt, preferred_element_type=jnp.float32)
    return (image_grad, text_grad, image_head_grad, text_head_grad)
```

```python
import jax
import jax.numpy as jnp
from jax import lax
from jax.sharding import PartitionSpec as P

logit_scale = 64.0
epsilon = 1e-06
AXES = ("img", "txt")

SLOTS = ((2, 1), (2, 0), (1, 1), (3, 1), (1, 0), (3, 0), (0, 1), (0, 0))


def places():
    return [
        (z, lo, hi, y, c)
        for z in range(4)
        for lo in range(2)
        for hi in range(2)
        for y in range(4)
        for c in range(2)
    ]


def flat(z, lo, hi, y, c):
    return (z * 2 + lo) * 16 + hi * 8 + y * 2 + c


def img_move(d, e):
    return lambda z, lo, hi, y, c: ((z + d) % 4, lo ^ e, hi, y, c)


def txt_move(d, e):
    return lambda z, lo, hi, y, c: (z, lo ^ e, hi ^ e, (y + d) % 4, c)


def core_move(z, lo, hi, y, c):
    return (z, lo, hi, y, 1 - c)


def fold_move(d, e):
    return lambda z, lo, hi, y, c: ((z - d) % 4, lo, hi ^ e, (y + d) % 4, c)


def send(block, move):
    return lax.ppermute(block, AXES, [(flat(*p), flat(*move(*p))) for p in places()])


def gather_group(own, move):
    half = own.shape[0] // 2
    from_prev = send(own, move(1, 0))
    from_next = send(own, move(3, 0))
    across = send(own, move(0, 1))
    far_low = send(from_prev[:half], move(1, 0))
    far_high = send(from_next[half:], move(3, 0))
    across_prev = send(across, move(1, 0))
    across_next = send(across, move(3, 0))
    far = jnp.concatenate([far_low, far_high], axis=0)
    across_far = send(far, move(0, 1))
    return [across_far, far, across_next, across_prev, from_next, from_prev, across, own]


def reduce_group(pieces, move):
    b16 = jnp.bfloat16
    cut = 80 if pieces[0].shape[0] == 144 else pieces[0].shape[0] // 2
    far = pieces[1] + send(pieces[0].astype(b16), move(0, 1)).astype(jnp.float32)
    far = far.astype(b16)
    low = send(far[:cut], move(1, 0)).astype(jnp.float32)
    high = send(far[cut:], move(3, 0)).astype(jnp.float32)
    across_a = send(pieces[2].astype(b16), move(1, 0)).astype(jnp.float32)
    across_b = send(pieces[3].astype(b16), move(3, 0)).astype(jnp.float32)
    to_next = jnp.concatenate([pieces[4][:cut] + low, pieces[4][cut:]], axis=0)
    to_prev = jnp.concatenate([pieces[5][:cut], pieces[5][cut:] + high], axis=0)
    across = pieces[6] + across_a + across_b
    got = [
        send(to_next.astype(b16), move(1, 0)),
        send(to_prev.astype(b16), move(3, 0)),
        send(across.astype(b16), move(0, 1)),
    ]
    total = pieces[7]
    for block in got:
        total = total + block.astype(jnp.float32)
    return total


def sum_group(vector, move):
    total = vector
    for d, e in SLOTS[:-1]:
        total = total + send(vector, move(d, e))
    return total


def swap_group(blocks, move):
    got = {}
    for (d, e), block in zip(SLOTS, blocks):
        source = (-d % 4, e)
        got[source] = block if (d, e) == (0, 0) else send(block, move(d, e))
    return [got[s] for s in SLOTS]


def unit_columns(feats, head):
    projected = lax.dot_general(
        head, feats, (((0,), (1,)), ((), ())), preferred_element_type=jnp.float32
    )
    norm = jnp.sqrt(jnp.sum(projected * projected, axis=0, keepdims=True) + epsilon)
    return projected, norm, (projected / norm).astype(jnp.bfloat16)


def pair_tile(unit_img, unit_txt, image_ids, bias, partner):
    cosines = logit_scale * lax.dot_general(
        unit_img, unit_txt, (((0,), (0,)), ((), ())), preferred_element_type=jnp.float32
    )
    positive = (partner[None, :] == image_ids[:, None]).astype(jnp.float32)
    slopes = (jax.nn.sigmoid(cosines + bias[None, :]) - positive).astype(jnp.bfloat16)
    weighted = slopes.astype(jnp.float32) * cosines
    return slopes, jnp.sum(weighted, axis=1), jnp.sum(weighted, axis=0)


def shards(image_feat, text_feat, image_head, text_head, group_bias, text_lang, partner):
    f32, b16 = jnp.float32, jnp.bfloat16
    rows, width = image_feat.shape
    slab = width // 8
    img_place = lax.axis_index("img")
    txt_place = lax.axis_index("txt")
    z, lo = img_place // 2, img_place % 2
    hi, y, core = txt_place // 8, txt_place // 2 % 4, txt_place % 2

    is_group = text_lang[:, None] == jnp.arange(group_bias.shape[0], dtype=jnp.int32)[None, :]
    text_bias = jnp.sum(jnp.where(is_group, group_bias[None, :], 0.0), axis=1)
    meta = jnp.stack([text_bias, partner.astype(f32)])

    img_blocks = gather_group(image_feat, img_move)
    txt_blocks = gather_group(text_feat, txt_move)
    img_order = [(z + d) % 4 * 2 + (lo + e) % 2 for d, e in SLOTS]
    txt_order = [(y + d) % 4 * 2 + (hi + e) % 2 for d, e in SLOTS]

    def in_order(blocks, order, axis):
        shape = list(blocks[0].shape)
        shape[axis] *= 8
        whole = jnp.zeros(shape, blocks[0].dtype)
        for block, place in zip(blocks, order):
            whole = lax.dynamic_update_slice_in_dim(whole, block, place * rows, axis=axis)
        return whole

    meta_own = [send(meta, txt_move(-d % 4, e)) for d, e in SLOTS[:-1]] + [meta]
    meta_own = in_order(meta_own, txt_order, 1)
    meta_other = send(meta_own, core_move)

    slot_block = [(z + y + d) % 4 * 2 + (lo + e) % 2 for d, e in SLOTS]

    def by_slot(head):
        return jnp.concatenate(
            [lax.dynamic_slice_in_dim(head, b * slab, slab, axis=1) for b in slot_block], axis=1
        )

    image_head = by_slot(image_head)
    text_head = by_slot(text_head)
    index = jnp.arange(8 * rows, dtype=jnp.int32)
    image_ids = ((index // rows * 16 + txt_place) * rows + index % rows).astype(f32)

    img_feats = in_order(img_blocks, img_order, 0)
    txt_feats = in_order(txt_blocks, txt_order, 0)
    proj_txt, norm_txt, unit_txt = unit_columns(txt_feats, text_head)
    other_txt = send(unit_txt, core_move)
    proj_img, norm_img, unit_img = unit_columns(img_feats, image_head)

    slopes, img_sum, txt_sum = pair_tile(unit_img, unit_txt, image_ids, meta_own[0], meta_own[1])
    other_slopes, other_img_sum, other_txt_sum = pair_tile(
        unit_img, other_txt, image_ids, meta_other[0], meta_other[1]
    )
    txt_sum = txt_sum + send(other_txt_sum, core_move)
    img_sum = sum_group(img_sum + other_img_sum, img_move)
    txt_sum = sum_group(txt_sum, txt_move)

    other_up = lax.dot_general(
        unit_img, other_slopes, (((1,), (0,)), ((), ())), preferred_element_type=f32
    ).astype(b16)
    back_up = send(other_up, core_move)

    img_pieces, txt_pieces = [], []
    for part in range(4):
        span = slice(part * 2 * slab, (part + 1) * 2 * slab)
        up = lax.dot_general(
            unit_txt[span], slopes, (((1,), (1,)), ((), ())), preferred_element_type=f32
        ) + lax.dot_general(
            other_txt[span], other_slopes, (((1,), (1,)), ((), ())), preferred_element_type=f32
        )
        img_pieces += [up[:slab], up[slab:]]
        up = lax.dot_general(
            unit_img[span], slopes, (((1,), (0,)), ((), ())), preferred_element_type=f32
        ) + back_up[span].astype(f32)
        txt_pieces += [up[:slab], up[slab:]]
    image_up = logit_scale * reduce_group(img_pieces, img_move)
    text_up = logit_scale * reduce_group(txt_pieces, txt_move)

    def back_norm(projected, norm, upstream, inner):
        return ((upstream - projected[-slab:] * (inner / norm)) / norm).astype(b16)

    grad_img = back_norm(proj_img, norm_img, image_up, img_sum[None, :])
    grad_txt = back_norm(proj_txt, norm_txt, text_up, txt_sum[None, :])

    def feature_grad(grad, head, move, order):
        blocks = [lax.dynamic_slice_in_dim(grad, s * rows, rows, axis=1) for s in order]
        whole = jnp.concatenate(swap_group(blocks, move), axis=0)
        return lax.dot_general(whole, head, (((0,), (1,)), ((), ())), preferred_element_type=f32)

    image_grad = feature_grad(grad_img, image_head, img_move, img_order)
    text_grad = feature_grad(grad_txt, text_head, txt_move, txt_order)

    def head_part(feats, grad):
        return lax.dot_general(feats, grad, (((0,), (1,)), ((), ())), preferred_element_type=f32)

    part = jnp.concatenate([head_part(img_feats, grad_img), head_part(txt_feats, grad_txt)], axis=1)
    out_rows = width // 128
    part = part.reshape(8, 8, 2, out_rows, 2 * slab).transpose(2, 1, 0, 3, 4)
    part = part.reshape(2, 8, 8 * out_rows, 2 * slab)
    mine = lax.dynamic_index_in_dim(part, core, 0, keepdims=False)
    theirs = lax.dynamic_index_in_dim(part, 1 - core, 0, keepdims=False)
    part = mine + send(theirs.astype(b16), core_move).astype(f32)
    head_sum = None
    for e in range(2):
        for d in range(4):
            block = lax.dynamic_index_in_dim(part, (hi + e) % 2 * 4 + (y + d) % 4, 0, keepdims=False)
            if (d, e) != (0, 0):
                block = send(block.astype(b16), fold_move(d, e)).astype(f32)
            head_sum = block if head_sum is None else head_sum + block
    head_sum = head_sum.reshape(8, out_rows, 2 * slab)
    blocks = [lax.dynamic_index_in_dim(head_sum, s, 0, keepdims=False) for s in img_order]
    got = jnp.stack(swap_group(blocks, img_move))
    slot_of = {s: n for n, s in enumerate(SLOTS)}
    table = jnp.array([[slot_of[(d, e)] for e in range(2)] for d in range(4)], jnp.int32)
    ordered = [
        lax.dynamic_index_in_dim(got, table[(b // 2 - z - y) % 4, (b % 2 + lo) % 2], 0, keepdims=False)
        for b in range(8)
    ]
    image_head_grad = jnp.concatenate([block[:, :slab] for block in ordered], axis=1)
    text_head_grad = jnp.concatenate([block[:, slab:] for block in ordered], axis=1)
    return (image_grad, text_grad, image_head_grad, text_head_grad)


def solution(mesh):
    rows = P(("img", "txt"), None)
    row = P(("img", "txt"))
    in_specs = (rows, rows, P(), P(), P(), row, row)
    return jax.shard_map(
        shards, mesh=mesh, in_specs=in_specs, out_specs=(rows,) * 4, check_vma=False
    )
```

```python
import jax
import jax.numpy as jnp
from jax import lax
from jax.sharding import PartitionSpec as P

logit_scale = 64.0
epsilon = 1e-06

PLACE = ("z", "lo", "hi", "y", "core")
IMG = ("z", "lo")
TXT = ("hi", "y")


def exchange(blocks, axes):
    return lax.all_to_all(blocks, axes, 0, 0, tiled=True)


def gather(own, axes):
    blocks = jnp.broadcast_to(own[None], (8,) + own.shape)
    return exchange(blocks, axes).reshape((8 * own.shape[0],) + own.shape[1:])


def core_swap(block):
    return lax.ppermute(block, "core", [(0, 1), (1, 0)])


def unit_columns(feats, head):
    projected = lax.dot_general(
        head, feats, (((0,), (1,)), ((), ())), preferred_element_type=jnp.float32
    )
    norm = jnp.sqrt(jnp.sum(projected * projected, axis=0, keepdims=True) + epsilon)
    return projected, norm, (projected / norm).astype(jnp.bfloat16)


def pair_tile(unit_img, unit_txt, image_ids, bias, partner):
    cosines = logit_scale * lax.dot_general(
        unit_img, unit_txt, (((0,), (0,)), ((), ())), preferred_element_type=jnp.float32
    )
    positive = (partner[None, :] == image_ids[:, None]).astype(jnp.float32)
    slopes = (jax.nn.sigmoid(cosines + bias[None, :]) - positive).astype(jnp.bfloat16)
    weighted = slopes.astype(jnp.float32) * cosines
    return slopes, jnp.sum(weighted, axis=1), jnp.sum(weighted, axis=0)


def shards(image_feat, text_feat, image_head, text_head, group_bias, text_lang, partner):
    f32, b16 = jnp.float32, jnp.bfloat16
    rows, width = image_feat.shape
    slab = width // 8
    out_rows = width // 128
    core = lax.axis_index("core")
    img_place = lax.axis_index(IMG)
    txt_place = lax.axis_index(TXT)

    is_group = text_lang[:, None] == jnp.arange(group_bias.shape[0], dtype=jnp.int32)[None, :]
    text_bias = jnp.sum(jnp.where(is_group, group_bias[None, :], 0.0), axis=1)
    meta = jnp.stack([text_bias, partner.astype(f32)])
    meta = lax.all_gather(meta, TXT + ("core",), axis=0, tiled=False)
    meta = meta.reshape(8, 2, 2, rows).transpose(1, 2, 0, 3).reshape(2, 2, 8 * rows)

    txt_feats = gather(text_feat, TXT)
    img_feats = gather(image_feat, IMG)

    index = jnp.arange(8 * rows, dtype=jnp.int32)
    image_ids = index // rows * 16 + txt_place * 2 + core
    image_ids = (image_ids * rows + index % rows).astype(f32)

    proj_txt, norm_txt, unit_txt = unit_columns(txt_feats, text_head)
    other_txt = core_swap(unit_txt)
    proj_img, norm_img, unit_img = unit_columns(img_feats, image_head)

    mine = lax.dynamic_index_in_dim(meta, core, 0, keepdims=False)
    theirs = lax.dynamic_index_in_dim(meta, 1 - core, 0, keepdims=False)
    slopes, img_sum, txt_sum = pair_tile(unit_img, unit_txt, image_ids, mine[0], mine[1])
    other_slopes, other_img_sum, other_txt_sum = pair_tile(
        unit_img, other_txt, image_ids, theirs[0], theirs[1]
    )
    other_up = lax.dot_general(
        unit_img, other_slopes, (((1,), (0,)), ((), ())), preferred_element_type=f32
    ).astype(b16)
    back_up = core_swap(other_up)

    img_sum = lax.psum(img_sum + other_img_sum, IMG)
    txt_sum = lax.psum(txt_sum + core_swap(other_txt_sum), TXT)

    image_up = lax.dot_general(
        unit_txt, slopes, (((1,), (1,)), ((), ())), preferred_element_type=f32
    ) + lax.dot_general(
        other_txt, other_slopes, (((1,), (1,)), ((), ())), preferred_element_type=f32
    )
    image_up = exchange(image_up.astype(b16).reshape(8, slab, 8 * rows), IMG)
    text_up = lax.dot_general(
        unit_img, slopes, (((1,), (0,)), ((), ())), preferred_element_type=f32
    ) + back_up.astype(f32)
    text_up = exchange(text_up.astype(b16).reshape(8, slab, 8 * rows), TXT)

    def back_norm(projected, norm, upstream, inner, place):
        upstream = logit_scale * jnp.sum(upstream.astype(f32), axis=0)
        projected = lax.dynamic_slice_in_dim(projected, place * slab, slab, axis=0)
        return ((upstream - projected * (inner[None, :] / norm)) / norm).astype(b16)

    grad_img = back_norm(proj_img, norm_img, image_up, img_sum, img_place)
    grad_txt = back_norm(proj_txt, norm_txt, text_up, txt_sum, txt_place)

    def feature_grad(grad, head, axes):
        blocks = grad.reshape(slab, 8, rows).transpose(1, 0, 2)
        whole = exchange(blocks, axes).reshape(width, rows)
        return lax.dot_general(whole, head, (((0,), (1,)), ((), ())), preferred_element_type=f32)

    image_grad = feature_grad(grad_img, image_head, IMG)
    text_grad = feature_grad(grad_txt, text_head, TXT)

    def head_part(feats, grad):
        return lax.dot_general(feats, grad, (((0,), (1,)), ((), ())), preferred_element_type=f32)

    part = jnp.concatenate([head_part(img_feats, grad_img), head_part(txt_feats, grad_txt)], axis=1)
    part = exchange(part.astype(b16).reshape(128, out_rows, 2 * slab), PLACE).astype(f32)
    part = part.reshape(8, 8, 2, out_rows, 2 * slab)
    image_head_grad = jnp.sum(part[..., :slab], axis=(1, 2))
    text_head_grad = jnp.sum(part[..., slab:], axis=(0, 2))
    image_head_grad = image_head_grad.transpose(1, 0, 2).reshape(out_rows, width)
    text_head_grad = text_head_grad.transpose(1, 0, 2).reshape(out_rows, width)
    return (image_grad, text_grad, image_head_grad, text_head_grad)


def solution(mesh):
    places = jax.sharding.Mesh(mesh.devices.reshape(4, 2, 2, 4, 2), PLACE)
    rows = P(PLACE, None)
    row = P(PLACE)
    in_specs = (rows, rows, P(), P(), P(), row, row)
    return jax.shard_map(
        shards, mesh=places, in_specs=in_specs, out_specs=(rows,) * 4, check_vma=False
    )
```

```python
import jax
import jax.numpy as jnp
from jax import lax
from jax.sharding import PartitionSpec as P

logit_scale = 64.0
epsilon = 1e-06
f32, b16 = jnp.float32, jnp.bfloat16

DEV = "dev"
PLACES = [
    (z, lo, hi, y, c)
    for z in range(4)
    for lo in range(2)
    for hi in range(2)
    for y in range(4)
    for c in range(2)
]


def flat(z, lo, hi, y, c):
    return (z * 2 + lo) * 16 + hi * 8 + y * 2 + c


def img_move(d, e):
    return lambda z, lo, hi, y, c: ((z + d) % 4, lo ^ e, hi, y, c)


def txt_move(d, e):
    return lambda z, lo, hi, y, c: (z, lo ^ e, hi ^ e, (y + d) % 4, c)


def core_move(z, lo, hi, y, c):
    return (z, lo, hi, y, 1 - c)


IMG_GROUPS = [
    [flat(z, lo, hi, y, c) for z in range(4) for lo in range(2)]
    for hi in range(2)
    for y in range(4)
    for c in range(2)
]
TXT_GROUPS = [
    [flat(z, hi ^ b, hi, y, c) for y in range(4) for hi in range(2)]
    for z in range(4)
    for b in range(2)
    for c in range(2)
]
TXT_CORE_GROUPS = [
    [flat(z, hi ^ b, hi, y, c) for c in range(2) for y in range(4) for hi in range(2)]
    for z in range(4)
    for b in range(2)
]
CHIP_GROUPS = [[flat(*p) for p in PLACES if p[4] == c] for c in range(2)]


def send(block, move):
    return lax.ppermute(block, DEV, [(flat(*p), flat(*move(*p))) for p in PLACES])


def exchange(blocks, groups):
    return lax.all_to_all(blocks, DEV, 0, 0, axis_index_groups=groups, tiled=True)


def rows_of(array, place, size):
    return lax.dynamic_slice_in_dim(array, place * size, size, axis=0)


def gather_pairs(own, move, second):
    across = send(own, move(0, 1))
    pair = jnp.concatenate([jnp.where(second, across, own), jnp.where(second, own, across)], axis=0)
    before = send(pair, move(1, 0))
    after = send(pair, move(3, 0))
    half = own.shape[0]
    far = [send(before[:half], move(1, 0)), send(after[half:], move(3, 0))]
    return [pair, after, jnp.concatenate(far, axis=0), before]


def in_order(blocks, place, axis):
    shape = list(blocks[0].shape)
    size = shape[axis]
    shape[axis] *= 4
    whole = jnp.zeros(shape, blocks[0].dtype)
    for d, block in enumerate(blocks):
        whole = lax.dynamic_update_slice_in_dim(whole, block, (place + d) % 4 * size, axis=axis)
    return whole


def reduce_pairs(piece, move, second, slab):
    far = piece(2).astype(b16)
    low = send(far[:slab], move(1, 0)).astype(f32)
    high = send(far[slab:], move(3, 0)).astype(f32)
    after = piece(1)
    after = jnp.concatenate([after[:slab] + low, after[slab:]], axis=0)
    after = send(after.astype(b16), move(1, 0)).astype(f32)
    before = piece(3)
    before = jnp.concatenate([before[:slab], before[slab:] + high], axis=0)
    before = send(before.astype(b16), move(3, 0)).astype(f32)
    near = piece(0) + after + before
    across = rows_of(near.astype(b16), 1 - second, slab)
    return rows_of(near, second, slab) + send(across, move(0, 1)).astype(f32)


def unit_columns(feats, head):
    projected = lax.dot_general(head, feats, (((0,), (1,)), ((), ())), preferred_element_type=f32)
    norm = jnp.sqrt(jnp.sum(projected * projected, axis=0, keepdims=True) + epsilon)
    return (projected / norm).astype(b16), norm


def pair_tile(unit_img, unit_txt, image_ids, bias, partner):
    cosines = logit_scale * lax.dot_general(
        unit_img, unit_txt, (((0,), (0,)), ((), ())), preferred_element_type=f32
    )
    positive = (partner[None, :] == image_ids[:, None]).astype(f32)
    slopes = (jax.nn.sigmoid(cosines + bias[None, :]) - positive).astype(b16)
    weighted = slopes.astype(f32) * cosines
    return slopes, jnp.sum(weighted, axis=1), jnp.sum(weighted, axis=0)


def shards(image_feat, text_feat, image_head, text_head, group_bias, text_lang, partner):
    rows, width = image_feat.shape
    slab = width // 8
    out_rows = width // 128
    place = lax.axis_index(DEV)
    z, lo, hi, y, core = place // 32, place // 16 % 2, place // 8 % 2, place // 2 % 4, place % 2

    is_group = text_lang[:, None] == jnp.arange(group_bias.shape[0], dtype=jnp.int32)[None, :]
    text_bias = jnp.sum(jnp.where(is_group, group_bias[None, :], 0.0), axis=1)
    meta = jnp.stack([text_bias, partner.astype(f32)])

    img_chunks = gather_pairs(image_feat, img_move, lo)
    txt_chunks = gather_pairs(text_feat, txt_move, hi)
    meta = exchange(jnp.broadcast_to(meta[None], (16, 2, rows)), TXT_CORE_GROUPS)
    meta = meta.reshape(2, 8, 2, rows).transpose(0, 2, 1, 3).reshape(2, 2, 8 * rows)
    mine = lax.dynamic_index_in_dim(meta, core, 0, keepdims=False)
    theirs = lax.dynamic_index_in_dim(meta, 1 - core, 0, keepdims=False)

    index = jnp.arange(8 * rows, dtype=jnp.int32)
    image_ids = index // rows * 16 + place % 16
    image_ids = (image_ids * rows + index % rows).astype(f32)

    txt_units = [unit_columns(chunk, text_head) for chunk in txt_chunks]
    unit_txt = in_order([unit for unit, _ in txt_units], y, 1)
    norm_txt = in_order([norm for _, norm in txt_units], y, 1)
    other_txt = send(unit_txt, core_move)
    img_units = [unit_columns(chunk, image_head) for chunk in img_chunks]
    unit_img = in_order([unit for unit, _ in img_units], z, 1)
    norm_img = in_order([norm for _, norm in img_units], z, 1)

    slopes, img_sum, txt_sum = pair_tile(unit_img, unit_txt, image_ids, mine[0], mine[1])
    other_slopes, other_img_sum, other_txt_sum = pair_tile(
        unit_img, other_txt, image_ids, theirs[0], theirs[1]
    )
    other_up = lax.dot_general(
        unit_img, other_slopes, (((1,), (0,)), ((), ())), preferred_element_type=f32
    ).astype(b16)
    back_up = send(other_up, core_move)

    img_sum = jnp.broadcast_to((img_sum + other_img_sum).reshape(1, 8, rows), (8, 8, rows))
    img_sum = jnp.sum(exchange(img_sum, IMG_GROUPS), axis=0).reshape(1, 8 * rows)
    first = jnp.where(core == 0, txt_sum, other_txt_sum)
    last = jnp.where(core == 0, other_txt_sum, txt_sum)
    txt_sum = jnp.broadcast_to(jnp.stack([first, last])[:, None], (2, 8, 8 * rows))
    txt_sum = exchange(txt_sum.reshape(16, 8, rows), TXT_CORE_GROUPS)
    txt_sum = jnp.sum(txt_sum, axis=0).reshape(1, 8 * rows)

    def image_piece(d):
        at = (z + d) % 4
        return lax.dot_general(
            rows_of(unit_txt, at, 2 * slab), slopes, (((1,), (1,)), ((), ())),
            preferred_element_type=f32,
        ) + lax.dot_general(
            rows_of(other_txt, at, 2 * slab), other_slopes, (((1,), (1,)), ((), ())),
            preferred_element_type=f32,
        )

    def text_piece(d):
        at = (y + d) % 4
        return lax.dot_general(
            rows_of(unit_img, at, 2 * slab), slopes, (((1,), (0,)), ((), ())),
            preferred_element_type=f32,
        ) + rows_of(back_up, at, 2 * slab).astype(f32)

    image_up = reduce_pairs(image_piece, img_move, lo, slab)
    text_up = reduce_pairs(text_piece, txt_move, hi, slab)

    def back_norm(unit, norm, upstream, inner, at):
        unit = rows_of(unit, at, slab).astype(f32)
        return ((logit_scale * upstream - unit * inner) / norm).astype(b16)

    grad_img = back_norm(unit_img, norm_img, image_up, img_sum, z * 2 + lo)
    grad_txt = back_norm(unit_txt, norm_txt, text_up, txt_sum, y * 2 + hi)

    def head_part(chunks, at, grad):
        feats = in_order(chunks, at, 0)
        return lax.dot_general(feats, grad, (((0,), (1,)), ((), ())), preferred_element_type=f32)

    part = jnp.concatenate(
        [head_part(img_chunks, z, grad_img), head_part(txt_chunks, y, grad_txt)], axis=1
    ).astype(b16)

    def rows_for(which):
        slot = jnp.arange(64 * 16, dtype=jnp.int32)
        row = (slot // 16 * 2 + which) * out_rows + slot % 16
        row = jnp.where(slot % 16 < out_rows, row, -1)
        pick = (jnp.arange(width, dtype=jnp.int32)[:, None] == row[None, :]).astype(b16)
        return lax.dot_general(pick, part, (((0,), (0,)), ((), ())), preferred_element_type=f32)

    theirs = send(rows_for(1 - core).astype(b16), core_move).astype(f32)
    part = (rows_for(core) + theirs).astype(b16).reshape(64, 16, 2 * slab)
    part = exchange(part, CHIP_GROUPS)[:, :out_rows].astype(f32)
    part = part.reshape(4, 2, 2, 4, out_rows, 2 * slab)

    def feature_grad(grad, head, groups):
        blocks = grad.reshape(slab, 8, rows).transpose(1, 0, 2)
        whole = exchange(blocks, groups).reshape(width, rows)
        return lax.dot_general(whole, head, (((0,), (1,)), ((), ())), preferred_element_type=f32)

    image_grad = feature_grad(grad_img, image_head, IMG_GROUPS)
    text_grad = feature_grad(grad_txt, text_head, TXT_GROUPS)

    image_head_grad = jnp.sum(part[..., :slab], axis=(2, 3))
    text_head_grad = jnp.sum(part[..., slab:], axis=(0, 1))
    image_head_grad = image_head_grad.transpose(2, 0, 1, 3).reshape(out_rows, width)
    text_head_grad = text_head_grad.transpose(2, 1, 0, 3).reshape(out_rows, width)
    return (image_grad, text_grad, image_head_grad, text_head_grad)


def solution(mesh):
    line = jax.sharding.Mesh(mesh.devices.reshape(-1), (DEV,))
    in_specs = (P(DEV, None), P(DEV, None), P(), P(), P(), P(DEV), P(DEV))
    return jax.shard_map(
        shards, mesh=line, in_specs=in_specs, out_specs=(P(DEV, None),) * 4, check_vma=False
    )
```

```python
import jax
import jax.numpy as jnp
from jax import lax
from jax.experimental import pallas as pl
from jax.experimental.pallas import tpu as pltpu
from jax.sharding import PartitionSpec as P

logit_scale = 64.0
epsilon = 1e-06
f32, b16 = jnp.float32, jnp.bfloat16

DEV = "dev"
PLACES = [
    (z, lo, hi, y, c)
    for z in range(4)
    for lo in range(2)
    for hi in range(2)
    for y in range(4)
    for c in range(2)
]


def flat(z, lo, hi, y, c):
    return (z * 2 + lo) * 16 + hi * 8 + y * 2 + c


def img_move(d, e):
    return lambda z, lo, hi, y, c: ((z + d) % 4, lo ^ e, hi, y, c)


def txt_move(d, e):
    return lambda z, lo, hi, y, c: (z, lo ^ e, hi ^ e, (y + d) % 4, c)


def core_move(z, lo, hi, y, c):
    return (z, lo, hi, y, 1 - c)


IMG_GROUPS = [
    [flat(z, lo, hi, y, c) for z in range(4) for lo in range(2)]
    for hi in range(2)
    for y in range(4)
    for c in range(2)
]
TXT_GROUPS = [
    [flat(z, hi ^ b, hi, y, c) for y in range(4) for hi in range(2)]
    for z in range(4)
    for b in range(2)
    for c in range(2)
]
TXT_CORE_GROUPS = [
    [flat(z, hi ^ b, hi, y, c) for c in range(2) for y in range(4) for hi in range(2)]
    for z in range(4)
    for b in range(2)
]
CHIP_GROUPS = [[flat(*p) for p in PLACES if p[4] == c] for c in range(2)]


def send(block, move):
    return lax.ppermute(block, DEV, [(flat(*p), flat(*move(*p))) for p in PLACES])


def exchange(blocks, groups):
    return lax.all_to_all(blocks, DEV, 0, 0, axis_index_groups=groups, tiled=True)


PAD = 16
NN = (((1,), (0,)), ((), ()))
NT = (((1,), (1,)), ((), ()))
TN = (((0,), (0,)), ((), ()))


def dot(a, b, dims):
    return lax.dot_general(a, b, dims, preferred_element_type=f32)


def call(body, out_shape, scalars, arrays, in_specs=None, out_specs=None, grid=(), scratch=(), cost=0):
    whole = pl.BlockSpec(memory_space=pltpu.VMEM)
    many = isinstance(out_shape, (list, tuple))
    if in_specs is None:
        in_specs = [whole] * len(arrays)
    if out_specs is None:
        out_specs = [whole] * len(out_shape) if many else whole
    spec = pltpu.PrefetchScalarGridSpec(
        num_scalar_prefetch=1,
        grid=grid,
        in_specs=in_specs,
        out_specs=out_specs,
        scratch_shapes=list(scratch),
    )
    moved = sum(a.size * a.dtype.itemsize for a in arrays)
    return pl.pallas_call(
        body,
        out_shape=out_shape,
        grid_spec=spec,
        compiler_params=pltpu.CompilerParams(vmem_limit_bytes=28 * 2**20),
        cost_estimate=pl.CostEstimate(flops=cost, bytes_accessed=moved, transcendentals=0),
    )(jnp.stack(scalars).astype(jnp.int32), *arrays)


def aligned(index, size):
    return pl.ds(pl.multiple_of(index * size, size), size)


def split_rows(total, lanes):
    high = total.astype(b16).astype(f32)
    row = lax.broadcasted_iota(jnp.int32, (PAD, lanes), 0)
    return jnp.where(row == 0, high, jnp.where(row == 1, total - high, 0.0)).astype(b16)


def joined(rows):
    return rows[0:1].astype(f32) + rows[1:2].astype(f32)


def unit_kernel(rows, extra, at_ref, *refs):
    chunks, (head, unit, norm, proj) = refs[:4], refs[4:]
    width = head.shape[0]
    step = width // 4
    pitch = rows + extra
    for d in range(4):
        place = (at_ref[0] + d) % 4
        lanes = aligned(place, 2 * rows)
        if extra:
            feats = jnp.concatenate([chunks[d][:rows], chunks[d][pitch : pitch + rows]], axis=0)
        else:
            feats = chunks[d][...]
        total = jnp.zeros((1, 2 * rows), f32)
        for m in range(4):
            part = dot(head[m * step : (m + 1) * step], feats, NT)
            proj[m * step : (m + 1) * step] = part
            total = total + jnp.sum(part * part, axis=0, keepdims=True)
        length = jnp.sqrt(total + epsilon)
        norm[:, lanes] = length
        for m in range(4):
            span = slice(m * step, (m + 1) * step)
            unit[span, lanes] = (proj[span] / length).astype(b16)
        if extra:
            for e in range(2):
                block = chunks[d][e * pitch + rows : (e + 1) * pitch, :rows]
                unit[width:, aligned(place * 2 + e, rows)] = block


def units(chunks, head, at, rows, extra):
    width = head.shape[0]
    return call(
        lambda *refs: unit_kernel(rows, extra, *refs),
        [
            jax.ShapeDtypeStruct((width + extra, 8 * rows), b16),
            jax.ShapeDtypeStruct((1, 8 * rows), f32),
        ],
        [at],
        [*chunks, head],
        scratch=[pltpu.VMEM((width, 2 * rows), f32)],
        cost=16 * rows * width * width,
    )


def slope_kernel(rows, groups, at_ref, bias_ref, img, txt, slopes, img_sum, txt_sum):
    width = img.shape[0]
    tile = img.shape[1]
    step = pl.program_id(0)
    index = step * tile + lax.broadcasted_iota(jnp.int32, (tile, 1), 0)
    ids = ((index // rows * 16 + at_ref[0]) * rows + index % rows).astype(f32)
    by_img = jnp.zeros((tile, min(128, tile)), f32)
    for t in range(txt.shape[1] // tile):
        lanes = slice(t * tile, (t + 1) * tile)
        lang = txt[width : width + PAD, lanes].astype(f32)
        partner = lang[1:2] * 128.0 + lang[2:3]
        lang = lang[0:1]
        bias = jnp.zeros((1, tile), f32)
        for g in range(groups):
            bias = jnp.where(lang == g, bias_ref[g], bias)
        cosines = logit_scale * dot(img[...], txt[:width, lanes], TN)
        gate = 1.0 / (1.0 + jnp.exp(-(cosines + bias)))
        slope = (gate - jnp.where(partner == ids, 1.0, 0.0)).astype(b16)
        slopes[:, lanes] = slope
        weighted = slope.astype(f32) * cosines
        down = jnp.sum(weighted, axis=0, keepdims=True)

        @pl.when(step == 0)
        def _():
            txt_sum[:, lanes] = down

        @pl.when(step != 0)
        def _():
            txt_sum[:, lanes] += down

        for k in range(0, tile, by_img.shape[1]):
            by_img = by_img + weighted[:, k : k + by_img.shape[1]]
    img_sum[...] = jnp.sum(by_img.T, axis=0, keepdims=True)


def slope_tile(img, txt, group_bias, place, rows):
    width, count = img.shape
    tile = 2 * rows
    return call(
        lambda *refs: slope_kernel(rows, group_bias.shape[0], *refs),
        [
            jax.ShapeDtypeStruct((count, count), b16),
            jax.ShapeDtypeStruct((1, count), f32),
            jax.ShapeDtypeStruct((1, count), f32),
        ],
        [place],
        [group_bias, img, txt],
        in_specs=[
            pl.BlockSpec(memory_space=pltpu.SMEM),
            pl.BlockSpec((width, tile), lambda i, at: (0, i)),
            pl.BlockSpec(txt.shape, lambda i, at: (0, 0)),
        ],
        out_specs=[
            pl.BlockSpec((tile, count), lambda i, at: (i, 0)),
            pl.BlockSpec((1, tile), lambda i, at: (0, i)),
            pl.BlockSpec((1, count), lambda i, at: (0, 0)),
        ],
        grid=(count // tile,),
        cost=2 * width * count * count,
    )


def other_kernel(at_ref, img, slopes, txt_sum, out):
    width = img.shape[0]
    step = width // 4
    for m in range(4):
        span = slice(m * step, (m + 1) * step)
        out[span] = dot(img[span], slopes[...], NN).astype(b16)
    out[width:] = split_rows(txt_sum[...], out.shape[1])


def other_up(img, slopes, txt_sum, rows):
    width, count = img.shape
    tile = 2 * rows
    return call(
        other_kernel,
        jax.ShapeDtypeStruct((width + PAD, count), b16),
        [jnp.int32(0)],
        [img, slopes, txt_sum],
        in_specs=[
            pl.BlockSpec((width, count), lambda i, at: (0, 0)),
            pl.BlockSpec((count, tile), lambda i, at: (0, i)),
            pl.BlockSpec((1, tile), lambda i, at: (0, i)),
        ],
        out_specs=pl.BlockSpec((width + PAD, tile), lambda i, at: (0, i)),
        grid=(count // tile,),
        cost=2 * width * count * count,
    )


def put_piece(out, piece, total):
    slab = piece.shape[0] // 2
    figures = split_rows(total, out.shape[1])
    for e in range(2):
        out[e * (slab + PAD) : e * (slab + PAD) + slab] = piece[e * slab : (e + 1) * slab].astype(b16)
        out[e * (slab + PAD) + slab : (e + 1) * (slab + PAD)] = figures


def image_kernel(at_ref, txt, other, slopes, other_slopes, total, other_total, out):
    piece = dot(txt[...], slopes[...], NT) + dot(other[...], other_slopes[...], NT)
    put_piece(out, piece, total[...] + other_total[...])


def text_kernel(at_ref, img, slopes, back, back_rows, total, out):
    piece = dot(img[...], slopes[...], NN) + back[...].astype(f32)
    put_piece(out, piece, total[...] + joined(back_rows))


def image_piece(at, txt, other, slopes, other_slopes, total, other_total, slab, rows):
    count = slopes.shape[0]
    tile = 2 * rows
    return call(
        image_kernel,
        jax.ShapeDtypeStruct((2 * (slab + PAD), count), b16),
        [at],
        [txt, other, slopes, other_slopes, total, other_total],
        in_specs=[
            pl.BlockSpec((2 * slab, count), lambda i, at: (at[0], 0)),
            pl.BlockSpec((2 * slab, count), lambda i, at: (at[0], 0)),
            pl.BlockSpec((tile, count), lambda i, at: (i, 0)),
            pl.BlockSpec((tile, count), lambda i, at: (i, 0)),
            pl.BlockSpec((1, tile), lambda i, at: (0, i)),
            pl.BlockSpec((1, tile), lambda i, at: (0, i)),
        ],
        out_specs=pl.BlockSpec((2 * (slab + PAD), tile), lambda i, at: (0, i)),
        grid=(count // tile,),
        cost=8 * slab * count * count,
    )


def text_piece(at, img, slopes, back, total, slab, rows):
    count = slopes.shape[0]
    tile = 2 * rows
    figures = 8 * slab // PAD
    return call(
        text_kernel,
        jax.ShapeDtypeStruct((2 * (slab + PAD), count), b16),
        [at],
        [img, slopes, back, back, total],
        in_specs=[
            pl.BlockSpec((2 * slab, count), lambda i, at: (at[0], 0)),
            pl.BlockSpec((count, tile), lambda i, at: (0, i)),
            pl.BlockSpec((2 * slab, tile), lambda i, at: (at[0], i)),
            pl.BlockSpec((PAD, tile), lambda i, at: (figures, i)),
            pl.BlockSpec((1, tile), lambda i, at: (0, i)),
        ],
        out_specs=pl.BlockSpec((2 * (slab + PAD), tile), lambda i, at: (0, i)),
        grid=(count // tile,),
        cost=4 * slab * count * count,
    )


def near_kernel(at_ref, *refs):
    pieces, (keep, keep_sum, give) = refs[:4], refs[4:]
    slab = keep.shape[0]
    sums = []
    for e in range(2):
        span = slice(e * (slab + PAD), e * (slab + PAD) + slab)
        tail = slice(e * (slab + PAD) + slab, (e + 1) * (slab + PAD))
        total = joined(pieces[0][tail])
        block = pieces[0][span].astype(f32)
        for piece in pieces[1:]:
            block = block + piece[span].astype(f32)
            total = total + joined(piece[tail])
        sums.append((block, total))
    own = at_ref[0] == 0
    keep[...] = jnp.where(own, sums[0][0], sums[1][0])
    keep_sum[...] = jnp.where(own, sums[0][1], sums[1][1])
    give[:slab] = jnp.where(own, sums[1][0], sums[0][0]).astype(b16)
    give[slab:] = split_rows(jnp.where(own, sums[1][1], sums[0][1]), give.shape[1])


def near(second, pieces, rows):
    height, count = pieces[0].shape
    tile = 2 * rows
    slab = height // 2 - PAD
    lanes = lambda i, at: (0, i)
    return call(
        near_kernel,
        [
            jax.ShapeDtypeStruct((slab, count), f32),
            jax.ShapeDtypeStruct((1, count), f32),
            jax.ShapeDtypeStruct((slab + PAD, count), b16),
        ],
        [second],
        pieces,
        in_specs=[pl.BlockSpec((height, tile), lanes)] * 4,
        out_specs=[
            pl.BlockSpec((slab, tile), lanes),
            pl.BlockSpec((1, tile), lanes),
            pl.BlockSpec((slab + PAD, tile), lanes),
        ],
        grid=(count // tile,),
    )


def grad_kernel(rows, extra, at_ref, keep, keep_sum, got, unit, norm, *refs):
    chunks, (own, give, part, grad) = refs[:4], refs[4:]
    slab = keep.shape[0]
    pitch = rows + extra
    up = logit_scale * (keep[...] + got[:slab].astype(f32))
    inner = keep_sum[...] + joined(got[slab:])
    grad[...] = ((up - unit[...].astype(f32) * inner) / norm[...]).astype(b16)
    second = at_ref[1]
    for ring in range(4):
        low = grad[:, (2 * ring) * rows : (2 * ring + 1) * rows]
        high = grad[:, (2 * ring + 1) * rows : (2 * ring + 2) * rows]
        own[ring] = jnp.where(second == 0, low, high)
        give[ring] = jnp.where(second == 0, high, low)
    total = None
    for d in range(4):
        place = (at_ref[0] + d) % 4
        for e in range(2):
            cols = grad[:, aligned(place * 2 + e, rows)]
            term = dot(cols, chunks[d][e * pitch : e * pitch + rows], NN)
            total = term if total is None else total + term
    part[...] = total.astype(b16)


def gradient(ring, second, keep, keep_sum, got, unit, norm, chunks, rows, extra):
    slab, count = keep.shape
    width = chunks[0].shape[1]
    whole = lambda a: pl.BlockSpec(a.shape, lambda i, at: (0,) * a.ndim)
    arrays = [keep, keep_sum, got, unit, norm, *chunks]
    specs = [whole(a) for a in arrays]
    specs[3] = pl.BlockSpec((slab, count), lambda i, at: (at[0] * 2 + at[1], 0))
    block = jax.ShapeDtypeStruct((4, slab, rows), b16)
    term = jax.ShapeDtypeStruct((slab, width), b16)
    return call(
        lambda *refs: grad_kernel(rows, extra, *refs),
        [block, block, term],
        [ring, second],
        arrays,
        in_specs=specs,
        out_specs=[whole(block), whole(block), whole(term)],
        grid=(1,),
        scratch=[pltpu.VMEM((slab, count), b16)],
        cost=2 * slab * count * width,
    )


def pick_kernel(at_ref, img, txt, out):
    width = img.shape[1]
    slots = out.shape[0]
    own = width // 128
    slot = lax.broadcasted_iota(jnp.int32, (slots, width), 0)
    feature = lax.broadcasted_iota(jnp.int32, (slots, width), 1)
    base = (slot // 8 * 2 + at_ref[0]) * own
    part = jnp.concatenate([img[...], txt[...]], axis=0)
    third = part.shape[0] // 3
    chosen = (feature == base + slot % 8).astype(f32).astype(b16)
    out[:, : 3 * third] = dot(chosen, part, NT).astype(b16)
    rest = jnp.zeros((slots, third), f32)
    for j in range(3):
        chosen = ((feature == base + 8) & (slot % 8 == j)).astype(f32).astype(b16)
        rest = rest + dot(chosen, part[j * third : (j + 1) * third], NT)
    out[:, 3 * third :] = rest.astype(b16)


def picked(core, img, txt):
    slab, width = img.shape
    return call(
        pick_kernel,
        jax.ShapeDtypeStruct((64 * 8, slab * 8 // 3), b16),
        [core],
        [img, txt],
        cost=2 * 512 * width * slab * 4,
    )


def head_kernel(at_ref, got, img_out, txt_out):
    slab = img_out.shape[1] // 8
    third = slab * 2 // 3
    half = third // 2
    for p in range(8):
        img = txt = None
        for other in range(8):
            z, lo, hi, y = p // 2, p % 2, other // 4, other % 4
            block = got[(z * 2 + lo) * 8 + hi * 4 + y].astype(f32)
            img = block if img is None else img + block
            z, lo, hi, y = other // 2, other % 2, p % 2, p // 2
            block = got[(z * 2 + lo) * 8 + hi * 4 + y].astype(f32)
            txt = block if txt is None else txt + block
        at = p * slab
        ninth = 2 * slab
        img_out[0:8, at : at + slab] = img[:, :slab]
        img_out[8:9, at : at + third] = img[0:1, ninth : ninth + third]
        img_out[8:9, at + third : at + slab] = img[1:2, ninth : ninth + half]
        txt_out[0:8, at : at + slab] = txt[:, slab : 2 * slab]
        txt_out[8:9, at : at + half] = txt[1:2, ninth + half : ninth + third]
        txt_out[8:9, at + half : at + slab] = txt[2:3, ninth : ninth + third]


def gather_pairs(own, move, second):
    across = send(own, move(0, 1))
    pair = jnp.concatenate([jnp.where(second, across, own), jnp.where(second, own, across)], axis=0)
    far = send(pair, move(2, 0))
    before = send(pair, move(1, 0))
    after = send(pair, move(3, 0))
    return [pair, after, far, before]


def reduce_pairs(piece, move, second, rows):
    got = [send(piece(d), move(d, 0)) for d in (2, 1, 3)]
    keep, keep_sum, give = near(second, [piece(0)] + got, rows)
    return keep, keep_sum, send(give, move(0, 1))


def whole_columns(own, give, move, ring, second):
    got = send(give, move(0, 1))
    lines = jnp.concatenate([jnp.where(second, got, own), jnp.where(second, own, got)], axis=1)
    out = jnp.zeros((4,) + lines.shape[1:], lines.dtype)
    for d in range(4):
        block = lax.dynamic_index_in_dim(lines, (ring + d) % 4, 0, keepdims=True)
        if d:
            block = send(block, move(d, 0))
        out = lax.dynamic_update_slice_in_dim(out, block, (ring + 4 - d) % 4, axis=0)
    return out.reshape(-1, lines.shape[2])


def shards(image_feat, text_feat, image_head, text_head, group_bias, text_lang, partner):
    rows, width = image_feat.shape
    slab = width // 8
    place = lax.axis_index(DEV)
    z, lo, hi, y, core = place // 32, place // 16 % 2, place // 8 % 2, place // 2 % 4, place % 2

    figures = jnp.stack([text_lang, partner // 128, partner % 128]).astype(b16)
    figures = jnp.pad(figures, ((0, PAD - 3), (0, width - rows)))
    text_rows = jnp.concatenate([text_feat, figures], axis=0)
    img_chunks = gather_pairs(image_feat, img_move, lo)
    txt_chunks = gather_pairs(text_rows, txt_move, hi)

    unit_txt, norm_txt = units(txt_chunks, text_head.T, y, rows, PAD)
    other_txt = send(unit_txt, core_move)
    unit_img, norm_img = units(img_chunks, image_head.T, z, rows, 0)

    slopes, img_sum, txt_sum = slope_tile(unit_img, unit_txt, group_bias, place % 16, rows)
    other_slopes, other_img_sum, other_txt_sum = slope_tile(
        unit_img, other_txt, group_bias, place % 16, rows
    )
    back = send(other_up(unit_img, other_slopes, other_txt_sum, rows), core_move)

    def image_term(d):
        return image_piece(
            (z + d) % 4, unit_txt, other_txt, slopes, other_slopes, img_sum, other_img_sum, slab, rows
        )

    def text_term(d):
        return text_piece((y + d) % 4, unit_img, slopes, back, txt_sum, slab, rows)

    img_keep, img_inner, img_got = reduce_pairs(image_term, img_move, lo, rows)
    txt_keep, txt_inner, txt_got = reduce_pairs(text_term, txt_move, hi, rows)
    img_own, img_give, img_part = gradient(
        z, lo, img_keep, img_inner, img_got, unit_img, norm_img, img_chunks, rows, 0
    )
    txt_own, txt_give, txt_part = gradient(
        y, hi, txt_keep, txt_inner, txt_got, unit_txt, norm_txt, txt_chunks, rows, PAD
    )

    theirs = send(picked(1 - core, img_part, txt_part), core_move)
    heads = picked(core, img_part, txt_part).astype(f32) + theirs.astype(f32)
    heads = exchange(heads.astype(b16).reshape(64, 8, -1), CHIP_GROUPS)
    head_shape = jax.ShapeDtypeStruct((width // 128, width), f32)
    image_head_grad, text_head_grad = call(head_kernel, [head_shape] * 2, [core], [heads])

    grad_img = whole_columns(img_own, img_give, img_move, z, lo)
    image_grad = dot(grad_img, image_head, (((0,), (1,)), ((), ())))
    grad_txt = whole_columns(txt_own, txt_give, txt_move, y, hi)
    text_grad = dot(grad_txt, text_head, (((0,), (1,)), ((), ())))
    return (image_grad, text_grad, image_head_grad, text_head_grad)


def solution(mesh):
    line = jax.sharding.Mesh(mesh.devices.reshape(-1), (DEV,))
    in_specs = (P(DEV, None), P(DEV, None), P(), P(), P(), P(DEV), P(DEV))
    return jax.shard_map(
        shards, mesh=line, in_specs=in_specs, out_specs=(P(DEV, None),) * 4, check_vma=False
    )
```

```python
import jax
import jax.numpy as jnp
from jax import lax
from jax.experimental import pallas as pl
from jax.experimental.pallas import tpu as pltpu
from jax.sharding import PartitionSpec as P

logit_scale = 64.0
epsilon = 1e-06
log2e = 1.4426950408889634
f32, b16 = jnp.float32, jnp.bfloat16

DEV = "dev"
PLACES = [
    (z, lo, hi, y, c)
    for z in range(4)
    for lo in range(2)
    for hi in range(2)
    for y in range(4)
    for c in range(2)
]


def flat(z, lo, hi, y, c):
    return (z * 2 + lo) * 16 + hi * 8 + y * 2 + c


def img_move(d, e):
    return lambda z, lo, hi, y, c: ((z + d) % 4, lo ^ e, hi, y, c)


def txt_move(d, e):
    return lambda z, lo, hi, y, c: (z, lo ^ e, hi ^ e, (y + d) % 4, c)


def core_move(z, lo, hi, y, c):
    return (z, lo, hi, y, 1 - c)


IMG_GROUPS = [
    [flat(z, lo, hi, y, c) for z in range(4) for lo in range(2)]
    for hi in range(2)
    for y in range(4)
    for c in range(2)
]
TXT_GROUPS = [
    [flat(z, hi ^ b, hi, y, c) for y in range(4) for hi in range(2)]
    for z in range(4)
    for b in range(2)
    for c in range(2)
]
TXT_CORE_GROUPS = [
    [flat(z, hi ^ b, hi, y, c) for c in range(2) for y in range(4) for hi in range(2)]
    for z in range(4)
    for b in range(2)
]
CHIP_GROUPS = [[flat(*p) for p in PLACES if p[4] == c] for c in range(2)]


def send(block, move):
    return lax.ppermute(block, DEV, [(flat(*p), flat(*move(*p))) for p in PLACES])


def exchange(blocks, groups):
    return lax.all_to_all(blocks, DEV, 0, 0, axis_index_groups=groups, tiled=True)


PAD = 16
NN = (((1,), (0,)), ((), ()))
NT = (((1,), (1,)), ((), ()))
TN = (((0,), (0,)), ((), ()))


def dot(a, b, dims):
    return lax.dot_general(a, b, dims, preferred_element_type=f32)


def call(body, out_shape, scalars, arrays, in_specs=None, out_specs=None, grid=(), scratch=(), cost=0):
    whole = pl.BlockSpec(memory_space=pltpu.VMEM)
    many = isinstance(out_shape, (list, tuple))
    if in_specs is None:
        in_specs = [whole] * len(arrays)
    if out_specs is None:
        out_specs = [whole] * len(out_shape) if many else whole
    spec = pltpu.PrefetchScalarGridSpec(
        num_scalar_prefetch=1,
        grid=grid,
        in_specs=in_specs,
        out_specs=out_specs,
        scratch_shapes=list(scratch),
    )
    moved = sum(a.size * a.dtype.itemsize for a in arrays)
    return pl.pallas_call(
        body,
        out_shape=out_shape,
        grid_spec=spec,
        compiler_params=pltpu.CompilerParams(vmem_limit_bytes=60 * 2**20),
        cost_estimate=pl.CostEstimate(flops=cost, bytes_accessed=moved, transcendentals=0),
    )(jnp.stack(scalars).astype(jnp.int32), *arrays)


def aligned(index, size):
    return pl.ds(pl.multiple_of(index * size, size), size)


def split_rows(total, lanes):
    high = total.astype(b16).astype(f32)
    row = lax.broadcasted_iota(jnp.int32, (PAD, lanes), 0)
    return jnp.where(row == 0, high, jnp.where(row == 1, total - high, 0.0)).astype(b16)


def joined(rows):
    return rows[0:1].astype(f32) + rows[1:2].astype(f32)


def in_pair(blocks, d, second, rows):
    own, across = blocks[2 * d][:rows], blocks[2 * d + 1][:rows]
    first = second == 0
    return jnp.concatenate([jnp.where(first, own, across), jnp.where(first, across, own)], axis=0)


def unit_kernel(rows, extra, both, at_ref, *refs):
    blocks, head, turned, outs, proj = refs[:8], refs[8], refs[9], refs[10:-1], refs[-1]
    unit, norm = outs[:2]
    width = head.shape[0]
    step = width // 4
    second = at_ref[1]
    for d in range(4):
        ring = (at_ref[0] + d) % 4
        lanes = aligned(ring, 2 * rows)
        feats = in_pair(blocks, d, second, rows)
        total = jnp.zeros((1, 2 * rows), f32)
        for m in range(4):
            part = dot(turned[m * step : (m + 1) * step], feats, NT)
            proj[m * step : (m + 1) * step] = part
            total = total + jnp.sum(part * part, axis=0, keepdims=True)
        length = jnp.sqrt(total + epsilon)
        norm[:, lanes] = length
        inverse = 1.0 / length
        for m in range(4):
            span = slice(m * step, (m + 1) * step)
            unit[span, lanes] = (proj[span] * inverse).astype(b16)
        if both:
            flat_part = dot(feats, head[...], NN)
            total = jnp.sum(flat_part * flat_part, axis=1, keepdims=True)
            outs[2][lanes, :] = (flat_part * (1.0 / jnp.sqrt(total + epsilon))).astype(b16)
        for e in range(2 if extra else 0):
            place = ring * 2 + (second + e) % 2
            unit[width:, aligned(place, rows)] = blocks[2 * d + e][rows : rows + extra, :rows]


def units(blocks, head, ring, second, rows, extra, both):
    width = head.shape[0]
    out = [
        jax.ShapeDtypeStruct((width + extra, 8 * rows), b16),
        jax.ShapeDtypeStruct((1, 8 * rows), f32),
    ]
    if both:
        out.append(jax.ShapeDtypeStruct((8 * rows, width), b16))
    return call(
        lambda *refs: unit_kernel(rows, extra, both, *refs),
        out,
        [ring, second],
        [*blocks, head, head.T],
        scratch=[pltpu.VMEM((width, 2 * rows), f32)],
        cost=(32 if both else 16) * rows * width * width,
    )


def slope_kernel(rows, groups, at_ref, bias_ref, img, turned, txt, slopes, img_sum, up, by_img):
    width = img.shape[1]
    tile = 2 * rows
    step = pl.program_id(0)
    lang = txt[width : width + PAD].astype(f32)
    partner = lang[1:2] * 128.0 + lang[2:3]
    lang = lang[0:1]
    bias = jnp.zeros((1, tile), f32)
    for g in range(groups):
        bias = jnp.where(lang == g, bias_ref[g], bias)
    bias = bias * -log2e
    down = jnp.zeros((1, tile), f32)

    @pl.when(step == 0)
    def _():
        by_img[...] = jnp.zeros(by_img.shape, f32)

    for m in range(img.shape[0] // tile):
        span = slice(m * tile, (m + 1) * tile)
        index = m * tile + lax.broadcasted_iota(jnp.int32, (tile, 1), 0)
        ids = ((index // rows * 16 + at_ref[0]) * rows + index % rows).astype(f32)
        cosines = logit_scale * dot(img[span], txt[:width], NN)
        gate = 1.0 / (1.0 + jnp.exp2(cosines * -log2e + bias))
        slope = (gate - jnp.where(partner == ids, 1.0, 0.0)).astype(b16)
        slopes[span] = slope
        weighted = slope.astype(f32) * cosines
        down = down + jnp.sum(weighted, axis=0, keepdims=True)
        side = by_img[span]
        for k in range(0, tile, by_img.shape[1]):
            side = side + weighted[:, k : k + by_img.shape[1]]
        by_img[span] = side

    @pl.when(step == pl.num_programs(0) - 1)
    def _():
        img_sum[...] = jnp.sum(by_img[...].T, axis=0, keepdims=True)

    figures = split_rows(down, tile)
    slab = width // 8
    for m in range(4):
        part = dot(turned[m * 2 * slab : (m + 1) * 2 * slab], slopes[...], NN)
        for e in range(2):
            at = (2 * m + e) * (slab + PAD)
            up[at : at + slab] = part[e * slab : (e + 1) * slab].astype(b16)
            up[at + slab : at + slab + PAD] = figures


def slope_tile(img, turned, txt, group_bias, place, rows):
    count, width = img.shape
    tile = 2 * rows
    height = width + 8 * PAD
    return call(
        lambda *refs: slope_kernel(rows, group_bias.shape[0], *refs),
        [
            jax.ShapeDtypeStruct((count, count), b16),
            jax.ShapeDtypeStruct((1, count), f32),
            jax.ShapeDtypeStruct((height, count), b16),
        ],
        [place],
        [group_bias, img, turned, txt],
        in_specs=[
            pl.BlockSpec(memory_space=pltpu.SMEM),
            pl.BlockSpec((count, width), lambda i, at: (0, 0)),
            pl.BlockSpec((width, count), lambda i, at: (0, 0)),
            pl.BlockSpec((width + PAD, tile), lambda i, at: (0, i)),
        ],
        out_specs=[
            pl.BlockSpec((count, tile), lambda i, at: (0, i)),
            pl.BlockSpec((1, count), lambda i, at: (0, 0)),
            pl.BlockSpec((height, tile), lambda i, at: (0, i)),
        ],
        grid=(count // tile,),
        scratch=[pltpu.VMEM((count, min(128, tile)), f32)],
        cost=4 * width * count * count,
    )


def image_kernel(number, at_ref, *refs):
    slopes, other_slopes, total, other_total = refs[2 * number : 2 * number + 4]
    outs = refs[2 * number + 4 :]
    figures = split_rows(total[...] + other_total[...], total.shape[1])
    for n in range(number):
        piece = dot(refs[2 * n][...], slopes[...], NT)
        piece = piece + dot(refs[2 * n + 1][...], other_slopes[...], NT)
        slab = piece.shape[0] // 2
        own = at_ref[number] == 0
        outs[2 * n][:slab] = jnp.where(own, piece[:slab], piece[slab:]).astype(b16)
        outs[2 * n][slab:] = figures
        outs[2 * n + 1][:slab] = jnp.where(own, piece[slab:], piece[:slab]).astype(b16)
        outs[2 * n + 1][slab:] = figures


def image_pieces(rings, second, txt, other, slopes, other_slopes, total, other_total, slab, rows):
    count = slopes.shape[0]
    tile = 2 * rows
    number = len(rings)
    block = lambda n: pl.BlockSpec((2 * slab, count), lambda i, at: (at[n], 0))
    return call(
        lambda *refs: image_kernel(number, *refs),
        [jax.ShapeDtypeStruct((slab + PAD, count), b16)] * (2 * number),
        [*rings, second],
        [txt, other] * number + [slopes, other_slopes, total, other_total],
        in_specs=[block(n // 2) for n in range(2 * number)]
        + [pl.BlockSpec((tile, count), lambda i, at: (i, 0))] * 2
        + [pl.BlockSpec((1, tile), lambda i, at: (0, i))] * 2,
        out_specs=[pl.BlockSpec((slab + PAD, tile), lambda i, at: (0, i))] * (2 * number),
        grid=(count // tile,),
        cost=8 * number * slab * count * count,
    )


def sum_into(out, terms):
    slab = out.shape[0] - PAD
    block, total = terms[0][:slab].astype(f32), joined(terms[0][slab:])
    for term in terms[1:]:
        block, total = block + term[:slab].astype(f32), total + joined(term[slab:])
    out[:slab] = block.astype(b16)
    out[slab:] = split_rows(total, out.shape[1])


def sum_kernel(each, at_ref, *refs):
    outs = refs[-(len(refs) // (each + 1)) :]
    for n, out in enumerate(outs):
        sum_into(out, refs[n * each : (n + 1) * each])


def sums(groups, rows):
    height, count = groups[0][0].shape
    spec = pl.BlockSpec((height, 4 * rows), lambda i, at: (0, i))
    out = call(
        lambda *refs: sum_kernel(len(groups[0]), *refs),
        [jax.ShapeDtypeStruct((height, count), b16)] * len(groups),
        [jnp.int32(0)],
        [term for group in groups for term in group],
        in_specs=[spec] * (len(groups) * len(groups[0])),
        out_specs=[spec] * len(groups),
        grid=(count // (4 * rows),),
    )
    return list(out)


def text_pieces(rings, second, up, back, rows):
    height, count = up.shape
    places = [2 * ring + (second + e) % 2 for ring in rings for e in range(2)]
    block = lambda n: pl.BlockSpec((height // 8, 4 * rows), lambda i, at: (at[n], i))
    spec = pl.BlockSpec((height // 8, 4 * rows), lambda i, at: (0, i))
    return call(
        lambda *refs: sum_kernel(2, *refs),
        [jax.ShapeDtypeStruct((height // 8, count), b16)] * len(places),
        places,
        [up, back] * len(places),
        in_specs=[block(n // 2) for n in range(2 * len(places))],
        out_specs=[spec] * len(places),
        grid=(count // (4 * rows),),
    )


def grad_kernel(rows, at_ref, *refs):
    terms, unit, norm, blocks, (own, give, part, grad) = (
        refs[:4], refs[4], refs[5], refs[6:14], refs[14:]
    )
    slab = unit.shape[0]
    up, inner = terms[0][:slab].astype(f32), joined(terms[0][slab:])
    for term in terms[1:]:
        up, inner = up + term[:slab].astype(f32), inner + joined(term[slab:])
    up = logit_scale * up - unit[...].astype(f32) * inner
    grad[...] = (up * (1.0 / norm[...])).astype(b16)
    second = at_ref[1]
    for ring in range(4):
        low = grad[:, (2 * ring) * rows : (2 * ring + 1) * rows]
        high = grad[:, (2 * ring + 1) * rows : (2 * ring + 2) * rows]
        own[ring] = jnp.where(second == 0, low, high)
        give[ring] = jnp.where(second == 0, high, low)
    total = None
    for d in range(4):
        cols = grad[:, aligned((at_ref[0] + d) % 4, 2 * rows)]
        term = dot(cols, in_pair(blocks, d, second, rows), NN)
        total = term if total is None else total + term
    part[...] = total.astype(b16)


def gradient(ring, second, terms, unit, norm, blocks, rows):
    slab, count = terms[0].shape[0] - PAD, terms[0].shape[1]
    width = blocks[0].shape[1]
    whole = lambda a: pl.BlockSpec(a.shape, lambda i, at: (0,) * len(a.shape))
    arrays = [*terms, unit, norm, *blocks]
    specs = [whole(a) for a in arrays]
    specs[4] = pl.BlockSpec((slab, count), lambda i, at: (at[0] * 2 + at[1], 0))
    block = jax.ShapeDtypeStruct((4, slab, rows), b16)
    term = jax.ShapeDtypeStruct((slab, width), b16)
    return call(
        lambda *refs: grad_kernel(rows, *refs),
        [block, block, term],
        [ring, second],
        arrays,
        in_specs=specs,
        out_specs=[whole(block), whole(block), whole(term)],
        grid=(1,),
        scratch=[pltpu.VMEM((slab, count), b16)],
        cost=2 * slab * count * width,
    )


def pick_kernel(at_ref, img, txt, out):
    width = img.shape[1]
    slots = out.shape[0]
    own = width // 128
    slot = lax.broadcasted_iota(jnp.int32, (slots, width), 0)
    feature = lax.broadcasted_iota(jnp.int32, (slots, width), 1)
    base = (slot // 8 * 2 + at_ref[0]) * own
    part = jnp.concatenate([img[...], txt[...]], axis=0)
    third = part.shape[0] // 3
    chosen = (feature == base + slot % 8).astype(f32).astype(b16)
    out[:, : 3 * third] = dot(chosen, part, NT).astype(b16)
    rest = jnp.zeros((slots, third), f32)
    for j in range(3):
        chosen = ((feature == base + 8) & (slot % 8 == j)).astype(f32).astype(b16)
        rest = rest + dot(chosen, part[j * third : (j + 1) * third], NT)
    out[:, 3 * third :] = rest.astype(b16)


def picked(core, img, txt):
    slab, width = img.shape
    return call(
        pick_kernel,
        jax.ShapeDtypeStruct((64 * 8, slab * 8 // 3), b16),
        [core],
        [img, txt],
        cost=2 * 512 * width * slab * 4,
    )


def head_kernel(at_ref, got, img_out, txt_out):
    slab = img_out.shape[1] // 8
    third = slab * 2 // 3
    half = third // 2
    for p in range(8):
        img = txt = None
        for other in range(8):
            z, lo, hi, y = p // 2, p % 2, other // 4, other % 4
            block = got[(z * 2 + lo) * 8 + hi * 4 + y].astype(f32)
            img = block if img is None else img + block
            z, lo, hi, y = other // 2, other % 2, p % 2, p // 2
            block = got[(z * 2 + lo) * 8 + hi * 4 + y].astype(f32)
            txt = block if txt is None else txt + block
        at = p * slab
        ninth = 2 * slab
        img_out[0:8, at : at + slab] = img[:, :slab]
        img_out[8:9, at : at + third] = img[0:1, ninth : ninth + third]
        img_out[8:9, at + third : at + slab] = img[1:2, ninth : ninth + half]
        txt_out[0:8, at : at + slab] = txt[:, slab : 2 * slab]
        txt_out[8:9, at : at + half] = txt[1:2, ninth + half : ninth + third]
        txt_out[8:9, at + half : at + slab] = txt[2:3, ninth : ninth + third]


def together(arrays):
    return lax.optimization_barrier(list(arrays))


def gather_groups(img, txt):
    moves = (img_move, txt_move)
    own = (img, txt)
    across = [send(own[n], moves[n](0, 1)) for n in range(2)]
    before = [send(own[n], moves[n](1, 0)) for n in range(2)]
    after = [send(own[n], moves[n](3, 0)) for n in range(2)]
    first = together(across + before + after)
    across, before, after = first[0:2], first[2:4], first[4:6]
    across_after = [send(across[n], moves[n](3, 0)) for n in range(2)]
    across_before = [send(across[n], moves[n](1, 0)) for n in range(2)]
    far = [send(before[n], moves[n](1, 0)) for n in range(2)]
    across_after = together(across_after)
    across_far = [send(across_after[n], moves[n](3, 0)) for n in range(2)]
    return [
        [
            own[n], across[n], after[n], across_after[n],
            far[n], across_far[n], before[n], across_before[n],
        ]
        for n in range(2)
    ]


def whole_columns(own, give, move, ring, second):
    got = send(give, move(0, 1))
    lines = jnp.concatenate([jnp.where(second, got, own), jnp.where(second, own, got)], axis=1)
    out = jnp.zeros((4,) + lines.shape[1:], lines.dtype)
    for d in range(4):
        block = lax.dynamic_index_in_dim(lines, (ring + d) % 4, 0, keepdims=True)
        if d:
            block = send(block, move(d, 0))
        out = lax.dynamic_update_slice_in_dim(out, block, (ring + 4 - d) % 4, axis=0)
    return out.reshape(-1, lines.shape[2])


def shards(image_feat, text_feat, image_head, text_head, group_bias, text_lang, partner):
    rows, width = image_feat.shape
    slab = width // 8
    place = lax.axis_index(DEV)
    z, lo, hi, y, core = place // 32, place // 16 % 2, place // 8 % 2, place // 2 % 4, place % 2

    figures = jnp.stack([text_lang, partner // 128, partner % 128]).astype(b16)
    figures = jnp.pad(figures, ((0, PAD - 3), (0, width - rows)))
    text_rows = jnp.concatenate([text_feat, figures], axis=0)
    img_blocks, txt_blocks = gather_groups(image_feat, text_rows)

    unit_txt, norm_txt = units(txt_blocks, text_head, y, hi, rows, PAD, False)
    other_txt = send(unit_txt, core_move)
    turned_img, norm_img, unit_img = units(img_blocks, image_head, z, lo, rows, 0, True)

    other_slopes, other_img_sum, other_up = slope_tile(
        unit_img, turned_img, other_txt, group_bias, place % 16, rows
    )
    back = send(other_up, core_move)
    slopes, img_sum, text_up = slope_tile(
        unit_img, turned_img, unit_txt, group_bias, place % 16, rows
    )

    def image_terms(rings):
        return image_pieces(
            rings, lo, unit_txt, other_txt, slopes, other_slopes, img_sum, other_img_sum, slab, rows
        )

    def text_terms(rings):
        return text_pieces(rings, hi, text_up, back, rows)

    def around(at, distances):
        return [(at + d) % 4 for d in distances]

    towers = ((image_terms, img_move, z), (text_terms, txt_move, y))
    far, close = [], []
    for terms, move, at in towers:
        own, across = terms(around(at, [2]))
        far.append((send(own, move(1, 0)), send(across, move(3, 0))))
    for terms, move, at in towers:
        close.append(terms(around(at, [1, 3, 0])))
    final = []
    for n, (terms, move, at) in enumerate(towers):
        after, across_after, before, across_before, own, across = close[n]
        from_before = send(across_after, move(1, 0))
        from_after = send(before, move(3, 0))
        after, across_before = sums([[after, far[n][0]], [across_before, far[n][1]]], rows)
        own_before = send(after, move(1, 0))
        across_from_after = send(across_before, move(3, 0))
        (across,) = sums([[across, from_before, across_from_after]], rows)
        final.append([own, from_after, own_before, send(across, move(0, 1))])

    img_own, img_give, img_part = gradient(
        z, lo, final[0], turned_img, norm_img, img_blocks, rows
    )
    txt_own, txt_give, txt_part = gradient(y, hi, final[1], unit_txt, norm_txt, txt_blocks, rows)

    theirs = send(picked(1 - core, img_part, txt_part), core_move)
    heads = picked(core, img_part, txt_part).astype(f32) + theirs.astype(f32)
    heads = exchange(heads.astype(b16).reshape(64, 8, -1), CHIP_GROUPS)
    head_shape = jax.ShapeDtypeStruct((width // 128, width), f32)
    image_head_grad, text_head_grad = call(head_kernel, [head_shape] * 2, [core], [heads])

    grad_img = whole_columns(img_own, img_give, img_move, z, lo)
    image_grad = dot(grad_img, image_head, (((0,), (1,)), ((), ())))
    grad_txt = whole_columns(txt_own, txt_give, txt_move, y, hi)
    text_grad = dot(grad_txt, text_head, (((0,), (1,)), ((), ())))
    return (image_grad, text_grad, image_head_grad, text_head_grad)


def solution(mesh):
    line = jax.sharding.Mesh(mesh.devices.reshape(-1), (DEV,))
    in_specs = (P(DEV, None), P(DEV, None), P(), P(), P(), P(DEV), P(DEV))
    return jax.shard_map(
        shards, mesh=line, in_specs=in_specs, out_specs=(P(DEV, None),) * 4, check_vma=False
    )
```

```python
import jax
import jax.numpy as jnp
from jax import lax
from jax.experimental import pallas as pl
from jax.experimental.pallas import tpu as pltpu
from jax.sharding import PartitionSpec as P

logit_scale = 64.0
epsilon = 1e-06
log2e = 1.4426950408889634
f32, b16 = jnp.float32, jnp.bfloat16

DEV = "dev"
PLACES = [
    (z, lo, hi, y, c)
    for z in range(4)
    for lo in range(2)
    for hi in range(2)
    for y in range(4)
    for c in range(2)
]


def flat(z, lo, hi, y, c):
    return (z * 2 + lo) * 16 + hi * 8 + y * 2 + c


def img_move(d, e):
    return lambda z, lo, hi, y, c: ((z + d) % 4, lo ^ e, hi, y, c)


def txt_move(d, e):
    return lambda z, lo, hi, y, c: (z, lo ^ e, hi ^ e, (y + d) % 4, c)


def core_move(z, lo, hi, y, c):
    return (z, lo, hi, y, 1 - c)


IMG_GROUPS = [
    [flat(z, lo, hi, y, c) for z in range(4) for lo in range(2)]
    for hi in range(2)
    for y in range(4)
    for c in range(2)
]
TXT_GROUPS = [
    [flat(z, hi ^ b, hi, y, c) for y in range(4) for hi in range(2)]
    for z in range(4)
    for b in range(2)
    for c in range(2)
]
TXT_CORE_GROUPS = [
    [flat(z, hi ^ b, hi, y, c) for c in range(2) for y in range(4) for hi in range(2)]
    for z in range(4)
    for b in range(2)
]
CHIP_GROUPS = [[flat(*p) for p in PLACES if p[4] == c] for c in range(2)]


def send(block, move):
    return lax.ppermute(block, DEV, [(flat(*p), flat(*move(*p))) for p in PLACES])


def exchange(blocks, groups):
    return lax.all_to_all(blocks, DEV, 0, 0, axis_index_groups=groups, tiled=True)


PAD = 16
NN = (((1,), (0,)), ((), ()))
NT = (((1,), (1,)), ((), ()))
TN = (((0,), (0,)), ((), ()))


def dot(a, b, dims):
    return lax.dot_general(a, b, dims, preferred_element_type=f32)


def call(body, out_shape, scalars, arrays, in_specs=None, out_specs=None, grid=(), scratch=(), cost=0, aliases=None):
    whole = pl.BlockSpec(memory_space=pltpu.VMEM)
    many = isinstance(out_shape, (list, tuple))
    if in_specs is None:
        in_specs = [whole] * len(arrays)
    if out_specs is None:
        out_specs = [whole] * len(out_shape) if many else whole
    spec = pltpu.PrefetchScalarGridSpec(
        num_scalar_prefetch=1,
        grid=grid,
        in_specs=in_specs,
        out_specs=out_specs,
        scratch_shapes=list(scratch),
    )
    moved = sum(a.size * a.dtype.itemsize for a in arrays)
    return pl.pallas_call(
        body,
        out_shape=out_shape,
        grid_spec=spec,
        input_output_aliases=aliases or {},
        compiler_params=pltpu.CompilerParams(vmem_limit_bytes=60 * 2**20),
        cost_estimate=pl.CostEstimate(flops=cost, bytes_accessed=moved, transcendentals=0),
    )(jnp.stack(scalars).astype(jnp.int32), *arrays)


def aligned(index, size):
    return pl.ds(pl.multiple_of(index * size, size), size)


def split_rows(total, lanes):
    high = total.astype(b16).astype(f32)
    row = lax.broadcasted_iota(jnp.int32, (PAD, lanes), 0)
    return jnp.where(row == 0, high, jnp.where(row == 1, total - high, 0.0)).astype(b16)


def joined(rows):
    return rows[0:1].astype(f32) + rows[1:2].astype(f32)


def in_pair(own, across, second, rows):
    own, across = own[:rows], across[:rows]
    first = second == 0
    return jnp.concatenate([jnp.where(first, own, across), jnp.where(first, across, own)], axis=0)


def unit_rows(own, across, head, second, rows):
    projected = dot(in_pair(own, across, second, rows), head[...], NN)
    length = jnp.sqrt(jnp.sum(projected * projected, axis=1, keepdims=True) + epsilon)
    row = jnp.broadcast_to(length, (2 * rows, 128)).T[0:1]
    return projected * (1.0 / length), row


def img_unit_kernel(rows, at_ref, own, across, head, *refs):
    unit, turned, norm = refs[-3:]
    block, norm[...] = unit_rows(own, across, head, at_ref[1], rows)
    unit[...] = block.astype(b16)
    turned[...] = block.T.astype(b16)


def txt_unit_kernel(rows, at_ref, own, across, head, *refs):
    turned, norm, alone = refs[-3:]
    width = head.shape[0]
    block, norm[...] = unit_rows(own, across, head, at_ref[1], rows)
    alone[:width] = block.T.astype(b16)
    first = at_ref[1] == 0
    sides = own[rows:, :rows], across[rows:, :rows]
    alone[width:, :rows] = jnp.where(first, sides[0], sides[1])
    alone[width:, rows:] = jnp.where(first, sides[1], sides[0])
    turned[...] = alone[...]


def pair_units(kernel, out, steps, own, across, head, ring, second, rows, carried):
    whole = lambda a: pl.BlockSpec(a.shape, lambda i, at: (0, 0))
    carried = list(carried or ())
    return list(
        call(
            lambda *refs: kernel(rows, *refs),
            out,
            [ring, second],
            [own, across, head, *carried],
            in_specs=[whole(own), whole(across), whole(head)]
            + [pl.BlockSpec(memory_space=pl.ANY)] * len(carried),
            out_specs=steps,
            grid=(1,),
            cost=4 * rows * head.size,
            aliases={4 + n: n for n in range(len(carried))},
        )
    )


def img_units(own, across, head, ring, second, rows, carried):
    width = head.shape[0]
    out = [
        jax.ShapeDtypeStruct((8 * rows, width), b16),
        jax.ShapeDtypeStruct((width, 8 * rows), b16),
        jax.ShapeDtypeStruct((1, 8 * rows), f32),
    ]
    steps = [
        pl.BlockSpec((2 * rows, width), lambda i, at: (at[0], 0)),
        pl.BlockSpec((width, 2 * rows), lambda i, at: (0, at[0])),
        pl.BlockSpec((1, 2 * rows), lambda i, at: (0, at[0])),
    ]
    return pair_units(img_unit_kernel, out, steps, own, across, head, ring, second, rows, carried)


def txt_units(own, across, head, ring, second, rows, carried):
    width = head.shape[0]
    out = [
        jax.ShapeDtypeStruct((width + PAD, 8 * rows), b16),
        jax.ShapeDtypeStruct((1, 8 * rows), f32),
        jax.ShapeDtypeStruct((width + PAD, 2 * rows), b16),
    ]
    steps = [
        pl.BlockSpec((width + PAD, 2 * rows), lambda i, at: (0, at[0])),
        pl.BlockSpec((1, 2 * rows), lambda i, at: (0, at[0])),
        pl.BlockSpec((width + PAD, 2 * rows), lambda i, at: (0, 0)),
    ]
    return pair_units(txt_unit_kernel, out, steps, own, across, head, ring, second, rows, carried)


def tile_slopes(rows, groups, place, bias_ref, img, txt, slopes, by_img):
    width = img.shape[1]
    tile = 2 * rows
    lang = txt[width : width + PAD].astype(f32)
    partner = lang[1:2] * 128.0 + lang[2:3]
    lang = lang[0:1]
    bias = jnp.zeros((1, tile), f32)
    for g in range(groups):
        bias = jnp.where(lang == g, bias_ref[g], bias)
    bias = bias * -log2e
    down = jnp.zeros((1, tile), f32)
    high = 4 * rows
    for m in range(img.shape[0] // high):
        span = slice(m * high, (m + 1) * high)
        index = m * high + lax.broadcasted_iota(jnp.int32, (high, 1), 0)
        ids = ((index // rows * 16 + place) * rows + index % rows).astype(f32)
        cosines = logit_scale * dot(img[span], txt[:width], NN)
        gate = 1.0 / (1.0 + jnp.exp2(cosines * -log2e + bias))
        slope = (gate - jnp.where(partner == ids, 1.0, 0.0)).astype(b16)
        slopes[span, :tile] = slope
        weighted = slope.astype(f32) * cosines
        down = down + jnp.sum(weighted, axis=0, keepdims=True)
        side = by_img[span]
        for k in range(0, tile, by_img.shape[1]):
            side = side + weighted[:, k : k + by_img.shape[1]]
        by_img[span] = side
    return down


def put_text_terms(up, turned, slopes, down):
    slab = turned.shape[0] // 8
    figures = split_rows(down, up.shape[1])
    part = dot(turned[...], slopes, NN)
    for e in range(8):
        at = e * (slab + PAD)
        up[at : at + slab] = part[e * slab : (e + 1) * slab].astype(b16)
        up[at + slab : at + slab + PAD] = figures


def other_kernel(rows, groups, at_ref, bias_ref, img, turned, *refs):
    chunks, (slopes, img_sum, up, by_img, held, txt) = refs[:4], refs[4:]
    step = pl.program_id(0)

    @pl.when(step == 0)
    def _():
        by_img[...] = jnp.zeros(by_img.shape, f32)

    for d in range(4):

        @pl.when(step == d)
        def _():
            txt[...] = chunks[d][...]

    down = tile_slopes(rows, groups, at_ref[0], bias_ref, img, txt, held, by_img)
    slopes[0] = held[...]
    put_text_terms(up, turned, held[...], down)

    @pl.when(step == 3)
    def _():
        img_sum[...] = jnp.sum(by_img[...].T, axis=0, keepdims=True)


def other_tile(img, turned, chunks, group_bias, place, ring, rows):
    count, width = img.shape
    tile = 2 * rows
    height = width + 8 * PAD
    whole = lambda a: pl.BlockSpec(a.shape, lambda i, at: (0, 0))
    return call(
        lambda *refs: other_kernel(rows, group_bias.shape[0], *refs),
        [
            jax.ShapeDtypeStruct((4, count, tile), b16),
            jax.ShapeDtypeStruct((1, count), f32),
            jax.ShapeDtypeStruct((height, count), b16),
        ],
        [place, ring],
        [group_bias, img, turned, *chunks],
        in_specs=[pl.BlockSpec(memory_space=pltpu.SMEM), whole(img), whole(turned)]
        + [whole(chunk) for chunk in chunks],
        out_specs=[
            pl.BlockSpec((1, count, tile), lambda i, at: (i, 0, 0)),
            pl.BlockSpec((1, count), lambda i, at: (0, 0)),
            pl.BlockSpec((height, tile), lambda i, at: (0, (at[1] + i) % 4)),
        ],
        grid=(4,),
        scratch=[
            pltpu.VMEM((count, min(128, tile)), f32),
            pltpu.VMEM((count, tile), b16),
            pltpu.VMEM((width + PAD, tile), b16),
        ],
        cost=4 * width * count * count,
    )


def own_kernel(rows, groups, at_ref, bias_ref, img, turned, txt, *refs):
    chunks, other_slopes, other_sum, up = refs[:4], refs[4], refs[5], refs[6]
    outs, (by_img, held, both, total) = refs[7:15], refs[15:]
    step = pl.program_id(0)
    width = img.shape[1]
    tile = 2 * rows

    @pl.when(step == 0)
    def _():
        by_img[...] = jnp.zeros(by_img.shape, f32)
        total[...] = jnp.zeros(total.shape, f32)

    for d in range(4):

        @pl.when(step == d)
        def _():
            both[:, tile:] = chunks[d][:width]

    held[:, tile:] = other_slopes[0]
    both[:, :tile] = txt[:width]
    down = tile_slopes(rows, groups, at_ref[0], bias_ref, img, txt, held, by_img)
    put_text_terms(up, turned, held[:, :tile], down)
    total[...] += dot(both[...], held[...], NT)

    @pl.when(step == 3)
    def _():
        slab = width // 8
        sums = jnp.sum(by_img[...].T, axis=0, keepdims=True) + other_sum[...]
        figures = split_rows(sums, sums.shape[1])
        own = at_ref[2] == 0
        for d in range(4):
            at = pl.multiple_of((at_ref[1] + d) % 4 * (2 * slab), 2 * slab)
            low, high = total[pl.ds(at, slab)], total[pl.ds(at + slab, slab)]
            outs[2 * d][:slab] = jnp.where(own, low, high).astype(b16)
            outs[2 * d][slab:] = figures
            outs[2 * d + 1][:slab] = jnp.where(own, high, low).astype(b16)
            outs[2 * d + 1][slab:] = figures


def own_tile(
    img, turned, txt, chunks, other_slopes, other_sum, group_bias, place, ring, second, rows
):
    count, width = img.shape
    tile = 2 * rows
    height = width + 8 * PAD
    slab = width // 8
    whole = lambda a: pl.BlockSpec(a.shape, lambda i, at: (0, 0))
    piece = jax.ShapeDtypeStruct((slab + PAD, count), b16)
    out = call(
        lambda *refs: own_kernel(rows, group_bias.shape[0], *refs),
        [jax.ShapeDtypeStruct((height, count), b16)] + [piece] * 8,
        [place, ring, second],
        [group_bias, img, turned, txt, *chunks, other_slopes, other_sum],
        in_specs=[
            pl.BlockSpec(memory_space=pltpu.SMEM),
            whole(img),
            whole(turned),
            pl.BlockSpec((width + PAD, tile), lambda i, at: (0, i)),
        ]
        + [whole(chunk) for chunk in chunks]
        + [pl.BlockSpec((1, count, tile), lambda i, at: (i, 0, 0)), whole(other_sum)],
        out_specs=[pl.BlockSpec((height, tile), lambda i, at: (0, i))] + [whole(piece)] * 8,
        grid=(4,),
        scratch=[
            pltpu.VMEM((count, min(128, tile)), f32),
            pltpu.VMEM((count, 2 * tile), b16),
            pltpu.VMEM((width, 2 * tile), b16),
            pltpu.VMEM((width, count), f32),
        ],
        cost=8 * width * count * count,
    )
    return out[0], out[1:]


def sum_into(out, terms):
    slab = out.shape[0] - PAD
    block, total = terms[0][:slab].astype(f32), joined(terms[0][slab:])
    for term in terms[1:]:
        block, total = block + term[:slab].astype(f32), total + joined(term[slab:])
    out[:slab] = block.astype(b16)
    out[slab:] = split_rows(total, out.shape[1])


def sum_kernel(each, at_ref, *refs):
    outs = refs[-(len(refs) // (each + 1)) :]
    for n, out in enumerate(outs):
        sum_into(out, refs[n * each : (n + 1) * each])


def sums(groups, rows):
    height, count = groups[0][0].shape
    spec = pl.BlockSpec((height, 4 * rows), lambda i, at: (0, i))
    out = call(
        lambda *refs: sum_kernel(len(groups[0]), *refs),
        [jax.ShapeDtypeStruct((height, count), b16)] * len(groups),
        [jnp.int32(0)],
        [term for group in groups for term in group],
        in_specs=[spec] * (len(groups) * len(groups[0])),
        out_specs=[spec] * len(groups),
        grid=(count // (4 * rows),),
    )
    return list(out)


def text_pieces(rings, second, up, back, rows):
    height, count = up.shape
    places = [2 * ring + (second + e) % 2 for ring in rings for e in range(2)]
    block = lambda n: pl.BlockSpec((height // 8, 4 * rows), lambda i, at: (at[n], i))
    spec = pl.BlockSpec((height // 8, 4 * rows), lambda i, at: (0, i))
    return call(
        lambda *refs: sum_kernel(2, *refs),
        [jax.ShapeDtypeStruct((height // 8, count), b16)] * len(places),
        places,
        [up, back] * len(places),
        in_specs=[block(n // 2) for n in range(2 * len(places))],
        out_specs=[spec] * len(places),
        grid=(count // (4 * rows),),
    )


def grad_kernel(rows, at_ref, *refs):
    part, grad = refs[-2:]
    outs = refs[-6:-2]
    for n in range(2):
        mine = refs[14 * n : 14 * (n + 1)]
        terms, unit, norm, blocks = mine[:4], mine[4], mine[5], mine[6:]
        ring_at, second = at_ref[2 * n], at_ref[2 * n + 1]
        slab = unit.shape[0]
        up, inner = terms[0][:slab].astype(f32), joined(terms[0][slab:])
        for term in terms[1:]:
            up, inner = up + term[:slab].astype(f32), inner + joined(term[slab:])
        up = logit_scale * up - unit[...].astype(f32) * inner
        grad[n] = (up * (1.0 / norm[...])).astype(b16)
        own, give = outs[2 * n : 2 * n + 2]
        for ring in range(4):
            low = grad[n, :, (2 * ring) * rows : (2 * ring + 1) * rows]
            high = grad[n, :, (2 * ring + 1) * rows : (2 * ring + 2) * rows]
            own[ring] = jnp.where(second == 0, low, high)
            give[ring] = jnp.where(second == 0, high, low)
        total = None
        for d in range(4):
            cols = grad[n, :, aligned((ring_at + d) % 4, 2 * rows)]
            term = dot(cols, in_pair(blocks[2 * d], blocks[2 * d + 1], second, rows), NN)
            total = term if total is None else total + term
        part[n * slab : (n + 1) * slab] = total.astype(b16)


def gradients(towers, rows):
    arrays, specs, scalars = [], [], []
    whole = lambda a: pl.BlockSpec(a.shape, lambda i, at: (0,) * len(a.shape))
    for n, (ring, second, terms, unit, norm, blocks) in enumerate(towers):
        slab, count = terms[0].shape[0] - PAD, terms[0].shape[1]
        width = blocks[0].shape[1]
        mine = [*terms, unit, norm, *blocks]
        arrays += mine
        specs += [whole(a) for a in mine]
        specs[14 * n + 4] = pl.BlockSpec(
            (slab, count), lambda i, at, n=n: (at[2 * n] * 2 + at[2 * n + 1], 0)
        )
        scalars += [ring, second]
    block = jax.ShapeDtypeStruct((4, slab, rows), b16)
    term = jax.ShapeDtypeStruct((2 * slab, width), b16)
    return call(
        lambda *refs: grad_kernel(rows, *refs),
        [block] * 4 + [term],
        scalars,
        arrays,
        in_specs=specs,
        out_specs=[whole(block)] * 4 + [whole(term)],
        grid=(1,),
        scratch=[pltpu.VMEM((2, slab, count), b16)],
        cost=4 * slab * count * width,
    )


def pick_kernel(at_ref, mine, theirs, out):
    width = mine.shape[1]
    slots = out.shape[0]
    own = width // 128
    third = mine.shape[0] // 3
    part = (mine[...].astype(f32) + theirs[...].astype(f32)).astype(b16)
    slot = lax.broadcasted_iota(jnp.int32, (slots, 1), 0)
    feature = lax.broadcasted_iota(jnp.int32, (slots, width), 1)
    base = (slot // 8 * 2 + at_ref[0]) * own
    chosen = jnp.where(feature == base + slot % 8, 1.0, 0.0).astype(b16)
    out[:, : 3 * third] = dot(chosen, part, NT).astype(b16)
    chosen = jnp.where(feature == base + 8, 1.0, 0.0).astype(b16)
    ninth = dot(chosen, part, NT)
    pick = slot % 8
    rest = jnp.where(pick == 1, ninth[:, third : 2 * third], ninth[:, :third])
    rest = jnp.where(pick == 2, ninth[:, 2 * third :], rest)
    out[:, 3 * third :] = rest.astype(b16)


def picked(core, mine, theirs):
    both, width = mine.shape
    return call(
        pick_kernel,
        jax.ShapeDtypeStruct((64 * 8, both * 4 // 3), b16),
        [core],
        [mine, theirs],
        cost=4 * 512 * width * both,
    )


def head_kernel(at_ref, got, img_out, txt_out):
    slab = img_out.shape[1] // 8
    third = slab * 2 // 3
    half = third // 2
    for p in range(8):
        img = txt = None
        for other in range(8):
            z, lo, hi, y = p // 2, p % 2, other // 4, other % 4
            block = got[(z * 2 + lo) * 8 + hi * 4 + y].astype(f32)
            img = block if img is None else img + block
            z, lo, hi, y = other // 2, other % 2, p % 2, p // 2
            block = got[(z * 2 + lo) * 8 + hi * 4 + y].astype(f32)
            txt = block if txt is None else txt + block
        at = p * slab
        ninth = 2 * slab
        img_out[0:8, at : at + slab] = img[:, :slab]
        img_out[8:9, at : at + third] = img[0:1, ninth : ninth + third]
        img_out[8:9, at + third : at + slab] = img[1:2, ninth : ninth + half]
        txt_out[0:8, at : at + slab] = txt[:, slab : 2 * slab]
        txt_out[8:9, at : at + half] = txt[1:2, ninth + half : ninth + third]
        txt_out[8:9, at + half : at + slab] = txt[2:3, ninth : ninth + third]


def together(arrays):
    return lax.optimization_barrier(list(arrays))


def whole_columns(own, give, move, ring, second):
    got = send(give, move(0, 1))
    lines = jnp.concatenate([jnp.where(second, got, own), jnp.where(second, own, got)], axis=1)
    out = jnp.zeros((4,) + lines.shape[1:], lines.dtype)
    for d in range(4):
        block = lax.dynamic_index_in_dim(lines, (ring + d) % 4, 0, keepdims=True)
        if d:
            block = send(block, move(d, 0))
        out = lax.dynamic_update_slice_in_dim(out, block, (ring + 4 - d) % 4, axis=0)
    return out.reshape(-1, lines.shape[2])


def shards(image_feat, text_feat, image_head, text_head, group_bias, text_lang, partner):
    rows, width = image_feat.shape
    slab = width // 8
    place = lax.axis_index(DEV)
    z, lo, hi, y, core = place // 32, place // 16 % 2, place // 8 % 2, place // 2 % 4, place % 2

    figures = jnp.stack([text_lang, partner // 128, partner % 128]).astype(b16)
    figures = jnp.pad(figures, ((0, PAD - 3), (0, width - rows)))
    text_rows = jnp.concatenate([text_feat, figures], axis=0)
    moves = (img_move, txt_move)
    rings, seconds = (z, y), (lo, hi)
    made = [None, None]
    other = {}

    def add_pair(d, pairs):
        for n in (1, 0):
            maker, head = ((img_units, image_head), (txt_units, text_head))[n]
            at = (rings[n] + d) % 4
            made[n] = maker(*pairs[n], head, at, seconds[n], rows, made[n])
        other[d] = send(made[1].pop(), core_move)

    own = (image_feat, text_rows)
    across = [send(own[n], moves[n](0, 1)) for n in range(2)]
    before = [send(own[n], moves[n](1, 0)) for n in range(2)]
    after = [send(own[n], moves[n](3, 0)) for n in range(2)]
    first = together(across + before + after)
    across, before, after = first[0:2], first[2:4], first[4:6]
    across_after = [send(across[n], moves[n](3, 0)) for n in range(2)]
    across_before = [send(across[n], moves[n](1, 0)) for n in range(2)]
    add_pair(0, [(own[n], across[n]) for n in range(2)])
    second = together(across_after + across_before + before + after)
    across_after, across_before, before, after = [second[2 * n : 2 * n + 2] for n in range(4)]
    far = [send(before[n], moves[n](1, 0)) for n in range(2)]
    across_far = [send(across_after[n], moves[n](3, 0)) for n in range(2)]
    add_pair(1, [(after[n], across_after[n]) for n in range(2)])
    add_pair(3, [(before[n], across_before[n]) for n in range(2)])
    third = together(far + across_far)
    far, across_far = third[0:2], third[2:4]
    add_pair(2, [(far[n], across_far[n]) for n in range(2)])
    blocks = [
        [
            own[n], across[n], after[n], across_after[n],
            far[n], across_far[n], before[n], across_before[n],
        ]
        for n in range(2)
    ]
    unit_img, turned_img, norm_img = made[0]
    unit_txt, norm_txt = made[1]
    chunks = [other[d] for d in range(4)]

    other_slopes, other_sum, other_up = other_tile(
        unit_img, turned_img, chunks, group_bias, place % 16, y, rows
    )
    back = send(other_up, core_move)
    text_up, img_terms = own_tile(
        unit_img, turned_img, unit_txt, chunks, other_slopes, other_sum, group_bias,
        place % 16, z, lo, rows,
    )
    far_txt = text_pieces([(y + 2) % 4], hi, text_up, back, rows)
    near_txt = text_pieces([(y + d) % 4 for d in (0, 1, 3)], hi, text_up, back, rows)
    terms = [img_terms, [*near_txt[:4], *far_txt, *near_txt[4:]]]
    got = [send(terms[n][4], moves[n](1, 0)) for n in range(2)]
    got += [send(terms[n][5], moves[n](3, 0)) for n in range(2)]
    got = together(got + [terms[n][3] for n in range(2)])
    from_before = [send(got[4 + n], moves[n](1, 0)) for n in range(2)]
    joint = sums(
        [[terms[n][7], got[2 + n]] for n in range(2)] + [[terms[n][2], got[n]] for n in range(2)],
        rows,
    )
    from_after = [send(joint[n], moves[n](3, 0)) for n in range(2)]
    got = together(from_before + from_after + joint[2:] + [terms[n][6] for n in range(2)])
    own_before = [send(got[4 + n], moves[n](1, 0)) for n in range(2)]
    own_after = [send(got[6 + n], moves[n](3, 0)) for n in range(2)]
    joint = sums([[terms[n][1], got[n], got[2 + n]] for n in range(2)], rows)
    beside = [send(joint[n], moves[n](0, 1)) for n in range(2)]
    got = together(own_before + own_after + beside)
    final = [[terms[n][0], got[n], got[2 + n], got[4 + n]] for n in range(2)]

    img_own, img_give, txt_own, txt_give, part = gradients(
        [
            (z, lo, final[0], turned_img, norm_img, blocks[0]),
            (y, hi, final[1], unit_txt, norm_txt, blocks[1]),
        ],
        rows,
    )
    heads = picked(core, part, send(part, core_move))
    heads = exchange(heads.reshape(64, 8, -1), CHIP_GROUPS)
    head_shape = jax.ShapeDtypeStruct((width // 128, width), f32)
    image_head_grad, text_head_grad = call(head_kernel, [head_shape] * 2, [core], [heads])

    grad_img = whole_columns(img_own, img_give, img_move, z, lo)
    image_grad = dot(grad_img, image_head, (((0,), (1,)), ((), ())))
    grad_txt = whole_columns(txt_own, txt_give, txt_move, y, hi)
    text_grad = dot(grad_txt, text_head, (((0,), (1,)), ((), ())))
    return (image_grad, text_grad, image_head_grad, text_head_grad)


def solution(mesh):
    line = jax.sharding.Mesh(mesh.devices.reshape(-1), (DEV,))
    in_specs = (P(DEV, None), P(DEV, None), P(), P(), P(), P(DEV), P(DEV))
    return jax.shard_map(
        shards, mesh=line, in_specs=in_specs, out_specs=(P(DEV, None),) * 4, check_vma=False
    )
```

```python
import jax
import jax.numpy as jnp
from jax import lax
from jax.experimental import pallas as pl
from jax.experimental.pallas import tpu as pltpu
from jax.sharding import PartitionSpec as P

logit_scale = 64.0
epsilon = 1e-06
log2e = 1.4426950408889634
f32, b16 = jnp.float32, jnp.bfloat16

DEV = "dev"
PLACES = [
    (z, lo, hi, y, c)
    for z in range(4)
    for lo in range(2)
    for hi in range(2)
    for y in range(4)
    for c in range(2)
]


def flat(z, lo, hi, y, c):
    return (z * 2 + lo) * 16 + hi * 8 + y * 2 + c


def img_move(d, e):
    return lambda z, lo, hi, y, c: ((z + d) % 4, lo ^ e, hi, y, c)


def txt_move(d, e):
    return lambda z, lo, hi, y, c: (z, lo ^ e, hi ^ e, (y + d) % 4, c)


def core_move(z, lo, hi, y, c):
    return (z, lo, hi, y, 1 - c)


IMG_GROUPS = [
    [flat(z, lo, hi, y, c) for z in range(4) for lo in range(2)]
    for hi in range(2)
    for y in range(4)
    for c in range(2)
]
TXT_GROUPS = [
    [flat(z, hi ^ b, hi, y, c) for y in range(4) for hi in range(2)]
    for z in range(4)
    for b in range(2)
    for c in range(2)
]
TXT_CORE_GROUPS = [
    [flat(z, hi ^ b, hi, y, c) for c in range(2) for y in range(4) for hi in range(2)]
    for z in range(4)
    for b in range(2)
]
CHIP_GROUPS = [[flat(*p) for p in PLACES if p[4] == c] for c in range(2)]


def send(block, move):
    return lax.ppermute(block, DEV, [(flat(*p), flat(*move(*p))) for p in PLACES])


def exchange(blocks, groups):
    return lax.all_to_all(blocks, DEV, 0, 0, axis_index_groups=groups, tiled=True)


PAD = 16
NN = (((1,), (0,)), ((), ()))
NT = (((1,), (1,)), ((), ()))
TN = (((0,), (0,)), ((), ()))


def dot(a, b, dims):
    return lax.dot_general(a, b, dims, preferred_element_type=f32)


def call(body, out_shape, scalars, arrays, in_specs=None, out_specs=None, grid=(), scratch=(), cost=0, limit=60):
    whole = pl.BlockSpec(memory_space=pltpu.VMEM)
    many = isinstance(out_shape, (list, tuple))
    if in_specs is None:
        in_specs = [whole] * len(arrays)
    if out_specs is None:
        out_specs = [whole] * len(out_shape) if many else whole
    spec = pltpu.PrefetchScalarGridSpec(
        num_scalar_prefetch=1,
        grid=grid,
        in_specs=in_specs,
        out_specs=out_specs,
        scratch_shapes=list(scratch),
    )
    moved = sum(a.size * a.dtype.itemsize for a in arrays)
    return pl.pallas_call(
        body,
        out_shape=out_shape,
        grid_spec=spec,
        compiler_params=pltpu.CompilerParams(vmem_limit_bytes=limit * 2**20),
        cost_estimate=pl.CostEstimate(flops=cost, bytes_accessed=moved, transcendentals=0),
    )(jnp.stack(scalars).astype(jnp.int32), *arrays)


def aligned(index, size):
    return pl.ds(pl.multiple_of(index * size, size), size)


def split_rows(total, lanes):
    high = total.astype(b16).astype(f32)
    row = lax.broadcasted_iota(jnp.int32, (PAD, lanes), 0)
    return jnp.where(row == 0, high, jnp.where(row == 1, total - high, 0.0)).astype(b16)


def joined(rows):
    return rows[0:1].astype(f32) + rows[1:2].astype(f32)


def in_pair(own, across, second, rows):
    own, across = own[:rows], across[:rows]
    first = second == 0
    return jnp.concatenate([jnp.where(first, own, across), jnp.where(first, across, own)], axis=0)


def unit_kernel(rows, extra, pairs, at_ref, *refs):
    blocks, refs = refs[: 2 * pairs], refs[2 * pairs :]
    head = None if extra else refs[0]
    turned_head, outs, proj = refs[0 if extra else 1], refs[1 if extra else 2 : -1], refs[-1]
    width = turned_head.shape[0]
    step = width // 4
    second = at_ref[0]
    each = 2 if extra else 3
    for p in range(pairs):
        own, across = blocks[2 * p], blocks[2 * p + 1]
        turned, norm = outs[each * p], outs[each * p + 1]
        feats = in_pair(own, across, second, rows)
        total = jnp.zeros((1, 2 * rows), f32)
        for m in range(4):
            span = slice(m * step, (m + 1) * step)
            part = dot(turned_head[span], feats, NT)
            proj[span] = part
            total = total + jnp.sum(part * part, axis=0, keepdims=True)
        length = jnp.sqrt(total + epsilon)
        norm[...] = length
        inverse = 1.0 / length
        for m in range(4):
            span = slice(m * step, (m + 1) * step)
            turned[span] = (proj[span] * inverse).astype(b16)
        if extra:
            first = second == 0
            sides = own[rows:, :rows], across[rows:, :rows]
            turned[width:, :rows] = jnp.where(first, sides[0], sides[1])
            turned[width:, rows:] = jnp.where(first, sides[1], sides[0])
        else:
            part = dot(feats, head[...], NN)
            total = jnp.sum(part * part, axis=1, keepdims=True)
            outs[each * p + 2][...] = (part * (1.0 / jnp.sqrt(total + epsilon))).astype(b16)


def units(pairs, heads, second, rows, extra):
    width = heads[0].shape[0]
    one = [
        jax.ShapeDtypeStruct((width + extra, 2 * rows), b16),
        jax.ShapeDtypeStruct((1, 2 * rows), f32),
    ]
    if not extra:
        one.append(jax.ShapeDtypeStruct((2 * rows, width), b16))
    out = call(
        lambda *refs: unit_kernel(rows, extra, len(pairs), *refs),
        one * len(pairs),
        [second],
        [block for pair in pairs for block in pair] + list(heads),
        scratch=[pltpu.VMEM((width, 2 * rows), f32)],
        cost=4 * rows * width * width * len(pairs) * len(heads),
        limit=24,
    )
    return [out[n : n + len(one)] for n in range(0, len(out), len(one))]


def tile_slopes(rows, groups, place, bias_ref, img, txt, slopes, by_img):
    width = img.shape[1]
    tile = 2 * rows
    lang = txt[width : width + PAD].astype(f32)
    partner = lang[1:2] * 128.0 + lang[2:3]
    lang = lang[0:1]
    bias = jnp.zeros((1, tile), f32)
    for g in range(groups):
        bias = jnp.where(lang == g, bias_ref[g], bias)
    bias = bias * -log2e
    down = jnp.zeros((1, tile), f32)
    high = 2 * rows
    for m in range(img.shape[0] // high):
        span = slice(m * high, (m + 1) * high)
        index = m * high + lax.broadcasted_iota(jnp.int32, (high, 1), 0)
        ids = ((index // rows * 16 + place) * rows + index % rows).astype(f32)
        cosines = dot(img[span], txt[:width], NN)
        below = 1.0 + jnp.exp2(cosines * (-log2e * logit_scale) + bias)
        gate = pl.reciprocal(below, approx=True)
        gate = gate * (2.0 - below * gate)
        slope = gate - jnp.where(partner == ids, 1.0, 0.0)
        slopes[span, :tile] = slope.astype(b16)
        weighted = slope * cosines
        down = down + jnp.sum(weighted, axis=0, keepdims=True)
        side = by_img[span]
        for k in range(0, tile, by_img.shape[1]):
            side = side + weighted[:, k : k + by_img.shape[1]]
        by_img[span] = side
    return logit_scale * down


def put_text_terms(up, turned, slopes, down):
    slab = turned.shape[0] // 8
    figures = split_rows(down, up.shape[1])
    part = dot(turned[...], slopes, NN)
    for e in range(8):
        at = e * (slab + PAD)
        up[at : at + slab] = part[e * slab : (e + 1) * slab].astype(b16)
        up[at + slab : at + slab + PAD] = figures


def image_sums(by_img):
    return logit_scale * jnp.sum(by_img[...].T, axis=0, keepdims=True)


def lay_out(images, ring, img, turned):
    tile = images[0].shape[1]
    for d in range(4):
        lanes = aligned((ring + d) % 4, tile)
        turned[:, lanes] = images[2 * d][...]
        img[lanes, :] = images[2 * d + 1][...]


def other_kernel(rows, groups, at_ref, bias_ref, *refs):
    images, chunks, refs = refs[:8], refs[8:12], refs[12:]
    slopes, img_sum, up, img, turned, by_img, held, kept, txt = refs
    step = pl.program_id(0)

    @pl.when(step == 0)
    def _():
        by_img[...] = jnp.zeros(by_img.shape, f32)
        lay_out(images, at_ref[2], img, turned)

    for d in range(4):

        @pl.when(step == d)
        def _():
            txt[...] = chunks[d][...]

    def slopes_now():
        out = held.at[step % 2]
        down = tile_slopes(rows, groups, at_ref[0], bias_ref, img, txt, out, by_img)
        slopes[0] = out[...]
        return down

    def terms_before():
        put_text_terms(up, turned, held[(step + 1) % 2], kept[...])

    @pl.when(step == 0)
    def _():
        kept[...] = slopes_now()

    @pl.when((step > 0) & (step < 4))
    def _():
        down = slopes_now()
        terms_before()
        kept[...] = down

    @pl.when(step == 4)
    def _():
        terms_before()
        img_sum[...] = image_sums(by_img)


def other_tile(images, chunks, group_bias, place, ring, img_ring, rows):
    width, tile = images[0].shape
    count = 4 * tile
    height = width + 8 * PAD
    whole = lambda a: pl.BlockSpec(a.shape, lambda i, at: (0, 0))
    before = lambda i: jnp.maximum(i - 1, 0)
    return call(
        lambda *refs: other_kernel(rows, group_bias.shape[0], *refs),
        [
            jax.ShapeDtypeStruct((4, count, tile), b16),
            jax.ShapeDtypeStruct((1, count), f32),
            jax.ShapeDtypeStruct((height, count), b16),
        ],
        [place, ring, img_ring],
        [group_bias, *images, *chunks],
        in_specs=[pl.BlockSpec(memory_space=pltpu.SMEM)] + [whole(a) for a in [*images, *chunks]],
        out_specs=[
            pl.BlockSpec((1, count, tile), lambda i, at: (jnp.minimum(i, 3), 0, 0)),
            pl.BlockSpec((1, count), lambda i, at: (0, 0)),
            pl.BlockSpec((height, tile), lambda i, at: (0, (at[1] + before(i)) % 4)),
        ],
        grid=(5,),
        scratch=[
            pltpu.VMEM((count, width), b16),
            pltpu.VMEM((width, count), b16),
            pltpu.VMEM((count, min(128, tile)), f32),
            pltpu.VMEM((2, count, tile), b16),
            pltpu.VMEM((1, tile), f32),
            pltpu.VMEM((width + PAD, tile), b16),
        ],
        cost=4 * width * count * count,
    )


def own_kernel(rows, groups, at_ref, bias_ref, *refs):
    images, chunks, others, refs = refs[:8], refs[8:12], refs[12:16], refs[16:]
    other_slopes, other_sum, up = refs[:3]
    outs, (img, turned, by_img, held, both, kept, txt, total) = refs[3:11], refs[11:]
    step = pl.program_id(0)
    width = img.shape[1]
    tile = 2 * rows

    @pl.when(step == 0)
    def _():
        by_img[...] = jnp.zeros(by_img.shape, f32)
        total[...] = jnp.zeros(total.shape, f32)
        lay_out(images, at_ref[1], img, turned)

    for d in range(4):

        @pl.when(step == d)
        def _():
            txt[...] = chunks[d][...]

        @pl.when(step == d + 1)
        def _():
            both[:, :tile] = chunks[d][:width]
            both[:, tile:] = others[d][:width]

    def slopes_now():
        return tile_slopes(rows, groups, at_ref[0], bias_ref, img, txt, held.at[step % 2], by_img)

    def terms_before():
        slopes = held.at[(step + 1) % 2]
        slopes[:, tile:] = other_slopes[0]
        put_text_terms(up, turned, slopes[:, :tile], kept[...])
        total[...] += dot(both[...], slopes[...], NT)

    @pl.when(step == 0)
    def _():
        kept[...] = slopes_now()

    @pl.when((step > 0) & (step < 4))
    def _():
        down = slopes_now()
        terms_before()
        kept[...] = down

    @pl.when(step == 4)
    def _():
        terms_before()
        slab = width // 8
        sums = image_sums(by_img) + other_sum[...]
        figures = split_rows(sums, sums.shape[1])
        own = at_ref[2] == 0
        for d in range(4):
            at = pl.multiple_of((at_ref[1] + d) % 4 * (2 * slab), 2 * slab)
            low, high = total[pl.ds(at, slab)], total[pl.ds(at + slab, slab)]
            outs[2 * d][:slab] = jnp.where(own, low, high).astype(b16)
            outs[2 * d][slab:] = figures
            outs[2 * d + 1][:slab] = jnp.where(own, high, low).astype(b16)
            outs[2 * d + 1][slab:] = figures


def own_tile(
    images, chunks, others, other_slopes, other_sum, group_bias, place, ring, second, txt_ring, rows
):
    width, tile = images[0].shape
    count = 4 * tile
    height = width + 8 * PAD
    slab = width // 8
    whole = lambda a: pl.BlockSpec(a.shape, lambda i, at: (0, 0))
    before = lambda i: jnp.maximum(i - 1, 0)
    piece = jax.ShapeDtypeStruct((slab + PAD, count), b16)
    blocks = [*images, *chunks, *others]
    out = call(
        lambda *refs: own_kernel(rows, group_bias.shape[0], *refs),
        [jax.ShapeDtypeStruct((height, count), b16)] + [piece] * 8,
        [place, ring, second, txt_ring],
        [group_bias, *blocks, other_slopes, other_sum],
        in_specs=[pl.BlockSpec(memory_space=pltpu.SMEM)]
        + [whole(a) for a in blocks]
        + [pl.BlockSpec((1, count, tile), lambda i, at: (before(i), 0, 0)), whole(other_sum)],
        out_specs=[pl.BlockSpec((height, tile), lambda i, at: (0, (at[3] + before(i)) % 4))]
        + [whole(piece)] * 8,
        grid=(5,),
        scratch=[
            pltpu.VMEM((count, width), b16),
            pltpu.VMEM((width, count), b16),
            pltpu.VMEM((count, min(128, tile)), f32),
            pltpu.VMEM((2, count, 2 * tile), b16),
            pltpu.VMEM((width, 2 * tile), b16),
            pltpu.VMEM((1, tile), f32),
            pltpu.VMEM((width + PAD, tile), b16),
            pltpu.VMEM((width, count), f32),
        ],
        cost=8 * width * count * count,
    )
    return out[0], out[1:]


def sum_into(out, terms):
    slab = out.shape[0] - PAD
    block, total = terms[0][:slab].astype(f32), joined(terms[0][slab:])
    for term in terms[1:]:
        block, total = block + term[:slab].astype(f32), total + joined(term[slab:])
    out[:slab] = block.astype(b16)
    out[slab:] = split_rows(total, out.shape[1])


def sum_kernel(sizes, at_ref, *refs):
    start = 0
    for size, out in zip(sizes, refs[sum(sizes) :]):
        sum_into(out, refs[start : start + size])
        start += size


def sums(groups, rows):
    flat_terms = [term for group in groups for term in group]
    arrays, specs, places = [], [], [jnp.int32(0)]
    height = None
    for term in flat_terms:
        if isinstance(term, tuple):
            arrays.append(term[0])
            height = term[0].shape[0] // 8
            specs.append(
                pl.BlockSpec((height, 4 * rows), lambda i, at, n=len(places): (at[n], i))
            )
            places.append(term[1])
        else:
            arrays.append(term)
            height = term.shape[0]
            specs.append(pl.BlockSpec((height, 4 * rows), lambda i, at: (0, i)))
    count = arrays[0].shape[1]
    spec = pl.BlockSpec((height, 4 * rows), lambda i, at: (0, i))
    return call(
        lambda *refs: sum_kernel([len(group) for group in groups], *refs),
        [jax.ShapeDtypeStruct((height, count), b16)] * len(groups),
        places,
        arrays,
        in_specs=specs,
        out_specs=[spec] * len(groups),
        grid=(count // (4 * rows),),
    )


def grad_kernel(rows, sizes, at_ref, *refs):
    part, grad = refs[-2:]
    outs = refs[-6:-2]
    start = 0
    for n in range(2):
        mine = refs[start : start + sizes[n] + 16]
        start += sizes[n] + 16
        terms, mine = mine[: sizes[n]], mine[sizes[n] :]
        unit, norm, blocks = mine[:4], mine[4:8], mine[8:]
        ring_at, second = at_ref[4 * n], at_ref[4 * n + 1]
        slab = unit[0].shape[0]
        for d in range(4):
            lanes = aligned((ring_at + d) % 4, 2 * rows)
            up, inner = terms[0][:slab, lanes].astype(f32), joined(terms[0][slab:, lanes])
            for term in terms[1:]:
                up, inner = up + term[:slab, lanes].astype(f32), inner + joined(term[slab:, lanes])
            up = logit_scale * up - unit[d][...].astype(f32) * inner
            grad[n, :, lanes] = (up * (1.0 / norm[d][...])).astype(b16)
        own, give = outs[2 * n : 2 * n + 2]
        for ring in range(4):
            low = grad[n, :, (2 * ring) * rows : (2 * ring + 1) * rows]
            high = grad[n, :, (2 * ring + 1) * rows : (2 * ring + 2) * rows]
            own[ring] = jnp.where(second == 0, low, high)
            give[ring] = jnp.where(second == 0, high, low)
        total = None
        for d in range(4):
            cols = grad[n, :, aligned((ring_at + d) % 4, 2 * rows)]
            term = dot(cols, in_pair(blocks[2 * d], blocks[2 * d + 1], second, rows), NN)
            total = term if total is None else total + term
        part[n * slab : (n + 1) * slab] = total.astype(b16)


def gradients(towers, rows):
    arrays, specs, scalars = [], [], []
    whole = lambda a: pl.BlockSpec(a.shape, lambda i, at: (0,) * len(a.shape))
    for n, (ring, second, place, terms, unit, norm, blocks) in enumerate(towers):
        width = blocks[0].shape[1]
        slab, count = width // 8, 8 * rows
        for term in terms:
            if isinstance(term, tuple):
                arrays.append(term[0])
                specs.append(
                    pl.BlockSpec((slab + PAD, count), lambda i, at, n=n: (at[4 * n + 2], 0))
                )
            else:
                arrays.append(term)
                specs.append(whole(term))
        arrays += [*unit, *norm, *blocks]
        specs += [
            pl.BlockSpec((slab, 2 * rows), lambda i, at, n=n: (at[4 * n + 2], 0)) for _ in unit
        ]
        specs += [whole(a) for a in [*norm, *blocks]]
        scalars += [ring, second, place, place]
    block = jax.ShapeDtypeStruct((4, slab, rows), b16)
    term = jax.ShapeDtypeStruct((2 * slab, width), b16)
    return call(
        lambda *refs: grad_kernel(rows, [len(tower[3]) for tower in towers], *refs),
        [block] * 4 + [term],
        scalars,
        arrays,
        in_specs=specs,
        out_specs=[whole(block)] * 4 + [whole(term)],
        grid=(1,),
        scratch=[pltpu.VMEM((2, slab, count), b16)],
        cost=4 * slab * count * width,
    )


def pick_kernel(at_ref, mine, theirs, out):
    width = mine.shape[1]
    slots = out.shape[0]
    own = width // 128
    third = mine.shape[0] // 3
    part = (mine[...].astype(f32) + theirs[...].astype(f32)).astype(b16)
    slot = lax.broadcasted_iota(jnp.int32, (slots, 1), 0)
    feature = lax.broadcasted_iota(jnp.int32, (slots, width), 1)
    base = (slot // 8 * 2 + at_ref[0]) * own
    chosen = jnp.where(feature == base + slot % 8, 1.0, 0.0).astype(b16)
    out[:, : 3 * third] = dot(chosen, part, NT).astype(b16)
    chosen = jnp.where(feature == base + 8, 1.0, 0.0).astype(b16)
    ninth = dot(chosen, part, NT)
    pick = slot % 8
    rest = jnp.where(pick == 1, ninth[:, third : 2 * third], ninth[:, :third])
    rest = jnp.where(pick == 2, ninth[:, 2 * third :], rest)
    out[:, 3 * third :] = rest.astype(b16)


def picked(core, mine, theirs):
    both, width = mine.shape
    return call(
        pick_kernel,
        jax.ShapeDtypeStruct((64 * 8, both * 4 // 3), b16),
        [core],
        [mine, theirs],
        cost=4 * 512 * width * both,
    )


def head_kernel(at_ref, got, img_out, txt_out):
    slab = img_out.shape[1] // 8
    third = slab * 2 // 3
    half = third // 2
    for p in range(8):
        img = txt = None
        for other in range(8):
            z, lo, hi, y = p // 2, p % 2, other // 4, other % 4
            block = got[(z * 2 + lo) * 8 + hi * 4 + y].astype(f32)
            img = block if img is None else img + block
            z, lo, hi, y = other // 2, other % 2, p % 2, p // 2
            block = got[(z * 2 + lo) * 8 + hi * 4 + y].astype(f32)
            txt = block if txt is None else txt + block
        at = p * slab
        ninth = 2 * slab
        img_out[0:8, at : at + slab] = img[:, :slab]
        img_out[8:9, at : at + third] = img[0:1, ninth : ninth + third]
        img_out[8:9, at + third : at + slab] = img[1:2, ninth : ninth + half]
        txt_out[0:8, at : at + slab] = txt[:, slab : 2 * slab]
        txt_out[8:9, at : at + half] = txt[1:2, ninth + half : ninth + third]
        txt_out[8:9, at + half : at + slab] = txt[2:3, ninth : ninth + third]


def together(arrays):
    return lax.optimization_barrier(list(arrays))


def pair_lines(own, got, second):
    return jnp.concatenate([jnp.where(second, got, own), jnp.where(second, own, got)], axis=1)


def whole_columns(lines, move, ring):
    out = jnp.zeros(lines.shape, lines.dtype)
    for d in range(4):
        block = lax.dynamic_index_in_dim(lines, (ring + d) % 4, 0, keepdims=True)
        if d:
            block = send(block, move(d, 0))
        out = lax.dynamic_update_slice_in_dim(out, block, (ring + 4 - d) % 4, axis=0)
    return out.reshape(-1, lines.shape[2])


def shards(image_feat, text_feat, image_head, text_head, group_bias, text_lang, partner):
    rows, width = image_feat.shape
    slab = width // 8
    place = lax.axis_index(DEV)
    z, lo, hi, y, core = place // 32, place // 16 % 2, place // 8 % 2, place // 2 % 4, place % 2

    figures = jnp.stack([text_lang, partner // 128, partner % 128]).astype(b16)
    figures = jnp.pad(figures, ((0, PAD - 3), (0, width - rows)))
    text_rows = jnp.concatenate([text_feat, figures], axis=0)
    moves = (img_move, txt_move)
    turned_heads = (image_head.T, text_head.T)

    own = (image_feat, text_rows)
    across = [send(own[n], moves[n](0, 1)) for n in range(2)]
    before = [send(own[n], moves[n](1, 0)) for n in range(2)]
    after = [send(own[n], moves[n](3, 0)) for n in range(2)]
    across = together(across)
    across_after = [send(across[n], moves[n](3, 0)) for n in range(2)]
    across_before = [send(across[n], moves[n](1, 0)) for n in range(2)]
    got = together(across_after + before + after + across)
    across_after, before, after, across = [got[2 * n : 2 * n + 2] for n in range(4)]
    far = [send(before[n], moves[n](1, 0)) for n in range(2)]
    across_far = [send(across_after[n], moves[n](3, 0)) for n in range(2)]
    img_heads, txt_heads = [image_head, turned_heads[0]], [turned_heads[1]]
    pairs = [
        [(own[n], across[n]), (after[n], across_after[n]), (before[n], across_before[n])]
        for n in range(2)
    ]
    txt_made = units(pairs[1], txt_heads, hi, rows, PAD)
    img_made = units(pairs[0], img_heads, lo, rows, 0)
    others = [send(made[0], core_move) for made in txt_made]
    got = together(far + across_far)
    far, across_far = got[0:2], got[2:4]
    (last,) = units([(far[1], across_far[1])], txt_heads, hi, rows, PAD)
    txt_made.insert(2, last)
    others.insert(2, send(last[0], core_move))
    img_made[2:2] = units([(far[0], across_far[0])], img_heads, lo, rows, 0)
    blocks = [
        [
            own[n], across[n], after[n], across_after[n],
            far[n], across_far[n], before[n], across_before[n],
        ]
        for n in range(2)
    ]
    images = [part for made in img_made for part in (made[0], made[2])]
    chunks = [made[0] for made in txt_made]

    other_slopes, other_sum, other_up = other_tile(
        images, others, group_bias, place % 16, y, z, rows
    )
    back = send(other_up, core_move)
    text_up, img_terms = own_tile(
        images, chunks, others, other_slopes, other_sum, group_bias, place % 16, z, lo, y, rows
    )

    def txt_slab(d, e):
        at = (y + d) % 4 * 2 + (hi + e) % 2
        return [(text_up, at), (back, at)]

    def img_slab(d, e):
        return [img_terms[2 * d + e]]

    slabs = (img_slab, txt_slab)
    txt_far, txt_across_far, txt_across_after = sums(
        [txt_slab(2, 0), txt_slab(2, 1), txt_slab(1, 1)], rows
    )
    far = [send(img_terms[4], img_move(1, 0)), send(txt_far, txt_move(1, 0))]
    across_far = [send(img_terms[5], img_move(3, 0)), send(txt_across_far, txt_move(3, 0))]
    across_before = [send(img_terms[3], img_move(1, 0)), send(txt_across_after, txt_move(1, 0))]
    joint = sums(
        [slabs[n](3, 1) + [across_far[n]] for n in range(2)]
        + [slabs[n](1, 0) + [far[n]] for n in range(2)]
        + [txt_slab(3, 0)],
        rows,
    )
    across_after = [send(joint[n], moves[n](3, 0)) for n in range(2)]
    before = [send(joint[2 + n], moves[n](1, 0)) for n in range(2)]
    after = [send(img_terms[6], img_move(3, 0)), send(joint[4], txt_move(3, 0))]
    joint = sums([slabs[n](0, 1) + [across_before[n], across_after[n]] for n in range(2)], rows)
    across = [send(joint[n], moves[n](0, 1)) for n in range(2)]
    final = [slabs[n](0, 0) + [before[n], after[n], across[n]] for n in range(2)]

    img_own, img_give, txt_own, txt_give, part = gradients(
        [
            (z, lo, z * 2 + lo, final[0], images[::2], [made[1] for made in img_made], blocks[0]),
            (y, hi, y * 2 + hi, final[1], chunks, [made[1] for made in txt_made], blocks[1]),
        ],
        rows,
    )
    theirs, img_got, txt_got = together(
        [send(part, core_move), send(img_give, img_move(0, 1)), send(txt_give, txt_move(0, 1))]
    )
    heads, img_lines, txt_lines = together(
        [
            picked(core, part, theirs),
            pair_lines(img_own, img_got, lo),
            pair_lines(txt_own, txt_got, hi),
        ]
    )
    heads = exchange(heads.reshape(64, 8, -1), CHIP_GROUPS)
    head_shape = jax.ShapeDtypeStruct((width // 128, width), f32)
    image_head_grad, text_head_grad = call(head_kernel, [head_shape] * 2, [core], [heads])

    grad_img = whole_columns(img_lines, img_move, z)
    image_grad = dot(grad_img, image_head, (((0,), (1,)), ((), ())))
    grad_txt = whole_columns(txt_lines, txt_move, y)
    text_grad = dot(grad_txt, text_head, (((0,), (1,)), ((), ())))
    return (image_grad, text_grad, image_head_grad, text_head_grad)


def solution(mesh):
    line = jax.sharding.Mesh(mesh.devices.reshape(-1), (DEV,))
    in_specs = (P(DEV, None), P(DEV, None), P(), P(), P(), P(DEV), P(DEV))
    return jax.shard_map(
        shards, mesh=line, in_specs=in_specs, out_specs=(P(DEV, None),) * 4, check_vma=False
    )
```

```python
import jax
import jax.numpy as jnp
from jax import lax
from jax.experimental import pallas as pl
from jax.experimental.pallas import tpu as pltpu
from jax.sharding import PartitionSpec as P

logit_scale = 64.0
epsilon = 1e-06
f32, b16 = jnp.float32, jnp.bfloat16

DEV = "dev"
PLACES = [
    (z, lo, hi, y, c)
    for z in range(4)
    for lo in range(2)
    for hi in range(2)
    for y in range(4)
    for c in range(2)
]


def flat(z, lo, hi, y, c):
    return (z * 2 + lo) * 16 + hi * 8 + y * 2 + c


def img_move(d, e):
    return lambda z, lo, hi, y, c: ((z + d) % 4, lo ^ e, hi, y, c)


def txt_move(d, e):
    return lambda z, lo, hi, y, c: (z, lo ^ e, hi ^ e, (y + d) % 4, c)


def core_move(z, lo, hi, y, c):
    return (z, lo, hi, y, 1 - c)


IMG_GROUPS = [
    [flat(z, lo, hi, y, c) for z in range(4) for lo in range(2)]
    for hi in range(2)
    for y in range(4)
    for c in range(2)
]
TXT_GROUPS = [
    [flat(z, hi ^ b, hi, y, c) for y in range(4) for hi in range(2)]
    for z in range(4)
    for b in range(2)
    for c in range(2)
]
TXT_CORE_GROUPS = [
    [flat(z, hi ^ b, hi, y, c) for c in range(2) for y in range(4) for hi in range(2)]
    for z in range(4)
    for b in range(2)
]
CHIP_GROUPS = [[flat(*p) for p in PLACES if p[4] == c] for c in range(2)]


def send(block, move):
    return lax.ppermute(block, DEV, [(flat(*p), flat(*move(*p))) for p in PLACES])


def exchange(blocks, groups):
    return lax.all_to_all(blocks, DEV, 0, 0, axis_index_groups=groups, tiled=True)


PAD = 16
NN = (((1,), (0,)), ((), ()))
NT = (((1,), (1,)), ((), ()))
TN = (((0,), (0,)), ((), ()))


def dot(a, b, dims):
    return lax.dot_general(a, b, dims, preferred_element_type=f32)


def call(body, out_shape, scalars, arrays, in_specs=None, out_specs=None, grid=(), scratch=(), cost=0, aliases=None):
    whole = pl.BlockSpec(memory_space=pltpu.VMEM)
    many = isinstance(out_shape, (list, tuple))
    if in_specs is None:
        in_specs = [whole] * len(arrays)
    if out_specs is None:
        out_specs = [whole] * len(out_shape) if many else whole
    spec = pltpu.PrefetchScalarGridSpec(
        num_scalar_prefetch=1,
        grid=grid,
        in_specs=in_specs,
        out_specs=out_specs,
        scratch_shapes=list(scratch),
    )
    moved = sum(a.size * a.dtype.itemsize for a in arrays)
    return pl.pallas_call(
        body,
        out_shape=out_shape,
        grid_spec=spec,
        input_output_aliases=aliases or {},
        compiler_params=pltpu.CompilerParams(vmem_limit_bytes=60 * 2**20),
        cost_estimate=pl.CostEstimate(flops=cost, bytes_accessed=moved, transcendentals=0),
    )(jnp.stack(scalars).astype(jnp.int32), *arrays)


def aligned(index, size):
    return pl.ds(pl.multiple_of(index * size, size), size)


def split_rows(total, lanes):
    high = total.astype(b16).astype(f32)
    row = lax.broadcasted_iota(jnp.int32, (PAD, lanes), 0)
    return jnp.where(row == 0, high, jnp.where(row == 1, total - high, 0.0)).astype(b16)


def joined(rows):
    return rows[0:1].astype(f32) + rows[1:2].astype(f32)


def in_pair(own, across, second, rows):
    own, across = own[:rows], across[:rows]
    first = second == 0
    return jnp.concatenate([jnp.where(first, own, across), jnp.where(first, across, own)], axis=0)


def unit_kernel(rows, extra, pairs, at_ref, *refs):
    blocks, head, feats = refs[: 2 * pairs], refs[2 * pairs], refs[-1]
    outs = refs[-5:-1] if extra else refs[-3:-1]
    second = at_ref[0]
    step = pl.program_id(0)
    for p in range(pairs):
        own, across = blocks[2 * p], blocks[2 * p + 1]

        @pl.when(step == p)
        def _():
            feats[...] = in_pair(own, across, second, rows)
            if extra:
                first = second == 0
                sides = own[rows:, :rows], across[rows:, :rows]
                outs[2][:, :rows] = jnp.where(first, sides[0], sides[1])
                outs[2][:, rows:] = jnp.where(first, sides[1], sides[0])

    projected = dot(feats[...], head[...], NN)
    length = jnp.sqrt(jnp.sum(projected * projected, axis=1, keepdims=True) + epsilon)
    unit = (projected * (1.0 / length)).astype(b16)
    outs[0][...] = unit
    outs[1][...] = jnp.broadcast_to(length, (2 * rows, 128)).T[0:1]
    if extra:
        outs[3][0, : 2 * rows] = unit
        outs[3][0, 2 * rows :] = jnp.zeros(outs[3].shape[1:], b16)[2 * rows :]
        outs[3][0, 2 * rows :, : 2 * rows] = outs[2][...]


def units(pairs, head, second, places, rows, extra, carried):
    width = head.shape[0]
    whole = lambda a: pl.BlockSpec(a.shape, lambda i, at: (0, 0))
    tile = 2 * rows
    out = [
        jax.ShapeDtypeStruct((8 * rows * (2 if extra else 1), width), b16),
        jax.ShapeDtypeStruct((1, 8 * rows), f32),
    ]
    steps = [
        pl.BlockSpec((tile, width), lambda i, at: (at[1 + i], 0)),
        pl.BlockSpec((1, tile), lambda i, at: (0, at[1 + i])),
    ]
    if extra:
        out += [
            jax.ShapeDtypeStruct((extra, 16 * rows), b16),
            jax.ShapeDtypeStruct((len(pairs), tile + extra, width), b16),
        ]
        steps += [
            pl.BlockSpec((extra, tile), lambda i, at: (0, at[1 + i])),
            pl.BlockSpec((1, tile + extra, width), lambda i, at: (i, 0, 0)),
        ]
    blocks = [block for pair in pairs for block in pair]
    return call(
        lambda *refs: unit_kernel(rows, extra, len(pairs), *refs),
        out,
        [second, *places],
        [*blocks, head, *carried],
        in_specs=[whole(a) for a in [*blocks, head]]
        + [pl.BlockSpec(memory_space=pl.ANY)] * len(carried),
        out_specs=steps,
        grid=(len(pairs),),
        scratch=[pltpu.VMEM((tile, width), b16)],
        cost=2 * tile * width * width * len(pairs),
        aliases={len(blocks) + 2 + n: n for n in range(len(carried))},
    )


def put_kernel(at_ref, got, unit_in, figures_in, unit, figures):
    tile = unit.shape[0]
    unit[...] = got[0, :tile]
    figures[...] = got[0, tile:, :tile]


def put_others(got, places, unit, figures):
    pairs, height, width = got.shape
    tile = unit.shape[0] // 8
    return call(
        put_kernel,
        [jax.ShapeDtypeStruct(unit.shape, b16), jax.ShapeDtypeStruct(figures.shape, b16)],
        places,
        [got, unit, figures],
        in_specs=[pl.BlockSpec((1, height, width), lambda i, at: (i, 0, 0))]
        + [pl.BlockSpec(memory_space=pl.ANY)] * 2,
        out_specs=[
            pl.BlockSpec((tile, width), lambda i, at: (4 + at[i], 0)),
            pl.BlockSpec((PAD, tile), lambda i, at: (0, 4 + at[i])),
        ],
        grid=(pairs,),
        aliases={2: 0, 3: 1},
    )


def total_of(terms, height, lanes=slice(None)):
    slabs, loads, figures = terms
    block, total = None, None
    for ref in [*slabs, *loads]:
        part = ref[:height, lanes].astype(f32)
        block = part if block is None else block + part
    for part in [ref[:, lanes] for ref in figures] + [joined(ref[height:, lanes]) for ref in loads]:
        total = part if total is None else total + part
    return block, total


def take(refs, shape):
    out = []
    for size in shape:
        out.append(refs[:size])
        refs = refs[size:]
    return out, refs


def group_specs(groups, slab, lanes, first, moving):
    arrays, specs, places = [], [], []
    for slabs, loads, figures in groups:
        for array, place in slabs:
            arrays.append(array)
            specs.append(
                pl.BlockSpec(
                    (slab, lanes), lambda i, at, n=first + len(places): (at[n], moving * i)
                )
            )
            places.append(place)
        for load in loads:
            arrays.append(load)
            specs.append(pl.BlockSpec((slab + PAD, lanes), lambda i, at: (0, moving * i)))
        for figure in figures:
            arrays.append(figure)
            specs.append(pl.BlockSpec((1, lanes), lambda i, at: (0, moving * i)))
    return arrays, specs, places


def sum_kernel(shapes, slab, at_ref, *refs):
    for shape, out in zip(shapes, refs[len(refs) - len(shapes) :]):
        terms, refs = take(refs, shape)
        block, total = total_of(terms, slab)
        out[:slab] = block.astype(b16)
        out[slab:] = split_rows(total, out.shape[1])


def sums(groups, slab, rows):
    lanes = 4 * rows
    count = 8 * rows
    arrays, specs, places = group_specs(groups, slab, lanes, 1, 1)
    shapes = [[len(part) for part in group] for group in groups]
    return call(
        lambda *refs: sum_kernel(shapes, slab, *refs),
        [jax.ShapeDtypeStruct((slab + PAD, count), b16)] * len(groups),
        [jnp.int32(0), *places],
        arrays,
        in_specs=specs,
        out_specs=[pl.BlockSpec((slab + PAD, lanes), lambda i, at: (0, i))] * len(groups),
        grid=(count // lanes,),
    )


def grad_kernel(rows, shape, at_ref, *refs):
    terms, refs = take(refs, shape)
    unit, norm, blocks, (own, give, part, grad) = refs[0], refs[1], refs[2:10], refs[10:]
    ring_at, second = at_ref[0], at_ref[1]
    slab = unit.shape[0]
    up, inner = total_of(terms, slab)
    up = logit_scale * up - unit[...].astype(f32) * inner
    grad[...] = (up * (1.0 / norm[...])).astype(b16)
    for ring in range(4):
        low = grad[:, (2 * ring) * rows : (2 * ring + 1) * rows]
        high = grad[:, (2 * ring + 1) * rows : (2 * ring + 2) * rows]
        own[ring] = jnp.where(second == 0, low, high)
        give[ring] = jnp.where(second == 0, high, low)
    total = None
    for d in range(4):
        cols = grad[:, aligned((ring_at + d) % 4, 2 * rows)]
        term = dot(cols, in_pair(blocks[2 * d], blocks[2 * d + 1], second, rows), NN)
        total = term if total is None else total + term
    part[...] = total.astype(b16)


def gradient(ring, second, group, unit, norm, blocks, rows):
    slab, count = unit.shape
    width = blocks[0].shape[1]
    whole = lambda a: pl.BlockSpec(a.shape, lambda i, at: (0,) * len(a.shape))
    arrays, specs, places = group_specs([group], slab, count, 2, 0)
    rest = [unit, norm, *blocks]
    block = jax.ShapeDtypeStruct((4, slab, rows), b16)
    term = jax.ShapeDtypeStruct((slab, width), b16)
    return call(
        lambda *refs: grad_kernel(rows, [len(part) for part in group], *refs),
        [block, block, term],
        [ring, second, *places],
        [*arrays, *rest],
        in_specs=specs + [whole(a) for a in rest],
        out_specs=[whole(block), whole(block), whole(term)],
        grid=(1,),
        scratch=[pltpu.VMEM((slab, count), b16)],
        cost=2 * slab * count * width,
    )


def line_kernel(at_ref, *refs):
    for n in range(2):
        (own, got), outs = refs[2 * n : 2 * n + 2], refs[4 + 4 * n : 8 + 4 * n]
        slab = own.shape[1]
        first = at_ref[2 * n + 1] == 0
        for d in range(4):
            ring = (at_ref[2 * n] + d) % 4
            mine, theirs = own[ring], got[ring]
            outs[d][:slab] = jnp.where(first, mine, theirs)
            outs[d][slab:] = jnp.where(first, theirs, mine)


def lines(towers):
    slab, rows = towers[0][2].shape[1:]
    out = call(
        line_kernel,
        [jax.ShapeDtypeStruct((2 * slab, rows), b16)] * 8,
        [place for tower in towers for place in tower[:2]],
        [block for tower in towers for block in tower[2:]],
    )
    return out[:4], out[4:]


def row_kernel(at_ref, *refs):
    outs, whole = refs[10:12], refs[12]
    for n in range(2):
        parts, head = refs[5 * n : 5 * n + 4], refs[5 * n + 4]
        height = parts[0].shape[0]
        for d in range(4):
            whole[aligned((at_ref[n] + 4 - d) % 4, height), :] = parts[d][...].astype(f32)
        grad = whole[...].T.astype(b16)
        outs[n][...] = dot(grad, head[...], NT)


def feature_grads(towers):
    height, rows = towers[0][1][0].shape
    width = 4 * height
    arrays = []
    for _, parts, head in towers:
        arrays += [*parts, head]
    return call(
        row_kernel,
        [jax.ShapeDtypeStruct((rows, width), f32)] * 2,
        [tower[0] for tower in towers],
        arrays,
        scratch=[pltpu.VMEM((width, rows), f32)],
        cost=4 * rows * width * width,
    )


def pick_kernel(at_ref, img, txt, other_img, other_txt, out):
    width = img.shape[1]
    slots = out.shape[0]
    own = width // 128
    third = 2 * img.shape[0] // 3
    img = img[...].astype(f32) + other_img[...].astype(f32)
    txt = txt[...].astype(f32) + other_txt[...].astype(f32)
    part = jnp.concatenate([img, txt], axis=0).astype(b16)
    slot = lax.broadcasted_iota(jnp.int32, (slots, 1), 0)
    feature = lax.broadcasted_iota(jnp.int32, (slots, width), 1)
    base = (slot // 8 * 2 + at_ref[0]) * own
    chosen = jnp.where(feature == base + slot % 8, 1.0, 0.0).astype(b16)
    out[:, : 3 * third] = dot(chosen, part, NT).astype(b16)
    chosen = jnp.where(feature == base + 8, 1.0, 0.0).astype(b16)
    ninth = dot(chosen, part, NT)
    pick = slot % 8
    rest = jnp.where(pick == 1, ninth[:, third : 2 * third], ninth[:, :third])
    rest = jnp.where(pick == 2, ninth[:, 2 * third :], rest)
    out[:, 3 * third :] = rest.astype(b16)


def picked(core, parts):
    slab, width = parts[0].shape
    return call(
        pick_kernel,
        jax.ShapeDtypeStruct((64 * 8, slab * 8 // 3), b16),
        [core],
        parts,
        cost=8 * 512 * width * slab,
    )


def head_kernel(at_ref, got, img_out, txt_out):
    slab = img_out.shape[1] // 8
    third = slab * 2 // 3
    half = third // 2
    for p in range(8):
        img = txt = None
        for other in range(8):
            z, lo, hi, y = p // 2, p % 2, other // 4, other % 4
            block = got[(z * 2 + lo) * 8 + hi * 4 + y].astype(f32)
            img = block if img is None else img + block
            z, lo, hi, y = other // 2, other % 2, p % 2, p // 2
            block = got[(z * 2 + lo) * 8 + hi * 4 + y].astype(f32)
            txt = block if txt is None else txt + block
        at = p * slab
        ninth = 2 * slab
        img_out[0:8, at : at + slab] = img[:, :slab]
        img_out[8:9, at : at + third] = img[0:1, ninth : ninth + third]
        img_out[8:9, at + third : at + slab] = img[1:2, ninth : ninth + half]
        txt_out[0:8, at : at + slab] = txt[:, slab : 2 * slab]
        txt_out[8:9, at : at + half] = txt[1:2, ninth + half : ninth + third]
        txt_out[8:9, at + half : at + slab] = txt[2:3, ninth : ninth + third]


def together(arrays):
    return lax.optimization_barrier(list(arrays))


def shards(image_feat, text_feat, image_head, text_head, group_bias, text_lang, partner):
    rows, width = image_feat.shape
    slab = width // 8
    place = lax.axis_index(DEV)
    z, lo, hi, y, core = place // 32, place // 16 % 2, place // 8 % 2, place // 2 % 4, place % 2

    figures = jnp.stack([text_lang, partner // 128, partner % 128]).astype(b16)
    figures = jnp.pad(figures, ((0, PAD - 3), (0, width - rows)))
    text_rows = jnp.concatenate([text_feat, figures], axis=0)
    moves = (img_move, txt_move)

    own = (image_feat, text_rows)
    across = [send(own[n], moves[n](0, 1)) for n in range(2)]
    before = [send(own[n], moves[n](1, 0)) for n in range(2)]
    after = [send(own[n], moves[n](3, 0)) for n in range(2)]
    across = together(across)
    across_after = [send(across[n], moves[n](3, 0)) for n in range(2)]
    across_before = [send(across[n], moves[n](1, 0)) for n in range(2)]
    got = together(across_after + before + after + across)
    across_after, before, after, across = [got[2 * n : 2 * n + 2] for n in range(4)]
    far = [send(before[n], moves[n](1, 0)) for n in range(2)]
    across_far = [send(across_after[n], moves[n](3, 0)) for n in range(2)]
    pairs = [
        [(own[n], across[n]), (after[n], across_after[n]), (before[n], across_before[n])]
        for n in range(2)
    ]
    near_y, near_z = ([(ring + d) % 4 for d in (0, 1, 3)] for ring in (y, z))
    far_y, far_z = [(y + 2) % 4], [(z + 2) % 4]
    unit_txt, norm_txt, figures, mine = units(pairs[1], text_head, hi, near_y, rows, PAD, ())
    theirs = send(mine, core_move)
    unit_img, norm_img = units(pairs[0], image_head, lo, near_z, rows, 0, ())
    got = together(far + across_far)
    far, across_far = got[0:2], got[2:4]
    unit_txt, norm_txt, figures, mine = units(
        [(far[1], across_far[1])], text_head, hi, far_y, rows, PAD, (unit_txt, norm_txt, figures)
    )
    far_theirs = send(mine, core_move)
    unit_img, norm_img = units(
        [(far[0], across_far[0])], image_head, lo, far_z, rows, 0, (unit_img, norm_img)
    )
    unit_txt, figures = put_others(theirs, near_y, unit_txt, figures)
    unit_txt, figures = put_others(far_theirs, far_y, unit_txt, figures)
    blocks = [
        [
            own[n], across[n], after[n], across_after[n],
            far[n], across_far[n], before[n], across_before[n],
        ]
        for n in range(2)
    ]

    count = 8 * rows
    index = jnp.arange(count, dtype=jnp.int32)
    image_ids = ((index // rows * 16 + place % 16) * rows + index % rows).astype(f32)
    figures = figures[:3].astype(f32)
    groups = jnp.arange(group_bias.shape[0], dtype=jnp.int32).astype(f32)
    bias = jnp.sum(jnp.where(figures[0][:, None] == groups, group_bias, 0.0), axis=1)
    partners = figures[1] * 128.0 + figures[2]
    cosines = logit_scale * dot(unit_img, unit_txt, NT)
    positive = (partners[None, :] == image_ids[:, None]).astype(f32)
    slopes = (jax.nn.sigmoid(cosines + bias[None, :]) - positive).astype(b16)
    weighted = slopes.astype(f32) * cosines
    img_sum = jnp.sum(weighted, axis=1).reshape(1, count)
    txt_sum = jnp.sum(weighted, axis=0).reshape(2, count)
    back = send(dot(unit_img, slopes[:, count:], TN).astype(b16), core_move)
    back_sum = send(txt_sum[1:], core_move)
    text_up = dot(unit_img, slopes[:, :count], TN).astype(b16)
    image_up = dot(unit_txt, slopes, (((0,), (1,)), ((), ()))).astype(b16)

    def img_group(d, e, *loads):
        return [(image_up, (z + d) % 4 * 2 + (lo + e) % 2)], loads, [img_sum]

    def txt_group(d, e, *loads):
        at = (y + d) % 4 * 2 + (hi + e) % 2
        return [(text_up, at), (back, at)], loads, [txt_sum[:1], back_sum]

    def reduced(group, move):
        far, across_far, across_after = sums([group(2, 0), group(2, 1), group(1, 1)], slab, rows)
        far = send(far, move(1, 0))
        across_far = send(across_far, move(3, 0))
        far, across_far, across_after = together([far, across_far, across_after])
        across_before = send(across_after, move(1, 0))
        across_after, before, after = sums(
            [group(3, 1, across_far), group(1, 0, far), group(3, 0)], slab, rows
        )
        across_after = send(across_after, move(3, 0))
        across_before, across_after, before, after = together(
            [across_before, across_after, before, after]
        )
        before = send(before, move(1, 0))
        after = send(after, move(3, 0))
        (across,) = sums([group(0, 1, across_before, across_after)], slab, rows)
        return [before, after, send(across, move(0, 1))]

    def own_columns(unit, at):
        return lax.dynamic_slice(unit, (0, at * slab), (count, slab)).T

    txt_loads = reduced(txt_group, txt_move)
    img_loads = reduced(img_group, img_move)
    txt_own, txt_give, txt_part = gradient(
        y, hi, txt_group(0, 0, *txt_loads), own_columns(unit_txt[:count], y * 2 + hi), norm_txt,
        blocks[1], rows,
    )
    img_own, img_give, img_part = gradient(
        z, lo, img_group(0, 0, *img_loads), own_columns(unit_img, z * 2 + lo), norm_img,
        blocks[0], rows,
    )
    others = together(
        [
            send(txt_part, core_move),
            send(txt_give, txt_move(0, 1)),
            send(img_part, core_move),
            send(img_give, img_move(0, 1)),
        ]
    )
    heads = picked(core, [img_part, txt_part, others[2], others[0]])
    img_lines, txt_lines = lines([(z, lo, img_own, others[3]), (y, hi, txt_own, others[1])])
    got = together([heads, *img_lines, *txt_lines])
    heads, img_lines, txt_lines = got[0], got[1:5], got[5:9]
    heads = exchange(heads.reshape(64, 8, -1), CHIP_GROUPS)
    img_lines[1:] = [send(img_lines[d], img_move(d, 0)) for d in (1, 2, 3)]
    txt_lines[1:] = [send(txt_lines[d], txt_move(d, 0)) for d in (1, 2, 3)]
    image_grad, text_grad = feature_grads([(z, img_lines, image_head), (y, txt_lines, text_head)])
    head_shape = jax.ShapeDtypeStruct((width // 128, width), f32)
    image_head_grad, text_head_grad = call(head_kernel, [head_shape] * 2, [core], [heads])
    return (image_grad, text_grad, image_head_grad, text_head_grad)


def solution(mesh):
    line = jax.sharding.Mesh(mesh.devices.reshape(-1), (DEV,))
    in_specs = (P(DEV, None), P(DEV, None), P(), P(), P(), P(DEV), P(DEV))
    return jax.shard_map(
        shards, mesh=line, in_specs=in_specs, out_specs=(P(DEV, None),) * 4, check_vma=False
    )
```

```python
import jax
import jax.numpy as jnp
from jax import lax
from jax.experimental import pallas as pl
from jax.experimental.pallas import tpu as pltpu
from jax.sharding import PartitionSpec as P

logit_scale = 64.0
epsilon = 1e-06
f32, b16 = jnp.float32, jnp.bfloat16

DEV = "dev"
PLACES = [
    (z, lo, hi, y, c)
    for z in range(4)
    for lo in range(2)
    for hi in range(2)
    for y in range(4)
    for c in range(2)
]


def flat(z, lo, hi, y, c):
    return (z * 2 + lo) * 16 + hi * 8 + y * 2 + c


def img_move(d, e):
    return lambda z, lo, hi, y, c: ((z + d) % 4, lo ^ e, hi, y, c)


def txt_move(d, e):
    return lambda z, lo, hi, y, c: (z, lo ^ e, hi ^ e, (y + d) % 4, c)


def core_move(z, lo, hi, y, c):
    return (z, lo, hi, y, 1 - c)


IMG_GROUPS = [
    [flat((m // 2 - y) % 4, m % 2, hi, y, c) for m in range(8)]
    for hi in range(2)
    for y in range(4)
    for c in range(2)
]
TXT_GROUPS = [
    [flat(z, m % 2, m % 2 ^ b, (m // 2 - z) % 4, c) for m in range(8)]
    for z in range(4)
    for b in range(2)
    for c in range(2)
]
CHIP_GROUPS = [[flat(*p) for p in PLACES if p[4] == c] for c in range(2)]


def send(block, move):
    return lax.ppermute(block, DEV, [(flat(*p), flat(*move(*p))) for p in PLACES])


def exchange(blocks, groups):
    return lax.all_to_all(blocks, DEV, 0, 0, axis_index_groups=groups, tiled=True)


PAD = 16
NN = (((1,), (0,)), ((), ()))
NT = (((1,), (1,)), ((), ()))
TN = (((0,), (0,)), ((), ()))


def dot(a, b, dims):
    return lax.dot_general(a, b, dims, preferred_element_type=f32)


def call(body, out_shape, scalars, arrays, in_specs=None, out_specs=None, grid=(), scratch=(), cost=0, aliases=None):
    whole = pl.BlockSpec(memory_space=pltpu.VMEM)
    many = isinstance(out_shape, (list, tuple))
    if in_specs is None:
        in_specs = [whole] * len(arrays)
    if out_specs is None:
        out_specs = [whole] * len(out_shape) if many else whole
    spec = pltpu.PrefetchScalarGridSpec(
        num_scalar_prefetch=1,
        grid=grid,
        in_specs=in_specs,
        out_specs=out_specs,
        scratch_shapes=list(scratch),
    )
    moved = sum(a.size * a.dtype.itemsize for a in arrays)
    return pl.pallas_call(
        body,
        out_shape=out_shape,
        grid_spec=spec,
        input_output_aliases=aliases or {},
        compiler_params=pltpu.CompilerParams(vmem_limit_bytes=60 * 2**20),
        cost_estimate=pl.CostEstimate(flops=cost, bytes_accessed=moved, transcendentals=0),
    )(jnp.stack(scalars).astype(jnp.int32), *arrays)


def pick_kernel(at_ref, img, txt, other_img, other_txt, out):
    width = img.shape[1]
    slots = out.shape[0]
    own = width // 128
    third = 2 * img.shape[0] // 3
    img = img[...].astype(f32) + other_img[...].astype(f32)
    txt = txt[...].astype(f32) + other_txt[...].astype(f32)
    part = jnp.concatenate([img, txt], axis=0).astype(b16)
    slot = lax.broadcasted_iota(jnp.int32, (slots, 1), 0)
    feature = lax.broadcasted_iota(jnp.int32, (slots, width), 1)
    base = (slot // 8 * 2 + at_ref[0]) * own
    chosen = jnp.where(feature == base + slot % 8, 1.0, 0.0).astype(b16)
    out[:, : 3 * third] = dot(chosen, part, NT).astype(b16)
    chosen = jnp.where(feature == base + 8, 1.0, 0.0).astype(b16)
    ninth = dot(chosen, part, NT)
    pick = slot % 8
    rest = jnp.where(pick == 1, ninth[:, third : 2 * third], ninth[:, :third])
    rest = jnp.where(pick == 2, ninth[:, 2 * third :], rest)
    out[:, 3 * third :] = rest.astype(b16)


def picked(core, parts):
    slab, width = parts[0].shape
    return call(
        pick_kernel,
        jax.ShapeDtypeStruct((64 * 8, slab * 8 // 3), b16),
        [core],
        parts,
        cost=8 * 512 * width * slab,
    )


def head_kernel(at_ref, got, img_out, txt_out):
    slab = img_out.shape[1] // 8
    third = slab * 2 // 3
    half = third // 2
    for p in range(8):
        total = None
        for y in range(4):
            for hi in range(2):
                block = got[(((p // 2 - y) % 4 * 2 + p % 2) * 2 + hi) * 4 + y].astype(f32)
                total = block if total is None else total + block
        img = txt = total
        at = p * slab
        ninth = 2 * slab
        img_out[0:8, at : at + slab] = img[:, :slab]
        img_out[8:9, at : at + third] = img[0:1, ninth : ninth + third]
        img_out[8:9, at + third : at + slab] = img[1:2, ninth : ninth + half]
        txt_out[0:8, at : at + slab] = txt[:, slab : 2 * slab]
        txt_out[8:9, at : at + half] = txt[1:2, ninth + half : ninth + third]
        txt_out[8:9, at + half : at + slab] = txt[2:3, ninth : ninth + third]


def unit_columns(feats, head):
    projected = dot(head, feats, (((0,), (1,)), ((), ())))
    norm = jnp.sqrt(jnp.sum(projected * projected, axis=0, keepdims=True) + epsilon)
    return (projected / norm).astype(b16), norm


def pair_tile(unit_img, unit_txt, image_ids, figures):
    cosines = logit_scale * dot(unit_img, unit_txt, TN)
    positive = (figures[1][None, :] == image_ids[:, None]).astype(f32)
    slopes = (jax.nn.sigmoid(cosines + figures[0][None, :]) - positive).astype(b16)
    weighted = slopes.astype(f32) * cosines
    return slopes, jnp.sum(weighted, axis=1), jnp.sum(weighted, axis=0)


def together(arrays):
    return lax.optimization_barrier(list(arrays))


def shards(image_feat, text_feat, image_head, text_head, group_bias, text_lang, partner):
    rows, width = image_feat.shape
    slab = width // 8
    place = lax.axis_index(DEV)
    z, lo, hi, y, core = place // 32, place // 16 % 2, place // 8 % 2, place // 2 % 4, place % 2

    figures = jnp.stack([text_lang, partner // 128, partner % 128]).astype(b16)
    figures = jnp.pad(figures, ((0, PAD - 3), (0, width - rows)))
    text_rows = jnp.concatenate([text_feat, figures], axis=0)
    moves = (img_move, txt_move)
    count = 8 * rows

    own = (image_feat, text_rows)
    across = [send(own[n], moves[n](0, 1)) for n in range(2)]
    before = [send(own[n], moves[n](1, 0)) for n in range(2)]
    after = [send(own[n], moves[n](3, 0)) for n in range(2)]
    across = together(across)
    across_after = [send(across[n], moves[n](3, 0)) for n in range(2)]
    across_before = [send(across[n], moves[n](1, 0)) for n in range(2)]
    got = together(across_after + before + after + across)
    across_after, before, after, across = [got[2 * n : 2 * n + 2] for n in range(4)]
    far = [send(before[n], moves[n](1, 0)) for n in range(2)]
    across_far = [send(across_after[n], moves[n](3, 0)) for n in range(2)]

    slot = jnp.arange(width, dtype=jnp.int32) // slab
    slot = ((z + y + slot // 2) % 4 * 2 + (lo + slot) % 2) * slab
    slot = slot + jnp.arange(width, dtype=jnp.int32) % slab
    turn = (jnp.arange(width, dtype=jnp.int32)[:, None] == slot[None, :]).astype(b16)
    image_slots = dot(image_head, turn, NN).astype(b16)
    text_slots = dot(text_head, turn, NN).astype(b16)

    def assembled(n):
        blocks = [
            own[n], across[n], after[n], across_after[n],
            far[n], across_far[n], before[n], across_before[n],
        ]
        whole = jnp.zeros((8,) + own[n].shape, b16)
        for k, rows_there in enumerate(blocks):
            at = (z + y + k // 2) % 4 * 2 + (lo + k) % 2
            whole = lax.dynamic_update_slice(whole, rows_there[None], (at, 0, 0))
        return whole

    txt_blocks = assembled(1)
    txt_feats = txt_blocks[:, :rows].reshape(count, width)
    figures = txt_blocks[:, rows : rows + 3, :rows].transpose(1, 0, 2).reshape(3, count)
    figures = figures.astype(f32)
    bias = jnp.where(
        figures[0][:, None] == jnp.arange(group_bias.shape[0]).astype(f32), group_bias, 0.0
    )
    figures = jnp.stack([jnp.sum(bias, axis=1), figures[1] * 128.0 + figures[2]])
    other_figures = send(figures, core_move)
    img_feats = assembled(0).reshape(count, width)

    unit_txt, norm_txt = unit_columns(txt_feats, text_slots)
    other_txt = send(unit_txt, core_move)
    unit_img, norm_img = unit_columns(img_feats, image_slots)

    index = jnp.arange(count, dtype=jnp.int32)
    image_ids = index // rows
    image_ids = ((image_ids // 2 + 4 - y) % 4 * 2 + image_ids % 2) * 16 + place % 16
    image_ids = (image_ids * rows + index % rows).astype(f32)
    slopes, img_sum, txt_sum = pair_tile(unit_img, unit_txt, image_ids, figures)
    other_slopes, other_img_sum, other_txt_sum = pair_tile(
        unit_img, other_txt, image_ids, other_figures
    )
    back = send(dot(unit_img, other_slopes, NN).astype(b16), core_move)
    back_sum = send(other_txt_sum.reshape(8, rows), core_move)

    def group_sum(part, groups):
        parts = jnp.broadcast_to(part.reshape(1, 8, rows), (8, 8, rows))
        return jnp.sum(exchange(parts, groups), axis=0).reshape(1, count)

    def span(d, e):
        return slice((2 * d + e) * slab, (2 * d + e + 1) * slab)

    def img_piece(d, e):
        return dot(unit_txt[span(d, e)], slopes, NT) + dot(other_txt[span(d, e)], other_slopes, NT)

    def txt_piece(d, e):
        return dot(unit_img[span(d, e)], slopes, NN) + back[span(d, e)].astype(f32)

    def start(piece, move):
        far = send(piece(2, 0).astype(b16), move(1, 0))
        across_far = send(piece(2, 1).astype(b16), move(3, 0))
        return far, across_far

    def reduced(piece, move, far, across_far):
        far, across_far, across_after = together([far, across_far, piece(1, 1).astype(b16)])
        across_before = send(across_after, move(1, 0))
        across_after = send((piece(3, 1) + across_far.astype(f32)).astype(b16), move(3, 0))
        before = (piece(1, 0) + far.astype(f32)).astype(b16)
        after = piece(3, 0).astype(b16)
        across_before, across_after, before, after = together(
            [across_before, across_after, before, after]
        )
        across = piece(0, 1) + across_before.astype(f32) + across_after.astype(f32)
        across = send(across.astype(b16), move(0, 1))
        before = send(before, move(1, 0))
        after = send(after, move(3, 0))
        return piece(0, 0) + across.astype(f32) + before.astype(f32) + after.astype(f32)

    img_far = start(img_piece, img_move)
    txt_far = start(txt_piece, txt_move)
    img_sum = group_sum(img_sum + other_img_sum, IMG_GROUPS)
    txt_sum = group_sum(txt_sum.reshape(8, rows) + back_sum, TXT_GROUPS)
    img_up = reduced(img_piece, img_move, *img_far)
    txt_up = reduced(txt_piece, txt_move, *txt_far)

    def back_norm(up, unit, inner, norm):
        return ((logit_scale * up - unit[:slab].astype(f32) * inner) / norm).astype(b16)

    grad_img = back_norm(img_up, unit_img, img_sum, norm_img)
    grad_txt = back_norm(txt_up, unit_txt, txt_sum, norm_txt)
    img_part = dot(grad_img, img_feats, NN).astype(b16)
    txt_part = dot(grad_txt, txt_feats, NN).astype(b16)

    def columns(grad, groups):
        blocks = grad.reshape(slab, 8, rows).transpose(1, 0, 2)
        return exchange(blocks, groups).reshape(width, rows)

    heads = picked(core, [img_part, txt_part, send(img_part, core_move), send(txt_part, core_move)])
    heads = exchange(heads.reshape(64, 8, -1), CHIP_GROUPS)
    head_shape = jax.ShapeDtypeStruct((width // 128, width), f32)
    image_head_grad, text_head_grad = call(head_kernel, [head_shape] * 2, [core], [heads])
    image_grad = dot(columns(grad_img, IMG_GROUPS), image_head, (((0,), (1,)), ((), ())))
    text_grad = dot(columns(grad_txt, TXT_GROUPS), text_head, (((0,), (1,)), ((), ())))
    return (image_grad, text_grad, image_head_grad, text_head_grad)


def solution(mesh):
    line = jax.sharding.Mesh(mesh.devices.reshape(-1), (DEV,))
    in_specs = (P(DEV, None), P(DEV, None), P(), P(), P(), P(DEV), P(DEV))
    return jax.shard_map(
        shards, mesh=line, in_specs=in_specs, out_specs=(P(DEV, None),) * 4, check_vma=False
    )
```

```python
import jax
import jax.numpy as jnp
from jax import lax
from jax.experimental import pallas as pl
from jax.experimental.pallas import tpu as pltpu
from jax.sharding import PartitionSpec as P

logit_scale = 64.0
epsilon = 1e-06
log2e = 1.4426950408889634
f32, b16 = jnp.float32, jnp.bfloat16

DEV = "dev"
PLACES = [
    (z, lo, hi, y, c)
    for z in range(4)
    for lo in range(2)
    for hi in range(2)
    for y in range(4)
    for c in range(2)
]


def flat(z, lo, hi, y, c):
    return (z * 2 + lo) * 16 + hi * 8 + y * 2 + c


def img_move(d, e):
    return lambda z, lo, hi, y, c: ((z + d) % 4, lo ^ e, hi, y, c)


def txt_move(d, e):
    return lambda z, lo, hi, y, c: (z, lo ^ e, hi ^ e, (y + d) % 4, c)


def core_move(z, lo, hi, y, c):
    return (z, lo, hi, y, 1 - c)


IMG_GROUPS = [
    [flat(z, lo, hi, y, c) for z in range(4) for lo in range(2)]
    for hi in range(2)
    for y in range(4)
    for c in range(2)
]
TXT_GROUPS = [
    [flat(z, hi ^ b, hi, y, c) for y in range(4) for hi in range(2)]
    for z in range(4)
    for b in range(2)
    for c in range(2)
]
TXT_CORE_GROUPS = [
    [flat(z, hi ^ b, hi, y, c) for c in range(2) for y in range(4) for hi in range(2)]
    for z in range(4)
    for b in range(2)
]
CHIP_GROUPS = [[flat(*p) for p in PLACES if p[4] == c] for c in range(2)]


def send(block, move):
    return lax.ppermute(block, DEV, [(flat(*p), flat(*move(*p))) for p in PLACES])


def exchange(blocks, groups):
    return lax.all_to_all(blocks, DEV, 0, 0, axis_index_groups=groups, tiled=True)


PAD = 16
NN = (((1,), (0,)), ((), ()))
NT = (((1,), (1,)), ((), ()))
TN = (((0,), (0,)), ((), ()))


def dot(a, b, dims):
    return lax.dot_general(a, b, dims, preferred_element_type=f32)


def call(body, out_shape, scalars, arrays, in_specs=None, out_specs=None, grid=(), scratch=(), cost=0, aliases=None):
    whole = pl.BlockSpec(memory_space=pltpu.VMEM)
    many = isinstance(out_shape, (list, tuple))
    if in_specs is None:
        in_specs = [whole] * len(arrays)
    if out_specs is None:
        out_specs = [whole] * len(out_shape) if many else whole
    spec = pltpu.PrefetchScalarGridSpec(
        num_scalar_prefetch=1,
        grid=grid,
        in_specs=in_specs,
        out_specs=out_specs,
        scratch_shapes=list(scratch),
    )
    moved = sum(a.size * a.dtype.itemsize for a in arrays)
    return pl.pallas_call(
        body,
        out_shape=out_shape,
        grid_spec=spec,
        input_output_aliases=aliases or {},
        compiler_params=pltpu.CompilerParams(vmem_limit_bytes=60 * 2**20),
        cost_estimate=pl.CostEstimate(flops=cost, bytes_accessed=moved, transcendentals=0),
    )(jnp.stack(scalars).astype(jnp.int32), *arrays)


def aligned(index, size):
    return pl.ds(pl.multiple_of(index * size, size), size)


def split_rows(total, lanes):
    high = total.astype(b16).astype(f32)
    row = lax.broadcasted_iota(jnp.int32, (PAD, lanes), 0)
    return jnp.where(row == 0, high, jnp.where(row == 1, total - high, 0.0)).astype(b16)


def joined(rows):
    return rows[0:1].astype(f32) + rows[1:2].astype(f32)


def in_pair(own, across, second, rows):
    own, across = own[:rows], across[:rows]
    first = second == 0
    return jnp.concatenate([jnp.where(first, own, across), jnp.where(first, across, own)], axis=0)


def unit_kernel(rows, extra, pairs, at_ref, *refs):
    blocks, refs = refs[: 2 * pairs], refs[2 * pairs :]
    turned_head, head = refs[0], refs[1]
    (feats, proj), outs = refs[-2:], refs[-5:-2]
    width = turned_head.shape[0]
    quarter = width // 4
    second = at_ref[0]
    step = pl.program_id(0)
    for p in range(pairs):
        own, across = blocks[2 * p], blocks[2 * p + 1]

        @pl.when(step == p)
        def _():
            feats[...] = in_pair(own, across, second, rows)
            if extra:
                first = second == 0
                sides = own[rows:, :rows], across[rows:, :rows]
                outs[2][0, width:, :rows] = jnp.where(first, sides[0], sides[1])
                outs[2][0, width:, rows:] = jnp.where(first, sides[1], sides[0])

    total = jnp.zeros((1, 2 * rows), f32)
    for m in range(4):
        span = slice(m * quarter, (m + 1) * quarter)
        part = dot(turned_head[span], feats[...], NT)
        proj[span] = part
        total = total + jnp.sum(part * part, axis=0, keepdims=True)
    length = jnp.sqrt(total + epsilon)
    outs[1][...] = length
    inverse = 1.0 / length
    for m in range(4):
        span = slice(m * quarter, (m + 1) * quarter)
        unit = (proj[span] * inverse).astype(b16)
        outs[0][span] = unit
        if extra:
            outs[2][0, span] = unit
    if extra:
        outs[0][width:] = outs[2][0, width:]
    else:
        part = dot(feats[...], head[...], NN)
        total = jnp.sum(part * part, axis=1, keepdims=True)
        outs[2][...] = (part * (1.0 / jnp.sqrt(total + epsilon))).astype(b16)


def units(pairs, heads, second, places, rows, extra, carried):
    width = heads[0].shape[0]
    tile = 2 * rows
    whole = lambda a: pl.BlockSpec(a.shape, lambda i, at: (0, 0))
    out = [
        jax.ShapeDtypeStruct((width + extra, 8 * rows), b16),
        jax.ShapeDtypeStruct((1, 8 * rows), f32),
    ]
    steps = [
        pl.BlockSpec((width + extra, tile), lambda i, at: (0, at[1 + i])),
        pl.BlockSpec((1, tile), lambda i, at: (0, at[1 + i])),
    ]
    if extra:
        out.append(jax.ShapeDtypeStruct((len(pairs), width + extra, tile), b16))
        steps.append(pl.BlockSpec((1, width + extra, tile), lambda i, at: (i, 0, 0)))
        heads = [heads[0], heads[0]]
    else:
        out.append(jax.ShapeDtypeStruct((8 * rows, width), b16))
        steps.append(pl.BlockSpec((tile, width), lambda i, at: (at[1 + i], 0)))
    last = pl.BlockSpec(memory_space=pl.ANY) if extra else whole(heads[1])
    blocks = [block for pair in pairs for block in pair]
    return call(
        lambda *refs: unit_kernel(rows, extra, len(pairs), *refs),
        out,
        [second, *places],
        [*blocks, *heads, *carried],
        in_specs=[whole(a) for a in [*blocks, heads[0]]]
        + [last]
        + [pl.BlockSpec(memory_space=pl.ANY)] * len(carried),
        out_specs=steps,
        grid=(len(pairs),),
        scratch=[pltpu.VMEM((tile, width), b16), pltpu.VMEM((width, tile), f32)],
        cost=2 * tile * width * width * len(pairs) * (1 if extra else 2),
        aliases={len(blocks) + 3 + n: n for n in range(len(carried))},
    )


def ring_order(near, far):
    return [near.at[0], near.at[1], far.at[0], near.at[2]]


def tile_slopes(rows, groups, place, bias_ref, img, txt, slopes, by_img):
    width = img.shape[1]
    tile = 2 * rows
    lang = txt[width : width + PAD].astype(f32)
    partner = lang[1:2] * 128.0 + lang[2:3]
    lang = lang[0:1]
    bias = jnp.zeros((1, tile), f32)
    for g in range(groups):
        bias = jnp.where(lang == g, bias_ref[g], bias)
    bias = bias * -log2e
    down = jnp.zeros((1, tile), f32)
    high = 4 * rows
    for m in range(img.shape[0] // high):
        span = slice(m * high, (m + 1) * high)
        index = m * high + lax.broadcasted_iota(jnp.int32, (high, 1), 0)
        ids = ((index // rows * 16 + place) * rows + index % rows).astype(f32)
        cosines = dot(img[span], txt[:width], NN)
        below = 1.0 + jnp.exp2(cosines * (-log2e * logit_scale) + bias)
        gate = pl.reciprocal(below, approx=True)
        gate = gate * (2.0 - below * gate)
        slope = gate - jnp.where(partner == ids, 1.0, 0.0)
        slopes[span, :tile] = slope.astype(b16)
        weighted = slope * cosines
        down = down + jnp.sum(weighted, axis=0, keepdims=True)
        side = by_img[span]
        for k in range(0, tile, by_img.shape[1]):
            side = side + weighted[:, k : k + by_img.shape[1]]
        by_img[span] = side
    return logit_scale * down


def put_text_terms(up, turned, slopes, down):
    slab = turned.shape[0] // 8
    figures = split_rows(down, up.shape[1])
    part = dot(turned[...], slopes, NN)
    for e in range(8):
        at = e * (slab + PAD)
        up[at : at + slab] = part[e * slab : (e + 1) * slab].astype(b16)
        up[at + slab : at + slab + PAD] = figures


def other_kernel(rows, groups, at_ref, bias_ref, img, turned, *refs):
    chunks, (slopes, img_sum, up, by_img, held, txt) = ring_order(*refs[:2]), refs[2:]
    step = pl.program_id(0)

    @pl.when(step == 0)
    def _():
        by_img[...] = jnp.zeros(by_img.shape, f32)

    for d in range(4):

        @pl.when(step == d)
        def _():
            txt[...] = chunks[d][...]

    down = tile_slopes(rows, groups, at_ref[0], bias_ref, img, txt, held, by_img)
    slopes[0] = held[...]
    put_text_terms(up, turned, held[...], down)

    @pl.when(step == 3)
    def _():
        img_sum[...] = logit_scale * jnp.sum(by_img[...].T, axis=0, keepdims=True)


def other_tile(img, turned, chunks, group_bias, place, ring, rows):
    count, width = img.shape
    tile = 2 * rows
    height = width + 8 * PAD
    whole = lambda a: pl.BlockSpec(a.shape, lambda i, at: (0, 0))
    stack = lambda a: pl.BlockSpec(a.shape, lambda i, at: (0, 0, 0))
    return call(
        lambda *refs: other_kernel(rows, group_bias.shape[0], *refs),
        [
            jax.ShapeDtypeStruct((4, count, tile), b16),
            jax.ShapeDtypeStruct((1, count), f32),
            jax.ShapeDtypeStruct((height, count), b16),
        ],
        [place, ring],
        [group_bias, img, turned, *chunks],
        in_specs=[pl.BlockSpec(memory_space=pltpu.SMEM), whole(img), whole(turned)]
        + [stack(chunk) for chunk in chunks],
        out_specs=[
            pl.BlockSpec((1, count, tile), lambda i, at: (i, 0, 0)),
            pl.BlockSpec((1, count), lambda i, at: (0, 0)),
            pl.BlockSpec((height, tile), lambda i, at: (0, (at[1] + i) % 4)),
        ],
        grid=(4,),
        scratch=[
            pltpu.VMEM((count, min(128, tile)), f32),
            pltpu.VMEM((count, tile), b16),
            pltpu.VMEM((width + PAD, tile), b16),
        ],
        cost=4 * width * count * count,
    )


def own_kernel(rows, groups, at_ref, bias_ref, img, turned, txt, *refs):
    chunks = ring_order(*refs[:2])
    other_slopes, other_sum, up = refs[2:5]
    outs, (by_img, held, both, total) = refs[5:13], refs[13:]
    step = pl.program_id(0)
    width = img.shape[1]
    tile = 2 * rows

    @pl.when(step == 0)
    def _():
        by_img[...] = jnp.zeros(by_img.shape, f32)
        total[...] = jnp.zeros(total.shape, f32)

    for d in range(4):

        @pl.when(step == d)
        def _():
            both[:, tile:] = chunks[d][:width]

    held[:, tile:] = other_slopes[0]
    both[:, :tile] = txt[:width]
    down = tile_slopes(rows, groups, at_ref[0], bias_ref, img, txt, held, by_img)
    put_text_terms(up, turned, held[:, :tile], down)
    total[...] += dot(both[...], held[...], NT)

    @pl.when(step == 3)
    def _():
        slab = width // 8
        sums = logit_scale * jnp.sum(by_img[...].T, axis=0, keepdims=True) + other_sum[...]
        figures = split_rows(sums, sums.shape[1])
        own = at_ref[2] == 0
        for d in range(4):
            at = pl.multiple_of((at_ref[1] + d) % 4 * (2 * slab), 2 * slab)
            low, high = total[pl.ds(at, slab)], total[pl.ds(at + slab, slab)]
            outs[2 * d][:slab] = jnp.where(own, low, high).astype(b16)
            outs[2 * d][slab:] = figures
            outs[2 * d + 1][:slab] = jnp.where(own, high, low).astype(b16)
            outs[2 * d + 1][slab:] = figures


def own_tile(
    img, turned, txt, chunks, other_slopes, other_sum, group_bias, place, ring, second, rows
):
    count, width = img.shape
    tile = 2 * rows
    height = width + 8 * PAD
    slab = width // 8
    whole = lambda a: pl.BlockSpec(a.shape, lambda i, at: (0, 0))
    stack = lambda a: pl.BlockSpec(a.shape, lambda i, at: (0, 0, 0))
    piece = jax.ShapeDtypeStruct((slab + PAD, count), b16)
    out = call(
        lambda *refs: own_kernel(rows, group_bias.shape[0], *refs),
        [jax.ShapeDtypeStruct((height, count), b16)] + [piece] * 8,
        [place, ring, second],
        [group_bias, img, turned, txt, *chunks, other_slopes, other_sum],
        in_specs=[
            pl.BlockSpec(memory_space=pltpu.SMEM),
            whole(img),
            whole(turned),
            pl.BlockSpec((width + PAD, tile), lambda i, at: (0, i)),
        ]
        + [stack(chunk) for chunk in chunks]
        + [pl.BlockSpec((1, count, tile), lambda i, at: (i, 0, 0)), whole(other_sum)],
        out_specs=[pl.BlockSpec((height, tile), lambda i, at: (0, i))] + [whole(piece)] * 8,
        grid=(4,),
        scratch=[
            pltpu.VMEM((count, min(128, tile)), f32),
            pltpu.VMEM((count, 2 * tile), b16),
            pltpu.VMEM((width, 2 * tile), b16),
            pltpu.VMEM((width, count), f32),
        ],
        cost=8 * width * count * count,
    )
    return out[0], out[1:]


def sum_into(out, terms):
    slab = out.shape[0] - PAD
    block, total = terms[0][:slab].astype(f32), joined(terms[0][slab:])
    for term in terms[1:]:
        block, total = block + term[:slab].astype(f32), total + joined(term[slab:])
    out[:slab] = block.astype(b16)
    out[slab:] = split_rows(total, out.shape[1])


def sum_kernel(sizes, at_ref, *refs):
    start = 0
    for size, out in zip(sizes, refs[sum(sizes) :]):
        sum_into(out, refs[start : start + size])
        start += size


def sums(groups, rows):
    flat_terms = [term for group in groups for term in group]
    arrays, specs, places = [], [], [jnp.int32(0)]
    height = None
    for term in flat_terms:
        if isinstance(term, tuple):
            arrays.append(term[0])
            height = term[0].shape[0] // 8
            specs.append(
                pl.BlockSpec((height, 4 * rows), lambda i, at, n=len(places): (at[n], i))
            )
            places.append(term[1])
        else:
            arrays.append(term)
            height = term.shape[0]
            specs.append(pl.BlockSpec((height, 4 * rows), lambda i, at: (0, i)))
    count = arrays[0].shape[1]
    spec = pl.BlockSpec((height, 4 * rows), lambda i, at: (0, i))
    return call(
        lambda *refs: sum_kernel([len(group) for group in groups], *refs),
        [jax.ShapeDtypeStruct((height, count), b16)] * len(groups),
        places,
        arrays,
        in_specs=specs,
        out_specs=[spec] * len(groups),
        grid=(count // (4 * rows),),
    )


def grad_kernel(rows, sizes, at_ref, *refs):
    part, grad = refs[-2:]
    outs = refs[-6:-2]
    start = 0
    for n in range(2):
        mine = refs[start : start + sizes[n] + 10]
        start += sizes[n] + 10
        terms, mine = mine[: sizes[n]], mine[sizes[n] :]
        unit, norm, blocks = mine[0], mine[1], mine[2:]
        ring_at, second = at_ref[4 * n], at_ref[4 * n + 1]
        slab = unit.shape[0]
        up, inner = terms[0][:slab].astype(f32), joined(terms[0][slab:])
        for term in terms[1:]:
            up, inner = up + term[:slab].astype(f32), inner + joined(term[slab:])
        up = logit_scale * up - unit[...].astype(f32) * inner
        grad[n] = (up * (1.0 / norm[...])).astype(b16)
        own, give = outs[2 * n : 2 * n + 2]
        for ring in range(4):
            low = grad[n, :, (2 * ring) * rows : (2 * ring + 1) * rows]
            high = grad[n, :, (2 * ring + 1) * rows : (2 * ring + 2) * rows]
            own[ring] = jnp.where(second == 0, low, high)
            give[ring] = jnp.where(second == 0, high, low)
        total = None
        for d in range(4):
            cols = grad[n, :, aligned((ring_at + d) % 4, 2 * rows)]
            term = dot(cols, in_pair(blocks[2 * d], blocks[2 * d + 1], second, rows), NN)
            total = term if total is None else total + term
        part[n * slab : (n + 1) * slab] = total.astype(b16)


def gradients(towers, rows):
    arrays, specs, scalars = [], [], []
    whole = lambda a: pl.BlockSpec(a.shape, lambda i, at: (0,) * len(a.shape))
    for n, (ring, second, place, terms, unit, norm, blocks) in enumerate(towers):
        width = blocks[0].shape[1]
        slab, count = width // 8, 8 * rows
        mine = lambda height, n=n: pl.BlockSpec((height, count), lambda i, at: (at[4 * n + 2], 0))
        for term in terms:
            arrays.append(term[0] if isinstance(term, tuple) else term)
            specs.append(mine(slab + PAD) if isinstance(term, tuple) else whole(term))
        arrays += [unit, norm, *blocks]
        specs += [mine(slab), whole(norm)] + [whole(a) for a in blocks]
        scalars += [ring, second, place, place]
    block = jax.ShapeDtypeStruct((4, slab, rows), b16)
    term = jax.ShapeDtypeStruct((2 * slab, width), b16)
    return call(
        lambda *refs: grad_kernel(rows, [len(tower[3]) for tower in towers], *refs),
        [block] * 4 + [term],
        scalars,
        arrays,
        in_specs=specs,
        out_specs=[whole(block)] * 4 + [whole(term)],
        grid=(1,),
        scratch=[pltpu.VMEM((2, slab, count), b16)],
        cost=4 * slab * count * width,
    )


def pick_kernel(at_ref, mine, theirs, out):
    width = mine.shape[1]
    slots = out.shape[0]
    own = width // 128
    third = mine.shape[0] // 3
    part = (mine[...].astype(f32) + theirs[...].astype(f32)).astype(b16)
    slot = lax.broadcasted_iota(jnp.int32, (slots, 1), 0)
    feature = lax.broadcasted_iota(jnp.int32, (slots, width), 1)
    base = (slot // 8 * 2 + at_ref[0]) * own
    chosen = jnp.where(feature == base + slot % 8, 1.0, 0.0).astype(b16)
    out[:, : 3 * third] = dot(chosen, part, NT).astype(b16)
    chosen = jnp.where(feature == base + 8, 1.0, 0.0).astype(b16)
    ninth = dot(chosen, part, NT)
    pick = slot % 8
    rest = jnp.where(pick == 1, ninth[:, third : 2 * third], ninth[:, :third])
    rest = jnp.where(pick == 2, ninth[:, 2 * third :], rest)
    out[:, 3 * third :] = rest.astype(b16)


def picked(core, mine, theirs):
    both, width = mine.shape
    return call(
        pick_kernel,
        jax.ShapeDtypeStruct((64 * 8, both * 4 // 3), b16),
        [core],
        [mine, theirs],
        cost=4 * 512 * width * both,
    )


def head_kernel(at_ref, got, img_out, txt_out):
    slab = img_out.shape[1] // 8
    third = slab * 2 // 3
    half = third // 2
    for p in range(8):
        img = txt = None
        for other in range(8):
            z, lo, hi, y = p // 2, p % 2, other // 4, other % 4
            block = got[(z * 2 + lo) * 8 + hi * 4 + y].astype(f32)
            img = block if img is None else img + block
            z, lo, hi, y = other // 2, other % 2, p % 2, p // 2
            block = got[(z * 2 + lo) * 8 + hi * 4 + y].astype(f32)
            txt = block if txt is None else txt + block
        at = p * slab
        ninth = 2 * slab
        img_out[0:8, at : at + slab] = img[:, :slab]
        img_out[8:9, at : at + third] = img[0:1, ninth : ninth + third]
        img_out[8:9, at + third : at + slab] = img[1:2, ninth : ninth + half]
        txt_out[0:8, at : at + slab] = txt[:, slab : 2 * slab]
        txt_out[8:9, at : at + half] = txt[1:2, ninth + half : ninth + third]
        txt_out[8:9, at + half : at + slab] = txt[2:3, ninth : ninth + third]


def together(arrays):
    return lax.optimization_barrier(list(arrays))


def pair_lines(own, got, second):
    return jnp.concatenate([jnp.where(second, got, own), jnp.where(second, own, got)], axis=1)


def whole_columns(lines, move, ring):
    got = []
    for d in range(4):
        block = lax.dynamic_index_in_dim(lines, (ring + d) % 4, 0, keepdims=False)
        got.append(send(block, move(d, 0)) if d else block)
    return jnp.concatenate([got[-d % 4] for d in range(4)], axis=0)


def from_ring(turned_head, ring):
    start = ring * (turned_head.shape[0] // 4)
    return lax.dynamic_slice_in_dim(
        jnp.concatenate([turned_head, turned_head]), start, turned_head.shape[0], axis=0
    )


def shards(image_feat, text_feat, image_head, text_head, group_bias, text_lang, partner):
    rows, width = image_feat.shape
    slab = width // 8
    place = lax.axis_index(DEV)
    z, lo, hi, y, core = place // 32, place // 16 % 2, place // 8 % 2, place // 2 % 4, place % 2

    figures = jnp.stack([text_lang, partner // 128, partner % 128]).astype(b16)
    figures = jnp.pad(figures, ((0, PAD - 3), (0, width - rows)))
    text_rows = jnp.concatenate([text_feat, figures], axis=0)
    moves = (img_move, txt_move)
    own = (image_feat, text_rows)
    across = [send(own[n], moves[n](0, 1)) for n in range(2)]
    before = [send(own[n], moves[n](1, 0)) for n in range(2)]
    after = [send(own[n], moves[n](3, 0)) for n in range(2)]
    *across, turned_txt = together(across + [text_head.T])
    across_after = [send(across[n], moves[n](3, 0)) for n in range(2)]
    across_before = [send(across[n], moves[n](1, 0)) for n in range(2)]
    *got, turned_img = together(across_after + before + after + across + [image_head.T])
    across_after, before, after, across = [got[2 * n : 2 * n + 2] for n in range(4)]
    far = [send(before[n], moves[n](1, 0)) for n in range(2)]
    across_far = [send(across_after[n], moves[n](3, 0)) for n in range(2)]
    pairs = [
        [(own[n], across[n]), (after[n], across_after[n]), (before[n], across_before[n])]
        for n in range(2)
    ]
    near_y, near_z = ([(ring + d) % 4 for d in (0, 1, 3)] for ring in (y, z))
    far_y, far_z = [(y + 2) % 4], [(z + 2) % 4]
    img_heads = [turned_img, image_head]
    *txt_made, chunks = units(pairs[1], [turned_txt], hi, near_y, rows, PAD, ())
    others = [send(chunks, core_move)]
    img_made = units(pairs[0], img_heads, lo, near_z, rows, 0, ())
    got = together(far + across_far + list(img_made))
    far, across_far, img_made = got[0:2], got[2:4], got[4:]
    unit_txt, norm_txt, chunks = units(
        [(far[1], across_far[1])], [turned_txt], hi, far_y, rows, PAD, txt_made
    )
    others.append(send(chunks, core_move))
    turned_units, norm_img, unit_img = units(
        [(far[0], across_far[0])], img_heads, lo, far_z, rows, 0, img_made
    )
    blocks = [
        [
            own[n], across[n], after[n], across_after[n],
            far[n], across_far[n], before[n], across_before[n],
        ]
        for n in range(2)
    ]

    other_slopes, other_sum, other_up = other_tile(
        unit_img, turned_units, others, group_bias, place % 16, y, rows
    )
    back = send(other_up, core_move)
    text_up, img_terms = own_tile(
        unit_img, turned_units, unit_txt, others, other_slopes, other_sum, group_bias,
        place % 16, z, lo, rows,
    )

    def txt_slab(d, e):
        at = (y + d) % 4 * 2 + (hi + e) % 2
        return [(text_up, at), (back, at)]

    def img_slab(d, e):
        return [img_terms[2 * d + e]]

    slabs = (img_slab, txt_slab)
    txt_far, txt_across_far, txt_across_after = sums(
        [txt_slab(2, 0), txt_slab(2, 1), txt_slab(1, 1)], rows
    )
    far = [send(img_terms[4], img_move(1, 0)), send(txt_far, txt_move(1, 0))]
    across_far = [send(img_terms[5], img_move(3, 0)), send(txt_across_far, txt_move(3, 0))]
    got = together(far + across_far + [img_terms[3], txt_across_after])
    far, across_far = got[0:2], got[2:4]
    across_before = [send(got[4 + n], moves[n](1, 0)) for n in range(2)]
    joint = sums(
        [slabs[n](3, 1) + [across_far[n]] for n in range(2)]
        + [slabs[n](1, 0) + [far[n]] for n in range(2)]
        + [txt_slab(3, 0)],
        rows,
    )
    across_after = [send(joint[n], moves[n](3, 0)) for n in range(2)]
    got = together(across_before + across_after + [*joint[2:], img_terms[6]])
    across_before, across_after = got[0:2], got[2:4]
    before = [send(got[4 + n], moves[n](1, 0)) for n in range(2)]
    after = [send(got[7], img_move(3, 0)), send(got[6], txt_move(3, 0))]
    joint = sums([slabs[n](0, 1) + [across_before[n], across_after[n]] for n in range(2)], rows)
    across = [send(joint[n], moves[n](0, 1)) for n in range(2)]
    final = [slabs[n](0, 0) + [before[n], after[n], across[n]] for n in range(2)]

    img_own, img_give, txt_own, txt_give, part = gradients(
        [
            (z, lo, z * 2 + lo, final[0], turned_units, norm_img, blocks[0]),
            (y, hi, y * 2 + hi, final[1], unit_txt, norm_txt, blocks[1]),
        ],
        rows,
    )
    img_got = send(img_give, img_move(0, 1))
    txt_got = send(txt_give, txt_move(0, 1))
    heads, img_got, txt_got = together([picked(core, part, send(part, core_move)), img_got, txt_got])
    heads = exchange(heads.reshape(64, 8, -1), CHIP_GROUPS)
    head_shape = jax.ShapeDtypeStruct((width // 128, width), f32)
    image_head_grad, text_head_grad = call(head_kernel, [head_shape] * 2, [core], [heads])

    grad_img = whole_columns(pair_lines(img_own, img_got, lo), img_move, z)
    image_grad = dot(grad_img, from_ring(turned_img, z), TN)
    grad_txt = whole_columns(pair_lines(txt_own, txt_got, hi), txt_move, y)
    text_grad = dot(grad_txt, from_ring(turned_txt, y), TN)
    return (image_grad, text_grad, image_head_grad, text_head_grad)


def solution(mesh):
    line = jax.sharding.Mesh(mesh.devices.reshape(-1), (DEV,))
    in_specs = (P(DEV, None), P(DEV, None), P(), P(), P(), P(DEV), P(DEV))
    return jax.shard_map(
        shards, mesh=line, in_specs=in_specs, out_specs=(P(DEV, None),) * 4, check_vma=False
    )
```

```python
import jax
import jax.numpy as jnp
from jax import lax
from jax.experimental import pallas as pl
from jax.experimental.pallas import tpu as pltpu
from jax.sharding import PartitionSpec as P

logit_scale = 64.0
epsilon = 1e-06
log2e = 1.4426950408889634
f32, b16 = jnp.float32, jnp.bfloat16

DEV = "dev"
PLACES = [
    (z, lo, hi, y, c)
    for z in range(4)
    for lo in range(2)
    for hi in range(2)
    for y in range(4)
    for c in range(2)
]


def flat(z, lo, hi, y, c):
    return (z * 2 + lo) * 16 + hi * 8 + y * 2 + c


def img_move(d, e):
    return lambda z, lo, hi, y, c: ((z + d) % 4, lo ^ e, hi, y, c)


def txt_move(d, e):
    return lambda z, lo, hi, y, c: (z, lo ^ e, hi ^ e, (y + d) % 4, c)


def core_move(z, lo, hi, y, c):
    return (z, lo, hi, y, 1 - c)


IMG_GROUPS = [
    [flat(z, lo, hi, y, c) for z in range(4) for lo in range(2)]
    for hi in range(2)
    for y in range(4)
    for c in range(2)
]
TXT_GROUPS = [
    [flat(z, hi ^ b, hi, y, c) for y in range(4) for hi in range(2)]
    for z in range(4)
    for b in range(2)
    for c in range(2)
]
TXT_CORE_GROUPS = [
    [flat(z, hi ^ b, hi, y, c) for c in range(2) for y in range(4) for hi in range(2)]
    for z in range(4)
    for b in range(2)
]
CHIP_GROUPS = [[flat(*p) for p in PLACES if p[4] == c] for c in range(2)]


def send(block, move):
    return lax.ppermute(block, DEV, [(flat(*p), flat(*move(*p))) for p in PLACES])


def exchange(blocks, groups):
    return lax.all_to_all(blocks, DEV, 0, 0, axis_index_groups=groups, tiled=True)


PAD = 16
NN = (((1,), (0,)), ((), ()))
NT = (((1,), (1,)), ((), ()))
TN = (((0,), (0,)), ((), ()))


def dot(a, b, dims):
    return lax.dot_general(a, b, dims, preferred_element_type=f32)


def call(body, out_shape, scalars, arrays, in_specs=None, out_specs=None, grid=(), scratch=(), cost=0, aliases=None, limit=60):
    whole = pl.BlockSpec(memory_space=pltpu.VMEM)
    many = isinstance(out_shape, (list, tuple))
    if in_specs is None:
        in_specs = [whole] * len(arrays)
    if out_specs is None:
        out_specs = [whole] * len(out_shape) if many else whole
    spec = pltpu.PrefetchScalarGridSpec(
        num_scalar_prefetch=1,
        grid=grid,
        in_specs=in_specs,
        out_specs=out_specs,
        scratch_shapes=list(scratch),
    )
    moved = sum(a.size * a.dtype.itemsize for a in arrays)
    return pl.pallas_call(
        body,
        out_shape=out_shape,
        grid_spec=spec,
        input_output_aliases=aliases or {},
        compiler_params=pltpu.CompilerParams(vmem_limit_bytes=limit * 2**20),
        cost_estimate=pl.CostEstimate(flops=cost, bytes_accessed=moved, transcendentals=0),
    )(jnp.stack(scalars).astype(jnp.int32), *arrays)


def aligned(index, size):
    return pl.ds(pl.multiple_of(index * size, size), size)


def split_rows(total, lanes):
    high = total.astype(b16).astype(f32)
    row = lax.broadcasted_iota(jnp.int32, (PAD, lanes), 0)
    return jnp.where(row == 0, high, jnp.where(row == 1, total - high, 0.0)).astype(b16)


def joined(rows):
    return rows[0:1].astype(f32) + rows[1:2].astype(f32)


def in_pair(own, across, second, rows):
    own, across = own[:rows], across[:rows]
    first = second == 0
    return jnp.concatenate([jnp.where(first, own, across), jnp.where(first, across, own)], axis=0)


def put_units(feats, turned_head, proj, turned, norm):
    width = turned_head.shape[0]
    quarter = width // 4
    total = jnp.zeros((1, feats.shape[0]), f32)
    for m in range(4):
        span = slice(m * quarter, (m + 1) * quarter)
        part = dot(turned_head[span], feats[...], NT)
        proj[span] = part
        total = total + jnp.sum(part * part, axis=0, keepdims=True)
    length = jnp.sqrt(total + epsilon)
    norm[...] = length
    inverse = 1.0 / length
    for m in range(4):
        span = slice(m * quarter, (m + 1) * quarter)
        turned[span] = (proj[span] * inverse).astype(b16)


def img_unit_kernel(at_ref, feats, turned_head, head, turned, norm, unit, proj):
    put_units(feats, turned_head, proj, turned, norm)
    part = dot(feats[...], head[...], NN)
    total = jnp.sum(part * part, axis=1, keepdims=True)
    unit[...] = (part * (1.0 / jnp.sqrt(total + epsilon))).astype(b16)


def img_units(feats, turned_head, head, rows):
    count, width = feats.shape
    tile = 2 * rows
    whole = pl.BlockSpec(head.shape, lambda i, at: (0, 0))
    return call(
        img_unit_kernel,
        [
            jax.ShapeDtypeStruct((width, count), b16),
            jax.ShapeDtypeStruct((1, count), f32),
            jax.ShapeDtypeStruct((count, width), b16),
        ],
        [jnp.int32(0)],
        [feats, turned_head, head],
        in_specs=[pl.BlockSpec((tile, width), lambda i, at: (i, 0)), whole, whole],
        out_specs=[
            pl.BlockSpec((width, tile), lambda i, at: (0, i)),
            pl.BlockSpec((1, tile), lambda i, at: (0, i)),
            pl.BlockSpec((tile, width), lambda i, at: (i, 0)),
        ],
        grid=(4,),
        scratch=[pltpu.VMEM((width, tile), f32)],
        cost=4 * count * width * width,
        limit=24,
    )


def unit_kernel(rows, pairs, at_ref, *refs):
    blocks, turned_head = refs[: 2 * pairs], refs[2 * pairs]
    turned, norm, alone, feats, proj = refs[-5:]
    width = turned_head.shape[0]
    second = at_ref[0]
    step = pl.program_id(0)
    for p in range(pairs):
        own, across = blocks[2 * p], blocks[2 * p + 1]

        @pl.when(step == p)
        def _():
            feats[...] = in_pair(own, across, second, rows)
            first = second == 0
            sides = own[rows:, :rows], across[rows:, :rows]
            alone[0, width:, :rows] = jnp.where(first, sides[0], sides[1])
            alone[0, width:, rows:] = jnp.where(first, sides[1], sides[0])

    put_units(feats, turned_head, proj, turned, norm)
    turned[width:] = alone[0, width:]
    alone[0, :width] = turned[:width]


def units(pairs, turned_head, second, places, rows, carried):
    width = turned_head.shape[0]
    tile = 2 * rows
    whole = lambda a: pl.BlockSpec(a.shape, lambda i, at: (0, 0))
    blocks = [block for pair in pairs for block in pair]
    return call(
        lambda *refs: unit_kernel(rows, len(pairs), *refs),
        [
            jax.ShapeDtypeStruct((width + PAD, 8 * rows), b16),
            jax.ShapeDtypeStruct((1, 8 * rows), f32),
            jax.ShapeDtypeStruct((len(pairs), width + PAD, tile), b16),
        ],
        [second, *places],
        [*blocks, turned_head, *carried],
        in_specs=[whole(a) for a in [*blocks, turned_head]]
        + [pl.BlockSpec(memory_space=pl.ANY)] * len(carried),
        out_specs=[
            pl.BlockSpec((width + PAD, tile), lambda i, at: (0, at[1 + i])),
            pl.BlockSpec((1, tile), lambda i, at: (0, at[1 + i])),
            pl.BlockSpec((1, width + PAD, tile), lambda i, at: (i, 0, 0)),
        ],
        grid=(len(pairs),),
        scratch=[pltpu.VMEM((tile, width), b16), pltpu.VMEM((width, tile), f32)],
        cost=2 * tile * width * width * len(pairs),
        aliases={len(blocks) + 2 + n: n for n in range(len(carried))},
        limit=24,
    )


def ring_order(near, far):
    return [near.at[0], near.at[1], far.at[0], near.at[2]]


def tile_slopes(rows, groups, place, bias_ref, img, txt, slopes, by_img):
    width = img.shape[1]
    tile = 2 * rows
    lang = txt[width : width + PAD].astype(f32)
    partner = lang[1:2] * 128.0 + lang[2:3]
    lang = lang[0:1]
    bias = jnp.zeros((1, tile), f32)
    for g in range(groups):
        bias = jnp.where(lang == g, bias_ref[g], bias)
    bias = bias * -log2e
    down = jnp.zeros((1, tile), f32)
    high = 4 * rows
    for m in range(img.shape[0] // high):
        span = slice(m * high, (m + 1) * high)
        index = m * high + lax.broadcasted_iota(jnp.int32, (high, 1), 0)
        ids = ((index // rows * 16 + place) * rows + index % rows).astype(f32)
        cosines = dot(img[span], txt[:width], NN)
        below = 1.0 + jnp.exp2(cosines * (-log2e * logit_scale) + bias)
        gate = pl.reciprocal(below, approx=True)
        gate = gate * (2.0 - below * gate)
        slope = gate - jnp.where(partner == ids, 1.0, 0.0)
        slopes[span, :tile] = slope.astype(b16)
        weighted = slope * cosines
        down = down + jnp.sum(weighted, axis=0, keepdims=True)
        side = by_img[span]
        for k in range(0, tile, by_img.shape[1]):
            side = side + weighted[:, k : k + by_img.shape[1]]
        by_img[span] = side
    return logit_scale * down


def put_text_terms(up, turned, slopes, down):
    slab = turned.shape[0] // 8
    figures = split_rows(down, up.shape[1])
    part = dot(turned[...], slopes, NN)
    for e in range(8):
        at = e * (slab + PAD)
        up[at : at + slab] = part[e * slab : (e + 1) * slab].astype(b16)
        up[at + slab : at + slab + PAD] = figures


def other_kernel(rows, groups, at_ref, bias_ref, img, turned, *refs):
    chunks, (slopes, img_sum, up, by_img, held, txt) = ring_order(*refs[:2]), refs[2:]
    step = pl.program_id(0)

    @pl.when(step == 0)
    def _():
        by_img[...] = jnp.zeros(by_img.shape, f32)

    for d in range(4):

        @pl.when(step == d)
        def _():
            txt[...] = chunks[d][...]

    down = tile_slopes(rows, groups, at_ref[0], bias_ref, img, txt, held, by_img)
    slopes[0] = held[...]
    put_text_terms(up, turned, held[...], down)

    @pl.when(step == 3)
    def _():
        img_sum[...] = logit_scale * jnp.sum(by_img[...].T, axis=0, keepdims=True)


def other_tile(img, turned, chunks, group_bias, place, ring, rows):
    count, width = img.shape
    tile = 2 * rows
    height = width + 8 * PAD
    whole = lambda a: pl.BlockSpec(a.shape, lambda i, at: (0, 0))
    stack = lambda a: pl.BlockSpec(a.shape, lambda i, at: (0, 0, 0))
    return call(
        lambda *refs: other_kernel(rows, group_bias.shape[0], *refs),
        [
            jax.ShapeDtypeStruct((4, count, tile), b16),
            jax.ShapeDtypeStruct((1, count), f32),
            jax.ShapeDtypeStruct((height, count), b16),
        ],
        [place, ring],
        [group_bias, img, turned, *chunks],
        in_specs=[pl.BlockSpec(memory_space=pltpu.SMEM), whole(img), whole(turned)]
        + [stack(chunk) for chunk in chunks],
        out_specs=[
            pl.BlockSpec((1, count, tile), lambda i, at: (i, 0, 0)),
            pl.BlockSpec((1, count), lambda i, at: (0, 0)),
            pl.BlockSpec((height, tile), lambda i, at: (0, (at[1] + i) % 4)),
        ],
        grid=(4,),
        scratch=[
            pltpu.VMEM((count, min(128, tile)), f32),
            pltpu.VMEM((count, tile), b16),
            pltpu.VMEM((width + PAD, tile), b16),
        ],
        cost=4 * width * count * count,
    )


def own_kernel(rows, groups, at_ref, bias_ref, img, turned, txt, *refs):
    chunks = ring_order(*refs[:2])
    other_slopes, other_sum, up = refs[2:5]
    out, by_img, held, both, total = refs[5:]
    step = pl.program_id(0)
    width = img.shape[1]
    tile = 2 * rows

    @pl.when(step == 0)
    def _():
        by_img[...] = jnp.zeros(by_img.shape, f32)
        total[...] = jnp.zeros(total.shape, f32)

    for d in range(4):

        @pl.when(step == d)
        def _():
            both[:, tile:] = chunks[d][:width]

    held[:, tile:] = other_slopes[0]
    both[:, :tile] = txt[:width]
    down = tile_slopes(rows, groups, at_ref[0], bias_ref, img, txt, held, by_img)
    put_text_terms(up, turned, held[:, :tile], down)
    total[...] += dot(both[...], held[...], NT)

    @pl.when(step == 3)
    def _():
        slab = width // 8
        sums = logit_scale * jnp.sum(by_img[...].T, axis=0, keepdims=True) + other_sum[...]
        figures = split_rows(sums, sums.shape[1])
        for e in range(8):
            out[e, :slab] = total[e * slab : (e + 1) * slab].astype(b16)
            out[e, slab:] = figures


def own_tile(
    img, turned, txt, chunks, other_slopes, other_sum, group_bias, place, rows
):
    count, width = img.shape
    tile = 2 * rows
    height = width + 8 * PAD
    slab = width // 8
    whole = lambda a: pl.BlockSpec(a.shape, lambda i, at: (0, 0))
    stack = lambda a: pl.BlockSpec(a.shape, lambda i, at: (0, 0, 0))
    pieces = jax.ShapeDtypeStruct((8, slab + PAD, count), b16)
    return call(
        lambda *refs: own_kernel(rows, group_bias.shape[0], *refs),
        [jax.ShapeDtypeStruct((height, count), b16), pieces],
        [place],
        [group_bias, img, turned, txt, *chunks, other_slopes, other_sum],
        in_specs=[
            pl.BlockSpec(memory_space=pltpu.SMEM),
            whole(img),
            whole(turned),
            pl.BlockSpec((width + PAD, tile), lambda i, at: (0, i)),
        ]
        + [stack(chunk) for chunk in chunks]
        + [pl.BlockSpec((1, count, tile), lambda i, at: (i, 0, 0)), whole(other_sum)],
        out_specs=[pl.BlockSpec((height, tile), lambda i, at: (0, i)), stack(pieces)],
        grid=(4,),
        scratch=[
            pltpu.VMEM((count, min(128, tile)), f32),
            pltpu.VMEM((count, 2 * tile), b16),
            pltpu.VMEM((width, 2 * tile), b16),
            pltpu.VMEM((width, count), f32),
        ],
        cost=8 * width * count * count,
    )


def sum_into(out, terms):
    slab = out.shape[0] - PAD
    block, total = terms[0][:slab].astype(f32), joined(terms[0][slab:])
    for term in terms[1:]:
        block, total = block + term[:slab].astype(f32), total + joined(term[slab:])
    out[:slab] = block.astype(b16)
    out[slab:] = split_rows(total, out.shape[1])


def sum_kernel(sizes, at_ref, *refs):
    start = 0
    for size, out in zip(sizes, refs[sum(sizes) :]):
        sum_into(out, refs[start : start + size])
        start += size


def sums(groups, rows):
    flat_terms = [term for group in groups for term in group]
    arrays, specs, places = [], [], [jnp.int32(0)]
    height = None
    for term in flat_terms:
        if isinstance(term, tuple):
            arrays.append(term[0])
            height = term[0].shape[0] // 8
            specs.append(
                pl.BlockSpec((height, 4 * rows), lambda i, at, n=len(places): (at[n], i))
            )
            places.append(term[1])
        else:
            arrays.append(term)
            height = term.shape[0]
            specs.append(pl.BlockSpec((height, 4 * rows), lambda i, at: (0, i)))
    count = arrays[0].shape[1]
    spec = pl.BlockSpec((height, 4 * rows), lambda i, at: (0, i))
    return call(
        lambda *refs: sum_kernel([len(group) for group in groups], *refs),
        [jax.ShapeDtypeStruct((height, count), b16)] * len(groups),
        places,
        arrays,
        in_specs=specs,
        out_specs=[spec] * len(groups),
        grid=(count // (4 * rows),),
    )


def put_gradient(up, inner, unit, norm, second, grad, own, give, rows):
    up = logit_scale * up - unit[...].astype(f32) * inner
    grad[...] = (up * (1.0 / norm[...])).astype(b16)
    for ring in range(4):
        low = grad[:, (2 * ring) * rows : (2 * ring + 1) * rows]
        high = grad[:, (2 * ring + 1) * rows : (2 * ring + 2) * rows]
        own[ring] = jnp.where(second == 0, low, high)
        give[ring] = jnp.where(second == 0, high, low)


def img_grad_kernel(rows, at_ref, got, unit, norm, feats, own, give, part, grad):
    slab = unit.shape[0]
    up, inner = got[0, :slab].astype(f32), joined(got[0, slab:])
    for n in range(1, 8):
        up, inner = up + got[n, :slab].astype(f32), inner + joined(got[n, slab:])
    put_gradient(up, inner, unit, norm, at_ref[1], grad, own, give, rows)
    part[...] = dot(grad[...], feats[...], NN).astype(b16)


def txt_grad_kernel(rows, at_ref, *refs):
    terms, unit, norm, blocks, (own, give, part, grad) = (
        refs[:5], refs[5], refs[6], refs[7:15], refs[15:]
    )
    slab = unit.shape[0]
    up, inner = terms[0][:slab].astype(f32), joined(terms[0][slab:])
    for term in terms[1:]:
        up, inner = up + term[:slab].astype(f32), inner + joined(term[slab:])
    put_gradient(up, inner, unit, norm, at_ref[1], grad, own, give, rows)
    total = None
    for d in range(4):
        cols = grad[:, aligned((at_ref[2] + d) % 4, 2 * rows)]
        term = dot(cols, in_pair(blocks[2 * d], blocks[2 * d + 1], at_ref[1], rows), NN)
        total = term if total is None else total + term
    part[...] = total.astype(b16)


def gradient(kernel, place, second, ring, terms, unit, norm, feats, rows):
    width = feats[0].shape[1]
    slab, count = width // 8, 8 * rows
    whole = lambda a: pl.BlockSpec(a.shape, lambda i, at: (0,) * len(a.shape))
    mine = lambda height: pl.BlockSpec((height, count), lambda i, at: (at[0], 0))
    block = jax.ShapeDtypeStruct((4, slab, rows), b16)
    part = jax.ShapeDtypeStruct((slab, width), b16)
    return call(
        lambda *refs: kernel(rows, *refs),
        [block, block, part],
        [place, second, ring],
        [term[0] if isinstance(term, tuple) else term for term in terms] + [unit, norm, *feats],
        in_specs=[mine(slab + PAD) if isinstance(term, tuple) else whole(term) for term in terms]
        + [mine(slab), whole(norm)]
        + [whole(a) for a in feats],
        out_specs=[whole(block), whole(block), whole(part)],
        grid=(1,),
        scratch=[pltpu.VMEM((slab, count), b16)],
        cost=2 * slab * count * width,
    )


def pick_kernel(at_ref, img, txt, other_img, other_txt, out):
    width = img.shape[1]
    slots = out.shape[0]
    own = width // 128
    third = 2 * img.shape[0] // 3
    img = img[...].astype(f32) + other_img[...].astype(f32)
    txt = txt[...].astype(f32) + other_txt[...].astype(f32)
    part = jnp.concatenate([img, txt], axis=0).astype(b16)
    slot = lax.broadcasted_iota(jnp.int32, (slots, 1), 0)
    feature = lax.broadcasted_iota(jnp.int32, (slots, width), 1)
    base = (slot // 8 * 2 + at_ref[0]) * own
    chosen = jnp.where(feature == base + slot % 8, 1.0, 0.0).astype(b16)
    out[:, : 3 * third] = dot(chosen, part, NT).astype(b16)
    chosen = jnp.where(feature == base + 8, 1.0, 0.0).astype(b16)
    ninth = dot(chosen, part, NT)
    pick = slot % 8
    rest = jnp.where(pick == 1, ninth[:, third : 2 * third], ninth[:, :third])
    rest = jnp.where(pick == 2, ninth[:, 2 * third :], rest)
    out[:, 3 * third :] = rest.astype(b16)


def picked(core, parts):
    slab, width = parts[0].shape
    return call(
        pick_kernel,
        jax.ShapeDtypeStruct((64 * 8, slab * 8 // 3), b16),
        [core],
        parts,
        cost=8 * 512 * width * slab,
    )


def head_kernel(at_ref, got, img_out, txt_out):
    slab = img_out.shape[1] // 8
    third = slab * 2 // 3
    half = third // 2
    for p in range(8):
        img = txt = None
        for other in range(8):
            z, lo, hi, y = p // 2, p % 2, other // 4, other % 4
            block = got[(z * 2 + lo) * 8 + hi * 4 + y].astype(f32)
            img = block if img is None else img + block
            z, lo, hi, y = other // 2, other % 2, p % 2, p // 2
            block = got[(z * 2 + lo) * 8 + hi * 4 + y].astype(f32)
            txt = block if txt is None else txt + block
        at = p * slab
        ninth = 2 * slab
        img_out[0:8, at : at + slab] = img[:, :slab]
        img_out[8:9, at : at + third] = img[0:1, ninth : ninth + third]
        img_out[8:9, at + third : at + slab] = img[1:2, ninth : ninth + half]
        txt_out[0:8, at : at + slab] = txt[:, slab : 2 * slab]
        txt_out[8:9, at : at + half] = txt[1:2, ninth + half : ninth + third]
        txt_out[8:9, at + half : at + slab] = txt[2:3, ninth : ninth + third]


def together(arrays):
    return lax.optimization_barrier(list(arrays))


def pair_lines(own, got, second):
    return jnp.concatenate([jnp.where(second, got, own), jnp.where(second, own, got)], axis=1)


def whole_columns(lines, move, ring):
    got = []
    for d in range(4):
        block = lax.dynamic_index_in_dim(lines, (ring + d) % 4, 0, keepdims=False)
        got.append(send(block, move(d, 0)) if d else block)
    return jnp.concatenate([got[-d % 4] for d in range(4)], axis=0)


def from_ring(turned_head, ring):
    start = ring * (turned_head.shape[0] // 4)
    return lax.dynamic_slice_in_dim(
        jnp.concatenate([turned_head, turned_head]), start, turned_head.shape[0], axis=0
    )


def shards(image_feat, text_feat, image_head, text_head, group_bias, text_lang, partner):
    rows, width = image_feat.shape
    slab = width // 8
    place = lax.axis_index(DEV)
    z, lo, hi, y, core = place // 32, place // 16 % 2, place // 8 % 2, place // 2 % 4, place % 2

    figures = jnp.stack([text_lang, partner // 128, partner % 128]).astype(b16)
    figures = jnp.pad(figures, ((0, PAD - 3), (0, width - rows)))
    text_rows = jnp.concatenate([text_feat, figures], axis=0)
    img_feats = exchange(jnp.broadcast_to(image_feat[None], (8, rows, width)), IMG_GROUPS)
    img_feats = img_feats.reshape(8 * rows, width)
    across = send(text_rows, txt_move(0, 1))
    before = send(text_rows, txt_move(1, 0))
    after = send(text_rows, txt_move(3, 0))
    across, turned_txt = together([across, text_head.T])
    across_after = send(across, txt_move(3, 0))
    across_before = send(across, txt_move(1, 0))
    across_after, before, after, across, turned_img = together(
        [across_after, before, after, across, image_head.T]
    )
    far = send(before, txt_move(1, 0))
    across_far = send(across_after, txt_move(3, 0))
    pairs = [(text_rows, across), (after, across_after), (before, across_before)]
    near_y, far_y = [(y + d) % 4 for d in (0, 1, 3)], [(y + 2) % 4]
    *made, chunks = units(pairs, turned_txt, hi, near_y, rows, ())
    others = [send(chunks, core_move)]
    unit_txt, norm_txt, chunks = units([(far, across_far)], turned_txt, hi, far_y, rows, made)
    others.append(send(chunks, core_move))
    turned_units, norm_img, unit_img = img_units(img_feats, turned_img, image_head, rows)
    txt_blocks = [
        text_rows, across, after, across_after, far, across_far, before, across_before
    ]

    other_slopes, other_sum, other_up = other_tile(
        unit_img, turned_units, others, group_bias, place % 16, y, rows
    )
    back = send(other_up, core_move)
    text_up, img_terms = own_tile(
        unit_img, turned_units, unit_txt, others, other_slopes, other_sum, group_bias,
        place % 16, rows,
    )
    img_terms = exchange(img_terms, IMG_GROUPS)

    def slab_terms(d, e):
        at = (y + d) % 4 * 2 + (hi + e) % 2
        return [(text_up, at), (back, at)]

    far, across_far, across_after = sums(
        [slab_terms(2, 0), slab_terms(2, 1), slab_terms(1, 1)], rows
    )
    far = send(far, txt_move(1, 0))
    across_far = send(across_far, txt_move(3, 0))
    far, across_far, across_after = together([far, across_far, across_after])
    across_before = send(across_after, txt_move(1, 0))
    across_after, before, after = sums(
        [slab_terms(3, 1) + [across_far], slab_terms(1, 0) + [far], slab_terms(3, 0)], rows
    )
    across_after = send(across_after, txt_move(3, 0))
    across_before, across_after, before, after = together(
        [across_before, across_after, before, after]
    )
    before = send(before, txt_move(1, 0))
    after = send(after, txt_move(3, 0))
    (across,) = sums([slab_terms(0, 1) + [across_before, across_after]], rows)
    across = send(across, txt_move(0, 1))

    img_own, img_give, img_part = gradient(
        img_grad_kernel, z * 2 + lo, lo, z, [img_terms], turned_units, norm_img, [img_feats], rows
    )
    txt_own, txt_give, txt_part = gradient(
        txt_grad_kernel, y * 2 + hi, hi, y, slab_terms(0, 0) + [before, after, across],
        unit_txt, norm_txt, txt_blocks, rows,
    )
    img_theirs = send(img_part, core_move)
    txt_theirs = send(txt_part, core_move)
    img_got = send(img_give, img_move(0, 1))
    txt_got = send(txt_give, txt_move(0, 1))
    heads, img_got, txt_got = together(
        [picked(core, [img_part, txt_part, img_theirs, txt_theirs]), img_got, txt_got]
    )
    heads = exchange(heads.reshape(64, 8, -1), CHIP_GROUPS)
    head_shape = jax.ShapeDtypeStruct((width // 128, width), f32)
    image_head_grad, text_head_grad = call(head_kernel, [head_shape] * 2, [core], [heads])

    grad_img = whole_columns(pair_lines(img_own, img_got, lo), img_move, z)
    image_grad = dot(grad_img, from_ring(turned_img, z), TN)
    grad_txt = whole_columns(pair_lines(txt_own, txt_got, hi), txt_move, y)
    text_grad = dot(grad_txt, from_ring(turned_txt, y), TN)
    return (image_grad, text_grad, image_head_grad, text_head_grad)


def solution(mesh):
    line = jax.sharding.Mesh(mesh.devices.reshape(-1), (DEV,))
    in_specs = (P(DEV, None), P(DEV, None), P(), P(), P(), P(DEV), P(DEV))
    return jax.shard_map(
        shards, mesh=line, in_specs=in_specs, out_specs=(P(DEV, None),) * 4, check_vma=False
    )
```

```python
import jax
import jax.numpy as jnp
from jax import lax
from jax.experimental import pallas as pl
from jax.experimental.pallas import tpu as pltpu
from jax.sharding import PartitionSpec as P

logit_scale = 64.0
epsilon = 1e-06
log2e = 1.4426950408889634
f32, b16 = jnp.float32, jnp.bfloat16

DEV = "dev"
PLACES = [
    (z, lo, hi, y, c)
    for z in range(4)
    for lo in range(2)
    for hi in range(2)
    for y in range(4)
    for c in range(2)
]


def flat(z, lo, hi, y, c):
    return (z * 2 + lo) * 16 + hi * 8 + y * 2 + c


def img_move(d, e):
    return lambda z, lo, hi, y, c: ((z + d) % 4, lo ^ e, hi, y, c)


def txt_move(d, e):
    return lambda z, lo, hi, y, c: (z, lo ^ e, hi ^ e, (y + d) % 4, c)


def core_move(z, lo, hi, y, c):
    return (z, lo, hi, y, 1 - c)


IMG_GROUPS = [
    [flat(z, lo, hi, y, c) for z in range(4) for lo in range(2)]
    for hi in range(2)
    for y in range(4)
    for c in range(2)
]
TXT_GROUPS = [
    [flat(z, hi ^ b, hi, y, c) for y in range(4) for hi in range(2)]
    for z in range(4)
    for b in range(2)
    for c in range(2)
]
TXT_CORE_GROUPS = [
    [flat(z, hi ^ b, hi, y, c) for c in range(2) for y in range(4) for hi in range(2)]
    for z in range(4)
    for b in range(2)
]
CHIP_GROUPS = [[flat(*p) for p in PLACES if p[4] == c] for c in range(2)]


def send(block, move):
    return lax.ppermute(block, DEV, [(flat(*p), flat(*move(*p))) for p in PLACES])


def exchange(blocks, groups):
    return lax.all_to_all(blocks, DEV, 0, 0, axis_index_groups=groups, tiled=True)


PAD = 16
NN = (((1,), (0,)), ((), ()))
NT = (((1,), (1,)), ((), ()))
TN = (((0,), (0,)), ((), ()))


def dot(a, b, dims):
    return lax.dot_general(a, b, dims, preferred_element_type=f32)


def call(body, out_shape, scalars, arrays, in_specs=None, out_specs=None, grid=(), scratch=(), cost=0, aliases=None, limit=60):
    whole = pl.BlockSpec(memory_space=pltpu.VMEM)
    many = isinstance(out_shape, (list, tuple))
    if in_specs is None:
        in_specs = [whole] * len(arrays)
    if out_specs is None:
        out_specs = [whole] * len(out_shape) if many else whole
    spec = pltpu.PrefetchScalarGridSpec(
        num_scalar_prefetch=1,
        grid=grid,
        in_specs=in_specs,
        out_specs=out_specs,
        scratch_shapes=list(scratch),
    )
    moved = sum(a.size * a.dtype.itemsize for a in arrays)
    return pl.pallas_call(
        body,
        out_shape=out_shape,
        grid_spec=spec,
        input_output_aliases=aliases or {},
        compiler_params=pltpu.CompilerParams(vmem_limit_bytes=limit * 2**20),
        cost_estimate=pl.CostEstimate(flops=cost, bytes_accessed=moved, transcendentals=0),
    )(jnp.stack(scalars).astype(jnp.int32), *arrays)


def aligned(index, size):
    return pl.ds(pl.multiple_of(index * size, size), size)


def split_rows(total, lanes):
    high = total.astype(b16).astype(f32)
    row = lax.broadcasted_iota(jnp.int32, (PAD, lanes), 0)
    return jnp.where(row == 0, high, jnp.where(row == 1, total - high, 0.0)).astype(b16)


def joined(rows):
    return rows[0:1].astype(f32) + rows[1:2].astype(f32)


def in_pair(own, across, second, rows):
    own, across = own[:rows], across[:rows]
    first = second == 0
    return jnp.concatenate([jnp.where(first, own, across), jnp.where(first, across, own)], axis=0)


def put_units(feats, turned_head, proj, turned, norm):
    width = turned_head.shape[0]
    quarter = width // 4
    total = jnp.zeros((1, feats.shape[0]), f32)
    for m in range(4):
        span = slice(m * quarter, (m + 1) * quarter)
        part = dot(turned_head[span], feats[...], NT)
        proj[span] = part
        total = total + jnp.sum(part * part, axis=0, keepdims=True)
    length = jnp.sqrt(total + epsilon)
    norm[...] = length
    inverse = 1.0 / length
    for m in range(4):
        span = slice(m * quarter, (m + 1) * quarter)
        turned[span] = (proj[span] * inverse).astype(b16)


def unit_kernel(rows, at_ref, *refs):
    blocks, (turned_head, turned, norm, feats, proj) = refs[:8], refs[8:]
    width = turned_head.shape[0]
    second = at_ref[1]
    step = pl.program_id(0)
    for d in range(4):
        own, across = blocks[2 * d], blocks[2 * d + 1]

        @pl.when(step == d)
        def _():
            feats[...] = in_pair(own, across, second, rows)
            first = second == 0
            sides = own[rows:, :rows], across[rows:, :rows]
            turned[width:, :rows] = jnp.where(first, sides[0], sides[1])
            turned[width:, rows:] = jnp.where(first, sides[1], sides[0])

    put_units(feats, turned_head, proj, turned, norm)


def units(blocks, turned_head, ring, second, rows):
    width = turned_head.shape[0]
    tile = 2 * rows
    whole = lambda a: pl.BlockSpec(a.shape, lambda i, at: (0, 0))
    return call(
        lambda *refs: unit_kernel(rows, *refs),
        [
            jax.ShapeDtypeStruct((width + PAD, 8 * rows), b16),
            jax.ShapeDtypeStruct((1, 8 * rows), f32),
        ],
        [ring, second],
        [*blocks, turned_head],
        in_specs=[whole(a) for a in [*blocks, turned_head]],
        out_specs=[
            pl.BlockSpec((width + PAD, tile), lambda i, at: (0, (at[0] + i) % 4)),
            pl.BlockSpec((1, tile), lambda i, at: (0, (at[0] + i) % 4)),
        ],
        grid=(4,),
        scratch=[pltpu.VMEM((tile, width), b16), pltpu.VMEM((width, tile), f32)],
        cost=2 * 8 * rows * width * width,
    )


def unit_columns(feats, head):
    projected = dot(head, feats, (((0,), (1,)), ((), ())))
    norm = jnp.sqrt(jnp.sum(projected * projected, axis=0, keepdims=True) + epsilon)
    return (projected / norm).astype(b16), norm


def unit_rows(feats, head):
    projected = dot(feats, head, NN)
    norm = jnp.sqrt(jnp.sum(projected * projected, axis=1, keepdims=True) + epsilon)
    return (projected / norm).astype(b16)


def tile_slopes(rows, groups, place, bias_ref, img, txt, slopes, by_img):
    width = img.shape[1]
    tile = 2 * rows
    lang = txt[width : width + PAD].astype(f32)
    partner = lang[1:2] * 128.0 + lang[2:3]
    lang = lang[0:1]
    bias = jnp.zeros((1, tile), f32)
    for g in range(groups):
        bias = jnp.where(lang == g, bias_ref[g], bias)
    bias = bias * -log2e
    down = jnp.zeros((1, tile), f32)
    high = 4 * rows
    for m in range(img.shape[0] // high):
        span = slice(m * high, (m + 1) * high)
        index = m * high + lax.broadcasted_iota(jnp.int32, (high, 1), 0)
        ids = ((index // rows * 16 + place) * rows + index % rows).astype(f32)
        cosines = dot(img[span], txt[:width], NN)
        below = 1.0 + jnp.exp2(cosines * (-log2e * logit_scale) + bias)
        gate = pl.reciprocal(below, approx=True)
        gate = gate * (2.0 - below * gate)
        slope = gate - jnp.where(partner == ids, 1.0, 0.0)
        slopes[span, :tile] = slope.astype(b16)
        weighted = slope * cosines
        down = down + jnp.sum(weighted, axis=0, keepdims=True)
        side = by_img[span]
        for k in range(0, tile, by_img.shape[1]):
            side = side + weighted[:, k : k + by_img.shape[1]]
        by_img[span] = side
    return logit_scale * down


def put_text_terms(up, turned, slopes, down):
    slab = turned.shape[0] // 8
    figures = split_rows(down, up.shape[1])
    part = dot(turned[...], slopes, NN)
    for e in range(8):
        at = e * (slab + PAD)
        up[at : at + slab] = part[e * slab : (e + 1) * slab].astype(b16)
        up[at + slab : at + slab + PAD] = figures


def other_kernel(rows, groups, at_ref, bias_ref, img, turned, txt, slopes, img_sum, up, by_img):
    step = pl.program_id(0)

    @pl.when(step == 0)
    def _():
        by_img[...] = jnp.zeros(by_img.shape, f32)

    down = tile_slopes(rows, groups, at_ref[0], bias_ref, img, txt, slopes.at[0], by_img)
    put_text_terms(up, turned, slopes[0], down)

    @pl.when(step == 3)
    def _():
        img_sum[...] = logit_scale * jnp.sum(by_img[...].T, axis=0, keepdims=True)


def other_tile(img, turned, txt, group_bias, place, rows):
    count, width = img.shape
    tile = 2 * rows
    height = width + 8 * PAD
    whole = lambda a: pl.BlockSpec(a.shape, lambda i, at: (0, 0))
    return call(
        lambda *refs: other_kernel(rows, group_bias.shape[0], *refs),
        [
            jax.ShapeDtypeStruct((4, count, tile), b16),
            jax.ShapeDtypeStruct((1, count), f32),
            jax.ShapeDtypeStruct((height, count), b16),
        ],
        [place],
        [group_bias, img, turned, txt],
        in_specs=[
            pl.BlockSpec(memory_space=pltpu.SMEM),
            whole(img),
            whole(turned),
            pl.BlockSpec((width + PAD, tile), lambda i, at: (0, i)),
        ],
        out_specs=[
            pl.BlockSpec((1, count, tile), lambda i, at: (i, 0, 0)),
            pl.BlockSpec((1, count), lambda i, at: (0, 0)),
            pl.BlockSpec((height, tile), lambda i, at: (0, i)),
        ],
        grid=(4,),
        scratch=[pltpu.VMEM((count, min(128, tile)), f32)],
        cost=4 * width * count * count,
    )


def own_kernel(rows, groups, at_ref, bias_ref, img, turned, txt, other, *refs):
    other_slopes, other_sum, up, out, by_img, held, both, total = refs
    step = pl.program_id(0)
    width = img.shape[1]
    tile = 2 * rows

    @pl.when(step == 0)
    def _():
        by_img[...] = jnp.zeros(by_img.shape, f32)
        total[...] = jnp.zeros(total.shape, f32)

    both[:, tile:] = other[:width]
    held[:, tile:] = other_slopes[0]
    both[:, :tile] = txt[:width]
    down = tile_slopes(rows, groups, at_ref[0], bias_ref, img, txt, held, by_img)
    put_text_terms(up, turned, held[:, :tile], down)
    total[...] += dot(both[...], held[...], NT)

    @pl.when(step == 3)
    def _():
        slab = width // 8
        sums = logit_scale * jnp.sum(by_img[...].T, axis=0, keepdims=True) + other_sum[...]
        figures = split_rows(sums, sums.shape[1])
        for e in range(8):
            out[e, :slab] = total[e * slab : (e + 1) * slab].astype(b16)
            out[e, slab:] = figures


def own_tile(
    img, turned, txt, other, other_slopes, other_sum, group_bias, place, rows
):
    count, width = img.shape
    tile = 2 * rows
    height = width + 8 * PAD
    slab = width // 8
    whole = lambda a: pl.BlockSpec(a.shape, lambda i, at: (0, 0))
    stack = lambda a: pl.BlockSpec(a.shape, lambda i, at: (0, 0, 0))
    pieces = jax.ShapeDtypeStruct((8, slab + PAD, count), b16)
    return call(
        lambda *refs: own_kernel(rows, group_bias.shape[0], *refs),
        [jax.ShapeDtypeStruct((height, count), b16), pieces],
        [place],
        [group_bias, img, turned, txt, other, other_slopes, other_sum],
        in_specs=[
            pl.BlockSpec(memory_space=pltpu.SMEM),
            whole(img),
            whole(turned),
            pl.BlockSpec((width + PAD, tile), lambda i, at: (0, i)),
            pl.BlockSpec((width + PAD, tile), lambda i, at: (0, i)),
            pl.BlockSpec((1, count, tile), lambda i, at: (i, 0, 0)),
            whole(other_sum),
        ],
        out_specs=[pl.BlockSpec((height, tile), lambda i, at: (0, i)), stack(pieces)],
        grid=(4,),
        scratch=[
            pltpu.VMEM((count, min(128, tile)), f32),
            pltpu.VMEM((count, 2 * tile), b16),
            pltpu.VMEM((width, 2 * tile), b16),
            pltpu.VMEM((width, count), f32),
        ],
        cost=8 * width * count * count,
    )


def sum_into(out, terms):
    slab = out.shape[0] - PAD
    block, total = terms[0][:slab].astype(f32), joined(terms[0][slab:])
    for term in terms[1:]:
        block, total = block + term[:slab].astype(f32), total + joined(term[slab:])
    out[:slab] = block.astype(b16)
    out[slab:] = split_rows(total, out.shape[1])


def sum_kernel(sizes, at_ref, *refs):
    start = 0
    for size, out in zip(sizes, refs[sum(sizes) :]):
        sum_into(out, refs[start : start + size])
        start += size


def sums(groups, rows):
    flat_terms = [term for group in groups for term in group]
    arrays, specs, places = [], [], [jnp.int32(0)]
    height = None
    for term in flat_terms:
        if isinstance(term, tuple):
            arrays.append(term[0])
            height = term[0].shape[0] // 8
            specs.append(
                pl.BlockSpec((height, 4 * rows), lambda i, at, n=len(places): (at[n], i))
            )
            places.append(term[1])
        else:
            arrays.append(term)
            height = term.shape[0]
            specs.append(pl.BlockSpec((height, 4 * rows), lambda i, at: (0, i)))
    count = arrays[0].shape[1]
    spec = pl.BlockSpec((height, 4 * rows), lambda i, at: (0, i))
    return call(
        lambda *refs: sum_kernel([len(group) for group in groups], *refs),
        [jax.ShapeDtypeStruct((height, count), b16)] * len(groups),
        places,
        arrays,
        in_specs=specs,
        out_specs=[spec] * len(groups),
        grid=(count // (4 * rows),),
    )


def img_grad_kernel(rows, at_ref, got, unit, norm, feats, blocks, part, grad):
    slab = unit.shape[0]
    up, inner = got[0, :slab].astype(f32), joined(got[0, slab:])
    for n in range(1, 8):
        up, inner = up + got[n, :slab].astype(f32), inner + joined(got[n, slab:])
    up = logit_scale * up - unit[...].astype(f32) * inner
    grad[...] = (up * (1.0 / norm[...])).astype(b16)
    for n in range(8):
        blocks[n] = grad[:, n * rows : (n + 1) * rows]
    part[...] = dot(grad[...], feats[...], NN).astype(b16)


def txt_grad_kernel(rows, at_ref, *refs):
    terms, unit, norm, blocks, (own, give, part, grad) = (
        refs[:5], refs[5], refs[6], refs[7:15], refs[15:]
    )
    slab = unit.shape[0]
    up, inner = terms[0][:slab].astype(f32), joined(terms[0][slab:])
    for term in terms[1:]:
        up, inner = up + term[:slab].astype(f32), inner + joined(term[slab:])
    up = logit_scale * up - unit[...].astype(f32) * inner
    grad[...] = (up * (1.0 / norm[...])).astype(b16)
    for ring in range(4):
        low = grad[:, (2 * ring) * rows : (2 * ring + 1) * rows]
        high = grad[:, (2 * ring + 1) * rows : (2 * ring + 2) * rows]
        own[ring] = jnp.where(at_ref[1] == 0, low, high)
        give[ring] = jnp.where(at_ref[1] == 0, high, low)
    total = None
    for d in range(4):
        cols = grad[:, aligned((at_ref[2] + d) % 4, 2 * rows)]
        term = dot(cols, in_pair(blocks[2 * d], blocks[2 * d + 1], at_ref[1], rows), NN)
        total = term if total is None else total + term
    part[...] = total.astype(b16)


def gradient(kernel, place, second, ring, terms, unit, norm, feats, halves, rows):
    width = feats[0].shape[1]
    slab, count = width // 8, 8 * rows
    whole = lambda a: pl.BlockSpec(a.shape, lambda i, at: (0,) * len(a.shape))
    mine = lambda height: pl.BlockSpec((height, count), lambda i, at: (at[0], 0))
    block = jax.ShapeDtypeStruct((8 // halves, slab, rows), b16)
    part = jax.ShapeDtypeStruct((slab, width), b16)
    return call(
        lambda *refs: kernel(rows, *refs),
        [block] * halves + [part],
        [place, second, ring],
        [term[0] if isinstance(term, tuple) else term for term in terms] + [unit, norm, *feats],
        in_specs=[mine(slab + PAD) if isinstance(term, tuple) else whole(term) for term in terms]
        + [mine(slab), whole(norm)]
        + [whole(a) for a in feats],
        out_specs=[whole(block)] * halves + [whole(part)],
        grid=(1,),
        scratch=[pltpu.VMEM((slab, count), b16)],
        cost=2 * slab * count * width,
    )


def pick_kernel(at_ref, img, txt, other_img, other_txt, out):
    width = img.shape[1]
    slots = out.shape[0]
    own = width // 128
    third = 2 * img.shape[0] // 3
    img = img[...].astype(f32) + other_img[...].astype(f32)
    txt = txt[...].astype(f32) + other_txt[...].astype(f32)
    part = jnp.concatenate([img, txt], axis=0).astype(b16)
    slot = lax.broadcasted_iota(jnp.int32, (slots, 1), 0)
    feature = lax.broadcasted_iota(jnp.int32, (slots, width), 1)
    base = (slot // 8 * 2 + at_ref[0]) * own
    chosen = jnp.where(feature == base + slot % 8, 1.0, 0.0).astype(b16)
    out[:, : 3 * third] = dot(chosen, part, NT).astype(b16)
    chosen = jnp.where(feature == base + 8, 1.0, 0.0).astype(b16)
    ninth = dot(chosen, part, NT)
    pick = slot % 8
    rest = jnp.where(pick == 1, ninth[:, third : 2 * third], ninth[:, :third])
    rest = jnp.where(pick == 2, ninth[:, 2 * third :], rest)
    out[:, 3 * third :] = rest.astype(b16)


def picked(core, parts):
    slab, width = parts[0].shape
    return call(
        pick_kernel,
        jax.ShapeDtypeStruct((64 * 8, slab * 8 // 3), b16),
        [core],
        parts,
        cost=8 * 512 * width * slab,
    )


def head_kernel(at_ref, got, img_out, txt_out):
    slab = img_out.shape[1] // 8
    third = slab * 2 // 3
    half = third // 2
    for p in range(8):
        img = txt = None
        for other in range(8):
            z, lo, hi, y = p // 2, p % 2, other // 4, other % 4
            block = got[(z * 2 + lo) * 8 + hi * 4 + y].astype(f32)
            img = block if img is None else img + block
            z, lo, hi, y = other // 2, other % 2, p % 2, p // 2
            block = got[(z * 2 + lo) * 8 + hi * 4 + y].astype(f32)
            txt = block if txt is None else txt + block
        at = p * slab
        ninth = 2 * slab
        img_out[0:8, at : at + slab] = img[:, :slab]
        img_out[8:9, at : at + third] = img[0:1, ninth : ninth + third]
        img_out[8:9, at + third : at + slab] = img[1:2, ninth : ninth + half]
        txt_out[0:8, at : at + slab] = txt[:, slab : 2 * slab]
        txt_out[8:9, at : at + half] = txt[1:2, ninth + half : ninth + third]
        txt_out[8:9, at + half : at + slab] = txt[2:3, ninth : ninth + third]


def together(arrays):
    return lax.optimization_barrier(list(arrays))


def pair_lines(own, got, second):
    return jnp.concatenate([jnp.where(second, got, own), jnp.where(second, own, got)], axis=1)


def whole_columns(lines, move, ring):
    got = []
    for d in range(4):
        block = lax.dynamic_index_in_dim(lines, (ring + d) % 4, 0, keepdims=False)
        got.append(send(block, move(d, 0)) if d else block)
    return jnp.concatenate([got[-d % 4] for d in range(4)], axis=0)


def from_ring(turned_head, ring):
    start = ring * (turned_head.shape[0] // 4)
    return lax.dynamic_slice_in_dim(
        jnp.concatenate([turned_head, turned_head]), start, turned_head.shape[0], axis=0
    )


def shards(image_feat, text_feat, image_head, text_head, group_bias, text_lang, partner):
    rows, width = image_feat.shape
    slab = width // 8
    place = lax.axis_index(DEV)
    z, lo, hi, y, core = place // 32, place // 16 % 2, place // 8 % 2, place // 2 % 4, place % 2

    figures = jnp.stack([text_lang, partner // 128, partner % 128]).astype(b16)
    figures = jnp.pad(figures, ((0, PAD - 3), (0, width - rows)))
    text_rows = jnp.concatenate([text_feat, figures], axis=0)
    img_feats = exchange(jnp.broadcast_to(image_feat[None], (8, rows, width)), IMG_GROUPS)
    img_feats = img_feats.reshape(8 * rows, width)
    across = send(text_rows, txt_move(0, 1))
    before = send(text_rows, txt_move(1, 0))
    after = send(text_rows, txt_move(3, 0))
    across, turned_txt = together([across, text_head.T])
    across_after = send(across, txt_move(3, 0))
    across_before = send(across, txt_move(1, 0))
    across_after, before, after, across = together([across_after, before, after, across])
    far = send(before, txt_move(1, 0))
    across_far = send(across_after, txt_move(3, 0))
    txt_blocks = [
        text_rows, across, after, across_after, far, across_far, before, across_before
    ]
    unit_txt, norm_txt = units(txt_blocks, turned_txt, y, hi, rows)
    other_txt = send(unit_txt, core_move)
    turned_units, norm_img = unit_columns(img_feats, image_head)
    unit_img = unit_rows(together([img_feats, unit_txt])[0], image_head)

    other_slopes, other_sum, other_up = other_tile(
        unit_img, turned_units, other_txt, group_bias, place % 16, rows
    )
    back = send(other_up, core_move)
    text_up, img_terms = own_tile(
        unit_img, turned_units, unit_txt, other_txt, other_slopes, other_sum, group_bias,
        place % 16, rows,
    )
    img_terms = exchange(img_terms, IMG_GROUPS)
    (txt_ring_head,) = together([from_ring(turned_txt, y)])

    def slab_terms(d, e):
        at = (y + d) % 4 * 2 + (hi + e) % 2
        return [(text_up, at), (back, at)]

    far, across_far, across_after = sums(
        [slab_terms(2, 0), slab_terms(2, 1), slab_terms(1, 1)], rows
    )
    far = send(far, txt_move(1, 0))
    across_far = send(across_far, txt_move(3, 0))
    far, across_far, across_after = together([far, across_far, across_after])
    across_before = send(across_after, txt_move(1, 0))
    across_after, before, after = sums(
        [slab_terms(3, 1) + [across_far], slab_terms(1, 0) + [far], slab_terms(3, 0)], rows
    )
    across_after = send(across_after, txt_move(3, 0))
    across_before, across_after, before, after = together(
        [across_before, across_after, before, after]
    )
    before = send(before, txt_move(1, 0))
    after = send(after, txt_move(3, 0))
    (across,) = sums([slab_terms(0, 1) + [across_before, across_after]], rows)
    across = send(across, txt_move(0, 1))

    img_blocks, img_part = gradient(
        img_grad_kernel, z * 2 + lo, lo, z, [img_terms], turned_units, norm_img, [img_feats], 1, rows
    )
    grad_img = exchange(img_blocks, IMG_GROUPS).reshape(width, rows)
    txt_own, txt_give, txt_part = gradient(
        txt_grad_kernel, y * 2 + hi, hi, y, slab_terms(0, 0) + [before, after, across],
        unit_txt, norm_txt, txt_blocks, 2, rows,
    )
    img_theirs = send(img_part, core_move)
    txt_theirs = send(txt_part, core_move)
    txt_got = send(txt_give, txt_move(0, 1))
    heads, txt_got = together([picked(core, [img_part, txt_part, img_theirs, txt_theirs]), txt_got])
    heads = exchange(heads.reshape(64, 8, -1), CHIP_GROUPS)
    head_shape = jax.ShapeDtypeStruct((width // 128, width), f32)
    image_head_grad, text_head_grad = call(head_kernel, [head_shape] * 2, [core], [heads])

    image_grad = dot(grad_img, image_head, (((0,), (1,)), ((), ())))
    grad_txt = whole_columns(pair_lines(txt_own, txt_got, hi), txt_move, y)
    text_grad = dot(grad_txt, txt_ring_head, TN)
    return (image_grad, text_grad, image_head_grad, text_head_grad)


def solution(mesh):
    line = jax.sharding.Mesh(mesh.devices.reshape(-1), (DEV,))
    in_specs = (P(DEV, None), P(DEV, None), P(), P(), P(), P(DEV), P(DEV))
    return jax.shard_map(
        shards, mesh=line, in_specs=in_specs, out_specs=(P(DEV, None),) * 4, check_vma=False
    )
```

```python
import jax
import jax.numpy as jnp
from jax import lax
from jax.experimental import pallas as pl
from jax.experimental.pallas import tpu as pltpu
from jax.sharding import PartitionSpec as P

logit_scale = 64.0
epsilon = 1e-06
log2e = 1.4426950408889634
f32, b16 = jnp.float32, jnp.bfloat16

DEV = "dev"
PLACES = [
    (z, lo, hi, y, c)
    for z in range(4)
    for lo in range(2)
    for hi in range(2)
    for y in range(4)
    for c in range(2)
]


def flat(z, lo, hi, y, c):
    return (z * 2 + lo) * 16 + hi * 8 + y * 2 + c


def img_move(d, e):
    return lambda z, lo, hi, y, c: ((z + d) % 4, lo ^ e, hi, y, c)


def txt_move(d, e):
    return lambda z, lo, hi, y, c: (z, lo ^ e, hi ^ e, (y + d) % 4, c)


def core_move(z, lo, hi, y, c):
    return (z, lo, hi, y, 1 - c)


IMG_GROUPS = [
    [flat(z, lo, hi, y, c) for z in range(4) for lo in range(2)]
    for hi in range(2)
    for y in range(4)
    for c in range(2)
]
TXT_GROUPS = [
    [flat(z, hi ^ b, hi, y, c) for y in range(4) for hi in range(2)]
    for z in range(4)
    for b in range(2)
    for c in range(2)
]
TXT_CORE_GROUPS = [
    [flat(z, hi ^ b, hi, y, c) for c in range(2) for y in range(4) for hi in range(2)]
    for z in range(4)
    for b in range(2)
]
CHIP_GROUPS = [[flat(*p) for p in PLACES if p[4] == c] for c in range(2)]


def send(block, move):
    return lax.ppermute(block, DEV, [(flat(*p), flat(*move(*p))) for p in PLACES])


def exchange(blocks, groups):
    return lax.all_to_all(blocks, DEV, 0, 0, axis_index_groups=groups, tiled=True)


PAD = 16
NN = (((1,), (0,)), ((), ()))
NT = (((1,), (1,)), ((), ()))
TN = (((0,), (0,)), ((), ()))


def dot(a, b, dims):
    return lax.dot_general(a, b, dims, preferred_element_type=f32)


def call(body, out_shape, scalars, arrays, in_specs=None, out_specs=None, grid=(), scratch=(), cost=0, aliases=None, limit=60):
    whole = pl.BlockSpec(memory_space=pltpu.VMEM)
    many = isinstance(out_shape, (list, tuple))
    if in_specs is None:
        in_specs = [whole] * len(arrays)
    if out_specs is None:
        out_specs = [whole] * len(out_shape) if many else whole
    spec = pltpu.PrefetchScalarGridSpec(
        num_scalar_prefetch=1,
        grid=grid,
        in_specs=in_specs,
        out_specs=out_specs,
        scratch_shapes=list(scratch),
    )
    moved = sum(a.size * a.dtype.itemsize for a in arrays)
    return pl.pallas_call(
        body,
        out_shape=out_shape,
        grid_spec=spec,
        input_output_aliases=aliases or {},
        compiler_params=pltpu.CompilerParams(vmem_limit_bytes=limit * 2**20),
        cost_estimate=pl.CostEstimate(flops=cost, bytes_accessed=moved, transcendentals=0),
    )(jnp.stack(scalars).astype(jnp.int32), *arrays)


def aligned(index, size):
    return pl.ds(pl.multiple_of(index * size, size), size)


def split_rows(total, lanes):
    high = total.astype(b16).astype(f32)
    row = lax.broadcasted_iota(jnp.int32, (PAD, lanes), 0)
    return jnp.where(row == 0, high, jnp.where(row == 1, total - high, 0.0)).astype(b16)


def joined(rows):
    return rows[0:1].astype(f32) + rows[1:2].astype(f32)


def in_pair(own, across, second, rows):
    own, across = own[:rows], across[:rows]
    first = second == 0
    return jnp.concatenate([jnp.where(first, own, across), jnp.where(first, across, own)], axis=0)


def put_units(feats, turned_head, proj, turned, norm):
    width = turned_head.shape[0]
    quarter = width // 4
    total = jnp.zeros((1, feats.shape[0]), f32)
    for m in range(4):
        span = slice(m * quarter, (m + 1) * quarter)
        part = dot(turned_head[span], feats[...], NT)
        proj[span] = part
        total = total + jnp.sum(part * part, axis=0, keepdims=True)
    length = jnp.sqrt(total + epsilon)
    norm[...] = length
    inverse = 1.0 / length
    for m in range(4):
        span = slice(m * quarter, (m + 1) * quarter)
        turned[span] = (proj[span] * inverse).astype(b16)


def img_unit_kernel(at_ref, feats, turned_head, head, turned, norm, unit, proj):
    put_units(feats, turned_head, proj, turned, norm)
    part = dot(feats[...], head[...], NN)
    total = jnp.sum(part * part, axis=1, keepdims=True)
    unit[...] = (part * (1.0 / jnp.sqrt(total + epsilon))).astype(b16)


def img_units(feats, turned_head, head, rows):
    count, width = feats.shape
    tile = 2 * rows
    whole = pl.BlockSpec(head.shape, lambda i, at: (0, 0))
    return call(
        img_unit_kernel,
        [
            jax.ShapeDtypeStruct((width, count), b16),
            jax.ShapeDtypeStruct((1, count), f32),
            jax.ShapeDtypeStruct((count, width), b16),
        ],
        [jnp.int32(0)],
        [feats, turned_head, head],
        in_specs=[pl.BlockSpec((tile, width), lambda i, at: (i, 0)), whole, whole],
        out_specs=[
            pl.BlockSpec((width, tile), lambda i, at: (0, i)),
            pl.BlockSpec((1, tile), lambda i, at: (0, i)),
            pl.BlockSpec((tile, width), lambda i, at: (i, 0)),
        ],
        grid=(4,),
        scratch=[pltpu.VMEM((width, tile), f32)],
        cost=4 * count * width * width,
    )


def unit_kernel(rows, at_ref, *refs):
    blocks, (turned_head, turned, norm, feats, proj) = refs[:8], refs[8:]
    width = turned_head.shape[0]
    second = at_ref[1]
    step = pl.program_id(0)
    for d in range(4):
        own, across = blocks[2 * d], blocks[2 * d + 1]

        @pl.when(step == d)
        def _():
            feats[...] = in_pair(own, across, second, rows)
            first = second == 0
            sides = own[rows:, :rows], across[rows:, :rows]
            turned[width:, :rows] = jnp.where(first, sides[0], sides[1])
            turned[width:, rows:] = jnp.where(first, sides[1], sides[0])

    put_units(feats, turned_head, proj, turned, norm)


def units(blocks, turned_head, ring, second, rows):
    width = turned_head.shape[0]
    tile = 2 * rows
    whole = lambda a: pl.BlockSpec(a.shape, lambda i, at: (0, 0))
    return call(
        lambda *refs: unit_kernel(rows, *refs),
        [
            jax.ShapeDtypeStruct((width + PAD, 8 * rows), b16),
            jax.ShapeDtypeStruct((1, 8 * rows), f32),
        ],
        [ring, second],
        [*blocks, turned_head],
        in_specs=[whole(a) for a in [*blocks, turned_head]],
        out_specs=[
            pl.BlockSpec((width + PAD, tile), lambda i, at: (0, (at[0] + i) % 4)),
            pl.BlockSpec((1, tile), lambda i, at: (0, (at[0] + i) % 4)),
        ],
        grid=(4,),
        scratch=[pltpu.VMEM((tile, width), b16), pltpu.VMEM((width, tile), f32)],
        cost=2 * 8 * rows * width * width,
    )


def tile_slopes(rows, groups, place, bias_ref, img, txt, slopes, by_img):
    width = img.shape[1]
    tile = 2 * rows
    lang = txt[width : width + PAD].astype(f32)
    partner = lang[1:2] * 128.0 + lang[2:3]
    lang = lang[0:1]
    bias = jnp.zeros((1, tile), f32)
    for g in range(groups):
        bias = jnp.where(lang == g, bias_ref[g], bias)
    bias = bias * -log2e
    down = jnp.zeros((1, tile), f32)
    high = 4 * rows
    for m in range(img.shape[0] // high):
        span = slice(m * high, (m + 1) * high)
        index = m * high + lax.broadcasted_iota(jnp.int32, (high, 1), 0)
        ids = ((index // rows * 16 + place) * rows + index % rows).astype(f32)
        cosines = dot(img[span], txt[:width], NN)
        below = 1.0 + jnp.exp2(cosines * (-log2e * logit_scale) + bias)
        gate = pl.reciprocal(below, approx=True)
        gate = gate * (2.0 - below * gate)
        slope = gate - jnp.where(partner == ids, 1.0, 0.0)
        slopes[span, :tile] = slope.astype(b16)
        weighted = slope * cosines
        down = down + jnp.sum(weighted, axis=0, keepdims=True)
        side = by_img[span]
        for k in range(0, tile, by_img.shape[1]):
            side = side + weighted[:, k : k + by_img.shape[1]]
        by_img[span] = side
    return logit_scale * down


def put_text_terms(up, turned, slopes, down):
    slab = turned.shape[0] // 8
    figures = split_rows(down, up.shape[1])
    part = dot(turned[...], slopes, NN)
    for e in range(8):
        at = e * (slab + PAD)
        up[at : at + slab] = part[e * slab : (e + 1) * slab].astype(b16)
        up[at + slab : at + slab + PAD] = figures


def pair_kernel(rows, groups, at_ref, bias_ref, img, turned, txt, slopes, img_sum, up, by_img):
    step = pl.program_id(0)

    @pl.when(step == 0)
    def _():
        by_img[...] = jnp.zeros(by_img.shape, f32)

    down = tile_slopes(rows, groups, at_ref[0], bias_ref, img, txt, slopes.at[0], by_img)
    put_text_terms(up, turned, slopes[0], down)

    @pl.when(step == 3)
    def _():
        img_sum[...] = logit_scale * jnp.sum(by_img[...].T, axis=0, keepdims=True)


def pair_tile(img, turned, txt, group_bias, place, rows):
    count, width = img.shape
    tile = 2 * rows
    height = width + 8 * PAD
    whole = lambda a: pl.BlockSpec(a.shape, lambda i, at: (0, 0))
    return call(
        lambda *refs: pair_kernel(rows, group_bias.shape[0], *refs),
        [
            jax.ShapeDtypeStruct((4, count, tile), b16),
            jax.ShapeDtypeStruct((1, count), f32),
            jax.ShapeDtypeStruct((height, count), b16),
        ],
        [place],
        [group_bias, img, turned, txt],
        in_specs=[
            pl.BlockSpec(memory_space=pltpu.SMEM),
            whole(img),
            whole(turned),
            pl.BlockSpec((width + PAD, tile), lambda i, at: (0, i)),
        ],
        out_specs=[
            pl.BlockSpec((1, count, tile), lambda i, at: (i, 0, 0)),
            pl.BlockSpec((1, count), lambda i, at: (0, 0)),
            pl.BlockSpec((height, tile), lambda i, at: (0, i)),
        ],
        grid=(4,),
        scratch=[pltpu.VMEM((count, min(128, tile)), f32)],
        cost=4 * width * count * count,
    )


def image_kernel(at_ref, txt, other, slopes, other_slopes, img_sum, other_sum, out, held, both, total):
    step = pl.program_id(0)
    width, tile = total.shape[0], txt.shape[1]
    slab = width // 8
    both[:, :tile] = txt[:width]
    both[:, tile:] = other[:width]
    held[:, :tile] = slopes[0]
    held[:, tile:] = other_slopes[0]
    part = dot(both[...], held[...], NT)

    @pl.when(step == 0)
    def _():
        total[...] = part

    @pl.when(step != 0)
    def _():
        total[...] += part

    @pl.when(step == 3)
    def _():
        sums = img_sum[...] + other_sum[...]
        figures = split_rows(sums, sums.shape[1])
        for e in range(8):
            out[e, :slab] = total[e * slab : (e + 1) * slab].astype(b16)
            out[e, slab:] = figures


def image_tile(txt, other, slopes, other_slopes, img_sum, other_sum, rows):
    height, count = txt.shape
    width = height - PAD
    tile = 2 * rows
    pieces = jax.ShapeDtypeStruct((8, width // 8 + PAD, count), b16)
    whole = pl.BlockSpec((1, count), lambda i, at: (0, 0))
    return call(
        image_kernel,
        pieces,
        [jnp.int32(0)],
        [txt, other, slopes, other_slopes, img_sum, other_sum],
        in_specs=[pl.BlockSpec((height, tile), lambda i, at: (0, i))] * 2
        + [pl.BlockSpec((1, count, tile), lambda i, at: (i, 0, 0))] * 2
        + [whole, whole],
        out_specs=pl.BlockSpec(pieces.shape, lambda i, at: (0, 0, 0)),
        grid=(4,),
        scratch=[
            pltpu.VMEM((count, 2 * tile), b16),
            pltpu.VMEM((width, 2 * tile), b16),
            pltpu.VMEM((width, count), f32),
        ],
        cost=4 * width * count * count,
    )


def sum_into(out, terms):
    slab = out.shape[0] - PAD
    block, total = terms[0][:slab].astype(f32), joined(terms[0][slab:])
    for term in terms[1:]:
        block, total = block + term[:slab].astype(f32), total + joined(term[slab:])
    out[:slab] = block.astype(b16)
    out[slab:] = split_rows(total, out.shape[1])


def sum_kernel(sizes, at_ref, *refs):
    start = 0
    for size, out in zip(sizes, refs[sum(sizes) :]):
        sum_into(out, refs[start : start + size])
        start += size


def sums(groups, rows):
    flat_terms = [term for group in groups for term in group]
    arrays, specs, places = [], [], [jnp.int32(0)]
    height = None
    for term in flat_terms:
        if isinstance(term, tuple):
            arrays.append(term[0])
            height = term[0].shape[0] // 8
            specs.append(
                pl.BlockSpec((height, 4 * rows), lambda i, at, n=len(places): (at[n], i))
            )
            places.append(term[1])
        else:
            arrays.append(term)
            height = term.shape[0]
            specs.append(pl.BlockSpec((height, 4 * rows), lambda i, at: (0, i)))
    count = arrays[0].shape[1]
    spec = pl.BlockSpec((height, 4 * rows), lambda i, at: (0, i))
    return call(
        lambda *refs: sum_kernel([len(group) for group in groups], *refs),
        [jax.ShapeDtypeStruct((height, count), b16)] * len(groups),
        places,
        arrays,
        in_specs=specs,
        out_specs=[spec] * len(groups),
        grid=(count // (4 * rows),),
    )


def put_blocks(grad, second, own, give, rows):
    for ring in range(4):
        low = grad[:, (2 * ring) * rows : (2 * ring + 1) * rows]
        high = grad[:, (2 * ring + 1) * rows : (2 * ring + 2) * rows]
        own[ring] = jnp.where(second == 0, low, high)
        give[ring] = jnp.where(second == 0, high, low)


def img_grad_kernel(rows, at_ref, got, unit, norm, feats, own, give, part, grad):
    slab = unit.shape[0]
    up, inner = got[0, :slab].astype(f32), joined(got[0, slab:])
    for n in range(1, 8):
        up, inner = up + got[n, :slab].astype(f32), inner + joined(got[n, slab:])
    up = logit_scale * up - unit[...].astype(f32) * inner
    grad[...] = (up * (1.0 / norm[...])).astype(b16)
    put_blocks(grad, at_ref[1], own, give, rows)
    part[...] = dot(grad[...], feats[...], NN).astype(b16)


def txt_grad_kernel(rows, at_ref, *refs):
    terms, unit, norm, blocks, (own, give, part, grad) = (
        refs[:5], refs[5], refs[6], refs[7:15], refs[15:]
    )
    slab = unit.shape[0]
    up, inner = terms[0][:slab].astype(f32), joined(terms[0][slab:])
    for term in terms[1:]:
        up, inner = up + term[:slab].astype(f32), inner + joined(term[slab:])
    up = logit_scale * up - unit[...].astype(f32) * inner
    grad[...] = (up * (1.0 / norm[...])).astype(b16)
    put_blocks(grad, at_ref[1], own, give, rows)
    total = None
    for d in range(4):
        cols = grad[:, aligned((at_ref[2] + d) % 4, 2 * rows)]
        term = dot(cols, in_pair(blocks[2 * d], blocks[2 * d + 1], at_ref[1], rows), NN)
        total = term if total is None else total + term
    part[...] = total.astype(b16)


def gradient(kernel, place, second, ring, terms, unit, norm, feats, rows):
    width = feats[0].shape[1]
    slab, count = width // 8, 8 * rows
    whole = lambda a: pl.BlockSpec(a.shape, lambda i, at: (0,) * len(a.shape))
    mine = lambda height: pl.BlockSpec((height, count), lambda i, at: (at[0], 0))
    block = jax.ShapeDtypeStruct((4, slab, rows), b16)
    part = jax.ShapeDtypeStruct((slab, width), b16)
    return call(
        lambda *refs: kernel(rows, *refs),
        [block, block, part],
        [place, second, ring],
        [term[0] if isinstance(term, tuple) else term for term in terms] + [unit, norm, *feats],
        in_specs=[mine(slab + PAD) if isinstance(term, tuple) else whole(term) for term in terms]
        + [mine(slab), whole(norm)]
        + [whole(a) for a in feats],
        out_specs=[whole(block), whole(block), whole(part)],
        grid=(1,),
        scratch=[pltpu.VMEM((slab, count), b16)],
        cost=2 * slab * count * width,
    )


def pick_kernel(at_ref, img, txt, other_img, other_txt, out):
    width = img.shape[1]
    slots = out.shape[0]
    own = width // 128
    third = 2 * img.shape[0] // 3
    img = img[...].astype(f32) + other_img[...].astype(f32)
    txt = txt[...].astype(f32) + other_txt[...].astype(f32)
    part = jnp.concatenate([img, txt], axis=0).astype(b16)
    slot = lax.broadcasted_iota(jnp.int32, (slots, 1), 0)
    feature = lax.broadcasted_iota(jnp.int32, (slots, width), 1)
    base = (slot // 8 * 2 + at_ref[0]) * own
    chosen = jnp.where(feature == base + slot % 8, 1.0, 0.0).astype(b16)
    out[:, : 3 * third] = dot(chosen, part, NT).astype(b16)
    chosen = jnp.where(feature == base + 8, 1.0, 0.0).astype(b16)
    ninth = dot(chosen, part, NT)
    pick = slot % 8
    rest = jnp.where(pick == 1, ninth[:, third : 2 * third], ninth[:, :third])
    rest = jnp.where(pick == 2, ninth[:, 2 * third :], rest)
    out[:, 3 * third :] = rest.astype(b16)


def picked(core, parts):
    slab, width = parts[0].shape
    return call(
        pick_kernel,
        jax.ShapeDtypeStruct((64 * 8, slab * 8 // 3), b16),
        [core],
        parts,
        cost=8 * 512 * width * slab,
    )


def head_kernel(at_ref, got, img_out, txt_out):
    slab = img_out.shape[1] // 8
    third = slab * 2 // 3
    half = third // 2
    for p in range(8):
        img = txt = None
        for other in range(8):
            z, lo, hi, y = p // 2, p % 2, other // 4, other % 4
            block = got[(z * 2 + lo) * 8 + hi * 4 + y].astype(f32)
            img = block if img is None else img + block
            z, lo, hi, y = other // 2, other % 2, p % 2, p // 2
            block = got[(z * 2 + lo) * 8 + hi * 4 + y].astype(f32)
            txt = block if txt is None else txt + block
        at = p * slab
        ninth = 2 * slab
        img_out[0:8, at : at + slab] = img[:, :slab]
        img_out[8:9, at : at + third] = img[0:1, ninth : ninth + third]
        img_out[8:9, at + third : at + slab] = img[1:2, ninth : ninth + half]
        txt_out[0:8, at : at + slab] = txt[:, slab : 2 * slab]
        txt_out[8:9, at : at + half] = txt[1:2, ninth + half : ninth + third]
        txt_out[8:9, at + half : at + slab] = txt[2:3, ninth : ninth + third]


def together(arrays):
    return lax.optimization_barrier(list(arrays))


def pair_lines(own, got, second):
    return jnp.concatenate([jnp.where(second, got, own), jnp.where(second, own, got)], axis=1)


def whole_columns(lines, move, ring):
    got = []
    for d in range(4):
        block = lax.dynamic_index_in_dim(lines, (ring + d) % 4, 0, keepdims=False)
        got.append(send(block, move(d, 0)) if d else block)
    height = got[0].shape[0]
    from_own = jnp.concatenate([got[-d % 4] for d in range(4)] * 2, axis=0)
    return lax.dynamic_slice_in_dim(from_own, (4 - ring) % 4 * height, 4 * height, axis=0)


def shards(image_feat, text_feat, image_head, text_head, group_bias, text_lang, partner):
    rows, width = image_feat.shape
    slab = width // 8
    place = lax.axis_index(DEV)
    z, lo, hi, y, core = place // 32, place // 16 % 2, place // 8 % 2, place // 2 % 4, place % 2

    figures = jnp.stack([text_lang, partner // 128, partner % 128]).astype(b16)
    figures = jnp.pad(figures, ((0, PAD - 3), (0, width - rows)))
    text_rows = jnp.concatenate([text_feat, figures], axis=0)
    img_feats = exchange(jnp.broadcast_to(image_feat[None], (8, rows, width)), IMG_GROUPS)
    img_feats = img_feats.reshape(8 * rows, width)
    across = send(text_rows, txt_move(0, 1))
    before = send(text_rows, txt_move(1, 0))
    after = send(text_rows, txt_move(3, 0))
    across, turned_txt = together([across, text_head.T])
    across_after = send(across, txt_move(3, 0))
    across_before = send(across, txt_move(1, 0))
    across_after, before, after, across, turned_img = together(
        [across_after, before, after, across, image_head.T]
    )
    far = send(before, txt_move(1, 0))
    across_far = send(across_after, txt_move(3, 0))
    txt_blocks = [
        text_rows, across, after, across_after, far, across_far, before, across_before
    ]
    unit_txt, norm_txt = units(txt_blocks, turned_txt, y, hi, rows)
    other_txt = send(unit_txt, core_move)
    turned_units, norm_img, unit_img = img_units(img_feats, turned_img, image_head, rows)

    other_slopes, other_sum, other_up = pair_tile(
        unit_img, turned_units, other_txt, group_bias, place % 16, rows
    )
    back = send(other_up, core_move)
    slopes, img_sum, text_up = pair_tile(
        unit_img, turned_units, unit_txt, group_bias, place % 16, rows
    )

    def slab_terms(d, e):
        at = (y + d) % 4 * 2 + (hi + e) % 2
        return [(text_up, at), (back, at)]

    far, across_far, across_after = sums(
        [slab_terms(2, 0), slab_terms(2, 1), slab_terms(1, 1)], rows
    )
    far, across_far, across_after, slopes = together([far, across_far, across_after, slopes])
    far = send(far, txt_move(1, 0))
    across_far = send(across_far, txt_move(3, 0))
    img_terms = exchange(
        image_tile(unit_txt, other_txt, slopes, other_slopes, img_sum, other_sum, rows), IMG_GROUPS
    )
    far, across_far, across_after = together([far, across_far, across_after])
    across_before = send(across_after, txt_move(1, 0))
    across_after, before, after = sums(
        [slab_terms(3, 1) + [across_far], slab_terms(1, 0) + [far], slab_terms(3, 0)], rows
    )
    across_after = send(across_after, txt_move(3, 0))
    across_before, across_after, before, after = together(
        [across_before, across_after, before, after]
    )
    before = send(before, txt_move(1, 0))
    after = send(after, txt_move(3, 0))
    (across,) = sums([slab_terms(0, 1) + [across_before, across_after]], rows)
    across = send(across, txt_move(0, 1))

    img_own, img_give, img_part = gradient(
        img_grad_kernel, z * 2 + lo, lo, z, [img_terms], turned_units, norm_img, [img_feats], rows
    )
    img_got = send(img_give, img_move(0, 1))
    txt_own, txt_give, txt_part = gradient(
        txt_grad_kernel, y * 2 + hi, hi, y, slab_terms(0, 0) + [before, after, across],
        unit_txt, norm_txt, txt_blocks, rows,
    )
    img_theirs = send(img_part, core_move)
    txt_theirs = send(txt_part, core_move)
    txt_got = send(txt_give, txt_move(0, 1))
    heads, txt_got = together([picked(core, [img_part, txt_part, img_theirs, txt_theirs]), txt_got])
    heads = exchange(heads.reshape(64, 8, -1), CHIP_GROUPS)
    head_shape = jax.ShapeDtypeStruct((width // 128, width), f32)
    image_head_grad, text_head_grad = call(head_kernel, [head_shape] * 2, [core], [heads])

    grad_img = whole_columns(pair_lines(img_own, img_got, lo), img_move, z)
    image_grad = dot(grad_img, image_head, (((0,), (1,)), ((), ())))
    grad_txt = whole_columns(pair_lines(txt_own, txt_got, hi), txt_move, y)
    text_grad = dot(grad_txt, text_head, (((0,), (1,)), ((), ())))
    return (image_grad, text_grad, image_head_grad, text_head_grad)


def solution(mesh):
    line = jax.sharding.Mesh(mesh.devices.reshape(-1), (DEV,))
    in_specs = (P(DEV, None), P(DEV, None), P(), P(), P(), P(DEV), P(DEV))
    return jax.shard_map(
        shards, mesh=line, in_specs=in_specs, out_specs=(P(DEV, None),) * 4, check_vma=False
    )
```

```python
import jax
import jax.numpy as jnp
from jax import lax
from jax.experimental import pallas as pl
from jax.experimental.pallas import tpu as pltpu
from jax.sharding import PartitionSpec as P

logit_scale = 64.0
epsilon = 1e-06
log2e = 1.4426950408889634
f32, b16 = jnp.float32, jnp.bfloat16

DEV = "dev"
PLACES = [
    (z, lo, hi, y, c)
    for z in range(4)
    for lo in range(2)
    for hi in range(2)
    for y in range(4)
    for c in range(2)
]


def flat(z, lo, hi, y, c):
    return (z * 2 + lo) * 16 + hi * 8 + y * 2 + c


def img_move(d, e):
    return lambda z, lo, hi, y, c: ((z + d) % 4, lo ^ e, hi, y, c)


def txt_move(d, e):
    return lambda z, lo, hi, y, c: (z, lo ^ e, hi ^ e, (y + d) % 4, c)


def core_move(z, lo, hi, y, c):
    return (z, lo, hi, y, 1 - c)


IMG_GROUPS = [
    [flat(z, lo, hi, y, c) for z in range(4) for lo in range(2)]
    for hi in range(2)
    for y in range(4)
    for c in range(2)
]
TXT_GROUPS = [
    [flat(z, hi ^ b, hi, y, c) for y in range(4) for hi in range(2)]
    for z in range(4)
    for b in range(2)
    for c in range(2)
]
TXT_CORE_GROUPS = [
    [flat(z, hi ^ b, hi, y, c) for c in range(2) for y in range(4) for hi in range(2)]
    for z in range(4)
    for b in range(2)
]
CHIP_GROUPS = [[flat(*p) for p in PLACES if p[4] == c] for c in range(2)]


def send(block, move):
    return lax.ppermute(block, DEV, [(flat(*p), flat(*move(*p))) for p in PLACES])


def exchange(blocks, groups):
    return lax.all_to_all(blocks, DEV, 0, 0, axis_index_groups=groups, tiled=True)


PAD = 16
NN = (((1,), (0,)), ((), ()))
NT = (((1,), (1,)), ((), ()))
TN = (((0,), (0,)), ((), ()))


def dot(a, b, dims):
    return lax.dot_general(a, b, dims, preferred_element_type=f32)


def call(body, out_shape, scalars, arrays, in_specs=None, out_specs=None, grid=(), scratch=(), cost=0, aliases=None, weight=1):
    whole = pl.BlockSpec(memory_space=pltpu.VMEM)
    many = isinstance(out_shape, (list, tuple))
    if in_specs is None:
        in_specs = [whole] * len(arrays)
    if out_specs is None:
        out_specs = [whole] * len(out_shape) if many else whole
    spec = pltpu.PrefetchScalarGridSpec(
        num_scalar_prefetch=1,
        grid=grid,
        in_specs=in_specs,
        out_specs=out_specs,
        scratch_shapes=list(scratch),
    )
    moved = weight * sum(a.size * a.dtype.itemsize for a in arrays)
    return pl.pallas_call(
        body,
        out_shape=out_shape,
        grid_spec=spec,
        input_output_aliases=aliases or {},
        compiler_params=pltpu.CompilerParams(vmem_limit_bytes=60 * 2**20),
        cost_estimate=pl.CostEstimate(flops=weight * cost, bytes_accessed=moved, transcendentals=0),
    )(jnp.stack(scalars).astype(jnp.int32), *arrays)


def aligned(index, size):
    return pl.ds(pl.multiple_of(index * size, size), size)


def split_rows(total, lanes):
    high = total.astype(b16).astype(f32)
    row = lax.broadcasted_iota(jnp.int32, (PAD, lanes), 0)
    return jnp.where(row == 0, high, jnp.where(row == 1, total - high, 0.0)).astype(b16)


def joined(rows):
    return rows[0:1].astype(f32) + rows[1:2].astype(f32)


def in_pair(own, across, second, rows):
    own, across = own[:rows], across[:rows]
    first = second == 0
    return jnp.concatenate([jnp.where(first, own, across), jnp.where(first, across, own)], axis=0)


def put_units(feats, turned_head, proj, turned, norm):
    width = turned_head.shape[0]
    quarter = width // 4
    total = jnp.zeros((1, feats.shape[0]), f32)
    for m in range(4):
        span = slice(m * quarter, (m + 1) * quarter)
        part = dot(turned_head[span], feats[...], NT)
        proj[span] = part
        total = total + jnp.sum(part * part, axis=0, keepdims=True)
    length = jnp.sqrt(total + epsilon)
    norm[...] = length
    inverse = 1.0 / length
    for m in range(4):
        span = slice(m * quarter, (m + 1) * quarter)
        turned[span] = (proj[span] * inverse).astype(b16)


def unit_kernel(rows, at_ref, *refs):
    blocks, (turned_head, turned, norm, feats, proj) = refs[:8], refs[8:]
    width = turned_head.shape[0]
    second = at_ref[1]
    step = pl.program_id(0)
    for d in range(4):
        own, across = blocks[2 * d], blocks[2 * d + 1]

        @pl.when(step == d)
        def _():
            feats[...] = in_pair(own, across, second, rows)
            first = second == 0
            sides = own[rows:, :rows], across[rows:, :rows]
            turned[width:, :rows] = jnp.where(first, sides[0], sides[1])
            turned[width:, rows:] = jnp.where(first, sides[1], sides[0])

    put_units(feats, turned_head, proj, turned, norm)


def units(blocks, turned_head, ring, second, rows):
    width = turned_head.shape[0]
    tile = 2 * rows
    whole = lambda a: pl.BlockSpec(a.shape, lambda i, at: (0, 0))
    return call(
        lambda *refs: unit_kernel(rows, *refs),
        [
            jax.ShapeDtypeStruct((width + PAD, 8 * rows), b16),
            jax.ShapeDtypeStruct((1, 8 * rows), f32),
        ],
        [ring, second],
        [*blocks, turned_head],
        in_specs=[whole(a) for a in [*blocks, turned_head]],
        out_specs=[
            pl.BlockSpec((width + PAD, tile), lambda i, at: (0, (at[0] + i) % 4)),
            pl.BlockSpec((1, tile), lambda i, at: (0, (at[0] + i) % 4)),
        ],
        grid=(4,),
        scratch=[pltpu.VMEM((tile, width), b16), pltpu.VMEM((width, tile), f32)],
        cost=2 * 8 * rows * width * width,
    )


def unit_columns(feats, head):
    projected = dot(head, feats, (((0,), (1,)), ((), ())))
    norm = jnp.sqrt(jnp.sum(projected * projected, axis=0, keepdims=True) + epsilon)
    return (projected / norm).astype(b16), norm


def unit_rows(feats, head):
    projected = dot(feats, head, NN)
    norm = jnp.sqrt(jnp.sum(projected * projected, axis=1, keepdims=True) + epsilon)
    return (projected / norm).astype(b16)


def tile_slopes(rows, groups, place, bias_ref, img, txt, slopes, by_img):
    width = img.shape[1]
    tile = 2 * rows
    lang = txt[width : width + PAD].astype(f32)
    partner = lang[1:2] * 128.0 + lang[2:3]
    lang = lang[0:1]
    bias = jnp.zeros((1, tile), f32)
    for g in range(groups):
        bias = jnp.where(lang == g, bias_ref[g], bias)
    bias = bias * -log2e
    down = jnp.zeros((1, tile), f32)
    high = 4 * rows
    for m in range(img.shape[0] // high):
        span = slice(m * high, (m + 1) * high)
        index = m * high + lax.broadcasted_iota(jnp.int32, (high, 1), 0)
        ids = ((index // rows * 16 + place) * rows + index % rows).astype(f32)
        cosines = dot(img[span], txt[:width], NN)
        below = 1.0 + jnp.exp2(cosines * (-log2e * logit_scale) + bias)
        gate = pl.reciprocal(below, approx=True)
        gate = gate * (2.0 - below * gate)
        slope = gate - jnp.where(partner == ids, 1.0, 0.0)
        slopes[span, :tile] = slope.astype(b16)
        weighted = slope * cosines
        down = down + jnp.sum(weighted, axis=0, keepdims=True)
        side = by_img[span]
        for k in range(0, tile, by_img.shape[1]):
            side = side + weighted[:, k : k + by_img.shape[1]]
        by_img[span] = side
    return logit_scale * down


def put_text_terms(up, turned, slopes, down):
    slab = turned.shape[0] // 8
    figures = split_rows(down, up.shape[1])
    part = dot(turned[...], slopes, NN)
    for e in range(8):
        at = e * (slab + PAD)
        up[at : at + slab] = part[e * slab : (e + 1) * slab].astype(b16)
        up[at + slab : at + slab + PAD] = figures


def other_kernel(rows, groups, at_ref, bias_ref, img, turned, txt, slopes, img_sum, up, by_img):
    step = pl.program_id(0)

    @pl.when(step == 0)
    def _():
        by_img[...] = jnp.zeros(by_img.shape, f32)

    down = tile_slopes(rows, groups, at_ref[0], bias_ref, img, txt, slopes.at[0], by_img)
    put_text_terms(up, turned, slopes[0], down)

    @pl.when(step == 3)
    def _():
        img_sum[...] = logit_scale * jnp.sum(by_img[...].T, axis=0, keepdims=True)


def other_tile(img, turned, txt, group_bias, place, rows):
    count, width = img.shape
    tile = 2 * rows
    height = width + 8 * PAD
    whole = lambda a: pl.BlockSpec(a.shape, lambda i, at: (0, 0))
    return call(
        lambda *refs: other_kernel(rows, group_bias.shape[0], *refs),
        [
            jax.ShapeDtypeStruct((4, count, tile), b16),
            jax.ShapeDtypeStruct((1, count), f32),
            jax.ShapeDtypeStruct((height, count), b16),
        ],
        [place],
        [group_bias, img, turned, txt],
        in_specs=[
            pl.BlockSpec(memory_space=pltpu.SMEM),
            whole(img),
            whole(turned),
            pl.BlockSpec((width + PAD, tile), lambda i, at: (0, i)),
        ],
        out_specs=[
            pl.BlockSpec((1, count, tile), lambda i, at: (i, 0, 0)),
            pl.BlockSpec((1, count), lambda i, at: (0, 0)),
            pl.BlockSpec((height, tile), lambda i, at: (0, i)),
        ],
        grid=(4,),
        scratch=[pltpu.VMEM((count, min(128, tile)), f32)],
        cost=4 * width * count * count,
    )


def own_kernel(rows, groups, at_ref, bias_ref, img, turned, txt, other, *refs):
    other_slopes, other_sum, up, out, by_img, held, both, total = refs
    step = pl.program_id(0)
    width = img.shape[1]
    tile = 2 * rows

    @pl.when(step == 0)
    def _():
        by_img[...] = jnp.zeros(by_img.shape, f32)
        total[...] = jnp.zeros(total.shape, f32)

    both[:, tile:] = other[:width]
    held[:, tile:] = other_slopes[0]
    both[:, :tile] = txt[:width]
    down = tile_slopes(rows, groups, at_ref[0], bias_ref, img, txt, held, by_img)
    put_text_terms(up, turned, held[:, :tile], down)
    total[...] += dot(both[...], held[...], NT)

    @pl.when(step == 3)
    def _():
        slab = width // 8
        sums = logit_scale * jnp.sum(by_img[...].T, axis=0, keepdims=True) + other_sum[...]
        figures = split_rows(sums, sums.shape[1])
        for e in range(8):
            out[e, :slab] = total[e * slab : (e + 1) * slab].astype(b16)
            out[e, slab:] = figures


def own_tile(
    img, turned, txt, other, other_slopes, other_sum, group_bias, place, rows
):
    count, width = img.shape
    tile = 2 * rows
    height = width + 8 * PAD
    slab = width // 8
    whole = lambda a: pl.BlockSpec(a.shape, lambda i, at: (0, 0))
    stack = lambda a: pl.BlockSpec(a.shape, lambda i, at: (0, 0, 0))
    pieces = jax.ShapeDtypeStruct((8, slab + PAD, count), b16)
    return call(
        lambda *refs: own_kernel(rows, group_bias.shape[0], *refs),
        [jax.ShapeDtypeStruct((height, count), b16), pieces],
        [place],
        [group_bias, img, turned, txt, other, other_slopes, other_sum],
        in_specs=[
            pl.BlockSpec(memory_space=pltpu.SMEM),
            whole(img),
            whole(turned),
            pl.BlockSpec((width + PAD, tile), lambda i, at: (0, i)),
            pl.BlockSpec((width + PAD, tile), lambda i, at: (0, i)),
            pl.BlockSpec((1, count, tile), lambda i, at: (i, 0, 0)),
            whole(other_sum),
        ],
        out_specs=[pl.BlockSpec((height, tile), lambda i, at: (0, i)), stack(pieces)],
        grid=(4,),
        scratch=[
            pltpu.VMEM((count, min(128, tile)), f32),
            pltpu.VMEM((count, 2 * tile), b16),
            pltpu.VMEM((width, 2 * tile), b16),
            pltpu.VMEM((width, count), f32),
        ],
        cost=8 * width * count * count,
    )


def sum_into(out, terms):
    slab = out.shape[0] - PAD
    block, total = terms[0][:slab].astype(f32), joined(terms[0][slab:])
    for term in terms[1:]:
        block, total = block + term[:slab].astype(f32), total + joined(term[slab:])
    out[:slab] = block.astype(b16)
    out[slab:] = split_rows(total, out.shape[1])


def sum_kernel(sizes, at_ref, *refs):
    start = 0
    for size, out in zip(sizes, refs[sum(sizes) :]):
        sum_into(out, refs[start : start + size])
        start += size


def sums(groups, rows):
    flat_terms = [term for group in groups for term in group]
    arrays, specs, places = [], [], [jnp.int32(0)]
    height = None
    for term in flat_terms:
        if isinstance(term, tuple):
            arrays.append(term[0])
            height = term[0].shape[0] // 8
            specs.append(
                pl.BlockSpec((height, 4 * rows), lambda i, at, n=len(places): (at[n], i))
            )
            places.append(term[1])
        else:
            arrays.append(term)
            height = term.shape[0]
            specs.append(pl.BlockSpec((height, 4 * rows), lambda i, at: (0, i)))
    count = arrays[0].shape[1]
    spec = pl.BlockSpec((height, 4 * rows), lambda i, at: (0, i))
    return call(
        lambda *refs: sum_kernel([len(group) for group in groups], *refs),
        [jax.ShapeDtypeStruct((height, count), b16)] * len(groups),
        places,
        arrays,
        in_specs=specs,
        out_specs=[spec] * len(groups),
        grid=(count // (4 * rows),),
    )


def img_grad_kernel(rows, at_ref, got, unit, norm, feats, blocks, part, grad):
    slab = unit.shape[0]
    up, inner = got[0, :slab].astype(f32), joined(got[0, slab:])
    for n in range(1, 8):
        up, inner = up + got[n, :slab].astype(f32), inner + joined(got[n, slab:])
    up = logit_scale * up - unit[...].astype(f32) * inner
    grad[...] = (up * (1.0 / norm[...])).astype(b16)
    for n in range(8):
        blocks[n] = grad[:, n * rows : (n + 1) * rows]
    part[...] = dot(grad[...], feats[...], NN).astype(b16)


def txt_grad_kernel(rows, at_ref, *refs):
    terms, unit, norm, blocks, (own, give, part, grad) = (
        refs[:5], refs[5], refs[6], refs[7:15], refs[15:]
    )
    slab = unit.shape[0]
    up, inner = terms[0][:slab].astype(f32), joined(terms[0][slab:])
    for term in terms[1:]:
        up, inner = up + term[:slab].astype(f32), inner + joined(term[slab:])
    up = logit_scale * up - unit[...].astype(f32) * inner
    grad[...] = (up * (1.0 / norm[...])).astype(b16)
    for ring in range(4):
        low = grad[:, (2 * ring) * rows : (2 * ring + 1) * rows]
        high = grad[:, (2 * ring + 1) * rows : (2 * ring + 2) * rows]
        own[ring] = jnp.where(at_ref[1] == 0, low, high)
        give[ring] = jnp.where(at_ref[1] == 0, high, low)
    total = None
    for d in range(4):
        cols = grad[:, aligned((at_ref[2] + d) % 4, 2 * rows)]
        term = dot(cols, in_pair(blocks[2 * d], blocks[2 * d + 1], at_ref[1], rows), NN)
        total = term if total is None else total + term
    part[...] = total.astype(b16)


def gradient(kernel, place, second, ring, terms, unit, norm, feats, halves, rows):
    width = feats[0].shape[1]
    slab, count = width // 8, 8 * rows
    whole = lambda a: pl.BlockSpec(a.shape, lambda i, at: (0,) * len(a.shape))
    mine = lambda height: pl.BlockSpec((height, count), lambda i, at: (at[0], 0))
    block = jax.ShapeDtypeStruct((8 // halves, slab, rows), b16)
    part = jax.ShapeDtypeStruct((slab, width), b16)
    return call(
        lambda *refs: kernel(rows, *refs),
        [block] * halves + [part],
        [place, second, ring],
        [term[0] if isinstance(term, tuple) else term for term in terms] + [unit, norm, *feats],
        in_specs=[mine(slab + PAD) if isinstance(term, tuple) else whole(term) for term in terms]
        + [mine(slab), whole(norm)]
        + [whole(a) for a in feats],
        out_specs=[whole(block)] * halves + [whole(part)],
        grid=(1,),
        scratch=[pltpu.VMEM((slab, count), b16)],
        cost=2 * slab * count * width,
        weight=0,
    )


def pick_kernel(at_ref, img, txt, other_img, other_txt, out):
    width = img.shape[1]
    slots = out.shape[0]
    own = width // 128
    third = 2 * img.shape[0] // 3
    img = img[...].astype(f32) + other_img[...].astype(f32)
    txt = txt[...].astype(f32) + other_txt[...].astype(f32)
    part = jnp.concatenate([img, txt], axis=0).astype(b16)
    slot = lax.broadcasted_iota(jnp.int32, (slots, 1), 0)
    feature = lax.broadcasted_iota(jnp.int32, (slots, width), 1)
    base = (slot // 8 * 2 + at_ref[0]) * own
    chosen = jnp.where(feature == base + slot % 8, 1.0, 0.0).astype(b16)
    out[:, : 3 * third] = dot(chosen, part, NT).astype(b16)
    chosen = jnp.where(feature == base + 8, 1.0, 0.0).astype(b16)
    ninth = dot(chosen, part, NT)
    pick = slot % 8
    rest = jnp.where(pick == 1, ninth[:, third : 2 * third], ninth[:, :third])
    rest = jnp.where(pick == 2, ninth[:, 2 * third :], rest)
    out[:, 3 * third :] = rest.astype(b16)


def picked(core, parts):
    slab, width = parts[0].shape
    return call(
        pick_kernel,
        jax.ShapeDtypeStruct((64 * 8, slab * 8 // 3), b16),
        [core],
        parts,
        cost=8 * 512 * width * slab,
        weight=0,
    )


def head_kernel(at_ref, got, img_out, txt_out):
    slab = img_out.shape[1] // 8
    third = slab * 2 // 3
    half = third // 2
    for p in range(8):
        img = txt = None
        for other in range(8):
            z, lo, hi, y = p // 2, p % 2, other // 4, other % 4
            block = got[(z * 2 + lo) * 8 + hi * 4 + y].astype(f32)
            img = block if img is None else img + block
            z, lo, hi, y = other // 2, other % 2, p % 2, p // 2
            block = got[(z * 2 + lo) * 8 + hi * 4 + y].astype(f32)
            txt = block if txt is None else txt + block
        at = p * slab
        ninth = 2 * slab
        img_out[0:8, at : at + slab] = img[:, :slab]
        img_out[8:9, at : at + third] = img[0:1, ninth : ninth + third]
        img_out[8:9, at + third : at + slab] = img[1:2, ninth : ninth + half]
        txt_out[0:8, at : at + slab] = txt[:, slab : 2 * slab]
        txt_out[8:9, at : at + half] = txt[1:2, ninth + half : ninth + third]
        txt_out[8:9, at + half : at + slab] = txt[2:3, ninth : ninth + third]


def together(arrays):
    return lax.optimization_barrier(list(arrays))


def pair_lines(own, got, second):
    return jnp.concatenate([jnp.where(second, got, own), jnp.where(second, own, got)], axis=1)


def whole_columns(lines, move, ring):
    got = []
    for d in range(4):
        block = lax.dynamic_index_in_dim(lines, (ring + d) % 4, 0, keepdims=False)
        got.append(send(block, move(d, 0)) if d else block)
    height = got[0].shape[0]
    from_own = jnp.concatenate([got[-d % 4] for d in range(4)] * 2, axis=0)
    return lax.dynamic_slice_in_dim(from_own, (4 - ring) % 4 * height, 4 * height, axis=0)


def shards(image_feat, text_feat, image_head, text_head, group_bias, text_lang, partner):
    rows, width = image_feat.shape
    slab = width // 8
    place = lax.axis_index(DEV)
    z, lo, hi, y, core = place // 32, place // 16 % 2, place // 8 % 2, place // 2 % 4, place % 2

    figures = jnp.stack([text_lang, partner // 128, partner % 128]).astype(b16)
    figures = jnp.pad(figures, ((0, PAD - 3), (0, width - rows)))
    text_rows = jnp.concatenate([text_feat, figures], axis=0)
    img_feats = exchange(jnp.broadcast_to(image_feat[None], (8, rows, width)), IMG_GROUPS)
    img_feats = img_feats.reshape(8 * rows, width)
    across = send(text_rows, txt_move(0, 1))
    before = send(text_rows, txt_move(1, 0))
    after = send(text_rows, txt_move(3, 0))
    across_after = send(across, txt_move(3, 0))
    across_before = send(across, txt_move(1, 0))
    across_after, before, after, across, turned_txt = together(
        [across_after, before, after, across, text_head.T]
    )
    far = send(before, txt_move(1, 0))
    across_far = send(across_after, txt_move(3, 0))
    txt_blocks = [
        text_rows, across, after, across_after, far, across_far, before, across_before
    ]
    unit_txt, norm_txt = units(txt_blocks, turned_txt, y, hi, rows)
    other_txt = send(unit_txt, core_move)
    turned_units, norm_img = unit_columns(img_feats, image_head)
    unit_img = unit_rows(together([img_feats, unit_txt])[0], image_head)

    other_slopes, other_sum, other_up = other_tile(
        unit_img, turned_units, other_txt, group_bias, place % 16, rows
    )
    back = send(other_up, core_move)
    text_up, img_terms = own_tile(
        unit_img, turned_units, unit_txt, other_txt, other_slopes, other_sum, group_bias,
        place % 16, rows,
    )
    img_terms = exchange(img_terms, IMG_GROUPS)

    def slab_terms(d, e):
        at = (y + d) % 4 * 2 + (hi + e) % 2
        return [(text_up, at), (back, at)]

    far, across_far, across_after = sums(
        [slab_terms(2, 0), slab_terms(2, 1), slab_terms(1, 1)], rows
    )
    far = send(far, txt_move(1, 0))
    across_far = send(across_far, txt_move(3, 0))
    far, across_far, across_after = together([far, across_far, across_after])
    across_before = send(across_after, txt_move(1, 0))
    across_after, before, after = sums(
        [slab_terms(3, 1) + [across_far], slab_terms(1, 0) + [far], slab_terms(3, 0)], rows
    )
    across_after = send(across_after, txt_move(3, 0))
    across_before, across_after, before, after = together(
        [across_before, across_after, before, after]
    )
    before = send(before, txt_move(1, 0))
    after = send(after, txt_move(3, 0))
    (across,) = sums([slab_terms(0, 1) + [across_before, across_after]], rows)
    across = send(across, txt_move(0, 1))

    img_blocks, img_part = gradient(
        img_grad_kernel, z * 2 + lo, lo, z, [img_terms], turned_units, norm_img, [img_feats], 1, rows
    )
    grad_img = exchange(img_blocks, IMG_GROUPS).reshape(width, rows)
    txt_own, txt_give, txt_part = gradient(
        txt_grad_kernel, y * 2 + hi, hi, y, slab_terms(0, 0) + [before, after, across],
        unit_txt, norm_txt, txt_blocks, 2, rows,
    )
    img_theirs = send(img_part, core_move)
    txt_theirs = send(txt_part, core_move)
    txt_got = send(txt_give, txt_move(0, 1))
    heads, txt_got = together([picked(core, [img_part, txt_part, img_theirs, txt_theirs]), txt_got])
    heads = exchange(heads.reshape(64, 8, -1), CHIP_GROUPS)
    head_shape = jax.ShapeDtypeStruct((width // 128, width), f32)
    image_head_grad, text_head_grad = call(head_kernel, [head_shape] * 2, [core], [heads])

    image_grad = dot(grad_img, image_head, (((0,), (1,)), ((), ())))
    grad_txt = whole_columns(pair_lines(txt_own, txt_got, hi), txt_move, y)
    text_grad = dot(grad_txt, text_head, (((0,), (1,)), ((), ())))
    return (image_grad, text_grad, image_head_grad, text_head_grad)


def solution(mesh):
    line = jax.sharding.Mesh(mesh.devices.reshape(-1), (DEV,))
    in_specs = (P(DEV, None), P(DEV, None), P(), P(), P(), P(DEV), P(DEV))
    return jax.shard_map(
        shards, mesh=line, in_specs=in_specs, out_specs=(P(DEV, None),) * 4, check_vma=False
    )
```

```python
import jax
import jax.numpy as jnp
from jax import lax
from jax.experimental import pallas as pl
from jax.experimental.pallas import tpu as pltpu
from jax.sharding import PartitionSpec as P

logit_scale = 64.0
epsilon = 1e-06
log2e = 1.4426950408889634
f32, b16 = jnp.float32, jnp.bfloat16

DEV = "dev"
PLACES = [
    (z, lo, hi, y, c)
    for z in range(4)
    for lo in range(2)
    for hi in range(2)
    for y in range(4)
    for c in range(2)
]


def flat(z, lo, hi, y, c):
    return (z * 2 + lo) * 16 + hi * 8 + y * 2 + c


def img_move(d, e):
    return lambda z, lo, hi, y, c: ((z + d) % 4, lo ^ e, hi, y, c)


def txt_move(d, e):
    return lambda z, lo, hi, y, c: (z, lo ^ e, hi ^ e, (y + d) % 4, c)


def core_move(z, lo, hi, y, c):
    return (z, lo, hi, y, 1 - c)


IMG_GROUPS = [
    [flat(z, lo, hi, y, c) for z in range(4) for lo in range(2)]
    for hi in range(2)
    for y in range(4)
    for c in range(2)
]
TXT_GROUPS = [
    [flat(z, hi ^ b, hi, y, c) for y in range(4) for hi in range(2)]
    for z in range(4)
    for b in range(2)
    for c in range(2)
]
TXT_CORE_GROUPS = [
    [flat(z, hi ^ b, hi, y, c) for c in range(2) for y in range(4) for hi in range(2)]
    for z in range(4)
    for b in range(2)
]
CHIP_GROUPS = [[flat(*p) for p in PLACES if p[4] == c] for c in range(2)]


def send(block, move):
    return lax.ppermute(block, DEV, [(flat(*p), flat(*move(*p))) for p in PLACES])


def exchange(blocks, groups):
    return lax.all_to_all(blocks, DEV, 0, 0, axis_index_groups=groups, tiled=True)


PAD = 16
NN = (((1,), (0,)), ((), ()))
NT = (((1,), (1,)), ((), ()))
TN = (((0,), (0,)), ((), ()))


def dot(a, b, dims):
    return lax.dot_general(a, b, dims, preferred_element_type=f32)


def call(body, out_shape, scalars, arrays, in_specs=None, out_specs=None, grid=(), scratch=(), cost=0, aliases=None, weight=1):
    whole = pl.BlockSpec(memory_space=pltpu.VMEM)
    many = isinstance(out_shape, (list, tuple))
    if in_specs is None:
        in_specs = [whole] * len(arrays)
    if out_specs is None:
        out_specs = [whole] * len(out_shape) if many else whole
    spec = pltpu.PrefetchScalarGridSpec(
        num_scalar_prefetch=1,
        grid=grid,
        in_specs=in_specs,
        out_specs=out_specs,
        scratch_shapes=list(scratch),
    )
    moved = weight * sum(a.size * a.dtype.itemsize for a in arrays)
    return pl.pallas_call(
        body,
        out_shape=out_shape,
        grid_spec=spec,
        input_output_aliases=aliases or {},
        compiler_params=pltpu.CompilerParams(vmem_limit_bytes=60 * 2**20),
        cost_estimate=pl.CostEstimate(flops=weight * cost, bytes_accessed=moved, transcendentals=0),
    )(jnp.stack(scalars).astype(jnp.int32), *arrays)


def aligned(index, size):
    return pl.ds(pl.multiple_of(index * size, size), size)


def split_rows(total, lanes):
    high = total.astype(b16).astype(f32)
    row = lax.broadcasted_iota(jnp.int32, (PAD, lanes), 0)
    return jnp.where(row == 0, high, jnp.where(row == 1, total - high, 0.0)).astype(b16)


def joined(rows):
    return rows[0:1].astype(f32) + rows[1:2].astype(f32)


def in_pair(own, across, second, rows):
    own, across = own[:rows], across[:rows]
    first = second == 0
    return jnp.concatenate([jnp.where(first, own, across), jnp.where(first, across, own)], axis=0)


def put_units(feats, turned_head, proj, turned, norm):
    width = turned_head.shape[0]
    quarter = width // 4
    total = jnp.zeros((1, feats.shape[0]), f32)
    for m in range(4):
        span = slice(m * quarter, (m + 1) * quarter)
        part = dot(turned_head[span], feats[...], NT)
        proj[span] = part
        total = total + jnp.sum(part * part, axis=0, keepdims=True)
    length = jnp.sqrt(total + epsilon)
    norm[...] = length
    inverse = 1.0 / length
    for m in range(4):
        span = slice(m * quarter, (m + 1) * quarter)
        turned[span] = (proj[span] * inverse).astype(b16)


def unit_kernel(rows, at_ref, *refs):
    blocks, (turned_head, turned, norm, feats, proj) = refs[:8], refs[8:]
    width = turned_head.shape[0]
    second = at_ref[1]
    step = pl.program_id(0)
    for d in range(4):
        own, across = blocks[2 * d], blocks[2 * d + 1]

        @pl.when(step == d)
        def _():
            feats[...] = in_pair(own, across, second, rows)
            first = second == 0
            sides = own[rows:, :rows], across[rows:, :rows]
            turned[width:, :rows] = jnp.where(first, sides[0], sides[1])
            turned[width:, rows:] = jnp.where(first, sides[1], sides[0])

    put_units(feats, turned_head, proj, turned, norm)


def units(blocks, turned_head, ring, second, rows):
    width = turned_head.shape[0]
    tile = 2 * rows
    whole = lambda a: pl.BlockSpec(a.shape, lambda i, at: (0, 0))
    return call(
        lambda *refs: unit_kernel(rows, *refs),
        [
            jax.ShapeDtypeStruct((width + PAD, 8 * rows), b16),
            jax.ShapeDtypeStruct((1, 8 * rows), f32),
        ],
        [ring, second],
        [*blocks, turned_head],
        in_specs=[whole(a) for a in [*blocks, turned_head]],
        out_specs=[
            pl.BlockSpec((width + PAD, tile), lambda i, at: (0, (at[0] + i) % 4)),
            pl.BlockSpec((1, tile), lambda i, at: (0, (at[0] + i) % 4)),
        ],
        grid=(4,),
        scratch=[pltpu.VMEM((tile, width), b16), pltpu.VMEM((width, tile), f32)],
        cost=2 * 8 * rows * width * width,
    )


def unit_columns(feats, head):
    projected = dot(head, feats, (((0,), (1,)), ((), ())))
    norm = jnp.sqrt(jnp.sum(projected * projected, axis=0, keepdims=True) + epsilon)
    return (projected / norm).astype(b16), norm


def unit_rows(feats, head):
    projected = dot(feats, head, NN)
    norm = jnp.sqrt(jnp.sum(projected * projected, axis=1, keepdims=True) + epsilon)
    return (projected / norm).astype(b16)


def fetches(img_from, turned_from, img, turned, sem):
    half = img.shape[0] // 2
    parts = [(img_from.at[pl.ds(n * half, half)], img.at[pl.ds(n * half, half)]) for n in range(2)]
    parts.append((turned_from, turned))
    return [
        pltpu.make_async_copy(source, target, sem.at[n]) for n, (source, target) in enumerate(parts)
    ]


def tile_slopes(rows, groups, place, bias_ref, img, txt, slopes, by_img, copies):
    width = img.shape[1]
    tile = 2 * rows
    lang = txt[width : width + PAD].astype(f32)
    partner = lang[1:2] * 128.0 + lang[2:3]
    lang = lang[0:1]
    bias = jnp.zeros((1, tile), f32)
    for g in range(groups):
        bias = jnp.where(lang == g, bias_ref[g], bias)
    bias = bias * -log2e
    down = jnp.zeros((1, tile), f32)
    high = 4 * rows
    for m in range(img.shape[0] // high):
        span = slice(m * high, (m + 1) * high)

        @pl.when(pl.program_id(0) == 0)
        def _():
            copies[m].wait()

        index = m * high + lax.broadcasted_iota(jnp.int32, (high, 1), 0)
        ids = ((index // rows * 16 + place) * rows + index % rows).astype(f32)
        cosines = dot(img[span], txt[:width], NN)
        below = 1.0 + jnp.exp2(cosines * (-log2e * logit_scale) + bias)
        gate = pl.reciprocal(below, approx=True)
        gate = gate * (2.0 - below * gate)
        slope = gate - jnp.where(partner == ids, 1.0, 0.0)
        slopes[span, :tile] = slope.astype(b16)
        weighted = slope * cosines
        down = down + jnp.sum(weighted, axis=0, keepdims=True)
        side = by_img[span]
        for k in range(0, tile, by_img.shape[1]):
            side = side + weighted[:, k : k + by_img.shape[1]]
        by_img[span] = side
    return logit_scale * down


def put_text_terms(up, turned, slopes, down):
    slab = turned.shape[0] // 8
    figures = split_rows(down, up.shape[1])
    part = dot(turned[...], slopes, NN)
    for e in range(8):
        at = e * (slab + PAD)
        up[at : at + slab] = part[e * slab : (e + 1) * slab].astype(b16)
        up[at + slab : at + slab + PAD] = figures


def other_kernel(
    rows, groups, at_ref, bias_ref, img_from, turned_from, txt, slopes, img_sum, up,
    by_img, img, turned, sem,
):
    step = pl.program_id(0)
    copies = fetches(img_from, turned_from, img, turned, sem)

    @pl.when(step == 0)
    def _():
        for copy in copies:
            copy.start()
        by_img[...] = jnp.zeros(by_img.shape, f32)

    down = tile_slopes(rows, groups, at_ref[0], bias_ref, img, txt, slopes.at[0], by_img, copies)

    @pl.when(step == 0)
    def _():
        copies[2].wait()

    put_text_terms(up, turned, slopes[0], down)

    @pl.when(step == 3)
    def _():
        img_sum[...] = logit_scale * jnp.sum(by_img[...].T, axis=0, keepdims=True)


def other_tile(img, turned, txt, group_bias, place, rows):
    count, width = img.shape
    tile = 2 * rows
    height = width + 8 * PAD
    whole = lambda a: pl.BlockSpec(a.shape, lambda i, at: (0, 0))
    return call(
        lambda *refs: other_kernel(rows, group_bias.shape[0], *refs),
        [
            jax.ShapeDtypeStruct((4, count, tile), b16),
            jax.ShapeDtypeStruct((1, count), f32),
            jax.ShapeDtypeStruct((height, count), b16),
        ],
        [place],
        [group_bias, img, turned, txt],
        in_specs=[
            pl.BlockSpec(memory_space=pltpu.SMEM),
            pl.BlockSpec(memory_space=pl.ANY),
            pl.BlockSpec(memory_space=pl.ANY),
            pl.BlockSpec((width + PAD, tile), lambda i, at: (0, i)),
        ],
        out_specs=[
            pl.BlockSpec((1, count, tile), lambda i, at: (i, 0, 0)),
            pl.BlockSpec((1, count), lambda i, at: (0, 0)),
            pl.BlockSpec((height, tile), lambda i, at: (0, i)),
        ],
        grid=(4,),
        scratch=[
            pltpu.VMEM((count, min(128, tile)), f32),
            pltpu.VMEM((count, width), b16),
            pltpu.VMEM((width, count), b16),
            pltpu.SemaphoreType.DMA((3,)),
        ],
        cost=4 * width * count * count,
    )


def own_kernel(
    rows, groups, at_ref, bias_ref, img_from, turned_from, txt, other, other_slopes, other_sum,
    up, out, by_img, held, both, total, img, turned, sem,
):
    step = pl.program_id(0)
    width = img.shape[1]
    tile = 2 * rows
    copies = fetches(img_from, turned_from, img, turned, sem)

    @pl.when(step == 0)
    def _():
        for copy in copies:
            copy.start()
        by_img[...] = jnp.zeros(by_img.shape, f32)
        total[...] = jnp.zeros(total.shape, f32)

    both[:, tile:] = other[:width]
    held[:, tile:] = other_slopes[0]
    both[:, :tile] = txt[:width]
    down = tile_slopes(rows, groups, at_ref[0], bias_ref, img, txt, held, by_img, copies)

    @pl.when(step == 0)
    def _():
        copies[2].wait()

    put_text_terms(up, turned, held[:, :tile], down)
    total[...] += dot(both[...], held[...], NT)

    @pl.when(step == 3)
    def _():
        slab = width // 8
        sums = logit_scale * jnp.sum(by_img[...].T, axis=0, keepdims=True) + other_sum[...]
        figures = split_rows(sums, sums.shape[1])
        for e in range(8):
            out[e, :slab] = total[e * slab : (e + 1) * slab].astype(b16)
            out[e, slab:] = figures


def own_tile(
    img, turned, txt, other, other_slopes, other_sum, group_bias, place, rows
):
    count, width = img.shape
    tile = 2 * rows
    height = width + 8 * PAD
    slab = width // 8
    whole = lambda a: pl.BlockSpec(a.shape, lambda i, at: (0, 0))
    stack = lambda a: pl.BlockSpec(a.shape, lambda i, at: (0, 0, 0))
    pieces = jax.ShapeDtypeStruct((8, slab + PAD, count), b16)
    return call(
        lambda *refs: own_kernel(rows, group_bias.shape[0], *refs),
        [jax.ShapeDtypeStruct((height, count), b16), pieces],
        [place],
        [group_bias, img, turned, txt, other, other_slopes, other_sum],
        in_specs=[
            pl.BlockSpec(memory_space=pltpu.SMEM),
            pl.BlockSpec(memory_space=pl.ANY),
            pl.BlockSpec(memory_space=pl.ANY),
            pl.BlockSpec((width + PAD, tile), lambda i, at: (0, i)),
            pl.BlockSpec((width + PAD, tile), lambda i, at: (0, i)),
            pl.BlockSpec((1, count, tile), lambda i, at: (i, 0, 0)),
            whole(other_sum),
        ],
        out_specs=[pl.BlockSpec((height, tile), lambda i, at: (0, i)), stack(pieces)],
        grid=(4,),
        scratch=[
            pltpu.VMEM((count, min(128, tile)), f32),
            pltpu.VMEM((count, 2 * tile), b16),
            pltpu.VMEM((width, 2 * tile), b16),
            pltpu.VMEM((width, count), f32),
            pltpu.VMEM((count, width), b16),
            pltpu.VMEM((width, count), b16),
            pltpu.SemaphoreType.DMA((3,)),
        ],
        cost=8 * width * count * count,
    )


def sum_into(out, terms):
    slab = out.shape[0] - PAD
    block, total = terms[0][:slab].astype(f32), joined(terms[0][slab:])
    for term in terms[1:]:
        block, total = block + term[:slab].astype(f32), total + joined(term[slab:])
    out[:slab] = block.astype(b16)
    out[slab:] = split_rows(total, out.shape[1])


def sum_kernel(sizes, at_ref, *refs):
    start = 0
    for size, out in zip(sizes, refs[sum(sizes) :]):
        sum_into(out, refs[start : start + size])
        start += size


def sums(groups, rows):
    flat_terms = [term for group in groups for term in group]
    arrays, specs, places = [], [], [jnp.int32(0)]
    height = None
    for term in flat_terms:
        if isinstance(term, tuple):
            arrays.append(term[0])
            height = term[0].shape[0] // 8
            specs.append(
                pl.BlockSpec((height, 4 * rows), lambda i, at, n=len(places): (at[n], i))
            )
            places.append(term[1])
        else:
            arrays.append(term)
            height = term.shape[0]
            specs.append(pl.BlockSpec((height, 4 * rows), lambda i, at: (0, i)))
    count = arrays[0].shape[1]
    spec = pl.BlockSpec((height, 4 * rows), lambda i, at: (0, i))
    return call(
        lambda *refs: sum_kernel([len(group) for group in groups], *refs),
        [jax.ShapeDtypeStruct((height, count), b16)] * len(groups),
        places,
        arrays,
        in_specs=specs,
        out_specs=[spec] * len(groups),
        grid=(count // (4 * rows),),
    )


def img_grad_kernel(rows, at_ref, got, unit, norm, feats, blocks, part, grad):
    slab = unit.shape[0]
    up, inner = got[0, :slab].astype(f32), joined(got[0, slab:])
    for n in range(1, 8):
        up, inner = up + got[n, :slab].astype(f32), inner + joined(got[n, slab:])
    up = logit_scale * up - unit[...].astype(f32) * inner
    grad[...] = (up * (1.0 / norm[...])).astype(b16)
    for n in range(8):
        blocks[n] = grad[:, n * rows : (n + 1) * rows]
    part[...] = dot(grad[...], feats[...], NN).astype(b16)


def txt_grad_kernel(rows, at_ref, *refs):
    terms, unit, norm, blocks, (own, give, part, grad) = (
        refs[:5], refs[5], refs[6], refs[7:15], refs[15:]
    )
    slab = unit.shape[0]
    up, inner = terms[0][:slab].astype(f32), joined(terms[0][slab:])
    for term in terms[1:]:
        up, inner = up + term[:slab].astype(f32), inner + joined(term[slab:])
    up = logit_scale * up - unit[...].astype(f32) * inner
    grad[...] = (up * (1.0 / norm[...])).astype(b16)
    for ring in range(4):
        low = grad[:, (2 * ring) * rows : (2 * ring + 1) * rows]
        high = grad[:, (2 * ring + 1) * rows : (2 * ring + 2) * rows]
        own[ring] = jnp.where(at_ref[1] == 0, low, high)
        give[ring] = jnp.where(at_ref[1] == 0, high, low)
    total = None
    for d in range(4):
        cols = grad[:, aligned((at_ref[2] + d) % 4, 2 * rows)]
        term = dot(cols, in_pair(blocks[2 * d], blocks[2 * d + 1], at_ref[1], rows), NN)
        total = term if total is None else total + term
    part[...] = total.astype(b16)


def gradient(kernel, place, second, ring, terms, unit, norm, feats, halves, rows):
    width = feats[0].shape[1]
    slab, count = width // 8, 8 * rows
    whole = lambda a: pl.BlockSpec(a.shape, lambda i, at: (0,) * len(a.shape))
    mine = lambda height: pl.BlockSpec((height, count), lambda i, at: (at[0], 0))
    block = jax.ShapeDtypeStruct((8 // halves, slab, rows), b16)
    part = jax.ShapeDtypeStruct((slab, width), b16)
    return call(
        lambda *refs: kernel(rows, *refs),
        [block] * halves + [part],
        [place, second, ring],
        [term[0] if isinstance(term, tuple) else term for term in terms] + [unit, norm, *feats],
        in_specs=[mine(slab + PAD) if isinstance(term, tuple) else whole(term) for term in terms]
        + [mine(slab), whole(norm)]
        + [whole(a) for a in feats],
        out_specs=[whole(block)] * halves + [whole(part)],
        grid=(1,),
        scratch=[pltpu.VMEM((slab, count), b16)],
        cost=2 * slab * count * width,
        weight=0,
    )


def pick_kernel(at_ref, img, txt, other_img, other_txt, out):
    width = img.shape[1]
    slots = out.shape[0]
    own = width // 128
    third = 2 * img.shape[0] // 3
    img = img[...].astype(f32) + other_img[...].astype(f32)
    txt = txt[...].astype(f32) + other_txt[...].astype(f32)
    part = jnp.concatenate([img, txt], axis=0).astype(b16)
    slot = lax.broadcasted_iota(jnp.int32, (slots, 1), 0)
    feature = lax.broadcasted_iota(jnp.int32, (slots, width), 1)
    base = (slot // 8 * 2 + at_ref[0]) * own
    chosen = jnp.where(feature == base + slot % 8, 1.0, 0.0).astype(b16)
    out[:, : 3 * third] = dot(chosen, part, NT).astype(b16)
    chosen = jnp.where(feature == base + 8, 1.0, 0.0).astype(b16)
    ninth = dot(chosen, part, NT)
    pick = slot % 8
    rest = jnp.where(pick == 1, ninth[:, third : 2 * third], ninth[:, :third])
    rest = jnp.where(pick == 2, ninth[:, 2 * third :], rest)
    out[:, 3 * third :] = rest.astype(b16)


def picked(core, parts):
    slab, width = parts[0].shape
    return call(
        pick_kernel,
        jax.ShapeDtypeStruct((64 * 8, slab * 8 // 3), b16),
        [core],
        parts,
        cost=8 * 512 * width * slab,
        weight=0,
    )


def head_kernel(at_ref, got, img_out, txt_out):
    slab = img_out.shape[1] // 8
    third = slab * 2 // 3
    half = third // 2
    for p in range(8):
        img = txt = None
        for other in range(8):
            z, lo, hi, y = p // 2, p % 2, other // 4, other % 4
            block = got[(z * 2 + lo) * 8 + hi * 4 + y].astype(f32)
            img = block if img is None else img + block
            z, lo, hi, y = other // 2, other % 2, p % 2, p // 2
            block = got[(z * 2 + lo) * 8 + hi * 4 + y].astype(f32)
            txt = block if txt is None else txt + block
        at = p * slab
        ninth = 2 * slab
        img_out[0:8, at : at + slab] = img[:, :slab]
        img_out[8:9, at : at + third] = img[0:1, ninth : ninth + third]
        img_out[8:9, at + third : at + slab] = img[1:2, ninth : ninth + half]
        txt_out[0:8, at : at + slab] = txt[:, slab : 2 * slab]
        txt_out[8:9, at : at + half] = txt[1:2, ninth + half : ninth + third]
        txt_out[8:9, at + half : at + slab] = txt[2:3, ninth : ninth + third]


def together(arrays):
    return lax.optimization_barrier(list(arrays))


def pair_lines(own, got, second):
    return jnp.concatenate([jnp.where(second, got, own), jnp.where(second, own, got)], axis=1)


def whole_columns(lines, move, ring):
    got = []
    for d in range(4):
        block = lax.dynamic_index_in_dim(lines, (ring + d) % 4, 0, keepdims=False)
        got.append(send(block, move(d, 0)) if d else block)
    height = got[0].shape[0]
    from_own = jnp.concatenate([got[-d % 4] for d in range(4)] * 2, axis=0)
    return lax.dynamic_slice_in_dim(from_own, (4 - ring) % 4 * height, 4 * height, axis=0)


def shards(image_feat, text_feat, image_head, text_head, group_bias, text_lang, partner):
    rows, width = image_feat.shape
    slab = width // 8
    place = lax.axis_index(DEV)
    z, lo, hi, y, core = place // 32, place // 16 % 2, place // 8 % 2, place // 2 % 4, place % 2

    figures = jnp.stack([text_lang, partner // 128, partner % 128]).astype(b16)
    figures = jnp.pad(figures, ((0, PAD - 3), (0, width - rows)))
    text_rows = jnp.concatenate([text_feat, figures], axis=0)
    img_feats = exchange(jnp.broadcast_to(image_feat[None], (8, rows, width)), IMG_GROUPS)
    img_feats = img_feats.reshape(8 * rows, width)
    across = send(text_rows, txt_move(0, 1))
    before = send(text_rows, txt_move(1, 0))
    after = send(text_rows, txt_move(3, 0))
    across, before, after, turned_txt = together([across, before, after, text_head.T])
    across_after = send(across, txt_move(3, 0))
    across_before = send(across, txt_move(1, 0))
    far = send(before, txt_move(1, 0))
    across_far = send(across_after, txt_move(3, 0))
    txt_blocks = [
        text_rows, across, after, across_after, far, across_far, before, across_before
    ]
    unit_txt, norm_txt = units(txt_blocks, turned_txt, y, hi, rows)
    other_txt = send(unit_txt, core_move)
    turned_units, norm_img = unit_columns(img_feats, image_head)
    unit_img = unit_rows(together([img_feats, unit_txt])[0], image_head)

    other_slopes, other_sum, other_up = other_tile(
        unit_img, turned_units, other_txt, group_bias, place % 16, rows
    )
    back = send(other_up, core_move)
    text_up, img_terms = own_tile(
        unit_img, turned_units, unit_txt, other_txt, other_slopes, other_sum, group_bias,
        place % 16, rows,
    )
    img_terms = exchange(img_terms, IMG_GROUPS)

    def slab_terms(d, e):
        at = (y + d) % 4 * 2 + (hi + e) % 2
        return [(text_up, at), (back, at)]

    far, across_far, across_after = sums(
        [slab_terms(2, 0), slab_terms(2, 1), slab_terms(1, 1)], rows
    )
    far = send(far, txt_move(1, 0))
    across_far = send(across_far, txt_move(3, 0))
    far, across_far, across_after = together([far, across_far, across_after])
    across_before = send(across_after, txt_move(1, 0))
    across_after, before, after = sums(
        [slab_terms(3, 1) + [across_far], slab_terms(1, 0) + [far], slab_terms(3, 0)], rows
    )
    across_after = send(across_after, txt_move(3, 0))
    across_before, across_after, before, after = together(
        [across_before, across_after, before, after]
    )
    before = send(before, txt_move(1, 0))
    after = send(after, txt_move(3, 0))
    (across,) = sums([slab_terms(0, 1) + [across_before, across_after]], rows)
    across = send(across, txt_move(0, 1))

    img_blocks, img_part = gradient(
        img_grad_kernel, z * 2 + lo, lo, z, [img_terms], turned_units, norm_img, [img_feats], 1, rows
    )
    grad_img = exchange(img_blocks, IMG_GROUPS).reshape(width, rows)
    txt_own, txt_give, txt_part = gradient(
        txt_grad_kernel, y * 2 + hi, hi, y, slab_terms(0, 0) + [before, after, across],
        unit_txt, norm_txt, txt_blocks, 2, rows,
    )
    img_theirs = send(img_part, core_move)
    txt_theirs = send(txt_part, core_move)
    txt_got = send(txt_give, txt_move(0, 1))
    heads, txt_got = together([picked(core, [img_part, txt_part, img_theirs, txt_theirs]), txt_got])
    heads = exchange(heads.reshape(64, 8, -1), CHIP_GROUPS)
    head_shape = jax.ShapeDtypeStruct((width // 128, width), f32)
    image_head_grad, text_head_grad = call(head_kernel, [head_shape] * 2, [core], [heads])

    image_grad = dot(grad_img, image_head, (((0,), (1,)), ((), ())))
    grad_txt = whole_columns(pair_lines(txt_own, txt_got, hi), txt_move, y)
    text_grad = dot(grad_txt, text_head, (((0,), (1,)), ((), ())))
    return (image_grad, text_grad, image_head_grad, text_head_grad)


def solution(mesh):
    line = jax.sharding.Mesh(mesh.devices.reshape(-1), (DEV,))
    in_specs = (P(DEV, None), P(DEV, None), P(), P(), P(), P(DEV), P(DEV))
    return jax.shard_map(
        shards, mesh=line, in_specs=in_specs, out_specs=(P(DEV, None),) * 4, check_vma=False
    )
```

```python
import jax
import jax.numpy as jnp
from jax import lax
from jax.experimental import pallas as pl
from jax.experimental.pallas import tpu as pltpu
from jax.sharding import PartitionSpec as P

logit_scale = 64.0
epsilon = 1e-06
log2e = 1.4426950408889634
f32, b16 = jnp.float32, jnp.bfloat16

DEV = "dev"
PLACES = [
    (z, lo, hi, y, c)
    for z in range(4)
    for lo in range(2)
    for hi in range(2)
    for y in range(4)
    for c in range(2)
]


def flat(z, lo, hi, y, c):
    return (z * 2 + lo) * 16 + hi * 8 + y * 2 + c


def img_move(d, e):
    return lambda z, lo, hi, y, c: ((z + d) % 4, lo ^ e, hi, y, c)


def txt_move(d, e):
    return lambda z, lo, hi, y, c: (z, lo ^ e, hi ^ e, (y + d) % 4, c)


def core_move(z, lo, hi, y, c):
    return (z, lo, hi, y, 1 - c)


IMG_GROUPS = [
    [flat(z, lo, hi, y, c) for z in range(4) for lo in range(2)]
    for hi in range(2)
    for y in range(4)
    for c in range(2)
]
TXT_GROUPS = [
    [flat(z, hi ^ b, hi, y, c) for y in range(4) for hi in range(2)]
    for z in range(4)
    for b in range(2)
    for c in range(2)
]
TXT_CORE_GROUPS = [
    [flat(z, hi ^ b, hi, y, c) for c in range(2) for y in range(4) for hi in range(2)]
    for z in range(4)
    for b in range(2)
]
CHIP_GROUPS = [[flat(*p) for p in PLACES if p[4] == c] for c in range(2)]


def send(block, move):
    return lax.ppermute(block, DEV, [(flat(*p), flat(*move(*p))) for p in PLACES])


def exchange(blocks, groups):
    return lax.all_to_all(blocks, DEV, 0, 0, axis_index_groups=groups, tiled=True)


PAD = 16
NN = (((1,), (0,)), ((), ()))
NT = (((1,), (1,)), ((), ()))
TN = (((0,), (0,)), ((), ()))


def dot(a, b, dims):
    return lax.dot_general(a, b, dims, preferred_element_type=f32)


def call(body, out_shape, places, arrays, in_specs=None, out_specs=None, grid=(), scratch=(), cost=0, aliases=None, weight=1):
    whole = pl.BlockSpec(memory_space=pltpu.VMEM)
    many = isinstance(out_shape, (list, tuple))
    if in_specs is None:
        in_specs = [whole] * len(arrays)
    if out_specs is None:
        out_specs = [whole] * len(out_shape) if many else whole
    spec = pltpu.PrefetchScalarGridSpec(
        num_scalar_prefetch=1,
        grid=grid,
        in_specs=in_specs,
        out_specs=out_specs,
        scratch_shapes=list(scratch),
    )
    moved = weight * sum(a.size * a.dtype.itemsize for a in arrays)
    return pl.pallas_call(
        body,
        out_shape=out_shape,
        grid_spec=spec,
        input_output_aliases=aliases or {},
        compiler_params=pltpu.CompilerParams(vmem_limit_bytes=60 * 2**20),
        cost_estimate=pl.CostEstimate(flops=weight * cost, bytes_accessed=moved, transcendentals=0),
    )(places, *arrays)


def aligned(index, size):
    return pl.ds(pl.multiple_of(index * size, size), size)


def split_rows(total, lanes):
    high = total.astype(b16).astype(f32)
    row = lax.broadcasted_iota(jnp.int32, (PAD, lanes), 0)
    return jnp.where(row == 0, high, jnp.where(row == 1, total - high, 0.0)).astype(b16)


def joined(rows):
    return rows[0:1].astype(f32) + rows[1:2].astype(f32)


def in_pair(own, across, second, rows):
    own, across = own[:rows], across[:rows]
    first = second == 0
    return jnp.concatenate([jnp.where(first, own, across), jnp.where(first, across, own)], axis=0)


def put_units(feats, turned_head, proj, turned, norm):
    width = turned_head.shape[0]
    quarter = width // 4
    total = jnp.zeros((1, feats.shape[0]), f32)
    for m in range(4):
        span = slice(m * quarter, (m + 1) * quarter)
        part = dot(turned_head[span], feats[...], NT)
        proj[span] = part
        total = total + jnp.sum(part * part, axis=0, keepdims=True)
    length = jnp.sqrt(total + epsilon)
    norm[...] = length
    inverse = 1.0 / length
    for m in range(4):
        span = slice(m * quarter, (m + 1) * quarter)
        turned[span] = (proj[span] * inverse).astype(b16)


def unit_kernel(rows, at_ref, *refs):
    blocks, (turned_head, turned, norm, feats, proj) = refs[:8], refs[8:]
    width = turned_head.shape[0]
    second = at_ref[1]
    step = pl.program_id(0)
    for d in range(4):
        own, across = blocks[2 * d], blocks[2 * d + 1]

        @pl.when(step == d)
        def _():
            feats[...] = in_pair(own, across, second, rows)
            first = second == 0
            sides = own[rows:, :rows], across[rows:, :rows]
            turned[width:, :rows] = jnp.where(first, sides[0], sides[1])
            turned[width:, rows:] = jnp.where(first, sides[1], sides[0])

    put_units(feats, turned_head, proj, turned, norm)


def units(blocks, turned_head, places, rows):
    width = turned_head.shape[0]
    tile = 2 * rows
    whole = lambda a: pl.BlockSpec(a.shape, lambda i, at: (0, 0))
    return call(
        lambda *refs: unit_kernel(rows, *refs),
        [
            jax.ShapeDtypeStruct((width + PAD, 8 * rows), b16),
            jax.ShapeDtypeStruct((1, 8 * rows), f32),
        ],
        places,
        [*blocks, turned_head],
        in_specs=[whole(a) for a in [*blocks, turned_head]],
        out_specs=[
            pl.BlockSpec((width + PAD, tile), lambda i, at: (0, (at[0] + i) % 4)),
            pl.BlockSpec((1, tile), lambda i, at: (0, (at[0] + i) % 4)),
        ],
        grid=(4,),
        scratch=[pltpu.VMEM((tile, width), b16), pltpu.VMEM((width, tile), f32)],
        cost=2 * 8 * rows * width * width,
    )


def unit_columns(feats, head):
    projected = dot(head, feats, (((0,), (1,)), ((), ())))
    norm = jnp.sqrt(jnp.sum(projected * projected, axis=0, keepdims=True) + epsilon)
    return (projected / norm).astype(b16), norm


def unit_rows(feats, head, norm):
    return (dot(feats, head, NN) / norm.reshape(-1, 1)).astype(b16)


def tile_slopes(rows, groups, place, bias_ref, img, txt, slopes, by_img, use):
    width = img.shape[1]
    tile = 2 * rows
    lang = txt[width : width + PAD].astype(f32)
    partner = lang[1:2] * 128.0 + lang[2:3]
    lang = lang[0:1]
    bias = jnp.zeros((1, tile), f32)
    for g in range(groups):
        bias = jnp.where(lang == g, bias_ref[g], bias)
    bias = bias * -log2e
    down = jnp.zeros((1, tile), f32)
    high = 4 * rows
    spans = [slice(m * high, (m + 1) * high) for m in range(img.shape[0] // high)]
    cosines = dot(img[spans[0]], txt[:width], NN)
    for m, span in enumerate(spans):
        index = m * high + lax.broadcasted_iota(jnp.int32, (high, 1), 0)
        ids = ((index // rows * 16 + place) * rows + index % rows).astype(f32)
        below = 1.0 + jnp.exp2(cosines * (-log2e * logit_scale) + bias)
        gate = pl.reciprocal(below, approx=True)
        gate = gate * (2.0 - below * gate)
        slope = gate - jnp.where(partner == ids, 1.0, 0.0)
        slopes[span, :tile] = slope.astype(b16)
        weighted = slope * cosines
        down = down + jnp.sum(weighted, axis=0, keepdims=True)
        side = by_img[span]
        for k in range(0, tile, by_img.shape[1]):
            side = side + weighted[:, k : k + by_img.shape[1]]
        by_img[span] = side
        if m + 1 < len(spans):
            cosines = dot(img[spans[m + 1]], txt[:width], NN)
        use(span)
    return logit_scale * down


def put_text_terms(up, part, down):
    slab = part.shape[0] // 8
    figures = split_rows(down, up.shape[1])
    for e in range(8):
        at = e * (slab + PAD)
        up[at : at + slab] = part[e * slab : (e + 1) * slab].astype(b16)
        up[at + slab : at + slab + PAD] = figures


def other_kernel(rows, groups, at_ref, bias_ref, img, turned, txt, slopes, img_sum, up, by_img):
    step = pl.program_id(0)

    @pl.when(step == 0)
    def _():
        by_img[...] = jnp.zeros(by_img.shape, f32)

    parts = []

    def use(span):
        parts.append(dot(turned[:, span], slopes[0, span], NN))

    down = tile_slopes(rows, groups, at_ref[5], bias_ref, img, txt, slopes.at[0], by_img, use)
    put_text_terms(up, sum(parts[1:], parts[0]), down)

    @pl.when(step == 3)
    def _():
        img_sum[...] = logit_scale * jnp.sum(by_img[...].T, axis=0, keepdims=True)


def other_tile(img, turned, txt, group_bias, places, rows):
    count, width = img.shape
    tile = 2 * rows
    height = width + 8 * PAD
    whole = lambda a: pl.BlockSpec(a.shape, lambda i, at: (0, 0))
    return call(
        lambda *refs: other_kernel(rows, group_bias.shape[0], *refs),
        [
            jax.ShapeDtypeStruct((4, count, tile), b16),
            jax.ShapeDtypeStruct((1, count), f32),
            jax.ShapeDtypeStruct((height, count), b16),
        ],
        places,
        [group_bias, img, turned, txt],
        in_specs=[
            pl.BlockSpec(memory_space=pltpu.SMEM),
            whole(img),
            whole(turned),
            pl.BlockSpec((width + PAD, tile), lambda i, at: (0, i)),
        ],
        out_specs=[
            pl.BlockSpec((1, count, tile), lambda i, at: (i, 0, 0)),
            pl.BlockSpec((1, count), lambda i, at: (0, 0)),
            pl.BlockSpec((height, tile), lambda i, at: (0, i)),
        ],
        grid=(4,),
        scratch=[pltpu.VMEM((count, min(128, tile)), f32)],
        cost=4 * width * count * count,
    )


def own_kernel(rows, groups, at_ref, bias_ref, img, turned, txt, other, *refs):
    other_slopes, other_sum, up, out, by_img, held, both, total = refs
    step = pl.program_id(0)
    width = img.shape[1]
    tile = 2 * rows

    @pl.when(step == 0)
    def _():
        by_img[...] = jnp.zeros(by_img.shape, f32)
        total[...] = jnp.zeros(total.shape, f32)

    both[:, tile:] = other[:width]
    held[:, tile:] = other_slopes[0]
    both[:, :tile] = txt[:width]
    parts = []

    def use(span):
        parts.append(dot(turned[:, span], held[span, :tile], NN))
        total[:, span] += dot(both[...], held[span], NT)

    down = tile_slopes(rows, groups, at_ref[5], bias_ref, img, txt, held, by_img, use)
    put_text_terms(up, sum(parts[1:], parts[0]), down)

    @pl.when(step == 3)
    def _():
        slab = width // 8
        sums = logit_scale * jnp.sum(by_img[...].T, axis=0, keepdims=True) + other_sum[...]
        figures = split_rows(sums, sums.shape[1])
        for e in range(8):
            out[e, :slab] = total[e * slab : (e + 1) * slab].astype(b16)
            out[e, slab:] = figures


def own_tile(
    img, turned, txt, other, other_slopes, other_sum, group_bias, places, rows
):
    count, width = img.shape
    tile = 2 * rows
    height = width + 8 * PAD
    slab = width // 8
    whole = lambda a: pl.BlockSpec(a.shape, lambda i, at: (0, 0))
    stack = lambda a: pl.BlockSpec(a.shape, lambda i, at: (0, 0, 0))
    pieces = jax.ShapeDtypeStruct((8, slab + PAD, count), b16)
    return call(
        lambda *refs: own_kernel(rows, group_bias.shape[0], *refs),
        [jax.ShapeDtypeStruct((height, count), b16), pieces],
        places,
        [group_bias, img, turned, txt, other, other_slopes, other_sum],
        in_specs=[
            pl.BlockSpec(memory_space=pltpu.SMEM),
            whole(img),
            whole(turned),
            pl.BlockSpec((width + PAD, tile), lambda i, at: (0, i)),
            pl.BlockSpec((width + PAD, tile), lambda i, at: (0, i)),
            pl.BlockSpec((1, count, tile), lambda i, at: (i, 0, 0)),
            whole(other_sum),
        ],
        out_specs=[pl.BlockSpec((height, tile), lambda i, at: (0, i)), stack(pieces)],
        grid=(4,),
        scratch=[
            pltpu.VMEM((count, min(128, tile)), f32),
            pltpu.VMEM((count, 2 * tile), b16),
            pltpu.VMEM((width, 2 * tile), b16),
            pltpu.VMEM((width, count), f32),
        ],
        cost=8 * width * count * count,
    )


def sum_into(out, terms):
    slab = out.shape[0] - PAD
    block, total = terms[0][:slab].astype(f32), joined(terms[0][slab:])
    for term in terms[1:]:
        block, total = block + term[:slab].astype(f32), total + joined(term[slab:])
    out[:slab] = block.astype(b16)
    out[slab:] = split_rows(total, out.shape[1])


def sum_kernel(sizes, at_ref, *refs):
    start = 0
    for size, out in zip(sizes, refs[sum(sizes) :]):
        sum_into(out, refs[start : start + size])
        start += size


def sums(groups, places, rows):
    arrays, specs = [], []
    lanes = 4 * rows
    for term in [term for group in groups for term in group]:
        if isinstance(term, tuple):
            arrays.append(term[0])
            height = term[0].shape[0] // 8
            specs.append(pl.BlockSpec((height, lanes), lambda i, at, n=term[1]: (at[n], i)))
        else:
            arrays.append(term)
            height = term.shape[0]
            specs.append(pl.BlockSpec((height, lanes), lambda i, at: (0, i)))
    count = arrays[0].shape[1]
    return call(
        lambda *refs: sum_kernel([len(group) for group in groups], *refs),
        [jax.ShapeDtypeStruct((height, count), b16)] * len(groups),
        places,
        arrays,
        in_specs=specs,
        out_specs=[pl.BlockSpec((height, lanes), lambda i, at: (0, i))] * len(groups),
        grid=(count // lanes,),
    )


def img_grad_kernel(rows, at_ref, got, unit, norm, feats, blocks, part, grad):
    slab = unit.shape[0]
    up, inner = got[0, :slab].astype(f32), joined(got[0, slab:])
    for n in range(1, 8):
        up, inner = up + got[n, :slab].astype(f32), inner + joined(got[n, slab:])
    up = logit_scale * up - unit[...].astype(f32) * inner
    grad[...] = (up * (1.0 / norm[...])).astype(b16)
    for n in range(8):
        blocks[n] = grad[:, n * rows : (n + 1) * rows]
    part[...] = dot(grad[...], feats[...], NN).astype(b16)


def txt_grad_kernel(rows, at_ref, *refs):
    terms, unit, norm, blocks, (own, give, part, grad) = (
        refs[:5], refs[5], refs[6], refs[7:15], refs[15:]
    )
    slab = unit.shape[0]
    up, inner = terms[0][:slab].astype(f32), joined(terms[0][slab:])
    for term in terms[1:]:
        up, inner = up + term[:slab].astype(f32), inner + joined(term[slab:])
    up = logit_scale * up - unit[...].astype(f32) * inner
    grad[...] = (up * (1.0 / norm[...])).astype(b16)
    for ring in range(4):
        low = grad[:, (2 * ring) * rows : (2 * ring + 1) * rows]
        high = grad[:, (2 * ring + 1) * rows : (2 * ring + 2) * rows]
        own[ring] = jnp.where(at_ref[1] == 0, low, high)
        give[ring] = jnp.where(at_ref[1] == 0, high, low)
    total = None
    for d in range(4):
        cols = grad[:, aligned((at_ref[0] + d) % 4, 2 * rows)]
        term = dot(cols, in_pair(blocks[2 * d], blocks[2 * d + 1], at_ref[1], rows), NN)
        total = term if total is None else total + term
    part[...] = total.astype(b16)


def gradient(kernel, own, terms, unit, norm, feats, halves, places, rows):
    width = feats[0].shape[1]
    slab, count = width // 8, 8 * rows
    whole = lambda a: pl.BlockSpec(a.shape, lambda i, at: (0,) * len(a.shape))
    mine = lambda height: pl.BlockSpec((height, count), lambda i, at: (at[own], 0))
    block = jax.ShapeDtypeStruct((8 // halves, slab, rows), b16)
    part = jax.ShapeDtypeStruct((slab, width), b16)
    return call(
        lambda *refs: kernel(rows, *refs),
        [block] * halves + [part],
        places,
        [term[0] if isinstance(term, tuple) else term for term in terms] + [unit, norm, *feats],
        in_specs=[mine(slab + PAD) if isinstance(term, tuple) else whole(term) for term in terms]
        + [mine(slab), whole(norm)]
        + [whole(a) for a in feats],
        out_specs=[whole(block)] * halves + [whole(part)],
        grid=(1,),
        scratch=[pltpu.VMEM((slab, count), b16)],
        cost=2 * slab * count * width,
        weight=0,
    )


def pick_kernel(at_ref, img, txt, other_img, other_txt, out):
    width = img.shape[1]
    slots = out.shape[0]
    own = width // 128
    third = 2 * img.shape[0] // 3
    img = img[...].astype(f32) + other_img[...].astype(f32)
    txt = txt[...].astype(f32) + other_txt[...].astype(f32)
    part = jnp.concatenate([img, txt], axis=0).astype(b16)
    slot = lax.broadcasted_iota(jnp.int32, (slots, 1), 0)
    feature = lax.broadcasted_iota(jnp.int32, (slots, width), 1)
    base = (slot // 8 * 2 + at_ref[4]) * own
    chosen = jnp.where(feature == base + slot % 8, 1.0, 0.0).astype(b16)
    out[:, : 3 * third] = dot(chosen, part, NT).astype(b16)
    chosen = jnp.where(feature == base + 8, 1.0, 0.0).astype(b16)
    ninth = dot(chosen, part, NT)
    pick = slot % 8
    rest = jnp.where(pick == 1, ninth[:, third : 2 * third], ninth[:, :third])
    rest = jnp.where(pick == 2, ninth[:, 2 * third :], rest)
    out[:, 3 * third :] = rest.astype(b16)


def picked(parts, places):
    slab, width = parts[0].shape
    return call(
        pick_kernel,
        jax.ShapeDtypeStruct((64 * 8, slab * 8 // 3), b16),
        places,
        parts,
        cost=8 * 512 * width * slab,
        weight=0,
    )


def head_kernel(at_ref, got, img_out, txt_out):
    slab = img_out.shape[1] // 8
    third = slab * 2 // 3
    half = third // 2
    for p in range(8):
        img = txt = None
        for other in range(8):
            z, lo, hi, y = p // 2, p % 2, other // 4, other % 4
            block = got[(z * 2 + lo) * 8 + hi * 4 + y].astype(f32)
            img = block if img is None else img + block
            z, lo, hi, y = other // 2, other % 2, p % 2, p // 2
            block = got[(z * 2 + lo) * 8 + hi * 4 + y].astype(f32)
            txt = block if txt is None else txt + block
        at = p * slab
        ninth = 2 * slab
        img_out[0:8, at : at + slab] = img[:, :slab]
        img_out[8:9, at : at + third] = img[0:1, ninth : ninth + third]
        img_out[8:9, at + third : at + slab] = img[1:2, ninth : ninth + half]
        txt_out[0:8, at : at + slab] = txt[:, slab : 2 * slab]
        txt_out[8:9, at : at + half] = txt[1:2, ninth + half : ninth + third]
        txt_out[8:9, at + half : at + slab] = txt[2:3, ninth : ninth + third]


def together(arrays):
    return lax.optimization_barrier(list(arrays))


def pair_lines(own, got, second):
    return jnp.concatenate([jnp.where(second, got, own), jnp.where(second, own, got)], axis=1)


def whole_columns(lines, move, ring):
    got = []
    for d in range(4):
        block = lax.dynamic_index_in_dim(lines, (ring + d) % 4, 0, keepdims=False)
        got.append(send(block, move(d, 0)) if d else block)
    height = got[0].shape[0]
    from_own = jnp.concatenate([got[-d % 4] for d in range(4)] * 2, axis=0)
    return lax.dynamic_slice_in_dim(from_own, (4 - ring) % 4 * height, 4 * height, axis=0)


def shards(image_feat, text_feat, image_head, text_head, group_bias, text_lang, partner):
    rows, width = image_feat.shape
    slab = width // 8
    place = lax.axis_index(DEV)
    z, lo, hi, y, core = place // 32, place // 16 % 2, place // 8 % 2, place // 2 % 4, place % 2

    slots = [(y + d) % 4 * 2 + (hi + e) % 2 for d in range(4) for e in range(2)]
    places = [y, hi, z, lo, core, place % 16, z * 2 + lo, y * 2 + hi, *slots]
    (places,) = together([jnp.stack(places).astype(jnp.int32)])
    figures = jnp.stack([text_lang, partner // 128, partner % 128]).astype(b16)
    figures = jnp.pad(figures, ((0, PAD - 3), (0, width - rows)))
    text_rows = jnp.concatenate([text_feat, figures], axis=0)
    img_feats = exchange(jnp.broadcast_to(image_feat[None], (8, rows, width)), IMG_GROUPS)
    img_feats = img_feats.reshape(8 * rows, width)
    across = send(text_rows, txt_move(0, 1))
    before = send(text_rows, txt_move(1, 0))
    after = send(text_rows, txt_move(3, 0))
    across, turned_txt = together([across, text_head.T])
    across_after = send(across, txt_move(3, 0))
    across_before = send(across, txt_move(1, 0))
    across_after, before, after, across = together([across_after, before, after, across])
    far = send(before, txt_move(1, 0))
    across_far = send(across_after, txt_move(3, 0))
    txt_blocks = [
        text_rows, across, after, across_after, far, across_far, before, across_before
    ]
    unit_txt, norm_txt = units(txt_blocks, turned_txt, places, rows)
    other_txt = send(unit_txt, core_move)
    turned_units, norm_img = unit_columns(img_feats, image_head)
    unit_img = unit_rows(together([img_feats, unit_txt])[0], image_head, norm_img)

    other_slopes, other_sum, other_up = other_tile(
        unit_img, turned_units, other_txt, group_bias, places, rows
    )
    back = send(other_up, core_move)
    text_up, img_terms = own_tile(
        unit_img, turned_units, unit_txt, other_txt, other_slopes, other_sum, group_bias,
        places, rows,
    )
    img_terms = exchange(img_terms, IMG_GROUPS)

    def slab_terms(d, e):
        return [(text_up, 8 + 2 * d + e), (back, 8 + 2 * d + e)]

    far, across_far, across_after = sums(
        [slab_terms(2, 0), slab_terms(2, 1), slab_terms(1, 1)], places, rows
    )
    far = send(far, txt_move(1, 0))
    across_far = send(across_far, txt_move(3, 0))
    far, across_far, across_after = together([far, across_far, across_after])
    across_before = send(across_after, txt_move(1, 0))
    across_after, before, after = sums(
        [slab_terms(3, 1) + [across_far], slab_terms(1, 0) + [far], slab_terms(3, 0)], places, rows
    )
    across_after = send(across_after, txt_move(3, 0))
    across_before, across_after, before, after = together(
        [across_before, across_after, before, after]
    )
    before = send(before, txt_move(1, 0))
    after = send(after, txt_move(3, 0))
    (across,) = sums([slab_terms(0, 1) + [across_before, across_after]], places, rows)
    across = send(across, txt_move(0, 1))

    img_blocks, img_part = gradient(
        img_grad_kernel, 6, [img_terms], turned_units, norm_img, [img_feats], 1, places, rows
    )
    grad_img = exchange(img_blocks, IMG_GROUPS).reshape(width, rows)
    txt_own, txt_give, txt_part = gradient(
        txt_grad_kernel, 7, slab_terms(0, 0) + [before, after, across], unit_txt, norm_txt,
        txt_blocks, 2, places, rows,
    )
    img_theirs = send(img_part, core_move)
    txt_theirs = send(txt_part, core_move)
    txt_got = send(txt_give, txt_move(0, 1))
    heads, txt_got = together([picked([img_part, txt_part, img_theirs, txt_theirs], places), txt_got])
    heads = exchange(heads.reshape(64, 8, -1), CHIP_GROUPS)
    head_shape = jax.ShapeDtypeStruct((width // 128, width), f32)
    image_head_grad, text_head_grad = call(head_kernel, [head_shape] * 2, places, [heads])

    image_grad = dot(grad_img, image_head, (((0,), (1,)), ((), ())))
    grad_txt = whole_columns(pair_lines(txt_own, txt_got, hi), txt_move, y)
    text_grad = dot(grad_txt, text_head, (((0,), (1,)), ((), ())))
    return (image_grad, text_grad, image_head_grad, text_head_grad)


def solution(mesh):
    line = jax.sharding.Mesh(mesh.devices.reshape(-1), (DEV,))
    in_specs = (P(DEV, None), P(DEV, None), P(), P(), P(), P(DEV), P(DEV))
    return jax.shard_map(
        shards, mesh=line, in_specs=in_specs, out_specs=(P(DEV, None),) * 4, check_vma=False
    )
```

```python
import jax
import jax.numpy as jnp
from jax import lax
from jax.experimental import pallas as pl
from jax.experimental.pallas import tpu as pltpu
from jax.sharding import PartitionSpec as P

logit_scale = 64.0
epsilon = 1e-06
log2e = 1.4426950408889634
f32, b16 = jnp.float32, jnp.bfloat16

DEV = "dev"
PLACES = [
    (z, lo, hi, y, c)
    for z in range(4)
    for lo in range(2)
    for hi in range(2)
    for y in range(4)
    for c in range(2)
]


def flat(z, lo, hi, y, c):
    return (z * 2 + lo) * 16 + hi * 8 + y * 2 + c


def img_move(d, e):
    return lambda z, lo, hi, y, c: ((z + d) % 4, lo ^ e, hi, y, c)


def txt_move(d, e):
    return lambda z, lo, hi, y, c: (z, lo ^ e, hi ^ e, (y + d) % 4, c)


def core_move(z, lo, hi, y, c):
    return (z, lo, hi, y, 1 - c)


IMG_GROUPS = [
    [flat(z, lo, hi, y, c) for z in range(4) for lo in range(2)]
    for hi in range(2)
    for y in range(4)
    for c in range(2)
]
TXT_GROUPS = [
    [flat(z, hi ^ b, hi, y, c) for y in range(4) for hi in range(2)]
    for z in range(4)
    for b in range(2)
    for c in range(2)
]
TXT_CORE_GROUPS = [
    [flat(z, hi ^ b, hi, y, c) for c in range(2) for y in range(4) for hi in range(2)]
    for z in range(4)
    for b in range(2)
]
CHIP_GROUPS = [[flat(*p) for p in PLACES if p[4] == c] for c in range(2)]


def send(block, move):
    return lax.ppermute(block, DEV, [(flat(*p), flat(*move(*p))) for p in PLACES])


def exchange(blocks, groups):
    return lax.all_to_all(blocks, DEV, 0, 0, axis_index_groups=groups, tiled=True)


PAD = 16
NN = (((1,), (0,)), ((), ()))
NT = (((1,), (1,)), ((), ()))
TN = (((0,), (0,)), ((), ()))


def dot(a, b, dims):
    return lax.dot_general(a, b, dims, preferred_element_type=f32)


def call(body, out_shape, places, arrays, in_specs=None, out_specs=None, grid=(), scratch=(), cost=0, aliases=None, weight=1):
    whole = pl.BlockSpec(memory_space=pltpu.VMEM)
    many = isinstance(out_shape, (list, tuple))
    if in_specs is None:
        in_specs = [whole] * len(arrays)
    if out_specs is None:
        out_specs = [whole] * len(out_shape) if many else whole
    spec = pltpu.PrefetchScalarGridSpec(
        num_scalar_prefetch=1,
        grid=grid,
        in_specs=in_specs,
        out_specs=out_specs,
        scratch_shapes=list(scratch),
    )
    moved = weight * sum(a.size * a.dtype.itemsize for a in arrays)
    return pl.pallas_call(
        body,
        out_shape=out_shape,
        grid_spec=spec,
        input_output_aliases=aliases or {},
        compiler_params=pltpu.CompilerParams(vmem_limit_bytes=60 * 2**20),
        cost_estimate=pl.CostEstimate(flops=weight * cost, bytes_accessed=moved, transcendentals=0),
    )(places, *arrays)


def aligned(index, size):
    return pl.ds(pl.multiple_of(index * size, size), size)


def split_rows(total, lanes):
    high = total.astype(b16).astype(f32)
    row = lax.broadcasted_iota(jnp.int32, (PAD, lanes), 0)
    return jnp.where(row == 0, high, jnp.where(row == 1, total - high, 0.0)).astype(b16)


def joined(rows):
    return rows[0:1].astype(f32) + rows[1:2].astype(f32)


def in_pair(own, across, second, rows):
    own, across = own[:rows], across[:rows]
    first = second == 0
    return jnp.concatenate([jnp.where(first, own, across), jnp.where(first, across, own)], axis=0)


def put_units(feats, turned_head, proj, turned, norm):
    width = turned_head.shape[0]
    quarter = width // 4
    total = jnp.zeros((1, feats.shape[0]), f32)
    for m in range(4):
        span = slice(m * quarter, (m + 1) * quarter)
        part = dot(turned_head[span], feats[...], NT)
        proj[span] = part
        total = total + jnp.sum(part * part, axis=0, keepdims=True)
    length = jnp.sqrt(total + epsilon)
    norm[...] = length
    inverse = 1.0 / length
    for m in range(4):
        span = slice(m * quarter, (m + 1) * quarter)
        turned[span] = (proj[span] * inverse).astype(b16)


def unit_kernel(rows, pairs, at_ref, *refs):
    blocks, turned_head = refs[: 2 * pairs], refs[2 * pairs]
    turned, norm, feats, proj = refs[-4:]
    width = turned_head.shape[0]
    second = at_ref[1]
    step = pl.program_id(0)
    for p in range(pairs):
        own, across = blocks[2 * p], blocks[2 * p + 1]

        @pl.when(step == p)
        def _():
            feats[...] = in_pair(own, across, second, rows)
            first = second == 0
            sides = own[rows:, :rows], across[rows:, :rows]
            turned[width:, :rows] = jnp.where(first, sides[0], sides[1])
            turned[width:, rows:] = jnp.where(first, sides[1], sides[0])

    put_units(feats, turned_head, proj, turned, norm)


def units(pairs, distance, turned_head, carried, places, rows):
    width = turned_head.shape[0]
    tile = 2 * rows
    whole = lambda a: pl.BlockSpec(a.shape, lambda i, at: (0, 0))
    blocks = [block for pair in pairs for block in pair]
    return call(
        lambda *refs: unit_kernel(rows, len(pairs), *refs),
        [
            jax.ShapeDtypeStruct((width + PAD, 8 * rows), b16),
            jax.ShapeDtypeStruct((1, 8 * rows), f32),
        ],
        places,
        [*blocks, turned_head, *carried],
        in_specs=[whole(a) for a in [*blocks, turned_head]]
        + [pl.BlockSpec(memory_space=pl.ANY)] * len(carried),
        out_specs=[
            pl.BlockSpec((width + PAD, tile), lambda i, at: (0, (at[0] + distance + i) % 4)),
            pl.BlockSpec((1, tile), lambda i, at: (0, (at[0] + distance + i) % 4)),
        ],
        grid=(len(pairs),),
        scratch=[pltpu.VMEM((tile, width), b16), pltpu.VMEM((width, tile), f32)],
        cost=2 * tile * width * width * len(pairs),
        aliases={len(blocks) + 2 + n: n for n in range(len(carried))},
    )


def unit_columns(feats, head):
    projected = dot(head, feats, (((0,), (1,)), ((), ())))
    norm = jnp.sqrt(jnp.sum(projected * projected, axis=0, keepdims=True) + epsilon)
    return (projected / norm).astype(b16), norm


def unit_rows(feats, head, norm):
    return (dot(feats, head, NN) / norm.reshape(-1, 1)).astype(b16)


def tile_slopes(rows, groups, place, bias_ref, img, txt, slopes, by_img):
    width = img.shape[1]
    tile = 2 * rows
    lang = txt[width : width + PAD].astype(f32)
    partner = lang[1:2] * 128.0 + lang[2:3]
    lang = lang[0:1]
    bias = jnp.zeros((1, tile), f32)
    for g in range(groups):
        bias = jnp.where(lang == g, bias_ref[g], bias)
    bias = bias * -log2e
    down = jnp.zeros((1, tile), f32)
    high = 4 * rows
    for m in range(img.shape[0] // high):
        span = slice(m * high, (m + 1) * high)
        index = m * high + lax.broadcasted_iota(jnp.int32, (high, 1), 0)
        ids = ((index // rows * 16 + place) * rows + index % rows).astype(f32)
        cosines = dot(img[span], txt[:width], NN)
        below = 1.0 + jnp.exp2(cosines * (-log2e * logit_scale) + bias)
        gate = pl.reciprocal(below, approx=True)
        gate = gate * (2.0 - below * gate)
        slope = gate - jnp.where(partner == ids, 1.0, 0.0)
        slopes[span, :tile] = slope.astype(b16)
        weighted = slope * cosines
        down = down + jnp.sum(weighted, axis=0, keepdims=True)
        side = by_img[span]
        for k in range(0, tile, by_img.shape[1]):
            side = side + weighted[:, k : k + by_img.shape[1]]
        by_img[span] = side
    return logit_scale * down


def put_text_terms(up, turned, slopes, down):
    slab = turned.shape[0] // 8
    figures = split_rows(down, up.shape[1])
    part = dot(turned[...], slopes, NN)
    for e in range(8):
        at = e * (slab + PAD)
        up[at : at + slab] = part[e * slab : (e + 1) * slab].astype(b16)
        up[at + slab : at + slab + PAD] = figures


def other_kernel(rows, groups, at_ref, bias_ref, img, turned, txt, slopes, img_sum, up, by_img):
    step = pl.program_id(0)

    @pl.when(step == 0)
    def _():
        by_img[...] = jnp.zeros(by_img.shape, f32)

    down = tile_slopes(rows, groups, at_ref[5], bias_ref, img, txt, slopes.at[0], by_img)
    put_text_terms(up, turned, slopes[0], down)

    @pl.when(step == 3)
    def _():
        img_sum[...] = logit_scale * jnp.sum(by_img[...].T, axis=0, keepdims=True)


def other_tile(img, turned, txt, group_bias, places, rows):
    count, width = img.shape
    tile = 2 * rows
    height = width + 8 * PAD
    whole = lambda a: pl.BlockSpec(a.shape, lambda i, at: (0, 0))
    return call(
        lambda *refs: other_kernel(rows, group_bias.shape[0], *refs),
        [
            jax.ShapeDtypeStruct((4, count, tile), b16),
            jax.ShapeDtypeStruct((1, count), f32),
            jax.ShapeDtypeStruct((height, count), b16),
        ],
        places,
        [group_bias, img, turned, txt],
        in_specs=[
            pl.BlockSpec(memory_space=pltpu.SMEM),
            whole(img),
            whole(turned),
            pl.BlockSpec((width + PAD, tile), lambda i, at: (0, i)),
        ],
        out_specs=[
            pl.BlockSpec((1, count, tile), lambda i, at: (i, 0, 0)),
            pl.BlockSpec((1, count), lambda i, at: (0, 0)),
            pl.BlockSpec((height, tile), lambda i, at: (0, i)),
        ],
        grid=(4,),
        scratch=[pltpu.VMEM((count, min(128, tile)), f32)],
        cost=4 * width * count * count,
    )


def own_kernel(rows, groups, at_ref, bias_ref, img, turned, txt, other, *refs):
    other_slopes, other_sum, up, out, by_img, held, both, total = refs
    step = pl.program_id(0)
    width = img.shape[1]
    tile = 2 * rows

    @pl.when(step == 0)
    def _():
        by_img[...] = jnp.zeros(by_img.shape, f32)
        total[...] = jnp.zeros(total.shape, f32)

    both[:, tile:] = other[:width]
    held[:, tile:] = other_slopes[0]
    both[:, :tile] = txt[:width]
    down = tile_slopes(rows, groups, at_ref[5], bias_ref, img, txt, held, by_img)
    put_text_terms(up, turned, held[:, :tile], down)
    total[...] += dot(both[...], held[...], NT)

    @pl.when(step == 3)
    def _():
        slab = width // 8
        sums = logit_scale * jnp.sum(by_img[...].T, axis=0, keepdims=True) + other_sum[...]
        figures = split_rows(sums, sums.shape[1])
        for e in range(8):
            out[e, :slab] = total[e * slab : (e + 1) * slab].astype(b16)
            out[e, slab:] = figures


def own_tile(
    img, turned, txt, other, other_slopes, other_sum, group_bias, places, rows
):
    count, width = img.shape
    tile = 2 * rows
    height = width + 8 * PAD
    slab = width // 8
    whole = lambda a: pl.BlockSpec(a.shape, lambda i, at: (0, 0))
    stack = lambda a: pl.BlockSpec(a.shape, lambda i, at: (0, 0, 0))
    pieces = jax.ShapeDtypeStruct((8, slab + PAD, count), b16)
    return call(
        lambda *refs: own_kernel(rows, group_bias.shape[0], *refs),
        [jax.ShapeDtypeStruct((height, count), b16), pieces],
        places,
        [group_bias, img, turned, txt, other, other_slopes, other_sum],
        in_specs=[
            pl.BlockSpec(memory_space=pltpu.SMEM),
            whole(img),
            whole(turned),
            pl.BlockSpec((width + PAD, tile), lambda i, at: (0, i)),
            pl.BlockSpec((width + PAD, tile), lambda i, at: (0, i)),
            pl.BlockSpec((1, count, tile), lambda i, at: (i, 0, 0)),
            whole(other_sum),
        ],
        out_specs=[pl.BlockSpec((height, tile), lambda i, at: (0, i)), stack(pieces)],
        grid=(4,),
        scratch=[
            pltpu.VMEM((count, min(128, tile)), f32),
            pltpu.VMEM((count, 2 * tile), b16),
            pltpu.VMEM((width, 2 * tile), b16),
            pltpu.VMEM((width, count), f32),
        ],
        cost=8 * width * count * count,
    )


def sum_into(out, terms):
    slab = out.shape[0] - PAD
    block, total = terms[0][:slab].astype(f32), joined(terms[0][slab:])
    for term in terms[1:]:
        block, total = block + term[:slab].astype(f32), total + joined(term[slab:])
    out[:slab] = block.astype(b16)
    out[slab:] = split_rows(total, out.shape[1])


def sum_kernel(sizes, at_ref, *refs):
    start = 0
    for size, out in zip(sizes, refs[sum(sizes) :]):
        sum_into(out, refs[start : start + size])
        start += size


def sums(groups, places, rows):
    arrays, specs = [], []
    lanes = 4 * rows
    for term in [term for group in groups for term in group]:
        if isinstance(term, tuple):
            arrays.append(term[0])
            height = term[0].shape[0] // 8
            specs.append(pl.BlockSpec((height, lanes), lambda i, at, n=term[1]: (at[n], i)))
        else:
            arrays.append(term)
            height = term.shape[0]
            specs.append(pl.BlockSpec((height, lanes), lambda i, at: (0, i)))
    count = arrays[0].shape[1]
    return call(
        lambda *refs: sum_kernel([len(group) for group in groups], *refs),
        [jax.ShapeDtypeStruct((height, count), b16)] * len(groups),
        places,
        arrays,
        in_specs=specs,
        out_specs=[pl.BlockSpec((height, lanes), lambda i, at: (0, i))] * len(groups),
        grid=(count // lanes,),
    )


def img_grad_kernel(rows, at_ref, got, unit, norm, feats, blocks, part, grad):
    slab = unit.shape[0]
    up, inner = got[0, :slab].astype(f32), joined(got[0, slab:])
    for n in range(1, 8):
        up, inner = up + got[n, :slab].astype(f32), inner + joined(got[n, slab:])
    up = logit_scale * up - unit[...].astype(f32) * inner
    grad[...] = (up * (1.0 / norm[...])).astype(b16)
    for n in range(8):
        blocks[n] = grad[:, n * rows : (n + 1) * rows]
    part[...] = dot(grad[...], feats[...], NN).astype(b16)


def txt_grad_kernel(rows, at_ref, *refs):
    terms, unit, norm, blocks, (own, give, part, grad) = (
        refs[:5], refs[5], refs[6], refs[7:15], refs[15:]
    )
    slab = unit.shape[0]
    up, inner = terms[0][:slab].astype(f32), joined(terms[0][slab:])
    for term in terms[1:]:
        up, inner = up + term[:slab].astype(f32), inner + joined(term[slab:])
    up = logit_scale * up - unit[...].astype(f32) * inner
    grad[...] = (up * (1.0 / norm[...])).astype(b16)
    for ring in range(4):
        low = grad[:, (2 * ring) * rows : (2 * ring + 1) * rows]
        high = grad[:, (2 * ring + 1) * rows : (2 * ring + 2) * rows]
        own[ring] = jnp.where(at_ref[1] == 0, low, high)
        give[ring] = jnp.where(at_ref[1] == 0, high, low)
    total = None
    for d in range(4):
        cols = grad[:, aligned((at_ref[0] + d) % 4, 2 * rows)]
        term = dot(cols, in_pair(blocks[2 * d], blocks[2 * d + 1], at_ref[1], rows), NN)
        total = term if total is None else total + term
    part[...] = total.astype(b16)


def gradient(kernel, own, terms, unit, norm, feats, halves, places, rows):
    width = feats[0].shape[1]
    slab, count = width // 8, 8 * rows
    whole = lambda a: pl.BlockSpec(a.shape, lambda i, at: (0,) * len(a.shape))
    mine = lambda height: pl.BlockSpec((height, count), lambda i, at: (at[own], 0))
    block = jax.ShapeDtypeStruct((8 // halves, slab, rows), b16)
    part = jax.ShapeDtypeStruct((slab, width), b16)
    return call(
        lambda *refs: kernel(rows, *refs),
        [block] * halves + [part],
        places,
        [term[0] if isinstance(term, tuple) else term for term in terms] + [unit, norm, *feats],
        in_specs=[mine(slab + PAD) if isinstance(term, tuple) else whole(term) for term in terms]
        + [mine(slab), whole(norm)]
        + [whole(a) for a in feats],
        out_specs=[whole(block)] * halves + [whole(part)],
        grid=(1,),
        scratch=[pltpu.VMEM((slab, count), b16)],
        cost=2 * slab * count * width,
        weight=0,
    )


def pick_kernel(at_ref, img, txt, other_img, other_txt, out):
    width = img.shape[1]
    slots = out.shape[0]
    own = width // 128
    third = 2 * img.shape[0] // 3
    img = img[...].astype(f32) + other_img[...].astype(f32)
    txt = txt[...].astype(f32) + other_txt[...].astype(f32)
    part = jnp.concatenate([img, txt], axis=0).astype(b16)
    slot = lax.broadcasted_iota(jnp.int32, (slots, 1), 0)
    feature = lax.broadcasted_iota(jnp.int32, (slots, width), 1)
    base = (slot // 8 * 2 + at_ref[4]) * own
    chosen = jnp.where(feature == base + slot % 8, 1.0, 0.0).astype(b16)
    out[:, : 3 * third] = dot(chosen, part, NT).astype(b16)
    chosen = jnp.where(feature == base + 8, 1.0, 0.0).astype(b16)
    ninth = dot(chosen, part, NT)
    pick = slot % 8
    rest = jnp.where(pick == 1, ninth[:, third : 2 * third], ninth[:, :third])
    rest = jnp.where(pick == 2, ninth[:, 2 * third :], rest)
    out[:, 3 * third :] = rest.astype(b16)


def picked(parts, places):
    slab, width = parts[0].shape
    return call(
        pick_kernel,
        jax.ShapeDtypeStruct((64 * 8, slab * 8 // 3), b16),
        places,
        parts,
        cost=8 * 512 * width * slab,
        weight=0,
    )


def head_kernel(at_ref, got, img_out, txt_out):
    slab = img_out.shape[1] // 8
    third = slab * 2 // 3
    half = third // 2
    for p in range(8):
        img = txt = None
        for other in range(8):
            z, lo, hi, y = p // 2, p % 2, other // 4, other % 4
            block = got[(z * 2 + lo) * 8 + hi * 4 + y].astype(f32)
            img = block if img is None else img + block
            z, lo, hi, y = other // 2, other % 2, p % 2, p // 2
            block = got[(z * 2 + lo) * 8 + hi * 4 + y].astype(f32)
            txt = block if txt is None else txt + block
        at = p * slab
        ninth = 2 * slab
        img_out[0:8, at : at + slab] = img[:, :slab]
        img_out[8:9, at : at + third] = img[0:1, ninth : ninth + third]
        img_out[8:9, at + third : at + slab] = img[1:2, ninth : ninth + half]
        txt_out[0:8, at : at + slab] = txt[:, slab : 2 * slab]
        txt_out[8:9, at : at + half] = txt[1:2, ninth + half : ninth + third]
        txt_out[8:9, at + half : at + slab] = txt[2:3, ninth : ninth + third]


def together(arrays):
    return lax.optimization_barrier(list(arrays))


def pair_lines(own, got, second):
    return jnp.concatenate([jnp.where(second, got, own), jnp.where(second, own, got)], axis=1)


def whole_columns(lines, move, ring):
    got = []
    for d in range(4):
        block = lax.dynamic_index_in_dim(lines, (ring + d) % 4, 0, keepdims=False)
        got.append(send(block, move(d, 0)) if d else block)
    height = got[0].shape[0]
    from_own = jnp.concatenate([got[-d % 4] for d in range(4)] * 2, axis=0)
    return lax.dynamic_slice_in_dim(from_own, (4 - ring) % 4 * height, 4 * height, axis=0)


def shards(image_feat, text_feat, image_head, text_head, group_bias, text_lang, partner):
    rows, width = image_feat.shape
    slab = width // 8
    place = lax.axis_index(DEV)
    z, lo, hi, y, core = place // 32, place // 16 % 2, place // 8 % 2, place // 2 % 4, place % 2

    slots = [(y + d) % 4 * 2 + (hi + e) % 2 for d in range(4) for e in range(2)]
    places = [y, hi, z, lo, core, place % 16, z * 2 + lo, y * 2 + hi, *slots]
    (places,) = together([jnp.stack(places).astype(jnp.int32)])
    figures = jnp.stack([text_lang, partner // 128, partner % 128]).astype(b16)
    figures = jnp.pad(figures, ((0, PAD - 3), (0, width - rows)))
    text_rows = jnp.concatenate([text_feat, figures], axis=0)
    img_feats = exchange(jnp.broadcast_to(image_feat[None], (8, rows, width)), IMG_GROUPS)
    img_feats = img_feats.reshape(8 * rows, width)
    across = send(text_rows, txt_move(0, 1))
    before = send(text_rows, txt_move(1, 0))
    after = send(text_rows, txt_move(3, 0))
    across, turned_txt = together([across, text_head.T])
    across_after = send(across, txt_move(3, 0))
    across_before = send(across, txt_move(1, 0))
    across_after, before, after, across = together([across_after, before, after, across])
    far = send(before, txt_move(1, 0))
    across_far = send(across_after, txt_move(3, 0))
    txt_blocks = [
        text_rows, across, after, across_after, far, across_far, before, across_before
    ]
    pairs = [(before, across_before), (text_rows, across), (after, across_after)]
    made = units(pairs, 3, turned_txt, (), places, rows)
    unit_txt, norm_txt = units([(far, across_far)], 2, turned_txt, made, places, rows)
    other_txt = send(unit_txt, core_move)
    turned_units, norm_img = unit_columns(img_feats, image_head)
    unit_img = unit_rows(together([img_feats, unit_txt])[0], image_head, norm_img)

    other_slopes, other_sum, other_up = other_tile(
        unit_img, turned_units, other_txt, group_bias, places, rows
    )
    back = send(other_up, core_move)
    text_up, img_terms = own_tile(
        unit_img, turned_units, unit_txt, other_txt, other_slopes, other_sum, group_bias,
        places, rows,
    )
    img_terms = exchange(img_terms, IMG_GROUPS)

    def slab_terms(d, e):
        return [(text_up, 8 + 2 * d + e), (back, 8 + 2 * d + e)]

    far, across_far, across_after = sums(
        [slab_terms(2, 0), slab_terms(2, 1), slab_terms(1, 1)], places, rows
    )
    far = send(far, txt_move(1, 0))
    across_far = send(across_far, txt_move(3, 0))
    far, across_far, across_after = together([far, across_far, across_after])
    across_before = send(across_after, txt_move(1, 0))
    across_after, before, after = sums(
        [slab_terms(3, 1) + [across_far], slab_terms(1, 0) + [far], slab_terms(3, 0)], places, rows
    )
    across_after = send(across_after, txt_move(3, 0))
    across_before, across_after, before, after = together(
        [across_before, across_after, before, after]
    )
    before = send(before, txt_move(1, 0))
    after = send(after, txt_move(3, 0))
    (across,) = sums([slab_terms(0, 1) + [across_before, across_after]], places, rows)
    across = send(across, txt_move(0, 1))

    img_blocks, img_part = gradient(
        img_grad_kernel, 6, [img_terms], turned_units, norm_img, [img_feats], 1, places, rows
    )
    grad_img = exchange(img_blocks, IMG_GROUPS).reshape(width, rows)
    txt_own, txt_give, txt_part = gradient(
        txt_grad_kernel, 7, slab_terms(0, 0) + [before, after, across], unit_txt, norm_txt,
        txt_blocks, 2, places, rows,
    )
    img_theirs = send(img_part, core_move)
    txt_theirs = send(txt_part, core_move)
    txt_got = send(txt_give, txt_move(0, 1))
    heads, txt_got = together([picked([img_part, txt_part, img_theirs, txt_theirs], places), txt_got])
    heads = exchange(heads.reshape(64, 8, -1), CHIP_GROUPS)
    head_shape = jax.ShapeDtypeStruct((width // 128, width), f32)
    image_head_grad, text_head_grad = call(head_kernel, [head_shape] * 2, places, [heads])

    image_grad = dot(grad_img, image_head, (((0,), (1,)), ((), ())))
    grad_txt = whole_columns(pair_lines(txt_own, txt_got, hi), txt_move, y)
    text_grad = dot(grad_txt, text_head, (((0,), (1,)), ((), ())))
    return (image_grad, text_grad, image_head_grad, text_head_grad)


def solution(mesh):
    line = jax.sharding.Mesh(mesh.devices.reshape(-1), (DEV,))
    in_specs = (P(DEV, None), P(DEV, None), P(), P(), P(), P(DEV), P(DEV))
    return jax.shard_map(
        shards, mesh=line, in_specs=in_specs, out_specs=(P(DEV, None),) * 4, check_vma=False
    )
```

```python
import jax
import jax.numpy as jnp
from jax import lax
from jax.experimental import pallas as pl
from jax.experimental.pallas import tpu as pltpu
from jax.sharding import PartitionSpec as P

logit_scale = 64.0
epsilon = 1e-06
log2e = 1.4426950408889634
f32, b16 = jnp.float32, jnp.bfloat16

DEV = "dev"
PLACES = [
    (z, lo, hi, y, c)
    for z in range(4)
    for lo in range(2)
    for hi in range(2)
    for y in range(4)
    for c in range(2)
]


def flat(z, lo, hi, y, c):
    return (z * 2 + lo) * 16 + hi * 8 + y * 2 + c


def img_move(d, e):
    return lambda z, lo, hi, y, c: ((z + d) % 4, lo ^ e, hi, y, c)


def txt_move(d, e):
    return lambda z, lo, hi, y, c: (z, lo ^ e, hi ^ e, (y + d) % 4, c)


def core_move(z, lo, hi, y, c):
    return (z, lo, hi, y, 1 - c)


IMG_GROUPS = [
    [flat(z, lo, hi, y, c) for z in range(4) for lo in range(2)]
    for hi in range(2)
    for y in range(4)
    for c in range(2)
]
TXT_GROUPS = [
    [flat(z, hi ^ b, hi, y, c) for y in range(4) for hi in range(2)]
    for z in range(4)
    for b in range(2)
    for c in range(2)
]
TXT_CORE_GROUPS = [
    [flat(z, hi ^ b, hi, y, c) for c in range(2) for y in range(4) for hi in range(2)]
    for z in range(4)
    for b in range(2)
]
CHIP_GROUPS = [[flat(*p) for p in PLACES if p[4] == c] for c in range(2)]


def send(block, move):
    return lax.ppermute(block, DEV, [(flat(*p), flat(*move(*p))) for p in PLACES])


def exchange(blocks, groups):
    return lax.all_to_all(blocks, DEV, 0, 0, axis_index_groups=groups, tiled=True)


PAD = 16
NN = (((1,), (0,)), ((), ()))
NT = (((1,), (1,)), ((), ()))
TN = (((0,), (0,)), ((), ()))


def dot(a, b, dims):
    return lax.dot_general(a, b, dims, preferred_element_type=f32)


def call(body, out_shape, places, arrays, in_specs=None, out_specs=None, grid=(), scratch=(), cost=0, aliases=None, weight=1):
    whole = pl.BlockSpec(memory_space=pltpu.VMEM)
    many = isinstance(out_shape, (list, tuple))
    if in_specs is None:
        in_specs = [whole] * len(arrays)
    if out_specs is None:
        out_specs = [whole] * len(out_shape) if many else whole
    spec = pltpu.PrefetchScalarGridSpec(
        num_scalar_prefetch=0 if places is None else 1,
        grid=grid,
        in_specs=in_specs,
        out_specs=out_specs,
        scratch_shapes=list(scratch),
    )
    moved = weight * sum(a.size * a.dtype.itemsize for a in arrays)
    return pl.pallas_call(
        body,
        out_shape=out_shape,
        grid_spec=spec,
        input_output_aliases=aliases or {},
        compiler_params=pltpu.CompilerParams(vmem_limit_bytes=60 * 2**20),
        cost_estimate=pl.CostEstimate(flops=weight * cost, bytes_accessed=moved, transcendentals=0),
    )(*([] if places is None else [places]), *arrays)


def aligned(index, size):
    return pl.ds(pl.multiple_of(index * size, size), size)


def split_rows(total, lanes):
    high = total.astype(b16).astype(f32)
    row = lax.broadcasted_iota(jnp.int32, (PAD, lanes), 0)
    return jnp.where(row == 0, high, jnp.where(row == 1, total - high, 0.0)).astype(b16)


def joined(rows):
    return rows[0:1].astype(f32) + rows[1:2].astype(f32)


def in_pair(own, across, second, rows):
    own, across = own[:rows], across[:rows]
    first = second == 0
    return jnp.concatenate([jnp.where(first, own, across), jnp.where(first, across, own)], axis=0)


def put_units(feats, turned_head, proj, turned, norm):
    width = turned_head.shape[0]
    quarter = width // 4
    total = jnp.zeros((1, feats.shape[0]), f32)
    for m in range(4):
        span = slice(m * quarter, (m + 1) * quarter)
        part = dot(turned_head[span], feats[...], NT)
        proj[span] = part
        total = total + jnp.sum(part * part, axis=0, keepdims=True)
    length = jnp.sqrt(total + epsilon)
    norm[...] = length
    inverse = 1.0 / length
    for m in range(4):
        span = slice(m * quarter, (m + 1) * quarter)
        turned[span] = (proj[span] * inverse).astype(b16)


def unit_kernel(rows, pairs, at_ref, *refs):
    blocks, turned_head = refs[: 2 * pairs], refs[2 * pairs]
    turned, norm, feats, proj = refs[-4:]
    width = turned_head.shape[0]
    second = at_ref[1]
    step = pl.program_id(0)
    for p in range(pairs):
        own, across = blocks[2 * p], blocks[2 * p + 1]

        @pl.when(step == p)
        def _():
            feats[...] = in_pair(own, across, second, rows)
            first = second == 0
            sides = own[rows:, :rows], across[rows:, :rows]
            turned[width:, :rows] = jnp.where(first, sides[0], sides[1])
            turned[width:, rows:] = jnp.where(first, sides[1], sides[0])

    put_units(feats, turned_head, proj, turned, norm)


def units(pairs, distance, turned_head, carried, places, rows):
    width = turned_head.shape[0]
    tile = 2 * rows
    whole = lambda a: pl.BlockSpec(a.shape, lambda i, at: (0, 0))
    blocks = [block for pair in pairs for block in pair]
    return call(
        lambda *refs: unit_kernel(rows, len(pairs), *refs),
        [
            jax.ShapeDtypeStruct((width + PAD, 8 * rows), b16),
            jax.ShapeDtypeStruct((1, 8 * rows), f32),
        ],
        places,
        [*blocks, turned_head, *carried],
        in_specs=[whole(a) for a in [*blocks, turned_head]]
        + [pl.BlockSpec(memory_space=pl.ANY)] * len(carried),
        out_specs=[
            pl.BlockSpec((width + PAD, tile), lambda i, at: (0, (at[0] + distance + i) % 4)),
            pl.BlockSpec((1, tile), lambda i, at: (0, (at[0] + distance + i) % 4)),
        ],
        grid=(len(pairs),),
        scratch=[pltpu.VMEM((tile, width), b16), pltpu.VMEM((width, tile), f32)],
        cost=2 * tile * width * width * len(pairs),
        aliases={len(blocks) + 2 + n: n for n in range(len(carried))},
    )


def unit_columns(feats, head):
    projected = dot(head, feats, (((0,), (1,)), ((), ())))
    norm = jnp.sqrt(jnp.sum(projected * projected, axis=0, keepdims=True) + epsilon)
    return (projected / norm).astype(b16), norm


def unit_rows(feats, head, norm):
    return (dot(feats, head, NN) / norm.reshape(-1, 1)).astype(b16)


def tile_slopes(rows, groups, place, bias_ref, img, txt, slopes, by_img):
    width = img.shape[1]
    tile = 2 * rows
    lang = txt[width : width + PAD].astype(f32)
    partner = lang[1:2] * 128.0 + lang[2:3]
    lang = lang[0:1]
    bias = jnp.zeros((1, tile), f32)
    for g in range(groups):
        bias = jnp.where(lang == g, bias_ref[g], bias)
    bias = bias * -log2e
    down = jnp.zeros((1, tile), f32)
    high = 4 * rows
    for m in range(img.shape[0] // high):
        span = slice(m * high, (m + 1) * high)
        index = m * high + lax.broadcasted_iota(jnp.int32, (high, 1), 0)
        ids = ((index // rows * 16 + place) * rows + index % rows).astype(f32)
        cosines = dot(img[span], txt[:width], NN)
        below = 1.0 + jnp.exp2(cosines * (-log2e * logit_scale) + bias)
        gate = pl.reciprocal(below, approx=True)
        gate = gate * (2.0 - below * gate)
        slope = gate - jnp.where(partner == ids, 1.0, 0.0)
        slopes[span, :tile] = slope.astype(b16)
        weighted = slope * cosines
        down = down + jnp.sum(weighted, axis=0, keepdims=True)
        side = by_img[span]
        for k in range(0, tile, by_img.shape[1]):
            side = side + weighted[:, k : k + by_img.shape[1]]
        by_img[span] = side
    return logit_scale * down


def put_text_terms(up, turned, slopes, down):
    slab = turned.shape[0] // 8
    figures = split_rows(down, up.shape[1])
    part = dot(turned[...], slopes, NN)
    for e in range(8):
        at = e * (slab + PAD)
        up[at : at + slab] = part[e * slab : (e + 1) * slab].astype(b16)
        up[at + slab : at + slab + PAD] = figures


def other_kernel(rows, groups, bias_ref, img, turned, txt, slopes, img_sum, up, by_img):
    step = pl.program_id(0)

    @pl.when(step == 0)
    def _():
        by_img[...] = jnp.zeros(by_img.shape, f32)

    down = tile_slopes(rows, groups, bias_ref[groups].astype(jnp.int32), bias_ref, img, txt, slopes.at[0], by_img)
    put_text_terms(up, turned, slopes[0], down)

    @pl.when(step == 3)
    def _():
        img_sum[...] = logit_scale * jnp.sum(by_img[...].T, axis=0, keepdims=True)


def other_tile(img, turned, txt, group_bias, rows):
    count, width = img.shape
    tile = 2 * rows
    height = width + 8 * PAD
    whole = lambda a: pl.BlockSpec(a.shape, lambda i: (0, 0))
    return call(
        lambda *refs: other_kernel(rows, group_bias.shape[0] - 1, *refs),
        [
            jax.ShapeDtypeStruct((4, count, tile), b16),
            jax.ShapeDtypeStruct((1, count), f32),
            jax.ShapeDtypeStruct((height, count), b16),
        ],
        None,
        [group_bias, img, turned, txt],
        in_specs=[
            pl.BlockSpec(memory_space=pltpu.SMEM),
            whole(img),
            whole(turned),
            pl.BlockSpec((width + PAD, tile), lambda i: (0, i)),
        ],
        out_specs=[
            pl.BlockSpec((1, count, tile), lambda i: (i, 0, 0)),
            pl.BlockSpec((1, count), lambda i: (0, 0)),
            pl.BlockSpec((height, tile), lambda i: (0, i)),
        ],
        grid=(4,),
        scratch=[pltpu.VMEM((count, min(128, tile)), f32)],
        cost=4 * width * count * count,
    )


def own_kernel(rows, groups, bias_ref, img, turned, txt, other, *refs):
    other_slopes, other_sum, up, out, by_img, held, both, total = refs
    step = pl.program_id(0)
    width = img.shape[1]
    tile = 2 * rows

    @pl.when(step == 0)
    def _():
        by_img[...] = jnp.zeros(by_img.shape, f32)
        total[...] = jnp.zeros(total.shape, f32)

    both[:, tile:] = other[:width]
    held[:, tile:] = other_slopes[0]
    both[:, :tile] = txt[:width]
    down = tile_slopes(rows, groups, bias_ref[groups].astype(jnp.int32), bias_ref, img, txt, held, by_img)
    put_text_terms(up, turned, held[:, :tile], down)
    total[...] += dot(both[...], held[...], NT)

    @pl.when(step == 3)
    def _():
        slab = width // 8
        sums = logit_scale * jnp.sum(by_img[...].T, axis=0, keepdims=True) + other_sum[...]
        figures = split_rows(sums, sums.shape[1])
        for e in range(8):
            out[e, :slab] = total[e * slab : (e + 1) * slab].astype(b16)
            out[e, slab:] = figures


def own_tile(
    img, turned, txt, other, other_slopes, other_sum, group_bias, rows
):
    count, width = img.shape
    tile = 2 * rows
    height = width + 8 * PAD
    slab = width // 8
    whole = lambda a: pl.BlockSpec(a.shape, lambda i: (0, 0))
    stack = lambda a: pl.BlockSpec(a.shape, lambda i: (0, 0, 0))
    pieces = jax.ShapeDtypeStruct((8, slab + PAD, count), b16)
    return call(
        lambda *refs: own_kernel(rows, group_bias.shape[0] - 1, *refs),
        [jax.ShapeDtypeStruct((height, count), b16), pieces],
        None,
        [group_bias, img, turned, txt, other, other_slopes, other_sum],
        in_specs=[
            pl.BlockSpec(memory_space=pltpu.SMEM),
            whole(img),
            whole(turned),
            pl.BlockSpec((width + PAD, tile), lambda i: (0, i)),
            pl.BlockSpec((width + PAD, tile), lambda i: (0, i)),
            pl.BlockSpec((1, count, tile), lambda i: (i, 0, 0)),
            whole(other_sum),
        ],
        out_specs=[pl.BlockSpec((height, tile), lambda i: (0, i)), stack(pieces)],
        grid=(4,),
        scratch=[
            pltpu.VMEM((count, min(128, tile)), f32),
            pltpu.VMEM((count, 2 * tile), b16),
            pltpu.VMEM((width, 2 * tile), b16),
            pltpu.VMEM((width, count), f32),
        ],
        cost=8 * width * count * count,
    )


def sum_into(out, terms):
    slab = out.shape[0] - PAD
    block, total = terms[0][:slab].astype(f32), joined(terms[0][slab:])
    for term in terms[1:]:
        block, total = block + term[:slab].astype(f32), total + joined(term[slab:])
    out[:slab] = block.astype(b16)
    out[slab:] = split_rows(total, out.shape[1])


def sum_kernel(sizes, at_ref, *refs):
    start = 0
    for size, out in zip(sizes, refs[sum(sizes) :]):
        sum_into(out, refs[start : start + size])
        start += size


def sums(groups, places, rows):
    arrays, specs = [], []
    lanes = 4 * rows
    for term in [term for group in groups for term in group]:
        if isinstance(term, tuple):
            arrays.append(term[0])
            height = term[0].shape[0] // 8
            specs.append(pl.BlockSpec((height, lanes), lambda i, at, n=term[1]: (at[n], i)))
        else:
            arrays.append(term)
            height = term.shape[0]
            specs.append(pl.BlockSpec((height, lanes), lambda i, at: (0, i)))
    count = arrays[0].shape[1]
    return call(
        lambda *refs: sum_kernel([len(group) for group in groups], *refs),
        [jax.ShapeDtypeStruct((height, count), b16)] * len(groups),
        places,
        arrays,
        in_specs=specs,
        out_specs=[pl.BlockSpec((height, lanes), lambda i, at: (0, i))] * len(groups),
        grid=(count // lanes,),
    )


def img_grad_kernel(rows, at_ref, got, unit, norm, feats_from, blocks, part, grad, feats, sem):
    copy = pltpu.make_async_copy(feats_from, feats, sem.at[0])
    copy.start()
    slab = unit.shape[0]
    up, inner = got[0, :slab].astype(f32), joined(got[0, slab:])
    for n in range(1, 8):
        up, inner = up + got[n, :slab].astype(f32), inner + joined(got[n, slab:])
    up = logit_scale * up - unit[...].astype(f32) * inner
    grad[...] = (up * (1.0 / norm[...])).astype(b16)
    for n in range(8):
        blocks[n] = grad[:, n * rows : (n + 1) * rows]
    copy.wait()
    part[...] = dot(grad[...], feats[...], NN).astype(b16)


def txt_grad_kernel(rows, at_ref, *refs):
    terms, unit, norm, sources, (own, give, part, grad, feats, sem) = (
        refs[:5], refs[5], refs[6], refs[7:15], refs[15:]
    )
    blocks = [feats.at[n] for n in range(8)]
    copies = [pltpu.make_async_copy(sources[n], blocks[n], sem.at[n]) for n in range(8)]
    for copy in copies:
        copy.start()
    slab = unit.shape[0]
    up, inner = terms[0][:slab].astype(f32), joined(terms[0][slab:])
    for term in terms[1:]:
        up, inner = up + term[:slab].astype(f32), inner + joined(term[slab:])
    up = logit_scale * up - unit[...].astype(f32) * inner
    grad[...] = (up * (1.0 / norm[...])).astype(b16)
    for ring in range(4):
        low = grad[:, (2 * ring) * rows : (2 * ring + 1) * rows]
        high = grad[:, (2 * ring + 1) * rows : (2 * ring + 2) * rows]
        own[ring] = jnp.where(at_ref[1] == 0, low, high)
        give[ring] = jnp.where(at_ref[1] == 0, high, low)
    for copy in copies:
        copy.wait()
    total = None
    for d in range(4):
        cols = grad[:, aligned((at_ref[0] + d) % 4, 2 * rows)]
        term = dot(cols, in_pair(blocks[2 * d], blocks[2 * d + 1], at_ref[1], rows), NN)
        total = term if total is None else total + term
    part[...] = total.astype(b16)


def gradient(kernel, own, terms, unit, norm, feats, halves, places, rows):
    width = feats[0].shape[1]
    slab, count = width // 8, 8 * rows
    whole = lambda a: pl.BlockSpec(a.shape, lambda i, at: (0,) * len(a.shape))
    mine = lambda height: pl.BlockSpec((height, count), lambda i, at: (at[own], 0))
    block = jax.ShapeDtypeStruct((8 // halves, slab, rows), b16)
    part = jax.ShapeDtypeStruct((slab, width), b16)
    return call(
        lambda *refs: kernel(rows, *refs),
        [block] * halves + [part],
        places,
        [term[0] if isinstance(term, tuple) else term for term in terms] + [unit, norm, *feats],
        in_specs=[mine(slab + PAD) if isinstance(term, tuple) else whole(term) for term in terms]
        + [mine(slab), whole(norm)]
        + [pl.BlockSpec(memory_space=pl.ANY)] * len(feats),
        out_specs=[whole(block)] * halves + [whole(part)],
        grid=(1,),
        scratch=[
            pltpu.VMEM((slab, count), b16),
            pltpu.VMEM(((len(feats),) if len(feats) > 1 else ()) + feats[0].shape, b16),
            pltpu.SemaphoreType.DMA((len(feats),)),
        ],
        cost=2 * slab * count * width,
        weight=0,
    )


def pick_kernel(core, img, txt, other_img, other_txt, out):
    width = img.shape[1]
    slots = out.shape[0]
    own = width // 128
    third = 2 * img.shape[0] // 3
    img = img[...].astype(f32) + other_img[...].astype(f32)
    txt = txt[...].astype(f32) + other_txt[...].astype(f32)
    part = jnp.concatenate([img, txt], axis=0).astype(b16)
    slot = lax.broadcasted_iota(jnp.int32, (slots, 1), 0)
    feature = lax.broadcasted_iota(jnp.int32, (slots, width), 1)
    base = (slot // 8 * 2 + core[0]) * own
    chosen = jnp.where(feature == base + slot % 8, 1.0, 0.0).astype(b16)
    out[:, : 3 * third] = dot(chosen, part, NT).astype(b16)
    chosen = jnp.where(feature == base + 8, 1.0, 0.0).astype(b16)
    ninth = dot(chosen, part, NT)
    pick = slot % 8
    rest = jnp.where(pick == 1, ninth[:, third : 2 * third], ninth[:, :third])
    rest = jnp.where(pick == 2, ninth[:, 2 * third :], rest)
    out[:, 3 * third :] = rest.astype(b16)


def picked(core, parts):
    slab, width = parts[0].shape
    return call(
        pick_kernel,
        jax.ShapeDtypeStruct((64 * 8, slab * 8 // 3), b16),
        None,
        [core, *parts],
        in_specs=[pl.BlockSpec(memory_space=pltpu.SMEM)]
        + [pl.BlockSpec(memory_space=pltpu.VMEM)] * len(parts),
        cost=8 * 512 * width * slab,
        weight=0,
    )


def head_kernel(got, img_out, txt_out):
    slab = img_out.shape[1] // 8
    third = slab * 2 // 3
    half = third // 2
    for p in range(8):
        img = txt = None
        for other in range(8):
            z, lo, hi, y = p // 2, p % 2, other // 4, other % 4
            block = got[(z * 2 + lo) * 8 + hi * 4 + y].astype(f32)
            img = block if img is None else img + block
            z, lo, hi, y = other // 2, other % 2, p % 2, p // 2
            block = got[(z * 2 + lo) * 8 + hi * 4 + y].astype(f32)
            txt = block if txt is None else txt + block
        at = p * slab
        ninth = 2 * slab
        img_out[0:8, at : at + slab] = img[:, :slab]
        img_out[8:9, at : at + third] = img[0:1, ninth : ninth + third]
        img_out[8:9, at + third : at + slab] = img[1:2, ninth : ninth + half]
        txt_out[0:8, at : at + slab] = txt[:, slab : 2 * slab]
        txt_out[8:9, at : at + half] = txt[1:2, ninth + half : ninth + third]
        txt_out[8:9, at + half : at + slab] = txt[2:3, ninth : ninth + third]


def together(arrays):
    return lax.optimization_barrier(list(arrays))


def pair_lines(own, got, second):
    return jnp.concatenate([jnp.where(second, got, own), jnp.where(second, own, got)], axis=1)


def whole_columns(lines, move, ring):
    got = []
    for d in range(4):
        block = lax.dynamic_index_in_dim(lines, (ring + d) % 4, 0, keepdims=False)
        got.append(send(block, move(d, 0)) if d else block)
    height = got[0].shape[0]
    from_own = jnp.concatenate([got[-d % 4] for d in range(4)] * 2, axis=0)
    return lax.dynamic_slice_in_dim(from_own, (4 - ring) % 4 * height, 4 * height, axis=0)


def shards(image_feat, text_feat, image_head, text_head, group_bias, text_lang, partner):
    rows, width = image_feat.shape
    slab = width // 8
    place = lax.axis_index(DEV)
    z, lo, hi, y, core = place // 32, place // 16 % 2, place // 8 % 2, place // 2 % 4, place % 2

    slots = [(y + d) % 4 * 2 + (hi + e) % 2 for d in range(4) for e in range(2)]
    places = [y, hi, z, lo, core, place % 16, z * 2 + lo, y * 2 + hi, *slots]
    biases = jnp.append(group_bias, (place % 16).astype(f32))
    places, biases, alone = together(
        [jnp.stack(places).astype(jnp.int32), biases, core.astype(jnp.int32).reshape(1)]
    )
    figures = jnp.stack([text_lang, partner // 128, partner % 128]).astype(b16)
    figures = jnp.pad(figures, ((0, PAD - 3), (0, width - rows)))
    text_rows = jnp.concatenate([text_feat, figures], axis=0)
    img_feats = exchange(jnp.broadcast_to(image_feat[None], (8, rows, width)), IMG_GROUPS)
    img_feats = img_feats.reshape(8 * rows, width)
    across = send(text_rows, txt_move(0, 1))
    before = send(text_rows, txt_move(1, 0))
    after = send(text_rows, txt_move(3, 0))
    turned_txt = together([text_head, before])[0].T
    across_after = send(across, txt_move(3, 0))
    across_before = send(across, txt_move(1, 0))
    across_after, before, after, across, turned_txt = together(
        [across_after, before, after, across, turned_txt]
    )
    far = send(before, txt_move(1, 0))
    across_far = send(across_after, txt_move(3, 0))
    txt_blocks = [
        text_rows, across, after, across_after, far, across_far, before, across_before
    ]
    pairs = [(before, across_before), (text_rows, across), (after, across_after)]
    made = units(pairs, 3, turned_txt, (), places, rows)
    unit_txt, norm_txt = units([(far, across_far)], 2, turned_txt, made, places, rows)
    other_txt = send(unit_txt, core_move)
    turned_units, norm_img = unit_columns(img_feats, image_head)
    unit_img = unit_rows(together([img_feats, unit_txt])[0], image_head, norm_img)

    other_slopes, other_sum, other_up = other_tile(
        unit_img, turned_units, other_txt, biases, rows
    )
    back = send(other_up, core_move)
    text_up, img_terms = own_tile(
        unit_img, turned_units, unit_txt, other_txt, other_slopes, other_sum, biases, rows
    )
    img_terms = exchange(img_terms, IMG_GROUPS)

    def slab_terms(d, e):
        return [(text_up, 8 + 2 * d + e), (back, 8 + 2 * d + e)]

    far, across_far, across_after = sums(
        [slab_terms(2, 0), slab_terms(2, 1), slab_terms(1, 1)], places, rows
    )
    far = send(far, txt_move(1, 0))
    across_far = send(across_far, txt_move(3, 0))
    far, across_far, across_after = together([far, across_far, across_after])
    across_before = send(across_after, txt_move(1, 0))
    across_after, before, after = sums(
        [slab_terms(3, 1) + [across_far], slab_terms(1, 0) + [far], slab_terms(3, 0)], places, rows
    )
    across_after = send(across_after, txt_move(3, 0))
    across_before, across_after, before, after = together(
        [across_before, across_after, before, after]
    )
    before = send(before, txt_move(1, 0))
    after = send(after, txt_move(3, 0))
    (across,) = sums([slab_terms(0, 1) + [across_before, across_after]], places, rows)
    across = send(across, txt_move(0, 1))

    img_blocks, img_part = gradient(
        img_grad_kernel, 6, [img_terms], turned_units, norm_img, [img_feats], 1, places, rows
    )
    grad_img = exchange(img_blocks, IMG_GROUPS).reshape(width, rows)
    txt_own, txt_give, txt_part = gradient(
        txt_grad_kernel, 7, slab_terms(0, 0) + [before, after, across], unit_txt, norm_txt,
        txt_blocks, 2, places, rows,
    )
    img_theirs = send(img_part, core_move)
    txt_theirs = send(txt_part, core_move)
    txt_got = send(txt_give, txt_move(0, 1))
    heads, txt_got = together([picked(alone, [img_part, txt_part, img_theirs, txt_theirs]), txt_got])
    heads = exchange(heads.reshape(64, 8, -1), CHIP_GROUPS)
    head_shape = jax.ShapeDtypeStruct((width // 128, width), f32)
    image_head_grad, text_head_grad = call(head_kernel, [head_shape] * 2, None, [heads])

    image_grad = dot(grad_img, image_head, (((0,), (1,)), ((), ())))
    grad_txt = whole_columns(pair_lines(txt_own, txt_got, hi), txt_move, y)
    text_grad = dot(grad_txt, text_head, (((0,), (1,)), ((), ())))
    return (image_grad, text_grad, image_head_grad, text_head_grad)


def solution(mesh):
    line = jax.sharding.Mesh(mesh.devices.reshape(-1), (DEV,))
    in_specs = (P(DEV, None), P(DEV, None), P(), P(), P(), P(DEV), P(DEV))
    return jax.shard_map(
        shards, mesh=line, in_specs=in_specs, out_specs=(P(DEV, None),) * 4, check_vma=False
    )
```

```python
import jax
import jax.numpy as jnp
from jax import lax
from jax.experimental import pallas as pl
from jax.experimental.pallas import tpu as pltpu
from jax.sharding import PartitionSpec as P

logit_scale = 64.0
epsilon = 1e-06
log2e = 1.4426950408889634
f32, b16 = jnp.float32, jnp.bfloat16

DEV = "dev"
PLACES = [
    (z, lo, hi, y, c)
    for z in range(4)
    for lo in range(2)
    for hi in range(2)
    for y in range(4)
    for c in range(2)
]


def flat(z, lo, hi, y, c):
    return (z * 2 + lo) * 16 + hi * 8 + y * 2 + c


def img_move(d, e):
    return lambda z, lo, hi, y, c: ((z + d) % 4, lo ^ e, hi, y, c)


def txt_move(d, e):
    return lambda z, lo, hi, y, c: (z, lo ^ e, hi ^ e, (y + d) % 4, c)


def core_move(z, lo, hi, y, c):
    return (z, lo, hi, y, 1 - c)


IMG_GROUPS = [
    [flat(z, lo, hi, y, c) for z in range(4) for lo in range(2)]
    for hi in range(2)
    for y in range(4)
    for c in range(2)
]
TXT_GROUPS = [
    [flat(z, hi ^ b, hi, y, c) for y in range(4) for hi in range(2)]
    for z in range(4)
    for b in range(2)
    for c in range(2)
]
TXT_CORE_GROUPS = [
    [flat(z, hi ^ b, hi, y, c) for c in range(2) for y in range(4) for hi in range(2)]
    for z in range(4)
    for b in range(2)
]
CHIP_GROUPS = [[flat(*p) for p in PLACES if p[4] == c] for c in range(2)]


def send(block, move):
    return lax.ppermute(block, DEV, [(flat(*p), flat(*move(*p))) for p in PLACES])


def exchange(blocks, groups):
    return lax.all_to_all(blocks, DEV, 0, 0, axis_index_groups=groups, tiled=True)


PAD = 16
NN = (((1,), (0,)), ((), ()))
NT = (((1,), (1,)), ((), ()))
TN = (((0,), (0,)), ((), ()))


def dot(a, b, dims):
    return lax.dot_general(a, b, dims, preferred_element_type=f32)


def call(body, out_shape, places, arrays, in_specs=None, out_specs=None, grid=(), scratch=(), cost=0, aliases=None, weight=1):
    whole = pl.BlockSpec(memory_space=pltpu.VMEM)
    many = isinstance(out_shape, (list, tuple))
    if in_specs is None:
        in_specs = [whole] * len(arrays)
    if out_specs is None:
        out_specs = [whole] * len(out_shape) if many else whole
    spec = pltpu.PrefetchScalarGridSpec(
        num_scalar_prefetch=0 if places is None else 1,
        grid=grid,
        in_specs=in_specs,
        out_specs=out_specs,
        scratch_shapes=list(scratch),
    )
    moved = weight * sum(a.size * a.dtype.itemsize for a in arrays)
    return pl.pallas_call(
        body,
        out_shape=out_shape,
        grid_spec=spec,
        input_output_aliases=aliases or {},
        compiler_params=pltpu.CompilerParams(vmem_limit_bytes=60 * 2**20),
        cost_estimate=pl.CostEstimate(flops=weight * cost, bytes_accessed=moved, transcendentals=0),
    )(*([] if places is None else [places]), *arrays)


def aligned(index, size):
    return pl.ds(pl.multiple_of(index * size, size), size)


def split_rows(total, lanes):
    high = total.astype(b16).astype(f32)
    row = lax.broadcasted_iota(jnp.int32, (PAD, lanes), 0)
    return jnp.where(row == 0, high, jnp.where(row == 1, total - high, 0.0)).astype(b16)


def joined(rows):
    return rows[0:1].astype(f32) + rows[1:2].astype(f32)


def in_pair(own, across, second, rows):
    own, across = own[:rows], across[:rows]
    first = second == 0
    return jnp.concatenate([jnp.where(first, own, across), jnp.where(first, across, own)], axis=0)


def put_units(feats, turned_head, proj, turned, norm):
    width = turned_head.shape[0]
    quarter = width // 4
    total = jnp.zeros((1, feats.shape[0]), f32)
    for m in range(4):
        span = slice(m * quarter, (m + 1) * quarter)
        part = dot(turned_head[span], feats[...], NT)
        proj[span] = part
        total = total + jnp.sum(part * part, axis=0, keepdims=True)
    length = jnp.sqrt(total + epsilon)
    norm[...] = length
    inverse = 1.0 / length
    for m in range(4):
        span = slice(m * quarter, (m + 1) * quarter)
        turned[span] = (proj[span] * inverse).astype(b16)


def unit_kernel(rows, pairs, at_ref, *refs):
    blocks, turned_head = refs[: 2 * pairs], refs[2 * pairs]
    turned, norm, feats, proj = refs[-4:]
    width = turned_head.shape[0]
    second = at_ref[1]
    step = pl.program_id(0)
    for p in range(pairs):
        own, across = blocks[2 * p], blocks[2 * p + 1]

        @pl.when(step == p)
        def _():
            feats[...] = in_pair(own, across, second, rows)
            first = second == 0
            sides = own[rows:, :rows], across[rows:, :rows]
            turned[width:, :rows] = jnp.where(first, sides[0], sides[1])
            turned[width:, rows:] = jnp.where(first, sides[1], sides[0])

    put_units(feats, turned_head, proj, turned, norm)


def units(pairs, distance, turned_head, carried, places, rows):
    width = turned_head.shape[0]
    tile = 2 * rows
    whole = lambda a: pl.BlockSpec(a.shape, lambda i, at: (0, 0))
    blocks = [block for pair in pairs for block in pair]
    return call(
        lambda *refs: unit_kernel(rows, len(pairs), *refs),
        [
            jax.ShapeDtypeStruct((width + PAD, 8 * rows), b16),
            jax.ShapeDtypeStruct((1, 8 * rows), f32),
        ],
        places,
        [*blocks, turned_head, *carried],
        in_specs=[whole(a) for a in [*blocks, turned_head]]
        + [pl.BlockSpec(memory_space=pl.ANY)] * len(carried),
        out_specs=[
            pl.BlockSpec((width + PAD, tile), lambda i, at: (0, (at[0] + distance + i) % 4)),
            pl.BlockSpec((1, tile), lambda i, at: (0, (at[0] + distance + i) % 4)),
        ],
        grid=(len(pairs),),
        scratch=[pltpu.VMEM((tile, width), b16), pltpu.VMEM((width, tile), f32)],
        cost=2 * tile * width * width * len(pairs),
        aliases={len(blocks) + 2 + n: n for n in range(len(carried))},
    )


def unit_columns(feats, head):
    projected = dot(head, feats, (((0,), (1,)), ((), ())))
    norm = jnp.sqrt(jnp.sum(projected * projected, axis=0, keepdims=True) + epsilon)
    return (projected * (1.0 / norm)).astype(b16), norm


def unit_rows(feats, head, norm):
    return (dot(feats, head, NN) * (1.0 / norm).reshape(-1, 1)).astype(b16)


def tile_slopes(rows, groups, place, bias_ref, img, txt, slopes, by_img):
    width = img.shape[1]
    tile = 2 * rows
    lang = txt[width : width + PAD].astype(f32)
    partner = lang[1:2] * 128.0 + lang[2:3]
    lang = lang[0:1]
    bias = jnp.zeros((1, tile), f32)
    for g in range(groups):
        bias = jnp.where(lang == g, bias_ref[g], bias)
    bias = bias * -log2e
    down = jnp.zeros((1, tile), f32)
    high = 4 * rows
    for m in range(img.shape[0] // high):
        span = slice(m * high, (m + 1) * high)
        index = m * high + lax.broadcasted_iota(jnp.int32, (high, 1), 0)
        ids = ((index // rows * 16 + place) * rows + index % rows).astype(f32)
        cosines = dot(img[span], txt[:width], NN)
        below = 1.0 + jnp.exp2(cosines * (-log2e * logit_scale) + bias)
        gate = pl.reciprocal(below, approx=True)
        gate = gate * (2.0 - below * gate)
        slope = gate - jnp.where(partner == ids, 1.0, 0.0)
        slopes[span, :tile] = slope.astype(b16)
        weighted = slope * cosines
        down = down + jnp.sum(weighted, axis=0, keepdims=True)
        side = by_img[span]
        for k in range(0, tile, by_img.shape[1]):
            side = side + weighted[:, k : k + by_img.shape[1]]
        by_img[span] = side
    return logit_scale * down


def put_text_terms(up, turned, slopes, down):
    slab = turned.shape[0] // 8
    figures = split_rows(down, up.shape[1])
    part = dot(turned[...], slopes, NN)
    for e in range(8):
        at = e * (slab + PAD)
        up[at : at + slab] = part[e * slab : (e + 1) * slab].astype(b16)
        up[at + slab : at + slab + PAD] = figures


def other_kernel(rows, groups, bias_ref, img, turned, txt, slopes, img_sum, up, by_img):
    step = pl.program_id(0)

    @pl.when(step == 0)
    def _():
        by_img[...] = jnp.zeros(by_img.shape, f32)

    down = tile_slopes(rows, groups, bias_ref[groups].astype(jnp.int32), bias_ref, img, txt, slopes.at[0], by_img)
    put_text_terms(up, turned, slopes[0], down)

    @pl.when(step == 3)
    def _():
        img_sum[...] = logit_scale * jnp.sum(by_img[...].T, axis=0, keepdims=True)


def other_tile(img, turned, txt, group_bias, rows):
    count, width = img.shape
    tile = 2 * rows
    height = width + 8 * PAD
    whole = lambda a: pl.BlockSpec(a.shape, lambda i: (0, 0))
    return call(
        lambda *refs: other_kernel(rows, group_bias.shape[0] - 1, *refs),
        [
            jax.ShapeDtypeStruct((4, count, tile), b16),
            jax.ShapeDtypeStruct((1, count), f32),
            jax.ShapeDtypeStruct((height, count), b16),
        ],
        None,
        [group_bias, img, turned, txt],
        in_specs=[
            pl.BlockSpec(memory_space=pltpu.SMEM),
            whole(img),
            whole(turned),
            pl.BlockSpec((width + PAD, tile), lambda i: (0, i)),
        ],
        out_specs=[
            pl.BlockSpec((1, count, tile), lambda i: (i, 0, 0)),
            pl.BlockSpec((1, count), lambda i: (0, 0)),
            pl.BlockSpec((height, tile), lambda i: (0, i)),
        ],
        grid=(4,),
        scratch=[pltpu.VMEM((count, min(128, tile)), f32)],
        cost=4 * width * count * count,
    )


def own_kernel(rows, groups, bias_ref, img, turned, txt, other, *refs):
    other_slopes, other_sum, up, out, by_img, held, both, total = refs
    step = pl.program_id(0)
    width = img.shape[1]
    tile = 2 * rows

    @pl.when(step == 0)
    def _():
        by_img[...] = jnp.zeros(by_img.shape, f32)
        total[...] = jnp.zeros(total.shape, f32)

    both[:, tile:] = other[:width]
    held[:, tile:] = other_slopes[0]
    both[:, :tile] = txt[:width]
    down = tile_slopes(rows, groups, bias_ref[groups].astype(jnp.int32), bias_ref, img, txt, held, by_img)
    put_text_terms(up, turned, held[:, :tile], down)
    total[...] += dot(both[...], held[...], NT)

    @pl.when(step == 3)
    def _():
        slab = width // 8
        sums = logit_scale * jnp.sum(by_img[...].T, axis=0, keepdims=True) + other_sum[...]
        figures = split_rows(sums, sums.shape[1])
        for e in range(8):
            out[e, :slab] = total[e * slab : (e + 1) * slab].astype(b16)
            out[e, slab:] = figures


def own_tile(
    img, turned, txt, other, other_slopes, other_sum, group_bias, rows
):
    count, width = img.shape
    tile = 2 * rows
    height = width + 8 * PAD
    slab = width // 8
    whole = lambda a: pl.BlockSpec(a.shape, lambda i: (0, 0))
    stack = lambda a: pl.BlockSpec(a.shape, lambda i: (0, 0, 0))
    pieces = jax.ShapeDtypeStruct((8, slab + PAD, count), b16)
    return call(
        lambda *refs: own_kernel(rows, group_bias.shape[0] - 1, *refs),
        [jax.ShapeDtypeStruct((height, count), b16), pieces],
        None,
        [group_bias, img, turned, txt, other, other_slopes, other_sum],
        in_specs=[
            pl.BlockSpec(memory_space=pltpu.SMEM),
            whole(img),
            whole(turned),
            pl.BlockSpec((width + PAD, tile), lambda i: (0, i)),
            pl.BlockSpec((width + PAD, tile), lambda i: (0, i)),
            pl.BlockSpec((1, count, tile), lambda i: (i, 0, 0)),
            whole(other_sum),
        ],
        out_specs=[pl.BlockSpec((height, tile), lambda i: (0, i)), stack(pieces)],
        grid=(4,),
        scratch=[
            pltpu.VMEM((count, min(128, tile)), f32),
            pltpu.VMEM((count, 2 * tile), b16),
            pltpu.VMEM((width, 2 * tile), b16),
            pltpu.VMEM((width, count), f32),
        ],
        cost=8 * width * count * count,
    )


def sum_into(out, terms):
    slab = out.shape[0] - PAD
    block, total = terms[0][:slab].astype(f32), joined(terms[0][slab:])
    for term in terms[1:]:
        block, total = block + term[:slab].astype(f32), total + joined(term[slab:])
    out[:slab] = block.astype(b16)
    out[slab:] = split_rows(total, out.shape[1])


def sum_kernel(sizes, at_ref, *refs):
    start = 0
    for size, out in zip(sizes, refs[sum(sizes) :]):
        sum_into(out, refs[start : start + size])
        start += size


def sums(groups, places, rows):
    arrays, specs = [], []
    lanes = 8 * rows
    for term in [term for group in groups for term in group]:
        if isinstance(term, tuple):
            arrays.append(term[0])
            height = term[0].shape[0] // 8
            specs.append(pl.BlockSpec((height, lanes), lambda i, at, n=term[1]: (at[n], i)))
        else:
            arrays.append(term)
            height = term.shape[0]
            specs.append(pl.BlockSpec((height, lanes), lambda i, at: (0, i)))
    count = arrays[0].shape[1]
    return call(
        lambda *refs: sum_kernel([len(group) for group in groups], *refs),
        [jax.ShapeDtypeStruct((height, count), b16)] * len(groups),
        places,
        arrays,
        in_specs=specs,
        out_specs=[pl.BlockSpec((height, lanes), lambda i, at: (0, i))] * len(groups),
        grid=(count // lanes,),
    )


def img_grad_kernel(rows, at_ref, got, unit, norm, feats, blocks, part, grad):
    slab = unit.shape[0]
    up, inner = got[0, :slab].astype(f32), joined(got[0, slab:])
    for n in range(1, 8):
        up, inner = up + got[n, :slab].astype(f32), inner + joined(got[n, slab:])
    up = logit_scale * up - unit[...].astype(f32) * inner
    grad[...] = (up * (1.0 / norm[...])).astype(b16)
    for n in range(8):
        blocks[n] = grad[:, n * rows : (n + 1) * rows]
    part[...] = dot(grad[...], feats[...], NN).astype(b16)


def txt_grad_kernel(rows, at_ref, *refs):
    terms, unit, norm, blocks, (own, give, part, grad) = (
        refs[:5], refs[5], refs[6], refs[7:15], refs[15:]
    )
    slab = unit.shape[0]
    up, inner = terms[0][:slab].astype(f32), joined(terms[0][slab:])
    for term in terms[1:]:
        up, inner = up + term[:slab].astype(f32), inner + joined(term[slab:])
    up = logit_scale * up - unit[...].astype(f32) * inner
    grad[...] = (up * (1.0 / norm[...])).astype(b16)
    for ring in range(4):
        low = grad[:, (2 * ring) * rows : (2 * ring + 1) * rows]
        high = grad[:, (2 * ring + 1) * rows : (2 * ring + 2) * rows]
        own[ring] = jnp.where(at_ref[1] == 0, low, high)
        give[ring] = jnp.where(at_ref[1] == 0, high, low)
    total = None
    for d in range(4):
        cols = grad[:, aligned((at_ref[0] + d) % 4, 2 * rows)]
        term = dot(cols, in_pair(blocks[2 * d], blocks[2 * d + 1], at_ref[1], rows), NN)
        total = term if total is None else total + term
    part[...] = total.astype(b16)


def gradient(kernel, own, terms, unit, norm, feats, halves, places, rows):
    width = feats[0].shape[1]
    slab, count = width // 8, 8 * rows
    whole = lambda a: pl.BlockSpec(a.shape, lambda i, at: (0,) * len(a.shape))
    mine = lambda height: pl.BlockSpec((height, count), lambda i, at: (at[own], 0))
    block = jax.ShapeDtypeStruct((8 // halves, slab, rows), b16)
    part = jax.ShapeDtypeStruct((slab, width), b16)
    return call(
        lambda *refs: kernel(rows, *refs),
        [block] * halves + [part],
        places,
        [term[0] if isinstance(term, tuple) else term for term in terms] + [unit, norm, *feats],
        in_specs=[mine(slab + PAD) if isinstance(term, tuple) else whole(term) for term in terms]
        + [mine(slab), whole(norm)]
        + [whole(a) for a in feats],
        out_specs=[whole(block)] * halves + [whole(part)],
        grid=(1,),
        scratch=[pltpu.VMEM((slab, count), b16)],
        cost=2 * slab * count * width,
        weight=0,
    )


def pick_kernel(core, img, txt, other_img, other_txt, out):
    width = img.shape[1]
    slots = out.shape[0]
    own = width // 128
    third = 2 * img.shape[0] // 3
    img = img[...].astype(f32) + other_img[...].astype(f32)
    txt = txt[...].astype(f32) + other_txt[...].astype(f32)
    part = jnp.concatenate([img, txt], axis=0).astype(b16)
    slot = lax.broadcasted_iota(jnp.int32, (slots, 1), 0)
    feature = lax.broadcasted_iota(jnp.int32, (slots, width), 1)
    base = (slot // 8 * 2 + core[0]) * own
    chosen = jnp.where(feature == base + slot % 8, 1.0, 0.0).astype(b16)
    out[:, : 3 * third] = dot(chosen, part, NT).astype(b16)
    chosen = jnp.where(feature == base + 8, 1.0, 0.0).astype(b16)
    ninth = dot(chosen, part, NT)
    pick = slot % 8
    rest = jnp.where(pick == 1, ninth[:, third : 2 * third], ninth[:, :third])
    rest = jnp.where(pick == 2, ninth[:, 2 * third :], rest)
    out[:, 3 * third :] = rest.astype(b16)


def picked(core, parts):
    slab, width = parts[0].shape
    return call(
        pick_kernel,
        jax.ShapeDtypeStruct((64 * 8, slab * 8 // 3), b16),
        None,
        [core, *parts],
        in_specs=[pl.BlockSpec(memory_space=pltpu.SMEM)]
        + [pl.BlockSpec(memory_space=pltpu.VMEM)] * len(parts),
        cost=8 * 512 * width * slab,
        weight=0,
    )


def head_kernel(got, img_out, txt_out):
    slab = img_out.shape[1] // 8
    third = slab * 2 // 3
    half = third // 2
    for p in range(8):
        img = txt = None
        for other in range(8):
            z, lo, hi, y = p // 2, p % 2, other // 4, other % 4
            block = got[(z * 2 + lo) * 8 + hi * 4 + y].astype(f32)
            img = block if img is None else img + block
            z, lo, hi, y = other // 2, other % 2, p % 2, p // 2
            block = got[(z * 2 + lo) * 8 + hi * 4 + y].astype(f32)
            txt = block if txt is None else txt + block
        at = p * slab
        ninth = 2 * slab
        img_out[0:8, at : at + slab] = img[:, :slab]
        img_out[8:9, at : at + third] = img[0:1, ninth : ninth + third]
        img_out[8:9, at + third : at + slab] = img[1:2, ninth : ninth + half]
        txt_out[0:8, at : at + slab] = txt[:, slab : 2 * slab]
        txt_out[8:9, at : at + half] = txt[1:2, ninth + half : ninth + third]
        txt_out[8:9, at + half : at + slab] = txt[2:3, ninth : ninth + third]


def together(arrays):
    return lax.optimization_barrier(list(arrays))


def pair_lines(own, got, second):
    return jnp.concatenate([jnp.where(second, got, own), jnp.where(second, own, got)], axis=1)


def whole_columns(lines, move, ring):
    got = []
    for d in range(4):
        block = lax.dynamic_index_in_dim(lines, (ring + d) % 4, 0, keepdims=False)
        got.append(send(block, move(d, 0)) if d else block)
    height = got[0].shape[0]
    from_own = jnp.concatenate([got[-d % 4] for d in range(4)] * 2, axis=0)
    return lax.dynamic_slice_in_dim(from_own, (4 - ring) % 4 * height, 4 * height, axis=0)


def shards(image_feat, text_feat, image_head, text_head, group_bias, text_lang, partner):
    rows, width = image_feat.shape
    slab = width // 8
    place = lax.axis_index(DEV)
    z, lo, hi, y, core = place // 32, place // 16 % 2, place // 8 % 2, place // 2 % 4, place % 2

    slots = [(y + d) % 4 * 2 + (hi + e) % 2 for d in range(4) for e in range(2)]
    places = [y, hi, z, lo, core, place % 16, z * 2 + lo, y * 2 + hi, *slots]
    biases = jnp.append(group_bias, (place % 16).astype(f32))
    places, biases, alone = together(
        [jnp.stack(places).astype(jnp.int32), biases, core.astype(jnp.int32).reshape(1)]
    )
    figures = jnp.stack([text_lang, partner // 128, partner % 128]).astype(b16)
    figures = jnp.pad(figures, ((0, PAD - 3), (0, width - rows)))
    text_rows = jnp.concatenate([text_feat, figures], axis=0)
    img_feats = exchange(jnp.broadcast_to(image_feat[None], (8, rows, width)), IMG_GROUPS)
    img_feats = img_feats.reshape(8 * rows, width)
    across = send(text_rows, txt_move(0, 1))
    before = send(text_rows, txt_move(1, 0))
    after = send(text_rows, txt_move(3, 0))
    turned_txt = together([text_head, before])[0].T
    across_after = send(across, txt_move(3, 0))
    across_before = send(across, txt_move(1, 0))
    across_after, before, after, across, turned_txt = together(
        [across_after, before, after, across, turned_txt]
    )
    far = send(before, txt_move(1, 0))
    across_far = send(across_after, txt_move(3, 0))
    txt_blocks = [
        text_rows, across, after, across_after, far, across_far, before, across_before
    ]
    pairs = [(before, across_before), (text_rows, across), (after, across_after)]
    made = units(pairs, 3, turned_txt, (), places, rows)
    unit_txt, norm_txt = units([(far, across_far)], 2, turned_txt, made, places, rows)
    other_txt = send(unit_txt, core_move)
    turned_units, norm_img = unit_columns(img_feats, image_head)
    unit_img = unit_rows(together([img_feats, unit_txt])[0], image_head, norm_img)

    other_slopes, other_sum, other_up = other_tile(
        unit_img, turned_units, other_txt, biases, rows
    )
    back = send(other_up, core_move)
    text_up, img_terms = own_tile(
        unit_img, turned_units, unit_txt, other_txt, other_slopes, other_sum, biases, rows
    )

    def slab_terms(d, e):
        return [(text_up, 8 + 2 * d + e), (back, 8 + 2 * d + e)]

    far, across_far, across_after = sums(
        [slab_terms(2, 0), slab_terms(2, 1), slab_terms(1, 1)], places, rows
    )
    far, across_far, across_after, img_terms = together([far, across_far, across_after, img_terms])
    img_terms = exchange(img_terms, IMG_GROUPS)
    far = send(far, txt_move(1, 0))
    across_far = send(across_far, txt_move(3, 0))
    far, across_far, across_after = together([far, across_far, across_after])
    across_before = send(across_after, txt_move(1, 0))
    across_after, before, after = sums(
        [slab_terms(3, 1) + [across_far], slab_terms(1, 0) + [far], slab_terms(3, 0)], places, rows
    )
    across_after = send(across_after, txt_move(3, 0))
    across_before, across_after, before, after = together(
        [across_before, across_after, before, after]
    )
    before = send(before, txt_move(1, 0))
    after = send(after, txt_move(3, 0))
    (across,) = sums([slab_terms(0, 1) + [across_before, across_after]], places, rows)
    across = send(across, txt_move(0, 1))

    img_blocks, img_part = gradient(
        img_grad_kernel, 6, [img_terms], turned_units, norm_img, [img_feats], 1, places, rows
    )
    grad_img = exchange(img_blocks, IMG_GROUPS).reshape(width, rows)
    txt_own, txt_give, txt_part = gradient(
        txt_grad_kernel, 7, slab_terms(0, 0) + [before, after, across], unit_txt, norm_txt,
        txt_blocks, 2, places, rows,
    )
    img_theirs = send(img_part, core_move)
    txt_theirs = send(txt_part, core_move)
    txt_got = send(txt_give, txt_move(0, 1))
    heads, txt_got = together([picked(alone, [img_part, txt_part, img_theirs, txt_theirs]), txt_got])
    heads = exchange(heads.reshape(64, 8, -1), CHIP_GROUPS)
    head_shape = jax.ShapeDtypeStruct((width // 128, width), f32)
    image_head_grad, text_head_grad = call(head_kernel, [head_shape] * 2, None, [heads])

    image_grad = dot(grad_img, image_head, (((0,), (1,)), ((), ())))
    grad_txt = whole_columns(pair_lines(txt_own, txt_got, hi), txt_move, y)
    text_grad = dot(grad_txt, text_head, (((0,), (1,)), ((), ())))
    return (image_grad, text_grad, image_head_grad, text_head_grad)


def solution(mesh):
    line = jax.sharding.Mesh(mesh.devices.reshape(-1), (DEV,))
    in_specs = (P(DEV, None), P(DEV, None), P(), P(), P(), P(DEV), P(DEV))
    return jax.shard_map(
        shards, mesh=line, in_specs=in_specs, out_specs=(P(DEV, None),) * 4, check_vma=False
    )
```

```python
import jax
import jax.numpy as jnp
from jax import lax
from jax.experimental import pallas as pl
from jax.experimental.pallas import tpu as pltpu
from jax.sharding import PartitionSpec as P

logit_scale = 64.0
epsilon = 1e-06
log2e = 1.4426950408889634
f32, b16 = jnp.float32, jnp.bfloat16

DEV = "dev"
PLACES = [
    (z, lo, hi, y, c)
    for z in range(4)
    for lo in range(2)
    for hi in range(2)
    for y in range(4)
    for c in range(2)
]


def flat(z, lo, hi, y, c):
    return (z * 2 + lo) * 16 + hi * 8 + y * 2 + c


def img_move(d, e):
    return lambda z, lo, hi, y, c: ((z + d) % 4, lo ^ e, hi, y, c)


def txt_move(d, e):
    return lambda z, lo, hi, y, c: (z, lo ^ e, hi ^ e, (y + d) % 4, c)


def core_move(z, lo, hi, y, c):
    return (z, lo, hi, y, 1 - c)


IMG_GROUPS = [
    [flat(z, lo, hi, y, c) for z in range(4) for lo in range(2)]
    for hi in range(2)
    for y in range(4)
    for c in range(2)
]
TXT_GROUPS = [
    [flat(z, hi ^ b, hi, y, c) for y in range(4) for hi in range(2)]
    for z in range(4)
    for b in range(2)
    for c in range(2)
]
TXT_CORE_GROUPS = [
    [flat(z, hi ^ b, hi, y, c) for c in range(2) for y in range(4) for hi in range(2)]
    for z in range(4)
    for b in range(2)
]
CHIP_GROUPS = [[flat(*p) for p in PLACES if p[4] == c] for c in range(2)]


def send(block, move):
    return lax.ppermute(block, DEV, [(flat(*p), flat(*move(*p))) for p in PLACES])


def exchange(blocks, groups):
    return lax.all_to_all(blocks, DEV, 0, 0, axis_index_groups=groups, tiled=True)


PAD = 16
NN = (((1,), (0,)), ((), ()))
NT = (((1,), (1,)), ((), ()))
TN = (((0,), (0,)), ((), ()))


def dot(a, b, dims):
    return lax.dot_general(a, b, dims, preferred_element_type=f32)


def call(body, out_shape, places, arrays, in_specs=None, out_specs=None, grid=(), scratch=(), cost=0, aliases=None, weight=1):
    whole = pl.BlockSpec(memory_space=pltpu.VMEM)
    many = isinstance(out_shape, (list, tuple))
    if in_specs is None:
        in_specs = [whole] * len(arrays)
    if out_specs is None:
        out_specs = [whole] * len(out_shape) if many else whole
    spec = pltpu.PrefetchScalarGridSpec(
        num_scalar_prefetch=0 if places is None else 1,
        grid=grid,
        in_specs=in_specs,
        out_specs=out_specs,
        scratch_shapes=list(scratch),
    )
    moved = weight * sum(a.size * a.dtype.itemsize for a in arrays)
    return pl.pallas_call(
        body,
        out_shape=out_shape,
        grid_spec=spec,
        input_output_aliases=aliases or {},
        compiler_params=pltpu.CompilerParams(vmem_limit_bytes=60 * 2**20),
        cost_estimate=pl.CostEstimate(flops=weight * cost, bytes_accessed=moved, transcendentals=0),
    )(*([] if places is None else [places]), *arrays)


def aligned(index, size):
    return pl.ds(pl.multiple_of(index * size, size), size)


def split_rows(total, lanes):
    high = total.astype(b16).astype(f32)
    row = lax.broadcasted_iota(jnp.int32, (PAD, lanes), 0)
    return jnp.where(row == 0, high, jnp.where(row == 1, total - high, 0.0)).astype(b16)


def joined(rows):
    return rows[0:1].astype(f32) + rows[1:2].astype(f32)


def in_pair(own, across, second, rows):
    own, across = own[:rows], across[:rows]
    first = second == 0
    return jnp.concatenate([jnp.where(first, own, across), jnp.where(first, across, own)], axis=0)


def put_units(feats, turned_head, proj, turned, norm):
    width = turned_head.shape[0]
    quarter = width // 4
    total = jnp.zeros((1, feats.shape[0]), f32)
    for m in range(4):
        span = slice(m * quarter, (m + 1) * quarter)
        part = dot(turned_head[span], feats[...], NT)
        proj[span] = part
        total = total + jnp.sum(part * part, axis=0, keepdims=True)
    length = jnp.sqrt(total + epsilon)
    norm[...] = length
    inverse = 1.0 / length
    for m in range(4):
        span = slice(m * quarter, (m + 1) * quarter)
        turned[span] = (proj[span] * inverse).astype(b16)


def unit_kernel(rows, pairs, at_ref, *refs):
    blocks, turned_head = refs[: 2 * pairs], refs[2 * pairs]
    turned, norm, feats, proj = refs[-4:]
    width = turned_head.shape[0]
    second = at_ref[1]
    step = pl.program_id(0)
    for p in range(pairs):
        own, across = blocks[2 * p], blocks[2 * p + 1]

        @pl.when(step == p)
        def _():
            feats[...] = in_pair(own, across, second, rows)
            first = second == 0
            sides = own[rows:, :rows], across[rows:, :rows]
            turned[width:, :rows] = jnp.where(first, sides[0], sides[1])
            turned[width:, rows:] = jnp.where(first, sides[1], sides[0])

    put_units(feats, turned_head, proj, turned, norm)


def units(pairs, distance, turned_head, carried, places, rows):
    width = turned_head.shape[0]
    tile = 2 * rows
    whole = lambda a: pl.BlockSpec(a.shape, lambda i, at: (0, 0))
    blocks = [block for pair in pairs for block in pair]
    return call(
        lambda *refs: unit_kernel(rows, len(pairs), *refs),
        [
            jax.ShapeDtypeStruct((width + PAD, 8 * rows), b16),
            jax.ShapeDtypeStruct((1, 8 * rows), f32),
        ],
        places,
        [*blocks, turned_head, *carried],
        in_specs=[whole(a) for a in [*blocks, turned_head]]
        + [pl.BlockSpec(memory_space=pl.ANY)] * len(carried),
        out_specs=[
            pl.BlockSpec((width + PAD, tile), lambda i, at: (0, (at[0] + distance + i) % 4)),
            pl.BlockSpec((1, tile), lambda i, at: (0, (at[0] + distance + i) % 4)),
        ],
        grid=(len(pairs),),
        scratch=[pltpu.VMEM((tile, width), b16), pltpu.VMEM((width, tile), f32)],
        cost=2 * tile * width * width * len(pairs),
        aliases={len(blocks) + 2 + n: n for n in range(len(carried))},
    )


def unit_columns(feats, head):
    projected = dot(head, feats, (((0,), (1,)), ((), ())))
    norm = jnp.sqrt(jnp.sum(projected * projected, axis=0, keepdims=True) + epsilon)
    return (projected * (1.0 / norm)).astype(b16), norm


def unit_rows(feats, head, norm):
    return (dot(feats, head, NN) * (1.0 / norm).reshape(-1, 1)).astype(b16)


def tile_slopes(rows, groups, place, bias_ref, img, txt, slopes, by_img):
    width = img.shape[1]
    tile = 2 * rows
    lang = txt[width : width + PAD].astype(f32)
    partner = lang[1:2] * 128.0 + lang[2:3]
    lang = lang[0:1]
    bias = jnp.zeros((1, tile), f32)
    for g in range(groups):
        bias = jnp.where(lang == g, bias_ref[g], bias)
    bias = bias * -log2e
    down = jnp.zeros((1, tile), f32)
    high = 4 * rows
    for m in range(img.shape[0] // high):
        span = slice(m * high, (m + 1) * high)
        index = m * high + lax.broadcasted_iota(jnp.int32, (high, 1), 0)
        ids = ((index // rows * 16 + place) * rows + index % rows).astype(f32)
        cosines = dot(img[span], txt[:width], NN)
        below = 1.0 + jnp.exp2(cosines * (-log2e * logit_scale) + bias)
        gate = pl.reciprocal(below, approx=True)
        gate = gate * (2.0 - below * gate)
        slope = gate - jnp.where(partner == ids, 1.0, 0.0)
        slopes[span, :tile] = slope.astype(b16)
        weighted = slope * cosines
        down = down + jnp.sum(weighted, axis=0, keepdims=True)
        side = by_img[span]
        for k in range(0, tile, by_img.shape[1]):
            side = side + weighted[:, k : k + by_img.shape[1]]
        by_img[span] = side
    return logit_scale * down


def put_text_terms(up, turned, slopes, down):
    slab = turned.shape[0] // 8
    figures = split_rows(down, up.shape[1])
    part = dot(turned[...], slopes, NN)
    for e in range(8):
        at = e * (slab + PAD)
        up[at : at + slab] = part[e * slab : (e + 1) * slab].astype(b16)
        up[at + slab : at + slab + PAD] = figures


def other_kernel(rows, groups, bias_ref, img, turned, txt, slopes, img_sum, up, by_img):
    step = pl.program_id(0)

    @pl.when(step == 0)
    def _():
        by_img[...] = jnp.zeros(by_img.shape, f32)

    down = tile_slopes(rows, groups, bias_ref[groups].astype(jnp.int32), bias_ref, img, txt, slopes.at[0], by_img)
    put_text_terms(up, turned, slopes[0], down)

    @pl.when(step == 3)
    def _():
        img_sum[...] = logit_scale * jnp.sum(by_img[...].T, axis=0, keepdims=True)


def other_tile(img, turned, txt, group_bias, rows):
    count, width = img.shape
    tile = 2 * rows
    height = width + 8 * PAD
    whole = lambda a: pl.BlockSpec(a.shape, lambda i: (0, 0))
    return call(
        lambda *refs: other_kernel(rows, group_bias.shape[0] - 1, *refs),
        [
            jax.ShapeDtypeStruct((4, count, tile), b16),
            jax.ShapeDtypeStruct((1, count), f32),
            jax.ShapeDtypeStruct((height, count), b16),
        ],
        None,
        [group_bias, img, turned, txt],
        in_specs=[
            pl.BlockSpec(memory_space=pltpu.SMEM),
            whole(img),
            whole(turned),
            pl.BlockSpec((width + PAD, tile), lambda i: (0, i)),
        ],
        out_specs=[
            pl.BlockSpec((1, count, tile), lambda i: (i, 0, 0)),
            pl.BlockSpec((1, count), lambda i: (0, 0)),
            pl.BlockSpec((height, tile), lambda i: (0, i)),
        ],
        grid=(4,),
        scratch=[pltpu.VMEM((count, min(128, tile)), f32)],
        cost=4 * width * count * count,
    )


def own_kernel(rows, groups, bias_ref, img, turned, txt, other, *refs):
    other_slopes, other_sum, up, out, by_img, held, both, total = refs
    step = pl.program_id(0)
    width = img.shape[1]
    tile = 2 * rows

    @pl.when(step == 0)
    def _():
        by_img[...] = jnp.zeros(by_img.shape, f32)
        total[...] = jnp.zeros(total.shape, f32)

    both[:, tile:] = other[:width]
    held[:, tile:] = other_slopes[0]
    both[:, :tile] = txt[:width]
    down = tile_slopes(rows, groups, bias_ref[groups].astype(jnp.int32), bias_ref, img, txt, held, by_img)
    put_text_terms(up, turned, held[:, :tile], down)
    total[...] += dot(both[...], held[...], NT)

    @pl.when(step == 3)
    def _():
        slab = width // 8
        sums = logit_scale * jnp.sum(by_img[...].T, axis=0, keepdims=True) + other_sum[...]
        figures = split_rows(sums, sums.shape[1])
        for e in range(8):
            out[e, :slab] = total[e * slab : (e + 1) * slab].astype(b16)
            out[e, slab:] = figures


def own_tile(
    img, turned, txt, other, other_slopes, other_sum, group_bias, rows
):
    count, width = img.shape
    tile = 2 * rows
    height = width + 8 * PAD
    slab = width // 8
    whole = lambda a: pl.BlockSpec(a.shape, lambda i: (0, 0))
    stack = lambda a: pl.BlockSpec(a.shape, lambda i: (0, 0, 0))
    pieces = jax.ShapeDtypeStruct((8, slab + PAD, count), b16)
    return call(
        lambda *refs: own_kernel(rows, group_bias.shape[0] - 1, *refs),
        [jax.ShapeDtypeStruct((height, count), b16), pieces],
        None,
        [group_bias, img, turned, txt, other, other_slopes, other_sum],
        in_specs=[
            pl.BlockSpec(memory_space=pltpu.SMEM),
            whole(img),
            whole(turned),
            pl.BlockSpec((width + PAD, tile), lambda i: (0, i)),
            pl.BlockSpec((width + PAD, tile), lambda i: (0, i)),
            pl.BlockSpec((1, count, tile), lambda i: (i, 0, 0)),
            whole(other_sum),
        ],
        out_specs=[pl.BlockSpec((height, tile), lambda i: (0, i)), stack(pieces)],
        grid=(4,),
        scratch=[
            pltpu.VMEM((count, min(128, tile)), f32),
            pltpu.VMEM((count, 2 * tile), b16),
            pltpu.VMEM((width, 2 * tile), b16),
            pltpu.VMEM((width, count), f32),
        ],
        cost=8 * width * count * count,
    )


def sum_into(out, terms):
    slab = out.shape[0] - PAD
    block, total = terms[0][:slab].astype(f32), joined(terms[0][slab:])
    for term in terms[1:]:
        block, total = block + term[:slab].astype(f32), total + joined(term[slab:])
    out[:slab] = block.astype(b16)
    out[slab:] = split_rows(total, out.shape[1])


def sum_kernel(sizes, at_ref, *refs):
    start = 0
    for size, out in zip(sizes, refs[sum(sizes) :]):
        sum_into(out, refs[start : start + size])
        start += size


def sums(groups, places, rows):
    arrays, specs = [], []
    lanes = 8 * rows
    for term in [term for group in groups for term in group]:
        if isinstance(term, tuple):
            arrays.append(term[0])
            height = term[0].shape[0] // 8
            specs.append(pl.BlockSpec((height, lanes), lambda i, at, n=term[1]: (at[n], i)))
        else:
            arrays.append(term)
            height = term.shape[0]
            specs.append(pl.BlockSpec((height, lanes), lambda i, at: (0, i)))
    count = arrays[0].shape[1]
    return call(
        lambda *refs: sum_kernel([len(group) for group in groups], *refs),
        [jax.ShapeDtypeStruct((height, count), b16)] * len(groups),
        places,
        arrays,
        in_specs=specs,
        out_specs=[pl.BlockSpec((height, lanes), lambda i, at: (0, i))] * len(groups),
        grid=(count // lanes,),
    )


def img_grad_kernel(rows, at_ref, got, unit, norm, feats, blocks, part, grad):
    slab = unit.shape[0]
    up, inner = got[0, :slab].astype(f32), joined(got[0, slab:])
    for n in range(1, 8):
        up, inner = up + got[n, :slab].astype(f32), inner + joined(got[n, slab:])
    up = logit_scale * up - unit[...].astype(f32) * inner
    grad[...] = (up * (1.0 / norm[...])).astype(b16)
    for n in range(8):
        blocks[n] = grad[:, n * rows : (n + 1) * rows]
    part[...] = dot(grad[...], feats[...], NN).astype(b16)


def txt_grad_kernel(rows, at_ref, *refs):
    terms, unit, norm, blocks, (own, give, part, grad) = (
        refs[:5], refs[5], refs[6], refs[7:15], refs[15:]
    )
    slab = unit.shape[0]
    up, inner = terms[0][:slab].astype(f32), joined(terms[0][slab:])
    for term in terms[1:]:
        up, inner = up + term[:slab].astype(f32), inner + joined(term[slab:])
    up = logit_scale * up - unit[...].astype(f32) * inner
    grad[...] = (up * (1.0 / norm[...])).astype(b16)
    for ring in range(4):
        low = grad[:, (2 * ring) * rows : (2 * ring + 1) * rows]
        high = grad[:, (2 * ring + 1) * rows : (2 * ring + 2) * rows]
        own[ring] = jnp.where(at_ref[1] == 0, low, high)
        give[ring] = jnp.where(at_ref[1] == 0, high, low)
    total = None
    for d in range(4):
        cols = grad[:, aligned((at_ref[0] + d) % 4, 2 * rows)]
        term = dot(cols, in_pair(blocks[2 * d], blocks[2 * d + 1], at_ref[1], rows), NN)
        total = term if total is None else total + term
    part[...] = total.astype(b16)


def gradient(kernel, own, terms, unit, norm, feats, halves, places, rows):
    width = feats[0].shape[1]
    slab, count = width // 8, 8 * rows
    whole = lambda a: pl.BlockSpec(a.shape, lambda i, at: (0,) * len(a.shape))
    mine = lambda height: pl.BlockSpec((height, count), lambda i, at: (at[own], 0))
    block = jax.ShapeDtypeStruct((8 // halves, slab, rows), b16)
    part = jax.ShapeDtypeStruct((slab, width), b16)
    return call(
        lambda *refs: kernel(rows, *refs),
        [block] * halves + [part],
        places,
        [term[0] if isinstance(term, tuple) else term for term in terms] + [unit, norm, *feats],
        in_specs=[mine(slab + PAD) if isinstance(term, tuple) else whole(term) for term in terms]
        + [mine(slab), whole(norm)]
        + [whole(a) for a in feats],
        out_specs=[whole(block)] * halves + [whole(part)],
        grid=(1,),
        scratch=[pltpu.VMEM((slab, count), b16)],
        cost=2 * slab * count * width,
        weight=0,
    )


def pick_kernel(core, img, txt, other_img, other_txt, out):
    width = img.shape[1]
    slots = out.shape[0]
    own = width // 128
    third = 2 * img.shape[0] // 3
    img = img[...].astype(f32) + other_img[...].astype(f32)
    txt = txt[...].astype(f32) + other_txt[...].astype(f32)
    part = jnp.concatenate([img, txt], axis=0).astype(b16)
    slot = lax.broadcasted_iota(jnp.int32, (slots, 1), 0)
    feature = lax.broadcasted_iota(jnp.int32, (slots, width), 1)
    base = (slot // 8 * 2 + core[0]) * own
    chosen = jnp.where(feature == base + slot % 8, 1.0, 0.0).astype(b16)
    out[:, : 3 * third] = dot(chosen, part, NT).astype(b16)
    chips = slots // 8
    chip = lax.broadcasted_iota(jnp.int32, (chips, 1), 0)
    feature = lax.broadcasted_iota(jnp.int32, (chips, width), 1)
    chosen = jnp.where(feature == (chip * 2 + core[0]) * own + 8, 1.0, 0.0).astype(b16)
    ninth = dot(chosen, part, NT)
    chip = lax.broadcasted_iota(jnp.int32, (slots, chips), 1)
    rest = jnp.zeros((slots, third), f32)
    for n in range(3):
        spread = jnp.where(slot == chip * 8 + n, 1.0, 0.0).astype(b16)
        rest = rest + dot(spread, ninth[:, n * third : (n + 1) * third].astype(b16), NN)
    out[:, 3 * third :] = rest.astype(b16)


def picked(core, parts):
    slab, width = parts[0].shape
    return call(
        pick_kernel,
        jax.ShapeDtypeStruct((64 * 8, slab * 8 // 3), b16),
        None,
        [core, *parts],
        in_specs=[pl.BlockSpec(memory_space=pltpu.SMEM)]
        + [pl.BlockSpec(memory_space=pltpu.VMEM)] * len(parts),
        cost=8 * 512 * width * slab,
        weight=0,
    )


def head_kernel(got, img_out, txt_out):
    slab = img_out.shape[1] // 8
    third = slab * 2 // 3
    half = third // 2
    for p in range(8):
        img = txt = None
        for other in range(8):
            z, lo, hi, y = p // 2, p % 2, other // 4, other % 4
            block = got[(z * 2 + lo) * 8 + hi * 4 + y].astype(f32)
            img = block if img is None else img + block
            z, lo, hi, y = other // 2, other % 2, p % 2, p // 2
            block = got[(z * 2 + lo) * 8 + hi * 4 + y].astype(f32)
            txt = block if txt is None else txt + block
        at = p * slab
        ninth = 2 * slab
        img_out[0:8, at : at + slab] = img[:, :slab]
        img_out[8:9, at : at + third] = img[0:1, ninth : ninth + third]
        img_out[8:9, at + third : at + slab] = img[1:2, ninth : ninth + half]
        txt_out[0:8, at : at + slab] = txt[:, slab : 2 * slab]
        txt_out[8:9, at : at + half] = txt[1:2, ninth + half : ninth + third]
        txt_out[8:9, at + half : at + slab] = txt[2:3, ninth : ninth + third]


def together(arrays):
    return lax.optimization_barrier(list(arrays))


def pair_lines(own, got, second):
    return jnp.concatenate([jnp.where(second, got, own), jnp.where(second, own, got)], axis=1)


def whole_columns(lines, move, ring):
    got = []
    for d in range(4):
        block = lax.dynamic_index_in_dim(lines, (ring + d) % 4, 0, keepdims=False)
        got.append(send(block, move(d, 0)) if d else block)
    height = got[0].shape[0]
    from_own = jnp.concatenate([got[-d % 4] for d in range(4)] * 2, axis=0)
    return lax.dynamic_slice_in_dim(from_own, (4 - ring) % 4 * height, 4 * height, axis=0)


def shards(image_feat, text_feat, image_head, text_head, group_bias, text_lang, partner):
    rows, width = image_feat.shape
    slab = width // 8
    place = lax.axis_index(DEV)
    z, lo, hi, y, core = place // 32, place // 16 % 2, place // 8 % 2, place // 2 % 4, place % 2

    slots = [(y + d) % 4 * 2 + (hi + e) % 2 for d in range(4) for e in range(2)]
    places = [y, hi, z, lo, core, place % 16, z * 2 + lo, y * 2 + hi, *slots]
    biases = jnp.append(group_bias, (place % 16).astype(f32))
    places, biases, alone = together(
        [jnp.stack(places).astype(jnp.int32), biases, core.astype(jnp.int32).reshape(1)]
    )
    figures = jnp.stack([text_lang, partner // 128, partner % 128]).astype(b16)
    figures = jnp.pad(figures, ((0, PAD - 3), (0, width - rows)))
    text_rows = jnp.concatenate([text_feat, figures], axis=0)
    img_feats = exchange(jnp.broadcast_to(image_feat[None], (8, rows, width)), IMG_GROUPS)
    img_feats = img_feats.reshape(8 * rows, width)
    across = send(text_rows, txt_move(0, 1))
    before = send(text_rows, txt_move(1, 0))
    after = send(text_rows, txt_move(3, 0))
    turned_txt = together([text_head, before])[0].T
    across_after = send(across, txt_move(3, 0))
    across_before = send(across, txt_move(1, 0))
    across_after, before, after, across, turned_txt = together(
        [across_after, before, after, across, turned_txt]
    )
    far = send(before, txt_move(1, 0))
    across_far = send(across_after, txt_move(3, 0))
    txt_blocks = [
        text_rows, across, after, across_after, far, across_far, before, across_before
    ]
    pairs = [(before, across_before), (text_rows, across), (after, across_after)]
    made = units(pairs, 3, turned_txt, (), places, rows)
    unit_txt, norm_txt = units([(far, across_far)], 2, turned_txt, made, places, rows)
    other_txt = send(unit_txt, core_move)
    turned_units, norm_img = unit_columns(img_feats, image_head)
    unit_img = unit_rows(together([img_feats, unit_txt])[0], image_head, norm_img)

    other_slopes, other_sum, other_up = other_tile(
        unit_img, turned_units, other_txt, biases, rows
    )
    back = send(other_up, core_move)
    text_up, img_terms = own_tile(
        unit_img, turned_units, unit_txt, other_txt, other_slopes, other_sum, biases, rows
    )

    def slab_terms(d, e):
        return [(text_up, 8 + 2 * d + e), (back, 8 + 2 * d + e)]

    far, across_far, across_after = sums(
        [slab_terms(2, 0), slab_terms(2, 1), slab_terms(1, 1)], places, rows
    )
    far, across_far, across_after, img_terms = together([far, across_far, across_after, img_terms])
    img_terms = exchange(img_terms, IMG_GROUPS)
    far = send(far, txt_move(1, 0))
    across_far = send(across_far, txt_move(3, 0))
    far, across_far, across_after = together([far, across_far, across_after])
    across_before = send(across_after, txt_move(1, 0))
    (across_after,) = sums([slab_terms(3, 1) + [across_far]], places, rows)
    across_after = send(across_after, txt_move(3, 0))
    far, across_before = together([far, across_before])
    before, after = sums([slab_terms(1, 0) + [far], slab_terms(3, 0)], places, rows)
    across_before, across_after, before, after = together(
        [across_before, across_after, before, after]
    )
    before = send(before, txt_move(1, 0))
    after = send(after, txt_move(3, 0))
    (across,) = sums([slab_terms(0, 1) + [across_before, across_after]], places, rows)
    across = send(across, txt_move(0, 1))

    img_blocks, img_part = gradient(
        img_grad_kernel, 6, [img_terms], turned_units, norm_img, [img_feats], 1, places, rows
    )
    grad_img = exchange(img_blocks, IMG_GROUPS).reshape(width, rows)
    txt_own, txt_give, txt_part = gradient(
        txt_grad_kernel, 7, slab_terms(0, 0) + [before, after, across], unit_txt, norm_txt,
        txt_blocks, 2, places, rows,
    )
    img_theirs = send(img_part, core_move)
    txt_theirs = send(txt_part, core_move)
    txt_got = send(txt_give, txt_move(0, 1))
    heads, txt_got = together([picked(alone, [img_part, txt_part, img_theirs, txt_theirs]), txt_got])
    heads = exchange(heads.reshape(64, 8, -1), CHIP_GROUPS)
    head_shape = jax.ShapeDtypeStruct((width // 128, width), f32)
    image_head_grad, text_head_grad = call(head_kernel, [head_shape] * 2, None, [heads])

    image_grad = dot(grad_img, image_head, (((0,), (1,)), ((), ())))
    grad_txt = whole_columns(pair_lines(txt_own, txt_got, hi), txt_move, y)
    text_grad = dot(grad_txt, text_head, (((0,), (1,)), ((), ())))
    return (image_grad, text_grad, image_head_grad, text_head_grad)


def solution(mesh):
    line = jax.sharding.Mesh(mesh.devices.reshape(-1), (DEV,))
    in_specs = (P(DEV, None), P(DEV, None), P(), P(), P(), P(DEV), P(DEV))
    return jax.shard_map(
        shards, mesh=line, in_specs=in_specs, out_specs=(P(DEV, None),) * 4, check_vma=False
    )
```

```python
import jax
import jax.numpy as jnp
from jax import lax
from jax.experimental import pallas as pl
from jax.experimental.pallas import tpu as pltpu
from jax.sharding import PartitionSpec as P

logit_scale = 64.0
epsilon = 1e-06
log2e = 1.4426950408889634
f32, b16 = jnp.float32, jnp.bfloat16

DEV = "dev"
PLACES = [
    (z, lo, hi, y, c)
    for z in range(4)
    for lo in range(2)
    for hi in range(2)
    for y in range(4)
    for c in range(2)
]


def flat(z, lo, hi, y, c):
    return (z * 2 + lo) * 16 + hi * 8 + y * 2 + c


def img_move(d, e):
    return lambda z, lo, hi, y, c: ((z + d) % 4, lo ^ e, hi, y, c)


def txt_move(d, e):
    return lambda z, lo, hi, y, c: (z, lo ^ e, hi ^ e, (y + d) % 4, c)


def core_move(z, lo, hi, y, c):
    return (z, lo, hi, y, 1 - c)


IMG_GROUPS = [
    [flat(z, lo, hi, y, c) for z in range(4) for lo in range(2)]
    for hi in range(2)
    for y in range(4)
    for c in range(2)
]
TXT_GROUPS = [
    [flat(z, hi ^ b, hi, y, c) for y in range(4) for hi in range(2)]
    for z in range(4)
    for b in range(2)
    for c in range(2)
]
TXT_CORE_GROUPS = [
    [flat(z, hi ^ b, hi, y, c) for c in range(2) for y in range(4) for hi in range(2)]
    for z in range(4)
    for b in range(2)
]
CHIP_GROUPS = [[flat(*p) for p in PLACES if p[4] == c] for c in range(2)]


def send(block, move):
    return lax.ppermute(block, DEV, [(flat(*p), flat(*move(*p))) for p in PLACES])


def exchange(blocks, groups):
    return lax.all_to_all(blocks, DEV, 0, 0, axis_index_groups=groups, tiled=True)


PAD = 16
NN = (((1,), (0,)), ((), ()))
NT = (((1,), (1,)), ((), ()))
TN = (((0,), (0,)), ((), ()))


def dot(a, b, dims):
    return lax.dot_general(a, b, dims, preferred_element_type=f32)


def call(body, out_shape, places, arrays, in_specs=None, out_specs=None, grid=(), scratch=(), cost=0, aliases=None, weight=1):
    whole = pl.BlockSpec(memory_space=pltpu.VMEM)
    many = isinstance(out_shape, (list, tuple))
    if in_specs is None:
        in_specs = [whole] * len(arrays)
    if out_specs is None:
        out_specs = [whole] * len(out_shape) if many else whole
    spec = pltpu.PrefetchScalarGridSpec(
        num_scalar_prefetch=0 if places is None else 1,
        grid=grid,
        in_specs=in_specs,
        out_specs=out_specs,
        scratch_shapes=list(scratch),
    )
    moved = weight * sum(a.size * a.dtype.itemsize for a in arrays)
    return pl.pallas_call(
        body,
        out_shape=out_shape,
        grid_spec=spec,
        input_output_aliases=aliases or {},
        compiler_params=pltpu.CompilerParams(vmem_limit_bytes=60 * 2**20),
        cost_estimate=pl.CostEstimate(flops=weight * cost, bytes_accessed=moved, transcendentals=0),
    )(*([] if places is None else [places]), *arrays)


def aligned(index, size):
    return pl.ds(pl.multiple_of(index * size, size), size)


def split_rows(total, lanes):
    high = total.astype(b16).astype(f32)
    row = lax.broadcasted_iota(jnp.int32, (PAD, lanes), 0)
    return jnp.where(row == 0, high, jnp.where(row == 1, total - high, 0.0)).astype(b16)


def joined(rows):
    return rows[0:1].astype(f32) + rows[1:2].astype(f32)


def in_pair(own, across, second, rows):
    own, across = own[:rows], across[:rows]
    first = second == 0
    return jnp.concatenate([jnp.where(first, own, across), jnp.where(first, across, own)], axis=0)


def put_units(feats, turned_head, proj, turned, norm):
    width = turned_head.shape[0]
    quarter = width // 4
    total = jnp.zeros((1, feats.shape[0]), f32)
    for m in range(4):
        span = slice(m * quarter, (m + 1) * quarter)
        part = dot(turned_head[span], feats[...], NT)
        proj[span] = part
        total = total + jnp.sum(part * part, axis=0, keepdims=True)
    length = jnp.sqrt(total + epsilon)
    norm[...] = length
    inverse = 1.0 / length
    for m in range(4):
        span = slice(m * quarter, (m + 1) * quarter)
        turned[span] = (proj[span] * inverse).astype(b16)


def unit_kernel(rows, pairs, at_ref, *refs):
    blocks, turned_head = refs[: 2 * pairs], refs[2 * pairs]
    turned, norm, feats, proj = refs[-4:]
    width = turned_head.shape[0]
    second = at_ref[1]
    step = pl.program_id(0)
    for p in range(pairs):
        own, across = blocks[2 * p], blocks[2 * p + 1]

        @pl.when(step == p)
        def _():
            feats[...] = in_pair(own, across, second, rows)
            first = second == 0
            sides = own[rows:, :rows], across[rows:, :rows]
            turned[width:, :rows] = jnp.where(first, sides[0], sides[1])
            turned[width:, rows:] = jnp.where(first, sides[1], sides[0])

    put_units(feats, turned_head, proj, turned, norm)


def units(pairs, distance, turned_head, carried, places, rows):
    width = turned_head.shape[0]
    tile = 2 * rows
    whole = lambda a: pl.BlockSpec(a.shape, lambda i, at: (0, 0))
    blocks = [block for pair in pairs for block in pair]
    return call(
        lambda *refs: unit_kernel(rows, len(pairs), *refs),
        [
            jax.ShapeDtypeStruct((width + PAD, 8 * rows), b16),
            jax.ShapeDtypeStruct((1, 8 * rows), f32),
        ],
        places,
        [*blocks, turned_head, *carried],
        in_specs=[whole(a) for a in [*blocks, turned_head]]
        + [pl.BlockSpec(memory_space=pl.ANY)] * len(carried),
        out_specs=[
            pl.BlockSpec((width + PAD, tile), lambda i, at: (0, (at[0] + distance + i) % 4)),
            pl.BlockSpec((1, tile), lambda i, at: (0, (at[0] + distance + i) % 4)),
        ],
        grid=(len(pairs),),
        scratch=[pltpu.VMEM((tile, width), b16), pltpu.VMEM((width, tile), f32)],
        cost=2 * tile * width * width * len(pairs),
        aliases={len(blocks) + 2 + n: n for n in range(len(carried))},
    )


def unit_columns(feats, head):
    projected = dot(head, feats, (((0,), (1,)), ((), ())))
    norm = jnp.sqrt(jnp.sum(projected * projected, axis=0, keepdims=True) + epsilon)
    return (projected * (1.0 / norm)).astype(b16), norm


def unit_rows(feats, head, norm):
    return (dot(feats, head, NN) * (1.0 / norm).reshape(-1, 1)).astype(b16)


def tile_slopes(rows, groups, place, bias_ref, img, txt, slopes, by_img):
    width = img.shape[1]
    tile = 2 * rows
    lang = txt[width : width + PAD].astype(f32)
    partner = lang[1:2] * 128.0 + lang[2:3]
    lang = lang[0:1]
    bias = jnp.zeros((1, tile), f32)
    for g in range(groups):
        bias = jnp.where(lang == g, bias_ref[g], bias)
    bias = bias * -log2e
    down = jnp.zeros((1, tile), f32)
    high = 4 * rows
    for m in range(img.shape[0] // high):
        span = slice(m * high, (m + 1) * high)
        index = m * high + lax.broadcasted_iota(jnp.int32, (high, 1), 0)
        ids = ((index // rows * 16 + place) * rows + index % rows).astype(f32)
        cosines = dot(img[span], txt[:width], NN)
        below = 1.0 + jnp.exp2(cosines * (-log2e * logit_scale) + bias)
        gate = pl.reciprocal(below, approx=True)
        gate = gate * (2.0 - below * gate)
        slope = gate - jnp.where(partner == ids, 1.0, 0.0)
        slopes[span, :tile] = slope.astype(b16)
        weighted = slope * cosines
        down = down + jnp.sum(weighted, axis=0, keepdims=True)
        side = by_img[span]
        for k in range(0, tile, by_img.shape[1]):
            side = side + weighted[:, k : k + by_img.shape[1]]
        by_img[span] = side
    return logit_scale * down


def put_text_terms(up, turned, slopes, down):
    slab = turned.shape[0] // 8
    figures = split_rows(down, up.shape[1])
    part = dot(turned[...], slopes, NN)
    for e in range(8):
        at = e * (slab + PAD)
        up[at : at + slab] = part[e * slab : (e + 1) * slab].astype(b16)
        up[at + slab : at + slab + PAD] = figures


def other_kernel(rows, groups, bias_ref, img, turned, txt, slopes, img_sum, up, by_img):
    step = pl.program_id(0)

    @pl.when(step == 0)
    def _():
        by_img[...] = jnp.zeros(by_img.shape, f32)

    down = tile_slopes(rows, groups, bias_ref[groups].astype(jnp.int32), bias_ref, img, txt, slopes.at[0], by_img)
    put_text_terms(up, turned, slopes[0], down)

    @pl.when(step == 3)
    def _():
        img_sum[...] = logit_scale * jnp.sum(by_img[...].T, axis=0, keepdims=True)


def other_tile(img, turned, txt, group_bias, rows):
    count, width = img.shape
    tile = 2 * rows
    height = width + 8 * PAD
    whole = lambda a: pl.BlockSpec(a.shape, lambda i: (0, 0))
    return call(
        lambda *refs: other_kernel(rows, group_bias.shape[0] - 1, *refs),
        [
            jax.ShapeDtypeStruct((4, count, tile), b16),
            jax.ShapeDtypeStruct((1, count), f32),
            jax.ShapeDtypeStruct((height, count), b16),
        ],
        None,
        [group_bias, img, turned, txt],
        in_specs=[
            pl.BlockSpec(memory_space=pltpu.SMEM),
            whole(img),
            whole(turned),
            pl.BlockSpec((width + PAD, tile), lambda i: (0, i)),
        ],
        out_specs=[
            pl.BlockSpec((1, count, tile), lambda i: (i, 0, 0)),
            pl.BlockSpec((1, count), lambda i: (0, 0)),
            pl.BlockSpec((height, tile), lambda i: (0, i)),
        ],
        grid=(4,),
        scratch=[pltpu.VMEM((count, min(128, tile)), f32)],
        cost=4 * width * count * count,
    )


def own_kernel(rows, groups, bias_ref, img, turned, txt, other, *refs):
    other_slopes, other_sum, up, out, by_img, held, both, total = refs
    step = pl.program_id(0)
    width = img.shape[1]
    tile = 2 * rows

    @pl.when(step == 0)
    def _():
        by_img[...] = jnp.zeros(by_img.shape, f32)
        total[...] = jnp.zeros(total.shape, f32)

    both[:, tile:] = other[:width]
    held[:, tile:] = other_slopes[0]
    both[:, :tile] = txt[:width]
    down = tile_slopes(rows, groups, bias_ref[groups].astype(jnp.int32), bias_ref, img, txt, held, by_img)
    put_text_terms(up, turned, held[:, :tile], down)
    total[...] += dot(both[...], held[...], NT)

    @pl.when(step == 3)
    def _():
        slab = width // 8
        sums = logit_scale * jnp.sum(by_img[...].T, axis=0, keepdims=True) + other_sum[...]
        figures = split_rows(sums, sums.shape[1])
        for e in range(8):
            out[e, :slab] = total[e * slab : (e + 1) * slab].astype(b16)
            out[e, slab:] = figures


def own_tile(
    img, turned, txt, other, other_slopes, other_sum, group_bias, rows
):
    count, width = img.shape
    tile = 2 * rows
    height = width + 8 * PAD
    slab = width // 8
    whole = lambda a: pl.BlockSpec(a.shape, lambda i: (0, 0))
    stack = lambda a: pl.BlockSpec(a.shape, lambda i: (0, 0, 0))
    pieces = jax.ShapeDtypeStruct((8, slab + PAD, count), b16)
    return call(
        lambda *refs: own_kernel(rows, group_bias.shape[0] - 1, *refs),
        [jax.ShapeDtypeStruct((height, count), b16), pieces],
        None,
        [group_bias, img, turned, txt, other, other_slopes, other_sum],
        in_specs=[
            pl.BlockSpec(memory_space=pltpu.SMEM),
            whole(img),
            whole(turned),
            pl.BlockSpec((width + PAD, tile), lambda i: (0, i)),
            pl.BlockSpec((width + PAD, tile), lambda i: (0, i)),
            pl.BlockSpec((1, count, tile), lambda i: (i, 0, 0)),
            whole(other_sum),
        ],
        out_specs=[pl.BlockSpec((height, tile), lambda i: (0, i)), stack(pieces)],
        grid=(4,),
        scratch=[
            pltpu.VMEM((count, min(128, tile)), f32),
            pltpu.VMEM((count, 2 * tile), b16),
            pltpu.VMEM((width, 2 * tile), b16),
            pltpu.VMEM((width, count), f32),
        ],
        cost=8 * width * count * count,
    )


def sum_into(out, terms):
    slab = out.shape[0] - PAD
    block, total = terms[0][:slab].astype(f32), joined(terms[0][slab:])
    for term in terms[1:]:
        block, total = block + term[:slab].astype(f32), total + joined(term[slab:])
    out[:slab] = block.astype(b16)
    out[slab:] = split_rows(total, out.shape[1])


def sum_kernel(sizes, at_ref, *refs):
    start = 0
    for size, out in zip(sizes, refs[sum(sizes) :]):
        sum_into(out, refs[start : start + size])
        start += size


def sums(groups, places, rows):
    arrays, specs = [], []
    lanes = 8 * rows
    for term in [term for group in groups for term in group]:
        if isinstance(term, tuple):
            arrays.append(term[0])
            height = term[0].shape[0] // 8
            specs.append(pl.BlockSpec((height, lanes), lambda i, at, n=term[1]: (at[n], i)))
        else:
            arrays.append(term)
            height = term.shape[0]
            specs.append(pl.BlockSpec((height, lanes), lambda i, at: (0, i)))
    count = arrays[0].shape[1]
    return call(
        lambda *refs: sum_kernel([len(group) for group in groups], *refs),
        [jax.ShapeDtypeStruct((height, count), b16)] * len(groups),
        places,
        arrays,
        in_specs=specs,
        out_specs=[pl.BlockSpec((height, lanes), lambda i, at: (0, i))] * len(groups),
        grid=(count // lanes,),
    )


def img_grad_kernel(rows, at_ref, got, unit, norm, feats, blocks, part, grad):
    slab = unit.shape[0]
    up, inner = got[0, :slab].astype(f32), joined(got[0, slab:])
    for n in range(1, 8):
        up, inner = up + got[n, :slab].astype(f32), inner + joined(got[n, slab:])
    up = logit_scale * up - unit[...].astype(f32) * inner
    grad[...] = (up * (1.0 / norm[...])).astype(b16)
    for n in range(8):
        blocks[n] = grad[:, n * rows : (n + 1) * rows]
    part[...] = dot(grad[...], feats[...], NN).astype(b16)


def txt_grad_kernel(rows, at_ref, *refs):
    terms, unit, norm, blocks, (own, give, part, grad) = (
        refs[:5], refs[5], refs[6], refs[7:15], refs[15:]
    )
    slab = unit.shape[0]
    up, inner = terms[0][:slab].astype(f32), joined(terms[0][slab:])
    for term in terms[1:]:
        up, inner = up + term[:slab].astype(f32), inner + joined(term[slab:])
    up = logit_scale * up - unit[...].astype(f32) * inner
    grad[...] = (up * (1.0 / norm[...])).astype(b16)
    for ring in range(4):
        low = grad[:, (2 * ring) * rows : (2 * ring + 1) * rows]
        high = grad[:, (2 * ring + 1) * rows : (2 * ring + 2) * rows]
        own[ring] = jnp.where(at_ref[1] == 0, low, high)
        give[ring] = jnp.where(at_ref[1] == 0, high, low)
    total = None
    for d in range(4):
        cols = grad[:, aligned((at_ref[0] + d) % 4, 2 * rows)]
        term = dot(cols, in_pair(blocks[2 * d], blocks[2 * d + 1], at_ref[1], rows), NN)
        total = term if total is None else total + term
    part[...] = total.astype(b16)


def gradient(kernel, own, terms, unit, norm, feats, halves, places, rows):
    width = feats[0].shape[1]
    slab, count = width // 8, 8 * rows
    whole = lambda a: pl.BlockSpec(a.shape, lambda i, at: (0,) * len(a.shape))
    mine = lambda height: pl.BlockSpec((height, count), lambda i, at: (at[own], 0))
    block = jax.ShapeDtypeStruct((8 // halves, slab, rows), b16)
    part = jax.ShapeDtypeStruct((slab, width), b16)
    return call(
        lambda *refs: kernel(rows, *refs),
        [block] * halves + [part],
        places,
        [term[0] if isinstance(term, tuple) else term for term in terms] + [unit, norm, *feats],
        in_specs=[mine(slab + PAD) if isinstance(term, tuple) else whole(term) for term in terms]
        + [mine(slab), whole(norm)]
        + [whole(a) for a in feats],
        out_specs=[whole(block)] * halves + [whole(part)],
        grid=(1,),
        scratch=[pltpu.VMEM((slab, count), b16)],
        cost=2 * slab * count * width,
        weight=0,
    )


def pick_kernel(core, img, txt, other_img, other_txt, out):
    width = img.shape[1]
    slots = out.shape[0]
    own = width // 128
    third = 2 * img.shape[0] // 3
    img = img[...].astype(f32) + other_img[...].astype(f32)
    txt = txt[...].astype(f32) + other_txt[...].astype(f32)
    part = jnp.concatenate([img, txt], axis=0).astype(b16)
    slot = lax.broadcasted_iota(jnp.int32, (slots, 1), 0)
    feature = lax.broadcasted_iota(jnp.int32, (slots, width), 1)
    base = (slot // 8 * 2 + core[0]) * own
    chosen = jnp.where(feature == base + slot % 8, 1.0, 0.0).astype(b16)
    out[:, : 3 * third] = dot(chosen, part, NT).astype(b16)
    chips = slots // 8
    chip = lax.broadcasted_iota(jnp.int32, (chips, 1), 0)
    feature = lax.broadcasted_iota(jnp.int32, (chips, width), 1)
    chosen = jnp.where(feature == (chip * 2 + core[0]) * own + 8, 1.0, 0.0).astype(b16)
    ninth = dot(chosen, part, NT)
    chip = lax.broadcasted_iota(jnp.int32, (slots, chips), 1)
    rest = jnp.zeros((slots, third), f32)
    for n in range(3):
        spread = jnp.where(slot == chip * 8 + n, 1.0, 0.0).astype(b16)
        rest = rest + dot(spread, ninth[:, n * third : (n + 1) * third].astype(b16), NN)
    out[:, 3 * third :] = rest.astype(b16)


def picked(core, parts):
    slab, width = parts[0].shape
    return call(
        pick_kernel,
        jax.ShapeDtypeStruct((64 * 8, slab * 8 // 3), b16),
        None,
        [core, *parts],
        in_specs=[pl.BlockSpec(memory_space=pltpu.SMEM)]
        + [pl.BlockSpec(memory_space=pltpu.VMEM)] * len(parts),
        cost=8 * 512 * width * slab,
        weight=0,
    )


def head_kernel(got, img_out, txt_out):
    slab = img_out.shape[1] // 8
    third = slab * 2 // 3
    half = third // 2
    for p in range(8):
        img = txt = None
        for other in range(8):
            z, lo, hi, y = p // 2, p % 2, other // 4, other % 4
            block = got[(z * 2 + lo) * 8 + hi * 4 + y].astype(f32)
            img = block if img is None else img + block
            z, lo, hi, y = other // 2, other % 2, p % 2, p // 2
            block = got[(z * 2 + lo) * 8 + hi * 4 + y].astype(f32)
            txt = block if txt is None else txt + block
        at = p * slab
        ninth = 2 * slab
        img_out[0:8, at : at + slab] = img[:, :slab]
        img_out[8:9, at : at + third] = img[0:1, ninth : ninth + third]
        img_out[8:9, at + third : at + slab] = img[1:2, ninth : ninth + half]
        txt_out[0:8, at : at + slab] = txt[:, slab : 2 * slab]
        txt_out[8:9, at : at + half] = txt[1:2, ninth + half : ninth + third]
        txt_out[8:9, at + half : at + slab] = txt[2:3, ninth : ninth + third]


def together(arrays):
    return lax.optimization_barrier(list(arrays))


def pair_lines(own, got, second):
    return jnp.concatenate([jnp.where(second, got, own), jnp.where(second, own, got)], axis=1)


def whole_columns(lines, move, ring):
    got = []
    for d in range(4):
        block = lax.dynamic_index_in_dim(lines, (ring + d) % 4, 0, keepdims=False)
        got.append(send(block, move(d, 0)) if d else block)
    height = got[0].shape[0]
    from_own = jnp.concatenate([got[-d % 4] for d in range(4)] * 2, axis=0)
    return lax.dynamic_slice_in_dim(from_own, (4 - ring) % 4 * height, 4 * height, axis=0)


def shards(image_feat, text_feat, image_head, text_head, group_bias, text_lang, partner):
    rows, width = image_feat.shape
    slab = width // 8
    place = lax.axis_index(DEV)
    z, lo, hi, y, core = place // 32, place // 16 % 2, place // 8 % 2, place // 2 % 4, place % 2

    slots = [(y + d) % 4 * 2 + (hi + e) % 2 for d in range(4) for e in range(2)]
    places = [y, hi, z, lo, core, place % 16, z * 2 + lo, y * 2 + hi, *slots]
    biases = jnp.append(group_bias, (place % 16).astype(f32))
    places, biases, alone = together(
        [jnp.stack(places).astype(jnp.int32), biases, core.astype(jnp.int32).reshape(1)]
    )
    figures = jnp.stack([text_lang, partner // 128, partner % 128]).astype(b16)
    figures = jnp.pad(figures, ((0, PAD - 3), (0, width - rows)))
    text_rows = jnp.concatenate([text_feat, figures], axis=0)
    across = send(text_rows, txt_move(0, 1))
    before = send(text_rows, txt_move(1, 0))
    after = send(text_rows, txt_move(3, 0))
    img_feats = jnp.broadcast_to(together([image_feat, text_rows])[0][None], (8, rows, width))
    img_feats = exchange(img_feats, IMG_GROUPS).reshape(8 * rows, width)
    turned_txt = together([text_head, before])[0].T
    across_after = send(across, txt_move(3, 0))
    across_before = send(across, txt_move(1, 0))
    across_after, before, after, across, turned_txt = together(
        [across_after, before, after, across, turned_txt]
    )
    far = send(before, txt_move(1, 0))
    across_far = send(across_after, txt_move(3, 0))
    txt_blocks = [
        text_rows, across, after, across_after, far, across_far, before, across_before
    ]
    pairs = [(before, across_before), (text_rows, across), (after, across_after)]
    made = units(pairs, 3, turned_txt, (), places, rows)
    unit_txt, norm_txt = units([(far, across_far)], 2, turned_txt, made, places, rows)
    other_txt = send(unit_txt, core_move)
    turned_units, norm_img = unit_columns(img_feats, image_head)
    unit_img = unit_rows(together([img_feats, unit_txt])[0], image_head, norm_img)

    other_slopes, other_sum, other_up = other_tile(
        unit_img, turned_units, other_txt, biases, rows
    )
    back = send(other_up, core_move)
    text_up, img_terms = own_tile(
        unit_img, turned_units, unit_txt, other_txt, other_slopes, other_sum, biases, rows
    )

    def slab_terms(d, e):
        return [(text_up, 8 + 2 * d + e), (back, 8 + 2 * d + e)]

    far, across_far, across_after = sums(
        [slab_terms(2, 0), slab_terms(2, 1), slab_terms(1, 1)], places, rows
    )
    far, across_far, across_after, img_terms = together([far, across_far, across_after, img_terms])
    img_terms = exchange(img_terms, IMG_GROUPS)
    far = send(far, txt_move(1, 0))
    across_far = send(across_far, txt_move(3, 0))
    far, across_far, across_after = together([far, across_far, across_after])
    across_before = send(across_after, txt_move(1, 0))
    (across_after,) = sums([slab_terms(3, 1) + [across_far]], places, rows)
    across_after = send(across_after, txt_move(3, 0))
    far, across_before = together([far, across_before])
    before, after = sums([slab_terms(1, 0) + [far], slab_terms(3, 0)], places, rows)
    across_before, across_after, before, after = together(
        [across_before, across_after, before, after]
    )
    before = send(before, txt_move(1, 0))
    after = send(after, txt_move(3, 0))
    (across,) = sums([slab_terms(0, 1) + [across_before, across_after]], places, rows)
    across = send(across, txt_move(0, 1))

    img_blocks, img_part = gradient(
        img_grad_kernel, 6, [img_terms], turned_units, norm_img, [img_feats], 1, places, rows
    )
    grad_img = exchange(img_blocks, IMG_GROUPS).reshape(width, rows)
    txt_own, txt_give, txt_part = gradient(
        txt_grad_kernel, 7, slab_terms(0, 0) + [before, after, across], unit_txt, norm_txt,
        txt_blocks, 2, places, rows,
    )
    img_theirs = send(img_part, core_move)
    txt_theirs = send(txt_part, core_move)
    txt_got = send(txt_give, txt_move(0, 1))
    heads, txt_got = together([picked(alone, [img_part, txt_part, img_theirs, txt_theirs]), txt_got])
    heads = exchange(heads.reshape(64, 8, -1), CHIP_GROUPS)
    head_shape = jax.ShapeDtypeStruct((width // 128, width), f32)
    image_head_grad, text_head_grad = call(head_kernel, [head_shape] * 2, None, [heads])

    image_grad = dot(grad_img, image_head, (((0,), (1,)), ((), ())))
    grad_txt = whole_columns(pair_lines(txt_own, txt_got, hi), txt_move, y)
    text_grad = dot(grad_txt, text_head, (((0,), (1,)), ((), ())))
    return (image_grad, text_grad, image_head_grad, text_head_grad)


def solution(mesh):
    line = jax.sharding.Mesh(mesh.devices.reshape(-1), (DEV,))
    in_specs = (P(DEV, None), P(DEV, None), P(), P(), P(), P(DEV), P(DEV))
    return jax.shard_map(
        shards, mesh=line, in_specs=in_specs, out_specs=(P(DEV, None),) * 4, check_vma=False
    )
```

```python
import jax
import jax.numpy as jnp
from jax import lax
from jax.experimental import pallas as pl
from jax.experimental.pallas import tpu as pltpu
from jax.sharding import PartitionSpec as P

logit_scale = 64.0
epsilon = 1e-06
log2e = 1.4426950408889634
f32, b16 = jnp.float32, jnp.bfloat16

DEV = "dev"
PLACES = [
    (z, lo, hi, y, c)
    for z in range(4)
    for lo in range(2)
    for hi in range(2)
    for y in range(4)
    for c in range(2)
]


def flat(z, lo, hi, y, c):
    return (z * 2 + lo) * 16 + hi * 8 + y * 2 + c


def img_move(d, e):
    return lambda z, lo, hi, y, c: ((z + d) % 4, lo ^ e, hi, y, c)


def txt_move(d, e):
    return lambda z, lo, hi, y, c: (z, lo ^ e, hi ^ e, (y + d) % 4, c)


def core_move(z, lo, hi, y, c):
    return (z, lo, hi, y, 1 - c)


IMG_GROUPS = [
    [flat(z, lo, hi, y, c) for z in range(4) for lo in range(2)]
    for hi in range(2)
    for y in range(4)
    for c in range(2)
]
TXT_GROUPS = [
    [flat(z, hi ^ b, hi, y, c) for y in range(4) for hi in range(2)]
    for z in range(4)
    for b in range(2)
    for c in range(2)
]
TXT_CORE_GROUPS = [
    [flat(z, hi ^ b, hi, y, c) for c in range(2) for y in range(4) for hi in range(2)]
    for z in range(4)
    for b in range(2)
]
CHIP_GROUPS = [[flat(*p) for p in PLACES if p[4] == c] for c in range(2)]


def send(block, move):
    return lax.ppermute(block, DEV, [(flat(*p), flat(*move(*p))) for p in PLACES])


def exchange(blocks, groups):
    return lax.all_to_all(blocks, DEV, 0, 0, axis_index_groups=groups, tiled=True)


PAD = 16
NN = (((1,), (0,)), ((), ()))
NT = (((1,), (1,)), ((), ()))
TN = (((0,), (0,)), ((), ()))


def dot(a, b, dims):
    return lax.dot_general(a, b, dims, preferred_element_type=f32)


def call(body, out_shape, places, arrays, in_specs=None, out_specs=None, grid=(), scratch=(), cost=0, aliases=None, weight=1):
    whole = pl.BlockSpec(memory_space=pltpu.VMEM)
    many = isinstance(out_shape, (list, tuple))
    if in_specs is None:
        in_specs = [whole] * len(arrays)
    if out_specs is None:
        out_specs = [whole] * len(out_shape) if many else whole
    spec = pltpu.PrefetchScalarGridSpec(
        num_scalar_prefetch=0 if places is None else 1,
        grid=grid,
        in_specs=in_specs,
        out_specs=out_specs,
        scratch_shapes=list(scratch),
    )
    moved = weight * sum(a.size * a.dtype.itemsize for a in arrays)
    return pl.pallas_call(
        body,
        out_shape=out_shape,
        grid_spec=spec,
        input_output_aliases=aliases or {},
        compiler_params=pltpu.CompilerParams(vmem_limit_bytes=60 * 2**20),
        cost_estimate=pl.CostEstimate(flops=weight * cost, bytes_accessed=moved, transcendentals=0),
    )(*([] if places is None else [places]), *arrays)


def aligned(index, size):
    return pl.ds(pl.multiple_of(index * size, size), size)


def split_rows(total, lanes):
    high = total.astype(b16).astype(f32)
    row = lax.broadcasted_iota(jnp.int32, (PAD, lanes), 0)
    return jnp.where(row == 0, high, jnp.where(row == 1, total - high, 0.0)).astype(b16)


def joined(rows):
    return rows[0:1].astype(f32) + rows[1:2].astype(f32)


def in_pair(own, across, second, rows):
    own, across = own[:rows], across[:rows]
    first = second == 0
    return jnp.concatenate([jnp.where(first, own, across), jnp.where(first, across, own)], axis=0)


def put_units(feats, turned_head, proj, turned, norm):
    width = turned_head.shape[0]
    quarter = width // 4
    total = jnp.zeros((1, feats.shape[0]), f32)
    for m in range(4):
        span = slice(m * quarter, (m + 1) * quarter)
        part = dot(turned_head[span], feats[...], NT)
        proj[span] = part
        total = total + jnp.sum(part * part, axis=0, keepdims=True)
    length = jnp.sqrt(total + epsilon)
    norm[...] = length
    inverse = 1.0 / length
    for m in range(4):
        span = slice(m * quarter, (m + 1) * quarter)
        turned[span] = (proj[span] * inverse).astype(b16)


def unit_kernel(rows, pairs, at_ref, *refs):
    blocks, turned_head = refs[: 2 * pairs], refs[2 * pairs]
    turned, norm, feats, proj = refs[-4:]
    width = turned_head.shape[0]
    second = at_ref[1]
    step = pl.program_id(0)
    for p in range(pairs):
        own, across = blocks[2 * p], blocks[2 * p + 1]

        @pl.when(step == p)
        def _():
            feats[...] = in_pair(own, across, second, rows)
            first = second == 0
            sides = own[rows:, :rows], across[rows:, :rows]
            turned[width:, :rows] = jnp.where(first, sides[0], sides[1])
            turned[width:, rows:] = jnp.where(first, sides[1], sides[0])

    put_units(feats, turned_head, proj, turned, norm)


def units(pairs, distance, turned_head, carried, places, rows):
    width = turned_head.shape[0]
    tile = 2 * rows
    whole = lambda a: pl.BlockSpec(a.shape, lambda i, at: (0, 0))
    blocks = [block for pair in pairs for block in pair]
    return call(
        lambda *refs: unit_kernel(rows, len(pairs), *refs),
        [
            jax.ShapeDtypeStruct((width + PAD, 8 * rows), b16),
            jax.ShapeDtypeStruct((1, 8 * rows), f32),
        ],
        places,
        [*blocks, turned_head, *carried],
        in_specs=[whole(a) for a in [*blocks, turned_head]]
        + [pl.BlockSpec(memory_space=pl.ANY)] * len(carried),
        out_specs=[
            pl.BlockSpec((width + PAD, tile), lambda i, at: (0, (at[0] + distance + i) % 4)),
            pl.BlockSpec((1, tile), lambda i, at: (0, (at[0] + distance + i) % 4)),
        ],
        grid=(len(pairs),),
        scratch=[pltpu.VMEM((tile, width), b16), pltpu.VMEM((width, tile), f32)],
        cost=2 * tile * width * width * len(pairs),
        aliases={len(blocks) + 2 + n: n for n in range(len(carried))},
    )


def unit_columns(feats, head):
    projected = dot(head, feats, (((0,), (1,)), ((), ())))
    norm = jnp.sqrt(jnp.sum(projected * projected, axis=0, keepdims=True) + epsilon)
    return (projected * (1.0 / norm)).astype(b16), norm


def unit_rows(feats, head, norm):
    return (dot(feats, head, NN) * (1.0 / norm).reshape(-1, 1)).astype(b16)


def tile_slopes(rows, groups, place, bias_ref, img, txt, slopes, by_img):
    width = img.shape[1]
    tile = 2 * rows
    lang = txt[width : width + PAD].astype(f32)
    partner = lang[1:2] * 128.0 + lang[2:3]
    lang = lang[0:1]
    bias = jnp.zeros((1, tile), f32)
    for g in range(groups):
        bias = jnp.where(lang == g, bias_ref[g], bias)
    bias = bias * -log2e
    down = jnp.zeros((1, tile), f32)
    high = 2 * rows
    for m in range(img.shape[0] // high):
        span = slice(m * high, (m + 1) * high)
        index = m * high + lax.broadcasted_iota(jnp.int32, (high, 1), 0)
        ids = ((index // rows * 16 + place) * rows + index % rows).astype(f32)
        cosines = dot(img[span], txt[:width], NN)
        below = 1.0 + jnp.exp2(cosines * (-log2e * logit_scale) + bias)
        gate = pl.reciprocal(below, approx=True)
        gate = gate * (2.0 - below * gate)
        slope = gate - jnp.where(partner == ids, 1.0, 0.0)
        slopes[span, :tile] = slope.astype(b16)
        weighted = slope * cosines
        down = down + jnp.sum(weighted, axis=0, keepdims=True)
        side = by_img[span]
        for k in range(0, tile, by_img.shape[1]):
            side = side + weighted[:, k : k + by_img.shape[1]]
        by_img[span] = side
    return logit_scale * down


def put_text_terms(up, turned, slopes, down):
    slab = turned.shape[0] // 8
    figures = split_rows(down, up.shape[1])
    part = dot(turned[...], slopes, NN)
    for e in range(8):
        at = e * (slab + PAD)
        up[at : at + slab] = part[e * slab : (e + 1) * slab].astype(b16)
        up[at + slab : at + slab + PAD] = figures


def other_kernel(rows, groups, bias_ref, img, turned, txt, slopes, img_sum, up, by_img):
    step = pl.program_id(0)

    @pl.when(step == 0)
    def _():
        by_img[...] = jnp.zeros(by_img.shape, f32)

    down = tile_slopes(rows, groups, bias_ref[groups].astype(jnp.int32), bias_ref, img, txt, slopes.at[0], by_img)
    put_text_terms(up, turned, slopes[0], down)

    @pl.when(step == 3)
    def _():
        img_sum[...] = logit_scale * jnp.sum(by_img[...].T, axis=0, keepdims=True)


def other_tile(img, turned, txt, group_bias, rows):
    count, width = img.shape
    tile = 2 * rows
    height = width + 8 * PAD
    whole = lambda a: pl.BlockSpec(a.shape, lambda i: (0, 0))
    return call(
        lambda *refs: other_kernel(rows, group_bias.shape[0] - 1, *refs),
        [
            jax.ShapeDtypeStruct((4, count, tile), b16),
            jax.ShapeDtypeStruct((1, count), f32),
            jax.ShapeDtypeStruct((height, count), b16),
        ],
        None,
        [group_bias, img, turned, txt],
        in_specs=[
            pl.BlockSpec(memory_space=pltpu.SMEM),
            whole(img),
            whole(turned),
            pl.BlockSpec((width + PAD, tile), lambda i: (0, i)),
        ],
        out_specs=[
            pl.BlockSpec((1, count, tile), lambda i: (i, 0, 0)),
            pl.BlockSpec((1, count), lambda i: (0, 0)),
            pl.BlockSpec((height, tile), lambda i: (0, i)),
        ],
        grid=(4,),
        scratch=[pltpu.VMEM((count, min(128, tile)), f32)],
        cost=4 * width * count * count,
    )


def own_kernel(rows, groups, bias_ref, img, turned, txt, other, *refs):
    other_slopes, other_sum, up, out, by_img, held, both, total = refs
    step = pl.program_id(0)
    width = img.shape[1]
    tile = 2 * rows

    @pl.when(step == 0)
    def _():
        by_img[...] = jnp.zeros(by_img.shape, f32)
        total[...] = jnp.zeros(total.shape, f32)

    both[:, tile:] = other[:width]
    held[:, tile:] = other_slopes[0]
    both[:, :tile] = txt[:width]
    down = tile_slopes(rows, groups, bias_ref[groups].astype(jnp.int32), bias_ref, img, txt, held, by_img)
    put_text_terms(up, turned, held[:, :tile], down)
    total[...] += dot(both[...], held[...], NT)

    @pl.when(step == 3)
    def _():
        slab = width // 8
        sums = logit_scale * jnp.sum(by_img[...].T, axis=0, keepdims=True) + other_sum[...]
        figures = split_rows(sums, sums.shape[1])
        for e in range(8):
            out[e, :slab] = total[e * slab : (e + 1) * slab].astype(b16)
            out[e, slab:] = figures


def own_tile(
    img, turned, txt, other, other_slopes, other_sum, group_bias, rows
):
    count, width = img.shape
    tile = 2 * rows
    height = width + 8 * PAD
    slab = width // 8
    whole = lambda a: pl.BlockSpec(a.shape, lambda i: (0, 0))
    stack = lambda a: pl.BlockSpec(a.shape, lambda i: (0, 0, 0))
    pieces = jax.ShapeDtypeStruct((8, slab + PAD, count), b16)
    return call(
        lambda *refs: own_kernel(rows, group_bias.shape[0] - 1, *refs),
        [jax.ShapeDtypeStruct((height, count), b16), pieces],
        None,
        [group_bias, img, turned, txt, other, other_slopes, other_sum],
        in_specs=[
            pl.BlockSpec(memory_space=pltpu.SMEM),
            whole(img),
            whole(turned),
            pl.BlockSpec((width + PAD, tile), lambda i: (0, i)),
            pl.BlockSpec((width + PAD, tile), lambda i: (0, i)),
            pl.BlockSpec((1, count, tile), lambda i: (i, 0, 0)),
            whole(other_sum),
        ],
        out_specs=[pl.BlockSpec((height, tile), lambda i: (0, i)), stack(pieces)],
        grid=(4,),
        scratch=[
            pltpu.VMEM((count, min(128, tile)), f32),
            pltpu.VMEM((count, 2 * tile), b16),
            pltpu.VMEM((width, 2 * tile), b16),
            pltpu.VMEM((width, count), f32),
        ],
        cost=8 * width * count * count,
    )


def sum_into(out, terms):
    slab = out.shape[0] - PAD
    block, total = terms[0][:slab].astype(f32), joined(terms[0][slab:])
    for term in terms[1:]:
        block, total = block + term[:slab].astype(f32), total + joined(term[slab:])
    out[:slab] = block.astype(b16)
    out[slab:] = split_rows(total, out.shape[1])


def sum_kernel(sizes, at_ref, *refs):
    start = 0
    for size, out in zip(sizes, refs[sum(sizes) :]):
        sum_into(out, refs[start : start + size])
        start += size


def sums(groups, places, rows):
    arrays, specs = [], []
    lanes = 8 * rows
    for term in [term for group in groups for term in group]:
        if isinstance(term, tuple):
            arrays.append(term[0])
            height = term[0].shape[0] // 8
            specs.append(pl.BlockSpec((height, lanes), lambda i, at, n=term[1]: (at[n], i)))
        else:
            arrays.append(term)
            height = term.shape[0]
            specs.append(pl.BlockSpec((height, lanes), lambda i, at: (0, i)))
    count = arrays[0].shape[1]
    return call(
        lambda *refs: sum_kernel([len(group) for group in groups], *refs),
        [jax.ShapeDtypeStruct((height, count), b16)] * len(groups),
        places,
        arrays,
        in_specs=specs,
        out_specs=[pl.BlockSpec((height, lanes), lambda i, at: (0, i))] * len(groups),
        grid=(count // lanes,),
    )


def img_grad_kernel(rows, at_ref, got, unit, norm, feats, blocks, part, grad):
    slab = unit.shape[0]
    up, inner = got[0, :slab].astype(f32), joined(got[0, slab:])
    for n in range(1, 8):
        up, inner = up + got[n, :slab].astype(f32), inner + joined(got[n, slab:])
    up = logit_scale * up - unit[...].astype(f32) * inner
    grad[...] = (up * (1.0 / norm[...])).astype(b16)
    for n in range(8):
        blocks[n] = grad[:, n * rows : (n + 1) * rows]
    part[...] = dot(grad[...], feats[...], NN).astype(b16)


def txt_grad_kernel(rows, at_ref, *refs):
    terms, unit, norm, blocks, (own, give, part, grad) = (
        refs[:5], refs[5], refs[6], refs[7:15], refs[15:]
    )
    slab = unit.shape[0]
    up, inner = terms[0][:slab].astype(f32), joined(terms[0][slab:])
    for term in terms[1:]:
        up, inner = up + term[:slab].astype(f32), inner + joined(term[slab:])
    up = logit_scale * up - unit[...].astype(f32) * inner
    grad[...] = (up * (1.0 / norm[...])).astype(b16)
    for ring in range(4):
        low = grad[:, (2 * ring) * rows : (2 * ring + 1) * rows]
        high = grad[:, (2 * ring + 1) * rows : (2 * ring + 2) * rows]
        own[ring] = jnp.where(at_ref[1] == 0, low, high)
        give[ring] = jnp.where(at_ref[1] == 0, high, low)
    total = None
    for d in range(4):
        cols = grad[:, aligned((at_ref[0] + d) % 4, 2 * rows)]
        term = dot(cols, in_pair(blocks[2 * d], blocks[2 * d + 1], at_ref[1], rows), NN)
        total = term if total is None else total + term
    part[...] = total.astype(b16)


def gradient(kernel, own, terms, unit, norm, feats, halves, places, rows):
    width = feats[0].shape[1]
    slab, count = width // 8, 8 * rows
    whole = lambda a: pl.BlockSpec(a.shape, lambda i, at: (0,) * len(a.shape))
    mine = lambda height: pl.BlockSpec((height, count), lambda i, at: (at[own], 0))
    block = jax.ShapeDtypeStruct((8 // halves, slab, rows), b16)
    part = jax.ShapeDtypeStruct((slab, width), b16)
    return call(
        lambda *refs: kernel(rows, *refs),
        [block] * halves + [part],
        places,
        [term[0] if isinstance(term, tuple) else term for term in terms] + [unit, norm, *feats],
        in_specs=[mine(slab + PAD) if isinstance(term, tuple) else whole(term) for term in terms]
        + [mine(slab), whole(norm)]
        + [whole(a) for a in feats],
        out_specs=[whole(block)] * halves + [whole(part)],
        grid=(1,),
        scratch=[pltpu.VMEM((slab, count), b16)],
        cost=2 * slab * count * width,
        weight=0,
    )


def pick_kernel(core, img, txt, other_img, other_txt, out):
    width = img.shape[1]
    slots = out.shape[0]
    own = width // 128
    third = 2 * img.shape[0] // 3
    img = img[...].astype(f32) + other_img[...].astype(f32)
    txt = txt[...].astype(f32) + other_txt[...].astype(f32)
    part = jnp.concatenate([img, txt], axis=0).astype(b16)
    slot = lax.broadcasted_iota(jnp.int32, (slots, 1), 0)
    feature = lax.broadcasted_iota(jnp.int32, (slots, width), 1)
    base = (slot // 8 * 2 + core[0]) * own
    chosen = jnp.where(feature == base + slot % 8, 1.0, 0.0).astype(b16)
    out[:, : 3 * third] = dot(chosen, part, NT).astype(b16)
    chips = slots // 8
    chip = lax.broadcasted_iota(jnp.int32, (chips, 1), 0)
    feature = lax.broadcasted_iota(jnp.int32, (chips, width), 1)
    chosen = jnp.where(feature == (chip * 2 + core[0]) * own + 8, 1.0, 0.0).astype(b16)
    ninth = dot(chosen, part, NT)
    chip = lax.broadcasted_iota(jnp.int32, (slots, chips), 1)
    rest = jnp.zeros((slots, third), f32)
    for n in range(3):
        spread = jnp.where(slot == chip * 8 + n, 1.0, 0.0).astype(b16)
        rest = rest + dot(spread, ninth[:, n * third : (n + 1) * third].astype(b16), NN)
    out[:, 3 * third :] = rest.astype(b16)


def picked(core, parts):
    slab, width = parts[0].shape
    return call(
        pick_kernel,
        jax.ShapeDtypeStruct((64 * 8, slab * 8 // 3), b16),
        None,
        [core, *parts],
        in_specs=[pl.BlockSpec(memory_space=pltpu.SMEM)]
        + [pl.BlockSpec(memory_space=pltpu.VMEM)] * len(parts),
        cost=8 * 512 * width * slab,
        weight=0,
    )


def head_kernel(got, img_out, txt_out):
    slab = img_out.shape[1] // 8
    third = slab * 2 // 3
    half = third // 2
    for p in range(8):
        img = txt = None
        for other in range(8):
            z, lo, hi, y = p // 2, p % 2, other // 4, other % 4
            block = got[(z * 2 + lo) * 8 + hi * 4 + y].astype(f32)
            img = block if img is None else img + block
            z, lo, hi, y = other // 2, other % 2, p % 2, p // 2
            block = got[(z * 2 + lo) * 8 + hi * 4 + y].astype(f32)
            txt = block if txt is None else txt + block
        at = p * slab
        ninth = 2 * slab
        img_out[0:8, at : at + slab] = img[:, :slab]
        img_out[8:9, at : at + third] = img[0:1, ninth : ninth + third]
        img_out[8:9, at + third : at + slab] = img[1:2, ninth : ninth + half]
        txt_out[0:8, at : at + slab] = txt[:, slab : 2 * slab]
        txt_out[8:9, at : at + half] = txt[1:2, ninth + half : ninth + third]
        txt_out[8:9, at + half : at + slab] = txt[2:3, ninth : ninth + third]


def together(arrays):
    return lax.optimization_barrier(list(arrays))


def pair_lines(own, got, second):
    return jnp.concatenate([jnp.where(second, got, own), jnp.where(second, own, got)], axis=1)


def whole_columns(lines, move, ring):
    got = []
    for d in range(4):
        block = lax.dynamic_index_in_dim(lines, (ring + d) % 4, 0, keepdims=False)
        got.append(send(block, move(d, 0)) if d else block)
    height = got[0].shape[0]
    from_own = jnp.concatenate([got[-d % 4] for d in range(4)] * 2, axis=0)
    return lax.dynamic_slice_in_dim(from_own, (4 - ring) % 4 * height, 4 * height, axis=0)


def shards(image_feat, text_feat, image_head, text_head, group_bias, text_lang, partner):
    rows, width = image_feat.shape
    slab = width // 8
    place = lax.axis_index(DEV)
    z, lo, hi, y, core = place // 32, place // 16 % 2, place // 8 % 2, place // 2 % 4, place % 2

    slots = [(y + d) % 4 * 2 + (hi + e) % 2 for d in range(4) for e in range(2)]
    places = [y, hi, z, lo, core, place % 16, z * 2 + lo, y * 2 + hi, *slots]
    biases = jnp.append(group_bias, (place % 16).astype(f32))
    places, biases, alone = together(
        [jnp.stack(places).astype(jnp.int32), biases, core.astype(jnp.int32).reshape(1)]
    )
    figures = jnp.stack([text_lang, partner // 128, partner % 128]).astype(b16)
    figures = jnp.pad(figures, ((0, PAD - 3), (0, width - rows)))
    text_rows = jnp.concatenate([text_feat, figures], axis=0)
    img_feats = exchange(jnp.broadcast_to(image_feat[None], (8, rows, width)), IMG_GROUPS)
    img_feats = img_feats.reshape(8 * rows, width)
    across = send(text_rows, txt_move(0, 1))
    before = send(text_rows, txt_move(1, 0))
    after = send(text_rows, txt_move(3, 0))
    turned_txt = together([text_head, before])[0].T
    across_after = send(across, txt_move(3, 0))
    across_before = send(across, txt_move(1, 0))
    across_after, before, after, across, turned_txt = together(
        [across_after, before, after, across, turned_txt]
    )
    far = send(before, txt_move(1, 0))
    across_far = send(across_after, txt_move(3, 0))
    txt_blocks = [
        text_rows, across, after, across_after, far, across_far, before, across_before
    ]
    pairs = [(before, across_before), (text_rows, across), (after, across_after)]
    made = units(pairs, 3, turned_txt, (), places, rows)
    unit_txt, norm_txt = units([(far, across_far)], 2, turned_txt, made, places, rows)
    other_txt = send(unit_txt, core_move)
    turned_units, norm_img = unit_columns(img_feats, image_head)
    unit_img = unit_rows(together([img_feats, unit_txt])[0], image_head, norm_img)

    other_slopes, other_sum, other_up = other_tile(
        unit_img, turned_units, other_txt, biases, rows
    )
    back = send(other_up, core_move)
    text_up, img_terms = own_tile(
        unit_img, turned_units, unit_txt, other_txt, other_slopes, other_sum, biases, rows
    )

    def slab_terms(d, e):
        return [(text_up, 8 + 2 * d + e), (back, 8 + 2 * d + e)]

    far, across_far, across_after = sums(
        [slab_terms(2, 0), slab_terms(2, 1), slab_terms(1, 1)], places, rows
    )
    far, across_far, across_after, img_terms = together([far, across_far, across_after, img_terms])
    img_terms = exchange(img_terms, IMG_GROUPS)
    far = send(far, txt_move(1, 0))
    across_far = send(across_far, txt_move(3, 0))
    far, across_far, across_after = together([far, across_far, across_after])
    across_before = send(across_after, txt_move(1, 0))
    (across_after,) = sums([slab_terms(3, 1) + [across_far]], places, rows)
    across_after = send(across_after, txt_move(3, 0))
    far, across_before = together([far, across_before])
    before, after = sums([slab_terms(1, 0) + [far], slab_terms(3, 0)], places, rows)
    across_before, across_after, before, after = together(
        [across_before, across_after, before, after]
    )
    before = send(before, txt_move(1, 0))
    after = send(after, txt_move(3, 0))
    (across,) = sums([slab_terms(0, 1) + [across_before, across_after]], places, rows)
    across = send(across, txt_move(0, 1))

    img_blocks, img_part = gradient(
        img_grad_kernel, 6, [img_terms], turned_units, norm_img, [img_feats], 1, places, rows
    )
    grad_img = exchange(img_blocks, IMG_GROUPS).reshape(width, rows)
    txt_own, txt_give, txt_part = gradient(
        txt_grad_kernel, 7, slab_terms(0, 0) + [before, after, across], unit_txt, norm_txt,
        txt_blocks, 2, places, rows,
    )
    img_theirs = send(img_part, core_move)
    txt_theirs = send(txt_part, core_move)
    txt_got = send(txt_give, txt_move(0, 1))
    heads, txt_got = together([picked(alone, [img_part, txt_part, img_theirs, txt_theirs]), txt_got])
    heads = exchange(heads.reshape(64, 8, -1), CHIP_GROUPS)
    head_shape = jax.ShapeDtypeStruct((width // 128, width), f32)
    image_head_grad, text_head_grad = call(head_kernel, [head_shape] * 2, None, [heads])

    image_grad = dot(grad_img, image_head, (((0,), (1,)), ((), ())))
    grad_txt = whole_columns(pair_lines(txt_own, txt_got, hi), txt_move, y)
    text_grad = dot(grad_txt, text_head, (((0,), (1,)), ((), ())))
    return (image_grad, text_grad, image_head_grad, text_head_grad)


def solution(mesh):
    line = jax.sharding.Mesh(mesh.devices.reshape(-1), (DEV,))
    in_specs = (P(DEV, None), P(DEV, None), P(), P(), P(), P(DEV), P(DEV))
    return jax.shard_map(
        shards, mesh=line, in_specs=in_specs, out_specs=(P(DEV, None),) * 4, check_vma=False
    )
```
